32 devices in a mesh: group: 2 (over x), inst: 8 (over z, y), tp: 2 (over core).
Axes of the slice: x: 2, y: 2, z: 4, core: 2. Of those that a mesh axis runs over, the one named last changes fastest.
Arguments:
- hidden_new: bfloat16 [2, 384, 5120], P(None, ('group', 'inst'), 'tp'), parts along dimension 1, may hold values from -6 to 6
- queries: bfloat16 [2, 384, 4096], P(None, ('group', 'inst'), 'tp'), parts along dimension 1
- kv_cache: bfloat16 [384, 2, 144, 512], P(('group', 'inst'), None, None, 'tp'), parts along dimension 0
- lengths: int32 [384], P(('group', 'inst')), parts along dimension 0, may hold values from 8 to 142
- destination: int32 [384], P(('group', 'inst')), parts along dimension 0, may hold values from 0 to 191, as said below
- key_weight: bfloat16 [5120, 512], P('tp'), may hold values from -0.078125 to 0.078125
- value_weight: bfloat16 [5120, 512], P('tp'), may hold values from -0.078125 to 0.078125
- key_gain: bfloat16 [128], replicated, may hold values from 0.099609375 to 1.8984375
Outputs:
- attended_out: bfloat16 [2, 384, 4096], P(None, ('group', 'inst'), 'tp'), parts along dimension 1
- moved_cache: bfloat16 [384, 2, 144, 512], P(('group', 'inst'), None, None, 'tp'), parts along dimension 0
The draws below stay inside these ranges and needn't reach their ends.
There are 2 independent parts, one for each index of `group`. The reference program is written for one: setup_inputs(seed, part) draws one part's arguments, and reference() takes and returns one part's arrays. A program takes and returns all parts, laid end to end along the dimension named above; an argument that names none is the same for every part. Nothing has to cross between parts.
Inputs may be any that keep to these rules, and one draw needn't show every extreme that they name: `destination`: A permutation of the 192 slots (slot = instance * 24 + position on the instance). A request that stays on its instance keeps its slot; an instance sends at most one request to any other instance and receives at most one from it.
All inputs are finite; a program needn't handle non-finite values.
Results may differ from the reference program's by a relative error of at most 0.0051.
Values may be sent and summed in bfloat16 or wider, within the bound.
No kernel may reach another device: no remote copies, remote signals or barrier semaphores. Data moves between devices by JAX's collectives and lax.ppermute only.
A program may use at most 128 MiB of HBM per device.

```python
import math
import jax
import jax.numpy as jnp
from jax import lax

D = 5120
QH = 32
KVH = 4
HD = 128
REQ_DEV = 24
CAP = 144
STEPS = 2
MOVES = 7
REQS = 192
N_INST = 8


def plan(key):
    key = jax.random.fold_in(key, 501)
    parts = jax.random.split(key, 4)
    reach = jax.random.randint(parts[0], (N_INST, 1), 8 + CAP // 16, CAP - 1)
    fraction = jax.random.randint(parts[1], (N_INST, REQ_DEV), 0, 1 << 20)
    spans = 8 + fraction * (reach - 7) // (1 << 20)
    forced_at = jax.random.randint(parts[2], (), 0, N_INST * REQ_DEV)
    flat_len = jnp.where(jnp.arange(N_INST * REQ_DEV) == forced_at, CAP - 2, spans.reshape(-1))
    spans = flat_len.reshape(N_INST, REQ_DEV)
    inst_ids = jnp.arange(N_INST)
    slot_ids = jnp.arange(REQ_DEV)
    load_key = jnp.sum(spans, axis=1) * N_INST + inst_ids
    order_key = spans * REQ_DEV + slot_ids[None, :]
    rank_asc = jnp.argsort(jnp.argsort(order_key, axis=1), axis=1)
    xor_masks = jax.random.permutation(parts[3], N_INST - 1)[:MOVES] + 1
    placed = (inst_ids[:, None] * REQ_DEV + slot_ids[None, :]).reshape(-1)
    for round_index in range(MOVES):
        partner = jnp.bitwise_xor(inst_ids, xor_masks[round_index])
        is_busy = load_key > load_key[partner]
        wanted = jnp.where(is_busy, REQ_DEV - 1 - round_index, round_index)
        chosen = jnp.sum(jnp.where(rank_asc == wanted[:, None], slot_ids[None, :], 0), axis=1)
        source = inst_ids * REQ_DEV + chosen
        target = partner * REQ_DEV + chosen[partner]
        placed = placed.at[source].set(target)
    return (flat_len.astype(jnp.int32), placed.astype(jnp.int32))


def cache_keys(key):
    return jax.random.normal(jax.random.fold_in(key, 777), (REQS, CAP, KVH * HD), jnp.float32)


def draw_lengths(key, part):
    return plan(key)[0]


def draw_destination(key, part):
    return plan(key)[1]


def draw_kv_cache(key, part):
    key_base = cache_keys(key)
    key = jax.random.fold_in(key, 11)
    stored_values = jax.random.normal(key, (REQS, CAP, KVH * HD), jnp.float32)
    return jnp.stack([key_base, stored_values], axis=1).astype(jnp.bfloat16)


def draw_queries(key, part):
    key = jax.random.fold_in(key, 12)
    parts = jax.random.split(key, 1)
    result = jax.random.normal(parts[0], (STEPS, REQS, QH * HD), jnp.float32)
    return result.astype(jnp.bfloat16)


def block_levels(stream_key, shape, cuts, least, high):
    def one(dim, blocks):
        draws = jax.random.uniform(jax.random.fold_in(jax.random.fold_in(stream_key, 6), dim), (blocks,), jnp.float32, least / len(cuts), high / len(cuts))
        return jnp.repeat(jnp.exp(draws), shape[dim] // blocks).reshape((-1,) + (1,) * (len(shape) - dim - 1))

    factor_of = one(*cuts[0])
    for cut in cuts[1:]:
        factor_of = factor_of * one(*cut)
    return factor_of


def gaussian(stream_key, extent, scale, bound, cuts=(), kind=jnp.bfloat16):
    loudness = block_levels(stream_key, extent, cuts, -0.22, 0.18) if cuts else 1.0
    entries = jax.random.normal(stream_key, extent, jnp.float32) * scale * loudness
    return jnp.minimum(jnp.maximum(entries, -bound), bound).astype(kind)


def setup_inputs(seed: int = 0, part: int = 0) -> dict:
    streams_of = jax.random.split(jax.random.key(seed), 9)
    part_splits = jax.random.split(jax.random.fold_in(streams_of[8], part), 9)
    hidden_new = gaussian(part_splits[0], (STEPS, REQS, D), 1.0, 6.0, ((1, 8), (2, 2)))
    queries = draw_queries(jax.random.fold_in(jax.random.fold_in(streams_of[8], part), 71), part)
    kv_cache = draw_kv_cache(jax.random.fold_in(jax.random.fold_in(streams_of[8], part), 71), part)
    lengths = draw_lengths(jax.random.fold_in(jax.random.fold_in(streams_of[8], part), 71), part)
    destination = draw_destination(jax.random.fold_in(jax.random.fold_in(streams_of[8], part), 71), part)
    key_weight = gaussian(streams_of[5], (D, KVH * HD), D ** -0.5, 0.078125, ((0, 2),))
    value_weight = gaussian(streams_of[6], (D, KVH * HD), D ** -0.5, 0.078125, ((0, 2),))
    key_gain = jnp.clip(1.0 + 0.18 * jax.random.normal(streams_of[7], (HD,), jnp.float32), 0.099609375, 1.8984375).astype(jnp.bfloat16)
    return dict(hidden_new=hidden_new, queries=queries, kv_cache=kv_cache, lengths=lengths, destination=destination, key_weight=key_weight, value_weight=value_weight, key_gain=key_gain)


ROPE_BASE = 1000000.0
NORM_EPS = 1e-06

def place_keys(projected, gain_vector, positions):
    row_count, step_count, lane_width = projected.shape
    head_count = lane_width // HD
    pieces = projected.reshape(row_count, step_count, head_count, HD)
    pieces = pieces * lax.rsqrt(lax.optimization_barrier(jnp.mean(pieces * pieces, axis=-1, keepdims=True)) + NORM_EPS)
    pieces = pieces * gain_vector.astype(jnp.float32)
    half_dim = HD // 2
    inverse = jnp.exp(-math.log(ROPE_BASE) * 2.0 * jnp.arange(half_dim, dtype=jnp.float32) / HD)
    angles = positions.astype(jnp.float32)[:, :, None, None] * inverse
    cosine = jnp.cos(angles)
    sine_part = jnp.sin(angles)
    front = pieces[..., :half_dim]
    back = pieces[..., half_dim:]
    turned = jnp.concatenate([front * cosine - back * sine_part, back * cosine + front * sine_part], axis=-1)
    return turned.reshape(row_count, step_count, lane_width).astype(jnp.bfloat16)

def attend(queries, kv_rows, lengths, new_keys, new_values):
    row_count, step_count, query_width = queries.shape
    capacity = kv_rows.shape[2]
    lane_width = kv_rows.shape[3]
    head_count = lane_width // HD
    group_size = query_width // lane_width
    grouped = queries.reshape(row_count, step_count, head_count, group_size, HD).astype(jnp.float32)
    cached_keys = kv_rows[:, 0].reshape(row_count, capacity, head_count, HD).astype(jnp.float32)
    cached_values = kv_rows[:, 1].reshape(row_count, capacity, head_count, HD).astype(jnp.float32)
    fresh_keys = new_keys.reshape(row_count, step_count, head_count, HD).astype(jnp.float32)
    fresh_values = new_values.reshape(row_count, step_count, head_count, HD).astype(jnp.float32)
    factor = 1.0 / math.sqrt(HD)
    cache_scores = jnp.einsum('rskgd,rckd->rskgc', grouped, cached_keys) * factor
    fresh_scores = jnp.einsum('rskgd,rtkd->rskgt', grouped, fresh_keys) * factor
    live = jnp.arange(capacity, dtype=jnp.int32)[None, None, None, None, :] < lengths[:, None, None, None, None]
    cache_scores = jnp.where(live, cache_scores, -jnp.inf)
    causal = jnp.arange(step_count)[None, :] <= jnp.arange(step_count)[:, None]
    fresh_scores = jnp.where(causal[None, :, None, None, :], fresh_scores, -jnp.inf)
    peak_score = jnp.maximum(lax.optimization_barrier(jnp.max(cache_scores, axis=-1)), lax.optimization_barrier(jnp.max(fresh_scores, axis=-1)))[..., None]
    cache_weights = jnp.exp(cache_scores - peak_score)
    fresh_weights = jnp.exp(fresh_scores - peak_score)
    normaliser = lax.optimization_barrier(jnp.sum(cache_weights, axis=-1, keepdims=True)) + lax.optimization_barrier(jnp.sum(fresh_weights, axis=-1, keepdims=True))
    cache_weights = (cache_weights / normaliser).astype(jnp.bfloat16).astype(jnp.float32)
    fresh_weights = (fresh_weights / normaliser).astype(jnp.bfloat16).astype(jnp.float32)
    mixture = jnp.einsum('rskgc,rckd->rskgd', cache_weights, cached_values)
    mixture = mixture + jnp.einsum('rskgt,rtkd->rskgd', fresh_weights, fresh_values)
    return mixture.reshape(row_count, step_count, query_width).astype(jnp.bfloat16)

def append(kv_rows, lengths, new_keys, new_values):
    capacity = kv_rows.shape[2]
    step_count = new_keys.shape[1]
    position = jnp.arange(capacity, dtype=jnp.int32)[None, :, None]
    live = position < lengths[:, None, None]
    stored_keys = jnp.where(live, kv_rows[:, 0], jnp.zeros((), jnp.bfloat16))
    stored_values = jnp.where(live, kv_rows[:, 1], jnp.zeros((), jnp.bfloat16))
    for step_index in range(step_count):
        landing = position == (lengths + step_index)[:, None, None]
        stored_keys = jnp.where(landing, new_keys[:, step_index][:, None, :], stored_keys)
        stored_values = jnp.where(landing, new_values[:, step_index][:, None, :], stored_values)
    return jnp.stack([stored_keys, stored_values], axis=1)

def reference(hidden_new, queries, kv_cache, lengths, destination, key_weight, value_weight, key_gain):
    hidden_flat = hidden_new.reshape(STEPS * REQS, D)
    key_raw = jnp.dot(hidden_flat, key_weight, preferred_element_type=jnp.float32).reshape(STEPS, REQS, KVH * HD)
    value_raw = jnp.dot(hidden_flat, value_weight, preferred_element_type=jnp.float32).reshape(STEPS, REQS, KVH * HD)
    positions = lengths[:, None] + jnp.arange(STEPS, dtype=jnp.int32)[None, :]
    new_keys = place_keys(jnp.swapaxes(key_raw, 0, 1), key_gain, positions)
    new_values = jnp.swapaxes(value_raw, 0, 1).astype(jnp.bfloat16)
    attended = attend(jnp.swapaxes(queries, 0, 1), kv_cache, lengths, new_keys, new_values)
    appended = append(kv_cache, lengths, new_keys, new_values)
    root = jnp.argsort(destination).astype(jnp.int32)
    return (jnp.swapaxes(attended[root], 0, 1), appended[root])
```

```python
import functools
import math

import jax
import jax.numpy as jnp
from jax import lax
from jax.experimental import pallas as pl
from jax.experimental.pallas import tpu as pltpu
from jax.sharding import PartitionSpec as P

HD = 128
ROPE_BASE = 1000000.0
NORM_EPS = 1e-06
VMEM_LIMIT = 48 * 1024 * 1024


def peer_after(index, shift, count):
    if count & (count - 1) == 0:
        return index ^ shift
    return (index + shift) % count


def peer_before(index, shift, count):
    if count & (count - 1) == 0:
        return index ^ shift
    return (index + count - shift) % count


def pack_kernel(count, dest_ref, kv_ref, *refs):
    outs, pick_ref, sems = refs[: count - 1], refs[count - 1], refs[count]
    rows = dest_ref.shape[0]
    me = lax.axis_index("inst")
    for peer in range(count):
        pick_ref[peer] = 0

    def note(row, carry):
        pick_ref[dest_ref[row] // rows] = row
        return carry

    lax.fori_loop(0, rows, note, 0)
    copies = []
    for shift in range(1, count):
        row = pick_ref[peer_after(me, shift, count)]
        copy = pltpu.make_async_copy(kv_ref.at[row], outs[shift - 1], sems.at[shift - 1])
        copy.start()
        copies.append(copy)
    for copy in copies:
        copy.wait()


def pack(kv_cache, destination, count):
    block = jax.ShapeDtypeStruct(kv_cache.shape[1:], kv_cache.dtype)
    smem = pl.BlockSpec(memory_space=pltpu.SMEM)
    hbm = pl.BlockSpec(memory_space=pl.ANY)
    outs = pl.pallas_call(
        functools.partial(pack_kernel, count),
        out_shape=[block] * (count - 1) + [jax.ShapeDtypeStruct((count,), jnp.int32)],
        in_specs=[smem, hbm],
        out_specs=[hbm] * (count - 1) + [smem],
        scratch_shapes=[pltpu.SemaphoreType.DMA((count - 1,))],
        name="pack",
    )(destination, kv_cache)
    return outs[:-1], outs[-1]


def project_kernel(hidden_ref, key_ref, value_ref, own_ref, other_ref, total):
    step = pl.program_id(0)
    width = key_ref.shape[1]

    @pl.when(step == 0)
    def _():
        total[...] = jnp.zeros_like(total)

    steps, rows, depth = hidden_ref.shape
    hidden = hidden_ref[...].reshape(steps * rows, depth)
    total[:, :width] += jnp.dot(hidden, key_ref[...], preferred_element_type=jnp.float32)
    total[:, width:] += jnp.dot(hidden, value_ref[...], preferred_element_type=jnp.float32)

    @pl.when(step == pl.num_programs(0) - 1)
    def _():
        half = width // 2
        me = lax.axis_index("tp")
        for ref, core in ((own_ref, me), (other_ref, 1 - me)):
            at = pl.multiple_of(core * half, half)
            ref[:, :half] = total[:, pl.ds(at, half)]
            ref[:, half:] = total[:, pl.ds(pl.multiple_of(width + at, half), half)]


def project(hidden_new, key_weight, value_weight):
    steps, rows, depth = hidden_new.shape
    width = key_weight.shape[1]
    part = depth // 5
    shape = jax.ShapeDtypeStruct((steps * rows, width), jnp.float32)
    whole = pl.BlockSpec((steps * rows, width), lambda i: (0, 0))
    return pl.pallas_call(
        project_kernel,
        grid=(depth // part,),
        out_shape=[shape, shape],
        in_specs=[
            pl.BlockSpec((steps, rows, part), lambda i: (0, 0, i)),
            pl.BlockSpec((part, width), lambda i: (i, 0)),
            pl.BlockSpec((part, width), lambda i: (i, 0)),
        ],
        out_specs=[whole, whole],
        scratch_shapes=[pltpu.VMEM((steps * rows, 2 * width), jnp.float32)],
        compiler_params=pltpu.CompilerParams(vmem_limit_bytes=VMEM_LIMIT),
        cost_estimate=pl.CostEstimate(
            flops=4 * steps * rows * depth * width,
            bytes_accessed=4 * depth * width,
            transcendentals=0,
        ),
        name="project",
    )(hidden_new, key_weight, value_weight)


def attend_kernel(
    count,
    block,
    length_ref,
    pick_ref,
    own_ref,
    got_ref,
    gain_ref,
    cos_ref,
    sin_ref,
    query_ref,
    kv_ref,
    moved_ref,
    mixed_ref,
    *refs,
):
    small_refs, (fresh, query_rows, mixed) = refs[: count - 1], refs[count - 1 :]
    part = pl.program_id(0)
    steps, rows, query_width = query_ref.shape
    capacity, lanes = kv_ref.shape[2:]
    heads = lanes // HD
    group = query_width // lanes
    per_head = steps * group
    per_row = heads * per_head

    def place(step, head, member):
        return head * per_head + step * group + member

    def spot(head, member):
        return slice((head * group + member) * HD, (head * group + member + 1) * HD)

    @pl.when(part == 0)
    def _():
        raw = own_ref[...] + got_ref[...]
        gain = gain_ref[...].astype(jnp.float32)
        for head in range(heads):
            at = slice(head * HD, (head + 1) * HD)
            piece = raw[:, at]
            mean = jnp.mean(piece * piece, axis=-1, keepdims=True)
            piece = piece * lax.rsqrt(mean + NORM_EPS) * gain
            swapped = jnp.concatenate([piece[:, HD // 2 :], piece[:, : HD // 2]], axis=1)
            turned = piece * cos_ref[...] + swapped * sin_ref[...]
            fresh[0, :, at] = turned.astype(jnp.bfloat16).astype(jnp.float32)
        fresh[1] = raw[:, lanes:].astype(jnp.bfloat16).astype(jnp.float32)
        for step in range(steps):
            for head in range(heads):
                for member in range(group):
                    query_rows[pl.ds(place(step, head, member), rows, stride=per_row), :] = (
                        query_ref[step, :, spot(head, member)].astype(jnp.float32)
                    )

    position = lax.broadcasted_iota(jnp.int32, (capacity, lanes), 0)
    lane_head = lax.broadcasted_iota(jnp.int32, (per_row, lanes), 1) // HD
    row_head = lax.broadcasted_iota(jnp.int32, (per_row, lanes), 0) // per_head
    column = lax.broadcasted_iota(jnp.int32, (per_row, capacity), 1)
    row_step = (lax.broadcasted_iota(jnp.int32, (per_row, capacity), 0) % per_head) // group
    factor = 1.0 / math.sqrt(HD)
    scores = []
    for item in range(block):
        row = part * block + item
        length = length_ref[row]
        for which in range(2):
            stored = jnp.where(position < length, kv_ref[item, which].astype(jnp.float32), 0.0)
            for step in range(steps):
                new = fresh[which, pl.ds(step * rows + row, 1), :]
                stored = jnp.where(position == length + step, new, stored)
            moved_ref[item, which] = stored.astype(jnp.bfloat16)
        query = query_rows[pl.ds(pl.multiple_of(row * per_row, per_row), per_row), :]
        query = jnp.where(lane_head == row_head, jnp.concatenate([query] * heads, axis=1), 0.0)
        score = lax.dot_general(
            query.astype(jnp.bfloat16),
            moved_ref[item, 0],
            (((1,), (1,)), ((), ())),
            preferred_element_type=jnp.float32,
        )
        scores.append(jnp.where(column <= length + row_step, score * factor, -jnp.inf))
    weights = []
    for score in scores:
        raised = jnp.exp(score - jnp.max(score, axis=-1, keepdims=True))
        normaliser = jnp.sum(raised, axis=-1, keepdims=True)
        weights.append((raised / normaliser).astype(jnp.bfloat16))
    for item in range(block):
        row = part * block + item
        result = jnp.dot(weights[item], moved_ref[item, 1], preferred_element_type=jnp.float32)
        for head in range(heads):
            mixed[pl.ds(pl.multiple_of(row * per_row + head * per_head, per_head), per_head), :] = (
                result[head * per_head : (head + 1) * per_head, head * HD : (head + 1) * HD]
            )

    @pl.when(part == pl.num_programs(0) - 1)
    def _():
        mixed_ref[...] = mixed[...].astype(jnp.bfloat16)
        me = lax.axis_index("inst")
        for shift in range(1, count):
            row = pick_ref[peer_after(me, shift, count)]
            small = small_refs[shift - 1]
            small[:per_row, :] = mixed[
                pl.ds(pl.multiple_of(row * per_row, per_row), per_row), :
            ].astype(jnp.bfloat16)
            news = []
            for which in range(2):
                for step in range(steps):
                    new = fresh[which, pl.ds(step * rows + row, 1), :]
                    news += [new[:, h * HD : (h + 1) * HD] for h in range(heads)]
            fill = small.shape[0] - per_row - len(news)
            news.append(jnp.zeros((fill, HD), jnp.float32))
            small[per_row:, :] = jnp.concatenate(news, axis=0).astype(jnp.bfloat16)


def attend(kv_cache, queries, own, got, gain, cosine, sine, lengths, pick, count):
    steps, rows, query_width = queries.shape
    capacity, lanes = kv_cache.shape[2:]
    heads = lanes // HD
    per_row = steps * query_width // HD
    block = 4
    small_rows = -(-(per_row + 2 * steps * heads) // 16) * 16
    small = jax.ShapeDtypeStruct((small_rows, HD), jnp.bfloat16)
    smem = pl.BlockSpec(memory_space=pltpu.SMEM)
    vmem = pl.BlockSpec(memory_space=pltpu.VMEM)
    cache_block = pl.BlockSpec((block, 2, capacity, lanes), lambda i: (i, 0, 0, 0))
    outs = pl.pallas_call(
        functools.partial(attend_kernel, count, block),
        grid=(rows // block,),
        out_shape=[
            jax.ShapeDtypeStruct(kv_cache.shape, kv_cache.dtype),
            jax.ShapeDtypeStruct((rows * per_row, HD), jnp.bfloat16),
        ]
        + [small] * (count - 1),
        in_specs=[smem, smem, vmem, vmem, vmem, vmem, vmem, vmem, cache_block],
        out_specs=[cache_block, vmem] + [vmem] * (count - 1),
        scratch_shapes=[
            pltpu.VMEM((2, steps * rows, lanes), jnp.float32),
            pltpu.VMEM((rows * per_row, HD), jnp.float32),
            pltpu.VMEM((rows * per_row, HD), jnp.float32),
        ],
        compiler_params=pltpu.CompilerParams(vmem_limit_bytes=VMEM_LIMIT),
        cost_estimate=pl.CostEstimate(
            flops=4 * rows * per_row * capacity * lanes,
            bytes_accessed=4 * kv_cache.size,
            transcendentals=rows * per_row * capacity,
        ),
        name="attend",
    )(lengths, pick, own, got, gain, cosine, sine, queries, kv_cache)
    return outs[0], outs[1], outs[2:]


def settle_kernel(count, shape, group, facts_ref, mixed_ref, *refs):
    small_refs = refs[: count - 1]
    out_ref, slot_ref, length_ref, mixed = refs[count - 1 :]
    steps, rows, query_width = shape
    per_row = steps * query_width // HD
    me = lax.axis_index("inst")
    mixed[...] = mixed_ref[...].astype(jnp.float32)
    slot_ref[0] = -1
    length_ref[0] = 0
    for shift in range(1, count):
        peer = peer_before(me, shift, count)
        slot_ref[shift] = -1
        length_ref[shift] = 0

        def look(row, carry):
            slot = facts_ref[peer, 0, row] - me * rows

            @pl.when((slot >= 0) & (slot < rows))
            def _():
                slot_ref[shift] = slot
                length_ref[shift] = facts_ref[peer, 1, row]

            return carry

        lax.fori_loop(0, rows, look, 0)
        slot = slot_ref[shift]

        @pl.when(slot >= 0)
        def _():
            mixed[pl.ds(pl.multiple_of(slot * per_row, per_row), per_row), :] = small_refs[
                shift - 1
            ][:per_row, :].astype(jnp.float32)

    for step in range(steps):
        for chunk in range(query_width // HD):
            head, member = chunk // group, chunk % group
            at = head * steps * group + step * group + member
            out_ref[step, :, chunk * HD : (chunk + 1) * HD] = mixed[
                pl.ds(at, rows, stride=per_row), :
            ].astype(jnp.bfloat16)


def settle(facts, mixed, smalls, shape, group, count):
    steps, rows, query_width = shape
    smem = pl.BlockSpec(memory_space=pltpu.SMEM)
    vmem = pl.BlockSpec(memory_space=pltpu.VMEM)
    scalars = jax.ShapeDtypeStruct((count,), jnp.int32)
    return pl.pallas_call(
        functools.partial(settle_kernel, count, shape, group),
        out_shape=[jax.ShapeDtypeStruct(shape, jnp.bfloat16), scalars, scalars],
        in_specs=[smem, vmem] + [vmem] * (count - 1),
        out_specs=[vmem, smem, smem],
        scratch_shapes=[pltpu.VMEM(mixed.shape, jnp.float32)],
        compiler_params=pltpu.CompilerParams(vmem_limit_bytes=VMEM_LIMIT),
        name="settle",
    )(facts, mixed, *smalls)


def land_kernel(count, steps, slot_ref, length_ref, *refs):
    cache_refs = refs[: count - 1]
    small_refs = refs[count - 1 : 2 * (count - 1)]
    _, out_ref, buffer, in_sems, out_sems = refs[2 * (count - 1) :]
    capacity, lanes = buffer.shape[2:]
    heads = lanes // HD
    position = lax.broadcasted_iota(jnp.int32, (capacity, lanes), 0)

    def fetch(shift):
        return pltpu.make_async_copy(
            cache_refs[shift - 1], buffer.at[shift - 1], in_sems.at[shift - 1]
        )

    def store(shift):
        slot = jnp.maximum(slot_ref[shift], 0)
        return pltpu.make_async_copy(
            buffer.at[shift - 1], out_ref.at[slot], out_sems.at[shift - 1]
        )

    for shift in range(1, count):
        fetch(shift).start()
    for shift in range(1, count):
        fetch(shift).wait()

        @pl.when(slot_ref[shift] >= 0)
        def _():
            length = length_ref[shift]
            small = small_refs[shift - 1]
            news = small[small.shape[0] - 16 :, :].astype(jnp.float32)
            for which in range(2):
                stored = buffer[shift - 1, which].astype(jnp.float32)
                stored = jnp.where(position < length, stored, 0.0)
                for step in range(steps):
                    at = (which * steps + step) * heads
                    new = jnp.concatenate([news[at + h : at + h + 1] for h in range(heads)], axis=1)
                    stored = jnp.where(position == length + step, new, stored)
                buffer[shift - 1, which] = stored.astype(jnp.bfloat16)
            store(shift).start()

    for shift in range(1, count):

        @pl.when(slot_ref[shift] >= 0)
        def _():
            store(shift).wait()


def land(slots, lengths, caches, smalls, moved, steps, count):
    smem = pl.BlockSpec(memory_space=pltpu.SMEM)
    vmem = pl.BlockSpec(memory_space=pltpu.VMEM)
    hbm = pl.BlockSpec(memory_space=pl.ANY)
    return pl.pallas_call(
        functools.partial(land_kernel, count, steps),
        out_shape=jax.ShapeDtypeStruct(moved.shape, moved.dtype),
        in_specs=[smem, smem] + [hbm] * (count - 1) + [vmem] * (count - 1) + [hbm],
        out_specs=hbm,
        scratch_shapes=[
            pltpu.VMEM((count - 1,) + moved.shape[1:], moved.dtype),
            pltpu.SemaphoreType.DMA((count - 1,)),
            pltpu.SemaphoreType.DMA((count - 1,)),
        ],
        input_output_aliases={2 + 2 * (count - 1): 0},
        compiler_params=pltpu.CompilerParams(vmem_limit_bytes=VMEM_LIMIT),
        name="land",
    )(slots, lengths, *caches, *smalls, moved)


def rotation(lengths, steps):
    half = HD // 2
    inverse = jnp.exp(-math.log(ROPE_BASE) * 2.0 * jnp.arange(half, dtype=jnp.float32) / HD)
    positions = (lengths[None, :] + jnp.arange(steps, dtype=jnp.int32)[:, None]).reshape(-1)
    angles = positions.astype(jnp.float32)[:, None] * inverse
    cosine, sine = jnp.cos(angles), jnp.sin(angles)
    return jnp.concatenate([cosine, cosine], axis=1), jnp.concatenate([-sine, sine], axis=1)


def local(hidden_new, queries, kv_cache, lengths, destination, key_weight, value_weight, key_gain):
    steps = queries.shape[0]
    group = queries.shape[2] // kv_cache.shape[3]
    count = lax.axis_size("inst")

    def exchange(block, shift):
        pairs = [(i, peer_after(i, shift, count)) for i in range(count)]
        return lax.ppermute(block, "inst", pairs)

    blocks, pick = pack(kv_cache, destination, count)
    order = range(count - 1, 0, -1)
    arriving = {shift: exchange(blocks[shift - 1], shift) for shift in order}
    facts = lax.all_gather(jnp.stack([destination, lengths]), "inst")
    own, other = project(hidden_new, key_weight, value_weight)
    got = lax.ppermute(other, "tp", [(0, 1), (1, 0)])
    cosine, sine = rotation(lengths, steps)
    moved, mixed, smalls = attend(
        kv_cache, queries, own, got, key_gain[None, :], cosine, sine, lengths, pick, count
    )
    small_arriving = {shift: exchange(smalls[shift - 1], shift) for shift in order}
    small_list = [small_arriving[shift] for shift in range(1, count)]
    attended, slots, arrived_lengths = settle(
        facts, mixed, small_list, queries.shape, group, count
    )
    moved = land(
        slots,
        arrived_lengths,
        [arriving[shift] for shift in range(1, count)],
        small_list,
        moved,
        steps,
        count,
    )
    return attended, moved


def solution(mesh):
    return jax.shard_map(
        local,
        mesh=mesh,
        in_specs=(
            P(None, ("group", "inst"), "tp"),
            P(None, ("group", "inst"), "tp"),
            P(("group", "inst"), None, None, "tp"),
            P(("group", "inst")),
            P(("group", "inst")),
            P("tp", None),
            P("tp", None),
            P(),
        ),
        out_specs=(P(None, ("group", "inst"), "tp"), P(("group", "inst"), None, None, "tp")),
        check_vma=False,
    )
```

```python
import functools
import math

import jax
import jax.numpy as jnp
from jax import lax
from jax.experimental import pallas as pl
from jax.experimental.pallas import tpu as pltpu
from jax.sharding import PartitionSpec as P

HD = 128
ROPE_BASE = 1000000.0
NORM_EPS = 1e-06
VMEM_LIMIT = 40 * 1024 * 1024
FACTS = 16
WINDOW = 32


def peer_to(index, shift, count, paired=None):
    if count & (count - 1) == 0:
        return index ^ (shift if paired is None else paired)
    return (index + shift) % count


def near_size(count):
    return 4 if count % 4 == 0 and count & (count - 1) == 0 else 1


def peer_of(me, piece, near, to):
    count = lax.axis_size("inst")
    if piece < near:
        return me // near * near + piece
    return peer_to(me, piece, count) if to else peer_to(me, count - piece, count, piece)


def pack_kernel(count, near, dest_ref, length_ref, kv_ref, near_ref, *refs):
    far_refs, pick_ref, sems = refs[: count - near], refs[count - near], refs[count - near + 1]
    rows = dest_ref.shape[0]
    capacity = kv_ref.shape[2]
    lanes = kv_ref.shape[3]
    me = lax.axis_index("inst")
    for peer in range(count):
        pick_ref[peer] = 0

    def note(row, carry):
        pick_ref[dest_ref[row] // rows] = row
        return carry

    lax.fori_loop(0, rows, note, 0)
    order = list(range(near, count)) + list(range(near))
    copies = []
    for piece in order:
        row = pick_ref[peer_of(me, piece, near, True)]
        block = near_ref.at[piece] if piece < near else far_refs[piece - near]
        for which in range(2):
            copy = pltpu.make_async_copy(
                kv_ref.at[row, which],
                block.at[pl.ds(which * capacity, capacity)],
                sems.at[piece, which],
            )
            copy.start()
            copies.append(copy)
    for piece in order:
        peer = peer_of(me, piece, near, True)
        row = pick_ref[peer]
        slot = jnp.where(dest_ref[row] // rows == peer, dest_ref[row] % rows, -1)
        block = near_ref.at[piece] if piece < near else far_refs[piece - near]
        line = lax.broadcasted_iota(jnp.int32, (FACTS, lanes), 0)
        facts = jnp.where(line == 0, slot, length_ref[row])
        block[2 * capacity :, :] = facts.astype(jnp.float32).astype(jnp.bfloat16)
    for copy in copies:
        copy.wait()


def pack(kv_cache, destination, lengths, count, near):
    height = 2 * kv_cache.shape[2] + FACTS
    width = kv_cache.shape[3]
    far = jax.ShapeDtypeStruct((height, width), kv_cache.dtype)
    smem = pl.BlockSpec(memory_space=pltpu.SMEM)
    vmem = pl.BlockSpec(memory_space=pltpu.VMEM)
    outs = pl.pallas_call(
        functools.partial(pack_kernel, count, near),
        out_shape=[jax.ShapeDtypeStruct((near, height, width), kv_cache.dtype)]
        + [far] * (count - near)
        + [jax.ShapeDtypeStruct((count,), jnp.int32)],
        in_specs=[smem, smem, pl.BlockSpec(memory_space=pltpu.HBM)],
        out_specs=[vmem] * (count - near + 1) + [smem],
        scratch_shapes=[pltpu.SemaphoreType.DMA((count, 2))],
        compiler_params=pltpu.CompilerParams(vmem_limit_bytes=VMEM_LIMIT),
        name="pack",
    )(destination, lengths, kv_cache)
    return outs[0], outs[1:-1], outs[-1]


def project_kernel(_, hidden_ref, key_ref, value_ref, own_ref, other_ref, total):
    step = pl.program_id(0)
    width = key_ref.shape[1]

    @pl.when(step == 0)
    def _():
        total[...] = jnp.zeros_like(total)

    steps, rows, depth = hidden_ref.shape
    hidden = hidden_ref[...].reshape(steps * rows, depth)
    total[:, :width] += jnp.dot(hidden, key_ref[...], preferred_element_type=jnp.float32)
    total[:, width:] += jnp.dot(hidden, value_ref[...], preferred_element_type=jnp.float32)

    @pl.when(step == pl.num_programs(0) - 1)
    def _():
        half = width // 2
        me = lax.axis_index("tp")
        for ref, core in ((own_ref, me), (other_ref, 1 - me)):
            at = pl.multiple_of(core * half, half)
            ref[:, :half] = total[:, pl.ds(at, half)]
            ref[:, half:] = total[:, pl.ds(pl.multiple_of(width + at, half), half)]


def project(hidden_new, key_weight, value_weight, pick):
    steps, rows, depth = hidden_new.shape
    width = key_weight.shape[1]
    part = depth // 5
    shape = jax.ShapeDtypeStruct((steps * rows, width), jnp.float32)
    whole = pl.BlockSpec((steps * rows, width), lambda i: (0, 0))
    return pl.pallas_call(
        project_kernel,
        grid=(depth // part,),
        out_shape=[shape, shape],
        in_specs=[
            pl.BlockSpec(memory_space=pltpu.SMEM),
            pl.BlockSpec((steps, rows, part), lambda i: (0, 0, i)),
            pl.BlockSpec((part, width), lambda i: (i, 0)),
            pl.BlockSpec((part, width), lambda i: (i, 0)),
        ],
        out_specs=[whole, whole],
        scratch_shapes=[pltpu.VMEM((steps * rows, 2 * width), jnp.float32)],
        compiler_params=pltpu.CompilerParams(vmem_limit_bytes=VMEM_LIMIT),
        cost_estimate=pl.CostEstimate(
            flops=4 * steps * rows * depth * width,
            bytes_accessed=4 * depth * width,
            transcendentals=0,
        ),
        name="project",
    )(pick, hidden_new, key_weight, value_weight)


def attend_kernel(
    count,
    block,
    length_ref,
    pick_ref,
    own_ref,
    got_ref,
    gain_ref,
    cos_ref,
    sin_ref,
    query_ref,
    kv_ref,
    moved_ref,
    mixed_ref,
    small_ref,
    fresh,
    query_rows,
    mixed,
):
    part = pl.program_id(0)
    steps, rows, query_width = query_ref.shape
    capacity, lanes = kv_ref.shape[2:]
    heads = lanes // HD
    group = query_width // lanes
    per_head = steps * group
    per_row = heads * per_head

    def place(step, head, member):
        return head * per_head + step * group + member

    def spot(head, member):
        return slice((head * group + member) * HD, (head * group + member + 1) * HD)

    @pl.when(part == 0)
    def _():
        raw = own_ref[...] + got_ref[...]
        gain = gain_ref[...].astype(jnp.float32)
        for head in range(heads):
            at = slice(head * HD, (head + 1) * HD)
            piece = raw[:, at]
            mean = jnp.mean(piece * piece, axis=-1, keepdims=True)
            piece = piece * lax.rsqrt(mean + NORM_EPS) * gain
            swapped = jnp.concatenate([piece[:, HD // 2 :], piece[:, : HD // 2]], axis=1)
            turned = piece * cos_ref[...] + swapped * sin_ref[...]
            fresh[0, :, at] = turned.astype(jnp.bfloat16).astype(jnp.float32)
        fresh[1] = raw[:, lanes:].astype(jnp.bfloat16).astype(jnp.float32)
        for step in range(steps):
            for head in range(heads):
                for member in range(group):
                    query_rows[pl.ds(place(step, head, member), rows, stride=per_row), :] = (
                        query_ref[step, :, spot(head, member)].astype(jnp.float32)
                    )

    position = lax.broadcasted_iota(jnp.int32, (capacity, HD), 0)
    lane_head = lax.broadcasted_iota(jnp.int32, (per_row, lanes), 1) // HD
    row_head = lax.broadcasted_iota(jnp.int32, (per_row, lanes), 0) // per_head
    column = lax.broadcasted_iota(jnp.int32, (per_row, capacity), 1)
    row_step = (lax.broadcasted_iota(jnp.int32, (per_row, capacity), 0) % per_head) // group
    factor = 1.0 / math.sqrt(HD)
    scores = []
    for item in range(block):
        row = part * block + item
        length = length_ref[row]
        kept = position < length
        landing = [position == length + step for step in range(steps)]
        for which in range(2):
            news = [fresh[which, pl.ds(step * rows + row, 1), :] for step in range(steps)]
            for head in range(heads):
                at = slice(head * HD, (head + 1) * HD)
                stored = jnp.where(kept, kv_ref[item, which, :, at].astype(jnp.float32), 0.0)
                for step in range(steps):
                    stored = jnp.where(landing[step], news[step][:, at], stored)
                moved_ref[item, which, :, at] = stored.astype(jnp.bfloat16)
        query = query_rows[pl.ds(pl.multiple_of(row * per_row, per_row), per_row), :]
        query = jnp.where(lane_head == row_head, jnp.concatenate([query] * heads, axis=1), 0.0)
        score = lax.dot_general(
            query.astype(jnp.bfloat16),
            moved_ref[item, 0],
            (((1,), (1,)), ((), ())),
            preferred_element_type=jnp.float32,
        )
        scores.append(jnp.where(column <= length + row_step, score * factor, -jnp.inf))
    weights = []
    for score in scores:
        raised = jnp.exp(score - jnp.max(score, axis=-1, keepdims=True))
        normaliser = jnp.sum(raised, axis=-1, keepdims=True)
        weights.append((raised / normaliser).astype(jnp.bfloat16))
    for item in range(block):
        row = part * block + item
        result = jnp.dot(weights[item], moved_ref[item, 1], preferred_element_type=jnp.float32)
        for head in range(heads):
            mixed[pl.ds(pl.multiple_of(row * per_row + head * per_head, per_head), per_head), :] = (
                result[head * per_head : (head + 1) * per_head, head * HD : (head + 1) * HD]
            )

    @pl.when(part == pl.num_programs(0) - 1)
    def _():
        mixed_ref[...] = mixed[...].astype(jnp.bfloat16)
        for peer in range(count):
            row = pick_ref[peer]
            small_ref[peer, :per_row, :] = mixed[
                pl.ds(pl.multiple_of(row * per_row, per_row), per_row), :
            ].astype(jnp.bfloat16)
            news = []
            for which in range(2):
                for step in range(steps):
                    new = fresh[which, pl.ds(step * rows + row, 1), :]
                    news += [new[:, h * HD : (h + 1) * HD] for h in range(heads)]
            fill = small_ref.shape[1] - per_row - len(news)
            news.append(jnp.zeros((fill, HD), jnp.float32))
            small_ref[peer, per_row:, :] = jnp.concatenate(news, axis=0).astype(jnp.bfloat16)


def attend(kv_cache, queries, own, got, gain, cosine, sine, lengths, pick, count):
    steps, rows, query_width = queries.shape
    capacity, lanes = kv_cache.shape[2:]
    heads = lanes // HD
    per_row = steps * query_width // HD
    block = 8
    small_rows = -(-(per_row + 2 * steps * heads) // 16) * 16
    small = jax.ShapeDtypeStruct((count, small_rows, HD), jnp.bfloat16)
    smem = pl.BlockSpec(memory_space=pltpu.SMEM)
    vmem = pl.BlockSpec(memory_space=pltpu.VMEM)
    cache_block = pl.BlockSpec((block, 2, capacity, lanes), lambda i: (i, 0, 0, 0))
    return pl.pallas_call(
        functools.partial(attend_kernel, count, block),
        grid=(rows // block,),
        out_shape=[
            jax.ShapeDtypeStruct(kv_cache.shape, kv_cache.dtype),
            jax.ShapeDtypeStruct((rows * per_row, HD), jnp.bfloat16),
            small,
        ],
        in_specs=[smem, smem, vmem, vmem, vmem, vmem, vmem, vmem, cache_block],
        out_specs=[cache_block, vmem, vmem],
        scratch_shapes=[
            pltpu.VMEM((2, steps * rows, lanes), jnp.float32),
            pltpu.VMEM((rows * per_row, HD), jnp.float32),
            pltpu.VMEM((rows * per_row, HD), jnp.float32),
        ],
        compiler_params=pltpu.CompilerParams(vmem_limit_bytes=VMEM_LIMIT),
        cost_estimate=pl.CostEstimate(
            flops=4 * rows * per_row * capacity * lanes,
            bytes_accessed=4 * kv_cache.size,
            transcendentals=rows * per_row * capacity,
        ),
        name="attend",
    )(lengths, pick, own, got, gain, cosine, sine, queries, kv_cache)


def window_start(length, capacity):
    return pl.multiple_of(jnp.minimum(length // 16 * 16, capacity - WINDOW), 16)


def land_kernel(count, near, near_ref, *refs):
    far_refs = refs[: count - near]
    _, out_ref, slot_ref, length_ref, window_ref, buffer, sems = refs[count - near :]
    capacity, lanes = buffer.shape[2:]
    position = lax.broadcasted_iota(jnp.int32, (capacity, HD), 0)
    me = lax.axis_index("inst")

    def store(piece):
        slot = jnp.maximum(slot_ref[piece], 0)
        return pltpu.make_async_copy(buffer.at[piece], out_ref.at[slot], sems.at[piece])

    blocks = [near_ref.at[piece] for piece in range(near)] + list(far_refs)
    for piece, block in enumerate(blocks):
        facts = block[2 * capacity :, :HD].astype(jnp.float32)
        slot = jnp.max(facts[0:1]).astype(jnp.int32)
        length = jnp.max(facts[1:2]).astype(jnp.int32)
        if piece < near:
            slot = jnp.where(me % near == piece, -1, slot)
        slot_ref[piece] = slot
        length_ref[piece] = length
    for piece, block in enumerate(blocks):

        @pl.when(slot_ref[piece] >= 0)
        def _():
            length = length_ref[piece]
            kept = position < length
            for which in range(2):
                for at in range(0, lanes, HD):
                    stored = block[which * capacity : (which + 1) * capacity, at : at + HD]
                    stored = jnp.where(kept, stored.astype(jnp.float32), 0.0)
                    buffer[piece, which, :, at : at + HD] = stored.astype(jnp.bfloat16)
            store(piece).start()
            start = window_start(length, capacity)
            window_ref[piece] = buffer[piece, :, pl.ds(start, WINDOW), :]

    for piece in range(count):

        @pl.when(slot_ref[piece] >= 0)
        def _():
            store(piece).wait()


def land(near_got, far_got, moved, count, near):
    smem = pl.BlockSpec(memory_space=pltpu.SMEM)
    vmem = pl.BlockSpec(memory_space=pltpu.VMEM)
    hbm = pl.BlockSpec(memory_space=pl.ANY)
    scalars = jax.ShapeDtypeStruct((count,), jnp.int32)
    lanes = moved.shape[3]
    return pl.pallas_call(
        functools.partial(land_kernel, count, near),
        out_shape=[
            jax.ShapeDtypeStruct(moved.shape, moved.dtype),
            scalars,
            scalars,
            jax.ShapeDtypeStruct((count, 2, WINDOW, lanes), moved.dtype),
        ],
        in_specs=[vmem] * (count - near + 1) + [hbm],
        out_specs=[hbm, smem, smem, vmem],
        scratch_shapes=[
            pltpu.VMEM((count,) + moved.shape[1:], moved.dtype),
            pltpu.SemaphoreType.DMA((count,)),
        ],
        input_output_aliases={count - near + 1: 0},
        compiler_params=pltpu.CompilerParams(vmem_limit_bytes=VMEM_LIMIT),
        name="land",
    )(near_got, *far_got, moved)


def settle_kernel(
    count,
    near,
    group,
    slot_ref,
    length_ref,
    mixed_ref,
    small_ref,
    window_ref,
    _,
    out_ref,
    moved_ref,
    mixed,
    windows,
    sems,
):
    steps, rows, query_width = out_ref.shape
    per_row = steps * query_width // HD
    capacity, lanes = moved_ref.shape[2:]
    heads = lanes // HD
    me = lax.axis_index("inst")
    position = lax.broadcasted_iota(jnp.int32, (WINDOW, lanes), 0)

    def store(piece):
        slot = jnp.maximum(slot_ref[piece], 0)
        start = window_start(length_ref[piece], capacity)
        return pltpu.make_async_copy(
            windows.at[piece], moved_ref.at[slot, :, pl.ds(start, WINDOW), :], sems.at[piece]
        )

    mixed[...] = mixed_ref[...].astype(jnp.float32)
    for piece in range(count):

        @pl.when(slot_ref[piece] >= 0)
        def _():
            slot, length = slot_ref[piece], length_ref[piece]
            peer = peer_of(me, piece, near, False)
            news = small_ref[peer, per_row:, :].astype(jnp.float32)
            ahead = length - window_start(length, capacity)
            for which in range(2):
                stored = window_ref[piece, which].astype(jnp.float32)
                for step in range(steps):
                    at = (which * steps + step) * heads
                    new = jnp.concatenate([news[at + h : at + h + 1] for h in range(heads)], axis=1)
                    stored = jnp.where(position == ahead + step, new, stored)
                windows[piece, which] = stored.astype(jnp.bfloat16)
            store(piece).start()
            mixed[pl.ds(pl.multiple_of(slot * per_row, per_row), per_row), :] = small_ref[
                peer, :per_row, :
            ].astype(jnp.float32)

    for step in range(steps):
        for chunk in range(query_width // HD):
            head, member = chunk // group, chunk % group
            at = head * steps * group + step * group + member
            out_ref[step, :, chunk * HD : (chunk + 1) * HD] = mixed[
                pl.ds(at, rows, stride=per_row), :
            ].astype(jnp.bfloat16)

    for piece in range(count):

        @pl.when(slot_ref[piece] >= 0)
        def _():
            store(piece).wait()


def settle(slots, lengths, mixed, small, windows, moved, shape, group, count, near):
    smem = pl.BlockSpec(memory_space=pltpu.SMEM)
    vmem = pl.BlockSpec(memory_space=pltpu.VMEM)
    hbm = pl.BlockSpec(memory_space=pl.ANY)
    return pl.pallas_call(
        functools.partial(settle_kernel, count, near, group),
        out_shape=[
            jax.ShapeDtypeStruct(shape, jnp.bfloat16),
            jax.ShapeDtypeStruct(moved.shape, moved.dtype),
        ],
        in_specs=[smem, smem, vmem, vmem, vmem, hbm],
        out_specs=[vmem, hbm],
        scratch_shapes=[
            pltpu.VMEM(mixed.shape, jnp.float32),
            pltpu.VMEM(windows.shape, windows.dtype),
            pltpu.SemaphoreType.DMA((count,)),
        ],
        input_output_aliases={5: 1},
        compiler_params=pltpu.CompilerParams(vmem_limit_bytes=VMEM_LIMIT),
        name="settle",
    )(slots, lengths, mixed, small, windows, moved)


def rotation(lengths, steps):
    half = HD // 2
    inverse = jnp.exp(-math.log(ROPE_BASE) * 2.0 * jnp.arange(half, dtype=jnp.float32) / HD)
    positions = (lengths[None, :] + jnp.arange(steps, dtype=jnp.int32)[:, None]).reshape(-1)
    angles = positions.astype(jnp.float32)[:, None] * inverse
    cosine, sine = jnp.cos(angles), jnp.sin(angles)
    return jnp.concatenate([cosine, cosine], axis=1), jnp.concatenate([-sine, sine], axis=1)


def local(hidden_new, queries, kv_cache, lengths, destination, key_weight, value_weight, key_gain):
    steps = queries.shape[0]
    group = queries.shape[2] // kv_cache.shape[3]
    count = lax.axis_size("inst")
    near = near_size(count)

    near_blocks, far_blocks, pick = pack(kv_cache, destination, lengths, count, near)
    far_got = []
    for piece, block in enumerate(far_blocks, near):
        pairs = [(i, int(peer_to(i, piece, count))) for i in range(count)]
        far_got.append(lax.ppermute(block, "inst", pairs))
    near_got = near_blocks
    if near > 1:
        teams = [list(range(i, i + near)) for i in range(0, count, near)]
        near_got = lax.all_to_all(
            near_blocks, "inst", 0, 0, axis_index_groups=teams, tiled=True
        )
    own, other = project(hidden_new, key_weight, value_weight, pick)
    got = lax.ppermute(other, "tp", [(0, 1), (1, 0)])
    cosine, sine = rotation(lengths, steps)
    moved, mixed, small = attend(
        kv_cache, queries, own, got, key_gain[None, :], cosine, sine, lengths, pick, count
    )
    small_got = lax.all_to_all(small, "inst", 0, 0, tiled=True)
    moved, slots, arrived, windows = land(near_got, far_got, moved, count, near)
    return tuple(
        settle(
            slots, arrived, mixed, small_got, windows, moved, queries.shape, group, count, near
        )
    )


def solution(mesh):
    return jax.shard_map(
        local,
        mesh=mesh,
        in_specs=(
            P(None, ("group", "inst"), "tp"),
            P(None, ("group", "inst"), "tp"),
            P(("group", "inst"), None, None, "tp"),
            P(("group", "inst")),
            P(("group", "inst")),
            P("tp", None),
            P("tp", None),
            P(),
        ),
        out_specs=(P(None, ("group", "inst"), "tp"), P(("group", "inst"), None, None, "tp")),
        check_vma=False,
    )
```

```python
import functools
import math

import jax
import jax.numpy as jnp
from jax import lax
from jax.experimental import pallas as pl
from jax.experimental.pallas import tpu as pltpu
from jax.sharding import PartitionSpec as P

HD = 128
ROPE_BASE = 1000000.0
NORM_EPS = 1e-06
VMEM_LIMIT = 62 * 1024 * 1024
SMALL_LIMIT = 40 * 1024 * 1024
FACTS = 16
LIGHT = pl.CostEstimate(flops=1, bytes_accessed=1, transcendentals=0)
HEAVY = pl.CostEstimate(flops=1 << 36, bytes_accessed=1 << 28, transcendentals=0)
WINDOW = 32


def peer_to(index, shift, count, paired=None):
    if count & (count - 1) == 0:
        return index ^ (shift if paired is None else paired)
    return (index + shift) % count


def near_size(count):
    return 4 if count % 4 == 0 and count & (count - 1) == 0 else 1


def peer_of(me, piece, near, to):
    count = lax.axis_size("inst")
    if piece < near:
        return me // near * near + piece
    return peer_to(me, piece, count) if to else peer_to(me, count - piece, count, piece)


def pack_kernel(count, near, dest_ref, length_ref, kv_ref, near_ref, *refs):
    far_refs = refs[: count - near]
    pick_ref, buffer, in_sems, out_sems = refs[count - near :]
    rows = dest_ref.shape[0]
    capacity, lanes = kv_ref.shape[2:]
    me = lax.axis_index("inst")
    for peer in range(count):
        pick_ref[peer] = 0

    def note(row, carry):
        pick_ref[dest_ref[row] // rows] = row
        return carry

    lax.fori_loop(0, rows, note, 0)
    order = list(range(near, count)) + list(range(near))
    fetches, stores = {}, {}
    for piece in order:
        row = pick_ref[peer_of(me, piece, near, True)]
        fetches[piece] = [
            pltpu.make_async_copy(
                kv_ref.at[row, which],
                buffer.at[piece, pl.ds(which * capacity, capacity)],
                in_sems.at[piece, which],
            )
            for which in range(2)
        ]
        for copy in fetches[piece]:
            copy.start()
    line = lax.broadcasted_iota(jnp.int32, (FACTS, lanes), 0)
    for piece in order:
        peer = peer_of(me, piece, near, True)
        row = pick_ref[peer]
        slot = jnp.where(dest_ref[row] // rows == peer, dest_ref[row] % rows, -1)
        facts = jnp.where(line == 0, slot, length_ref[row])
        buffer[piece, 2 * capacity :, :] = facts.astype(jnp.float32).astype(jnp.bfloat16)
        for copy in fetches[piece]:
            copy.wait()
        stores[piece] = pltpu.make_async_copy(
            buffer.at[piece],
            near_ref.at[piece] if piece < near else far_refs[piece - near],
            out_sems.at[piece],
        )
        stores[piece].start()
    for piece in order:
        stores[piece].wait()


def pack(kv_cache, destination, lengths, count, near):
    height = 2 * kv_cache.shape[2] + FACTS
    width = kv_cache.shape[3]
    far = jax.ShapeDtypeStruct((height, width), kv_cache.dtype)
    smem = pl.BlockSpec(memory_space=pltpu.SMEM)
    hbm = pl.BlockSpec(memory_space=pl.ANY)
    outs = pl.pallas_call(
        functools.partial(pack_kernel, count, near),
        out_shape=[jax.ShapeDtypeStruct((near, height, width), kv_cache.dtype)]
        + [far] * (count - near)
        + [jax.ShapeDtypeStruct((count,), jnp.int32)],
        in_specs=[smem, smem, hbm],
        out_specs=[hbm] * (count - near + 1) + [smem],
        scratch_shapes=[
            pltpu.VMEM((count, height, width), kv_cache.dtype),
            pltpu.SemaphoreType.DMA((count, 2)),
            pltpu.SemaphoreType.DMA((count,)),
        ],
        compiler_params=pltpu.CompilerParams(vmem_limit_bytes=VMEM_LIMIT),
        cost_estimate=LIGHT,
        name="pack",
    )(destination, lengths, kv_cache)
    return outs[0], outs[1:-1], outs[-1]


def project_kernel(_, hidden_ref, key_ref, value_ref, own_ref, other_ref, near_ref, total):
    del near_ref
    step = pl.program_id(0)
    width = key_ref.shape[1]

    @pl.when(step == 0)
    def _():
        total[...] = jnp.zeros_like(total)

    steps, rows, depth = hidden_ref.shape
    hidden = hidden_ref[...].reshape(steps * rows, depth)
    total[:, :width] += jnp.dot(hidden, key_ref[...], preferred_element_type=jnp.float32)
    total[:, width:] += jnp.dot(hidden, value_ref[...], preferred_element_type=jnp.float32)

    @pl.when(step == pl.num_programs(0) - 1)
    def _():
        half = width // 2
        me = lax.axis_index("tp")
        for ref, core in ((own_ref, me), (other_ref, 1 - me)):
            at = pl.multiple_of(core * half, half)
            ref[:, :half] = total[:, pl.ds(at, half)]
            ref[:, half:] = total[:, pl.ds(pl.multiple_of(width + at, half), half)]


def project(hidden_new, key_weight, value_weight, near_blocks):
    steps, rows, depth = hidden_new.shape
    width = key_weight.shape[1]
    part = depth // 5
    shape = jax.ShapeDtypeStruct((steps * rows, width), jnp.float32)
    whole = pl.BlockSpec((steps * rows, width), lambda i: (0, 0))
    return pl.pallas_call(
        project_kernel,
        grid=(depth // part,),
        out_shape=[shape, shape, jax.ShapeDtypeStruct(near_blocks.shape, near_blocks.dtype)],
        in_specs=[
            pl.BlockSpec(memory_space=pl.ANY),
            pl.BlockSpec((steps, rows, part), lambda i: (0, 0, i)),
            pl.BlockSpec((part, width), lambda i: (i, 0)),
            pl.BlockSpec((part, width), lambda i: (i, 0)),
        ],
        out_specs=[whole, whole, pl.BlockSpec(memory_space=pl.ANY)],
        scratch_shapes=[pltpu.VMEM((steps * rows, 2 * width), jnp.float32)],
        compiler_params=pltpu.CompilerParams(vmem_limit_bytes=VMEM_LIMIT),
        input_output_aliases={0: 2},
        cost_estimate=LIGHT,
        name="project",
    )(near_blocks, hidden_new, key_weight, value_weight)


def rotation(length_ref, steps, rows):
    half = HD // 2
    line = lax.broadcasted_iota(jnp.int32, (steps * rows, HD), 0)
    lane = lax.broadcasted_iota(jnp.int32, (steps * rows, HD), 1)
    position = jnp.zeros((steps * rows, HD), jnp.int32)
    for step in range(steps):
        for row in range(rows):
            position = jnp.where(line == step * rows + row, length_ref[row] + step, position)
    order = (lane % half).astype(jnp.float32)
    angle = position.astype(jnp.float32) * jnp.exp(-math.log(ROPE_BASE) * 2.0 * order / HD)
    sine = jnp.sin(angle)
    return jnp.cos(angle), jnp.where(lane < half, -sine, sine)


def attend_kernel(
    count,
    block,
    length_ref,
    pick_ref,
    own_ref,
    got_ref,
    gain_ref,
    query_ref,
    kv_ref,
    moved_ref,
    mixed_ref,
    small_ref,
    fresh,
    query_rows,
    mixed,
):
    part = pl.program_id(0)
    steps, rows, query_width = query_ref.shape
    capacity, lanes = kv_ref.shape[2:]
    heads = lanes // HD
    group = query_width // lanes
    per_head = steps * group
    per_row = heads * per_head

    def place(step, head, member):
        return head * per_head + step * group + member

    def spot(head, member):
        return slice((head * group + member) * HD, (head * group + member + 1) * HD)

    @pl.when(part == 0)
    def _():
        raw = own_ref[...] + got_ref[...]
        cosine, sine = rotation(length_ref, steps, rows)
        gain = gain_ref[...].astype(jnp.float32)
        for head in range(heads):
            at = slice(head * HD, (head + 1) * HD)
            piece = raw[:, at]
            mean = jnp.mean(piece * piece, axis=-1, keepdims=True)
            piece = piece * lax.rsqrt(mean + NORM_EPS) * gain
            swapped = jnp.concatenate([piece[:, HD // 2 :], piece[:, : HD // 2]], axis=1)
            turned = piece * cosine + swapped * sine
            fresh[0, :, at] = turned.astype(jnp.bfloat16).astype(jnp.float32)
        fresh[1] = raw[:, lanes:].astype(jnp.bfloat16).astype(jnp.float32)
        for step in range(steps):
            for head in range(heads):
                for member in range(group):
                    query_rows[pl.ds(place(step, head, member), rows, stride=per_row), :] = (
                        query_ref[step, :, spot(head, member)].astype(jnp.float32)
                    )

    position = lax.broadcasted_iota(jnp.int32, (capacity, HD), 0)
    lane_head = lax.broadcasted_iota(jnp.int32, (per_row, lanes), 1) // HD
    row_head = lax.broadcasted_iota(jnp.int32, (per_row, lanes), 0) // per_head
    column = lax.broadcasted_iota(jnp.int32, (per_row, capacity), 1)
    row_step = (lax.broadcasted_iota(jnp.int32, (per_row, capacity), 0) % per_head) // group
    factor = 1.0 / math.sqrt(HD)
    scores = []
    for item in range(block):
        row = part * block + item
        length = length_ref[row]
        kept = position < length
        landing = [position == length + step for step in range(steps)]
        for which in range(2):
            news = [fresh[which, pl.ds(step * rows + row, 1), :] for step in range(steps)]
            for head in range(heads):
                at = slice(head * HD, (head + 1) * HD)
                stored = jnp.where(kept, kv_ref[item, which, :, at].astype(jnp.float32), 0.0)
                for step in range(steps):
                    stored = jnp.where(landing[step], news[step][:, at], stored)
                moved_ref[item, which, :, at] = stored.astype(jnp.bfloat16)
        query = query_rows[pl.ds(pl.multiple_of(row * per_row, per_row), per_row), :]
        query = jnp.where(lane_head == row_head, jnp.concatenate([query] * heads, axis=1), 0.0)
        score = lax.dot_general(
            query.astype(jnp.bfloat16),
            moved_ref[item, 0],
            (((1,), (1,)), ((), ())),
            preferred_element_type=jnp.float32,
        )
        scores.append(jnp.where(column <= length + row_step, score * factor, -jnp.inf))
    weights = []
    for score in scores:
        raised = jnp.exp(score - jnp.max(score, axis=-1, keepdims=True))
        normaliser = jnp.sum(raised, axis=-1, keepdims=True)
        weights.append((raised / normaliser).astype(jnp.bfloat16))
    for item in range(block):
        row = part * block + item
        result = jnp.dot(weights[item], moved_ref[item, 1], preferred_element_type=jnp.float32)
        for head in range(heads):
            mixed[pl.ds(pl.multiple_of(row * per_row + head * per_head, per_head), per_head), :] = (
                result[head * per_head : (head + 1) * per_head, head * HD : (head + 1) * HD]
            )

    @pl.when(part == pl.num_programs(0) - 1)
    def _():
        mixed_ref[...] = mixed[...].astype(jnp.bfloat16)
        for peer in range(count):
            row = pick_ref[peer]
            small_ref[peer, :per_row, :] = mixed[
                pl.ds(pl.multiple_of(row * per_row, per_row), per_row), :
            ].astype(jnp.bfloat16)
            news = []
            for which in range(2):
                for step in range(steps):
                    new = fresh[which, pl.ds(step * rows + row, 1), :]
                    news += [new[:, h * HD : (h + 1) * HD] for h in range(heads)]
            fill = small_ref.shape[1] - per_row - len(news)
            news.append(jnp.zeros((fill, HD), jnp.float32))
            small_ref[peer, per_row:, :] = jnp.concatenate(news, axis=0).astype(jnp.bfloat16)


def attend(kv_cache, queries, own, got, gain, lengths, pick, count):
    steps, rows, query_width = queries.shape
    capacity, lanes = kv_cache.shape[2:]
    heads = lanes // HD
    per_row = steps * query_width // HD
    block = 8
    small_rows = -(-(per_row + 2 * steps * heads) // 16) * 16
    small = jax.ShapeDtypeStruct((count, small_rows, HD), jnp.bfloat16)
    smem = pl.BlockSpec(memory_space=pltpu.SMEM)
    vmem = pl.BlockSpec(memory_space=pltpu.VMEM)
    cache_block = pl.BlockSpec((block, 2, capacity, lanes), lambda i: (i, 0, 0, 0))
    return pl.pallas_call(
        functools.partial(attend_kernel, count, block),
        grid=(rows // block,),
        out_shape=[
            jax.ShapeDtypeStruct(kv_cache.shape, kv_cache.dtype),
            jax.ShapeDtypeStruct((rows * per_row, HD), jnp.bfloat16),
            small,
        ],
        in_specs=[smem, smem, vmem, vmem, vmem, vmem, cache_block],
        out_specs=[cache_block, vmem, vmem],
        scratch_shapes=[
            pltpu.VMEM((2, steps * rows, lanes), jnp.float32),
            pltpu.VMEM((rows * per_row, HD), jnp.float32),
            pltpu.VMEM((rows * per_row, HD), jnp.float32),
        ],
        compiler_params=pltpu.CompilerParams(vmem_limit_bytes=VMEM_LIMIT),
        cost_estimate=LIGHT,
        name="attend",
    )(lengths, pick, own, got, gain, queries, kv_cache)


def window_start(length, capacity):
    return pl.multiple_of(jnp.minimum(length // 16 * 16, capacity - WINDOW), 16)


def land_kernel(count, near, near_ref, *refs):
    far_refs = refs[: count - near]
    _, out_ref, slot_ref, length_ref, window_ref, buffer, sems = refs[count - near :]
    capacity, lanes = buffer.shape[2:]
    position = lax.broadcasted_iota(jnp.int32, (capacity, HD), 0)
    me = lax.axis_index("inst")

    def store(piece):
        slot = jnp.maximum(slot_ref[piece], 0)
        return pltpu.make_async_copy(buffer.at[piece], out_ref.at[slot], sems.at[piece])

    blocks = [near_ref.at[piece] for piece in range(near)] + list(far_refs)
    for piece, block in enumerate(blocks):
        facts = block[2 * capacity :, :HD].astype(jnp.float32)
        slot = jnp.max(facts[0:1]).astype(jnp.int32)
        length = jnp.max(facts[1:2]).astype(jnp.int32)
        if piece < near:
            slot = jnp.where(me % near == piece, -1, slot)
        slot_ref[piece] = slot
        length_ref[piece] = length
    for piece, block in enumerate(blocks):

        @pl.when(slot_ref[piece] >= 0)
        def _():
            length = length_ref[piece]
            kept = position < length
            for which in range(2):
                for at in range(0, lanes, HD):
                    stored = block[which * capacity : (which + 1) * capacity, at : at + HD]
                    stored = jnp.where(kept, stored.astype(jnp.float32), 0.0)
                    buffer[piece, which, :, at : at + HD] = stored.astype(jnp.bfloat16)
            store(piece).start()
            start = window_start(length, capacity)
            window_ref[piece] = buffer[piece, :, pl.ds(start, WINDOW), :]

    for piece in range(count):

        @pl.when(slot_ref[piece] >= 0)
        def _():
            store(piece).wait()


def land(near_got, far_got, moved, count, near):
    smem = pl.BlockSpec(memory_space=pltpu.SMEM)
    vmem = pl.BlockSpec(memory_space=pltpu.VMEM)
    hbm = pl.BlockSpec(memory_space=pl.ANY)
    scalars = jax.ShapeDtypeStruct((count,), jnp.int32)
    lanes = moved.shape[3]
    return pl.pallas_call(
        functools.partial(land_kernel, count, near),
        out_shape=[
            jax.ShapeDtypeStruct(moved.shape, moved.dtype),
            scalars,
            scalars,
            jax.ShapeDtypeStruct((count, 2, WINDOW, lanes), moved.dtype),
        ],
        in_specs=[vmem] * (count - near + 1) + [hbm],
        out_specs=[hbm, smem, smem, vmem],
        scratch_shapes=[
            pltpu.VMEM((count,) + moved.shape[1:], moved.dtype),
            pltpu.SemaphoreType.DMA((count,)),
        ],
        input_output_aliases={count - near + 1: 0},
        compiler_params=pltpu.CompilerParams(vmem_limit_bytes=SMALL_LIMIT),
        cost_estimate=HEAVY,
        name="land",
    )(near_got, *far_got, moved)


def settle_kernel(
    count,
    near,
    group,
    slot_ref,
    length_ref,
    mixed_ref,
    small_ref,
    window_ref,
    _,
    out_ref,
    moved_ref,
    mixed,
    windows,
    sems,
):
    steps, rows, query_width = out_ref.shape
    per_row = steps * query_width // HD
    capacity, lanes = moved_ref.shape[2:]
    heads = lanes // HD
    me = lax.axis_index("inst")
    position = lax.broadcasted_iota(jnp.int32, (WINDOW, lanes), 0)

    def store(piece):
        slot = jnp.maximum(slot_ref[piece], 0)
        start = window_start(length_ref[piece], capacity)
        return pltpu.make_async_copy(
            windows.at[piece], moved_ref.at[slot, :, pl.ds(start, WINDOW), :], sems.at[piece]
        )

    mixed[...] = mixed_ref[...].astype(jnp.float32)
    for piece in range(count):

        @pl.when(slot_ref[piece] >= 0)
        def _():
            slot, length = slot_ref[piece], length_ref[piece]
            peer = peer_of(me, piece, near, False)
            news = small_ref[peer, per_row:, :].astype(jnp.float32)
            ahead = length - window_start(length, capacity)
            for which in range(2):
                stored = window_ref[piece, which].astype(jnp.float32)
                for step in range(steps):
                    at = (which * steps + step) * heads
                    new = jnp.concatenate([news[at + h : at + h + 1] for h in range(heads)], axis=1)
                    stored = jnp.where(position == ahead + step, new, stored)
                windows[piece, which] = stored.astype(jnp.bfloat16)
            store(piece).start()
            mixed[pl.ds(pl.multiple_of(slot * per_row, per_row), per_row), :] = small_ref[
                peer, :per_row, :
            ].astype(jnp.float32)

    for step in range(steps):
        for chunk in range(query_width // HD):
            head, member = chunk // group, chunk % group
            at = head * steps * group + step * group + member
            out_ref[step, :, chunk * HD : (chunk + 1) * HD] = mixed[
                pl.ds(at, rows, stride=per_row), :
            ].astype(jnp.bfloat16)

    for piece in range(count):

        @pl.when(slot_ref[piece] >= 0)
        def _():
            store(piece).wait()


def settle(slots, lengths, mixed, small, windows, moved, shape, group, count, near):
    smem = pl.BlockSpec(memory_space=pltpu.SMEM)
    vmem = pl.BlockSpec(memory_space=pltpu.VMEM)
    hbm = pl.BlockSpec(memory_space=pl.ANY)
    return pl.pallas_call(
        functools.partial(settle_kernel, count, near, group),
        out_shape=[
            jax.ShapeDtypeStruct(shape, jnp.bfloat16),
            jax.ShapeDtypeStruct(moved.shape, moved.dtype),
        ],
        in_specs=[smem, smem, vmem, vmem, vmem, hbm],
        out_specs=[vmem, hbm],
        scratch_shapes=[
            pltpu.VMEM(mixed.shape, jnp.float32),
            pltpu.VMEM(windows.shape, windows.dtype),
            pltpu.SemaphoreType.DMA((count,)),
        ],
        input_output_aliases={5: 1},
        compiler_params=pltpu.CompilerParams(vmem_limit_bytes=SMALL_LIMIT),
        cost_estimate=LIGHT,
        name="settle",
    )(slots, lengths, mixed, small, windows, moved)


def local(hidden_new, queries, kv_cache, lengths, destination, key_weight, value_weight, key_gain):
    group = queries.shape[2] // kv_cache.shape[3]
    count = lax.axis_size("inst")
    near = near_size(count)

    near_blocks, far_blocks, pick = pack(kv_cache, destination, lengths, count, near)
    far_got = []
    for piece, block in enumerate(far_blocks, near):
        pairs = [(i, int(peer_to(i, piece, count))) for i in range(count)]
        far_got.append(lax.ppermute(block, "inst", pairs))
    own, other, near_blocks = project(hidden_new, key_weight, value_weight, near_blocks)
    near_got = near_blocks
    if near > 1:
        teams = [list(range(i, i + near)) for i in range(0, count, near)]
        near_got = lax.all_to_all(
            near_blocks, "inst", 0, 0, axis_index_groups=teams, tiled=True
        )
    got = lax.ppermute(other, "tp", [(0, 1), (1, 0)])
    moved, mixed, small = attend(
        kv_cache, queries, own, got, key_gain[None, :], lengths, pick, count
    )
    small_got = lax.all_to_all(small, "inst", 0, 0, tiled=True)
    moved, slots, arrived, windows = land(near_got, far_got, moved, count, near)
    return tuple(
        settle(
            slots, arrived, mixed, small_got, windows, moved, queries.shape, group, count, near
        )
    )


def solution(mesh):
    return jax.shard_map(
        local,
        mesh=mesh,
        in_specs=(
            P(None, ("group", "inst"), "tp"),
            P(None, ("group", "inst"), "tp"),
            P(("group", "inst"), None, None, "tp"),
            P(("group", "inst")),
            P(("group", "inst")),
            P("tp", None),
            P("tp", None),
            P(),
        ),
        out_specs=(P(None, ("group", "inst"), "tp"), P(("group", "inst"), None, None, "tp")),
        check_vma=False,
    )
```

```python
import functools
import math

import jax
import jax.numpy as jnp
from jax import lax
from jax.experimental import pallas as pl
from jax.experimental.pallas import tpu as pltpu
from jax.sharding import PartitionSpec as P

HD = 128
ROPE_BASE = 1000000.0
NORM_EPS = 1e-06
VMEM_LIMIT = 62 * 1024 * 1024
PACK_LIMIT = 59 * 1024 * 1024
SMALL_LIMIT = 40 * 1024 * 1024
LIGHT = pl.CostEstimate(flops=1, bytes_accessed=1, transcendentals=0)
HEAVY = pl.CostEstimate(flops=1 << 36, bytes_accessed=1 << 28, transcendentals=0)
TILE = 16
WINDOW = 32


def quotient(value, divisor, bound):
    factor = -(-(1 << 16) // divisor)
    if bound * factor < 1 << 31 and all(
        (x * factor) >> 16 == x // divisor for x in range(bound)
    ):
        return (value * factor) >> 16
    return value // divisor


def peer_to(index, shift, count, paired=None):
    if count & (count - 1) == 0:
        return index ^ (shift if paired is None else paired)
    return (index + shift) % count


def near_size(count):
    return 4 if count % 4 == 0 and count & (count - 1) == 0 else 1


def peer_of(me, piece, near, to):
    count = lax.axis_size("inst")
    if piece < near:
        return me // near * near + piece
    return peer_to(me, piece, count) if to else peer_to(me, count - piece, count, piece)


def pack_kernel(count, near, dest_ref, length_ref, kv_ref, near_ref, *refs):
    far_refs = refs[: count - near]
    pick_ref, sems = refs[count - near :]
    rows = dest_ref.shape[0]
    capacity, lanes = kv_ref.shape[2:]
    me = lax.axis_index("inst")
    for peer in range(count):
        pick_ref[peer] = 0
    for row in range(rows):
        pick_ref[quotient(dest_ref[row], rows, rows * count)] = row
    order = list(range(near)) + list(range(near, count))
    blocks = [near_ref.at[piece] for piece in range(near)] + list(far_refs)
    copies = {}
    for piece in order:
        row = pick_ref[peer_of(me, piece, near, True)]
        copies[piece] = pltpu.make_async_copy(kv_ref.at[row], blocks[piece], sems.at[piece])
        copies[piece].start()
    tile = (TILE, lanes)
    last = lax.broadcasted_iota(jnp.int32, tile, 0) == TILE - 1
    first_lanes = lax.broadcasted_iota(jnp.int32, tile, 1) < HD
    for piece in order:
        peer = peer_of(me, piece, near, True)
        row = pick_ref[peer]
        slot = dest_ref[row] - peer * rows
        slot = jnp.where((slot >= 0) & (slot < rows), slot, -1)
        facts = jnp.where(first_lanes, slot, length_ref[row]).astype(jnp.float32)
        copies[piece].wait()
        end = blocks[piece][0, capacity - TILE :, :].astype(jnp.float32)
        blocks[piece][0, capacity - TILE :, :] = jnp.where(last, facts, end).astype(jnp.bfloat16)


def pack(kv_cache, destination, lengths, count, near):
    shape = kv_cache.shape[1:]
    smem = pl.BlockSpec(memory_space=pltpu.SMEM)
    vmem = pl.BlockSpec(memory_space=pltpu.VMEM)
    outs = pl.pallas_call(
        functools.partial(pack_kernel, count, near),
        out_shape=[jax.ShapeDtypeStruct((near,) + shape, kv_cache.dtype)]
        + [jax.ShapeDtypeStruct(shape, kv_cache.dtype)] * (count - near)
        + [jax.ShapeDtypeStruct((count,), jnp.int32)],
        in_specs=[smem, smem, pl.BlockSpec(memory_space=pl.ANY)],
        out_specs=[vmem] * (count - near + 1) + [smem],
        scratch_shapes=[pltpu.SemaphoreType.DMA((count,))],
        compiler_params=pltpu.CompilerParams(vmem_limit_bytes=PACK_LIMIT),
        cost_estimate=LIGHT,
        name="pack",
    )(destination, lengths, kv_cache)
    return outs[0], outs[1:-1], outs[-1]


def project_kernel(chunks, hidden_ref, key_ref, value_ref, own_ref, other_ref, held, total, sems):
    steps, rows, depth = hidden_ref.shape
    width = key_ref.shape[1]
    part = depth // chunks
    copies = []
    for chunk in range(chunks):
        span = pl.ds(chunk * part, part)
        for which, ref in enumerate((key_ref, value_ref)):
            copies.append(
                pltpu.make_async_copy(
                    ref.at[span], held.at[which, span], sems.at[chunk, which]
                )
            )
            copies[-1].start()
    hidden = hidden_ref[...].reshape(steps * rows, depth)
    sums = [None, None]
    for chunk in range(chunks):
        for which in range(2):
            copies[2 * chunk + which].wait()
            product = jnp.dot(
                hidden[:, chunk * part : (chunk + 1) * part],
                held[which, chunk * part : (chunk + 1) * part, :],
                preferred_element_type=jnp.float32,
            )
            sums[which] = product if chunk == 0 else sums[which] + product
    total[:, :width] = sums[0]
    total[:, width:] = sums[1]
    half = width // 2
    me = lax.axis_index("tp")
    for ref, core in ((own_ref, me), (other_ref, 1 - me)):
        at = pl.multiple_of(core * half, half)
        ref[:, :half] = total[:, pl.ds(at, half)]
        ref[:, half:] = total[:, pl.ds(pl.multiple_of(width + at, half), half)]


def project(hidden_new, key_weight, value_weight):
    steps, rows, depth = hidden_new.shape
    width = key_weight.shape[1]
    chunks = 5
    shape = jax.ShapeDtypeStruct((steps * rows, width), jnp.float32)
    vmem = pl.BlockSpec(memory_space=pltpu.VMEM)
    hbm = pl.BlockSpec(memory_space=pl.ANY)
    return pl.pallas_call(
        functools.partial(project_kernel, chunks),
        out_shape=[shape, shape],
        in_specs=[vmem, hbm, hbm],
        out_specs=[vmem, vmem],
        scratch_shapes=[
            pltpu.VMEM((2, depth, width), key_weight.dtype),
            pltpu.VMEM((steps * rows, 2 * width), jnp.float32),
            pltpu.SemaphoreType.DMA((chunks, 2)),
        ],
        compiler_params=pltpu.CompilerParams(vmem_limit_bytes=VMEM_LIMIT),
        cost_estimate=LIGHT,
        name="project",
    )(hidden_new, key_weight, value_weight)


def rotation(length_ref, steps, rows):
    half = HD // 2
    line = lax.broadcasted_iota(jnp.int32, (steps * rows, HD), 0)
    lane = lax.broadcasted_iota(jnp.int32, (steps * rows, HD), 1)
    position = jnp.zeros((steps * rows, HD), jnp.int32)
    for step in range(steps):
        for row in range(rows):
            position = jnp.where(line == step * rows + row, length_ref[row] + step, position)
    order = (lane % half).astype(jnp.float32)
    angle = position.astype(jnp.float32) * jnp.exp(-math.log(ROPE_BASE) * 2.0 * order / HD)
    sine = jnp.sin(angle)
    return jnp.cos(angle), jnp.where(lane < half, -sine, sine)


def attend_kernel(
    count,
    block,
    length_ref,
    dest_ref,
    pick_ref,
    own_ref,
    got_ref,
    gain_ref,
    query_ref,
    kv_ref,
    _,
    moved_ref,
    mixed_ref,
    small_ref,
    late_ref,
    fresh,
    query_rows,
    query_columns,
    mixed,
):
    del late_ref
    part = pl.program_id(0)
    steps, rows, query_width = query_ref.shape
    capacity, lanes = kv_ref.shape[2:]
    heads = lanes // HD
    group = query_width // lanes
    per_head = steps * group
    per_row = heads * per_head
    team = HD // per_row

    @pl.when(part == 0)
    def _():
        raw = own_ref[...] + got_ref[...]
        cosine, sine = rotation(length_ref, steps, rows)
        gain = gain_ref[...].astype(jnp.float32)
        for head in range(heads):
            at = slice(head * HD, (head + 1) * HD)
            piece = raw[:, at]
            mean = jnp.mean(piece * piece, axis=-1, keepdims=True)
            piece = piece * lax.rsqrt(mean + NORM_EPS) * gain
            swapped = jnp.concatenate([piece[:, HD // 2 :], piece[:, : HD // 2]], axis=1)
            turned = piece * cosine + swapped * sine
            fresh[0, :, at] = turned.astype(jnp.bfloat16).astype(jnp.float32)
        fresh[1] = raw[:, lanes:].astype(jnp.bfloat16).astype(jnp.float32)
        for step in range(steps):
            for chunk in range(query_width // HD):
                head, member = chunk // group, chunk % group
                at = head * per_head + step * group + member
                query_rows[pl.ds(at, rows, stride=per_row), :] = query_ref[
                    step, :, chunk * HD : (chunk + 1) * HD
                ].astype(jnp.float32)
        for index in range(rows // team):
            query_columns[index] = query_rows[index * HD : (index + 1) * HD, :].T

    position = lax.broadcasted_iota(jnp.int32, (capacity, HD), 0)
    column = lax.broadcasted_iota(jnp.int32, (capacity, HD), 1)
    column_item = column // per_row
    column_step = (column % per_head) // group
    column_head = lax.broadcasted_iota(jnp.int32, (HD, HD), 1) % per_row // per_head
    factor = 1.0 / math.sqrt(HD)
    teams = range(block // team)
    scores = []
    for index in teams:
        queries = query_columns[part * (block // team) + index]
        queries = jnp.concatenate(
            [jnp.where(column_head == head, queries, 0.0) for head in range(heads)], axis=0
        ).astype(jnp.bfloat16)
        score, limit = None, None
        for member in range(team):
            item = index * team + member
            row = part * block + item
            length = length_ref[row]
            kept = position < length
            landing = [position == length + step for step in range(steps)]
            for which in range(2):
                news = [fresh[which, pl.ds(step * rows + row, 1), :] for step in range(steps)]
                for head in range(heads):
                    at = slice(head * HD, (head + 1) * HD)
                    stored = jnp.where(kept, kv_ref[item, which, :, at].astype(jnp.float32), 0.0)
                    for step in range(steps):
                        stored = jnp.where(landing[step], news[step][:, at], stored)
                    moved_ref[item, which, :, at] = stored.astype(jnp.bfloat16)
            one = jnp.dot(moved_ref[item, 0], queries, preferred_element_type=jnp.float32)
            score = one if member == 0 else jnp.where(column_item == member, one, score)
            limit = length if member == 0 else jnp.where(column_item == member, length, limit)
        scores.append(jnp.where(position <= limit + column_step, score * factor, -jnp.inf))
    weights = []
    for score in scores:
        raised = jnp.exp(score - jnp.max(score, axis=0, keepdims=True))
        normaliser = jnp.sum(raised, axis=0, keepdims=True)
        weights.append((raised / normaliser).T.astype(jnp.bfloat16))
    for index in teams:
        for member in range(team):
            item = index * team + member
            row = part * block + item
            result = jnp.dot(
                weights[index][member * per_row : (member + 1) * per_row],
                moved_ref[item, 1],
                preferred_element_type=jnp.float32,
            )
            for head in range(heads):
                at = pl.multiple_of(row * per_row + head * per_head, per_head)
                mixed[pl.ds(at, per_head), :] = result[
                    head * per_head : (head + 1) * per_head, head * HD : (head + 1) * HD
                ]

    @pl.when(part == pl.num_programs(0) - 1)
    def _():
        mixed_ref[...] = mixed[...].astype(jnp.bfloat16)
        for peer in range(count):
            row = pick_ref[peer]
            small_ref[peer, :per_row, :] = mixed[
                pl.ds(pl.multiple_of(row * per_row, per_row), per_row), :
            ].astype(jnp.bfloat16)
            news = []
            for which in range(2):
                for step in range(steps):
                    new = fresh[which, pl.ds(step * rows + row, 1), :]
                    news += [new[:, h * HD : (h + 1) * HD] for h in range(heads)]
            slot = dest_ref[row] - peer * rows
            slot = jnp.where((slot >= 0) & (slot < rows), slot, -1).astype(jnp.float32)
            fill = small_ref.shape[1] - per_row - len(news)
            news.append(jnp.full((fill, HD), slot))
            small_ref[peer, per_row:, :] = jnp.concatenate(news, axis=0).astype(jnp.bfloat16)


def attend(
    kv_cache, queries, own, got, gain, lengths, destination, pick, late, count
):
    steps, rows, query_width = queries.shape
    capacity, lanes = kv_cache.shape[2:]
    heads = lanes // HD
    per_row = steps * query_width // HD
    block = 8
    small_rows = per_row + -(-(2 * steps * heads + 1) // TILE) * TILE
    small = jax.ShapeDtypeStruct((count, small_rows, HD), jnp.bfloat16)
    smem = pl.BlockSpec(memory_space=pltpu.SMEM)
    vmem = pl.BlockSpec(memory_space=pltpu.VMEM)
    hbm = pl.BlockSpec(memory_space=pl.ANY)
    cache_block = pl.BlockSpec((block, 2, capacity, lanes), lambda i: (i, 0, 0, 0))
    return pl.pallas_call(
        functools.partial(attend_kernel, count, block),
        grid=(rows // block,),
        out_shape=[
            jax.ShapeDtypeStruct(kv_cache.shape, kv_cache.dtype),
            jax.ShapeDtypeStruct((rows * per_row, HD), jnp.bfloat16),
            small,
            jax.ShapeDtypeStruct(late.shape, late.dtype),
        ],
        in_specs=[smem, smem, smem, vmem, vmem, vmem, vmem, cache_block, hbm],
        out_specs=[cache_block, vmem, vmem, hbm],
        scratch_shapes=[
            pltpu.VMEM((2, steps * rows, lanes), jnp.float32),
            pltpu.VMEM((rows * per_row, HD), jnp.float32),
            pltpu.VMEM((rows * per_row // HD, HD, HD), jnp.float32),
            pltpu.VMEM((rows * per_row, HD), jnp.float32),
        ],
        input_output_aliases={8: 3},
        compiler_params=pltpu.CompilerParams(vmem_limit_bytes=VMEM_LIMIT),
        cost_estimate=LIGHT,
        name="attend",
    )(lengths, destination, pick, own, got, gain, queries, kv_cache, late)


def read_facts(block):
    capacity = block.shape[1]
    facts = block[0, capacity - TILE :, :].astype(jnp.float32)[TILE - 1 :]
    return (
        jnp.max(facts[:, :HD]).astype(jnp.int32),
        jnp.max(facts[:, HD : 2 * HD]).astype(jnp.int32),
    )


def window_start(length, capacity):
    return pl.multiple_of(jnp.minimum(length // TILE * TILE, capacity - WINDOW), TILE)


def clean(block, length, out):
    capacity, lanes = block.shape[1:]
    kept = lax.broadcasted_iota(jnp.int32, (capacity, HD), 0) < length
    for which in range(2):
        for at in range(0, lanes, HD):
            stored = block[which, :, at : at + HD].astype(jnp.float32)
            out[which, :, at : at + HD] = jnp.where(kept, stored, 0.0).astype(jnp.bfloat16)


def insert(window, news, ahead, steps, out):
    height, lanes = window.shape[1:]
    heads = lanes // HD
    position = lax.broadcasted_iota(jnp.int32, (height, lanes), 0)
    for which in range(2):
        stored = window[which].astype(jnp.float32)
        for step in range(steps):
            at = (which * steps + step) * heads
            new = jnp.concatenate([news[at + h : at + h + 1] for h in range(heads)], axis=1)
            stored = jnp.where(position == ahead + step, new, stored)
        out[which] = stored.astype(jnp.bfloat16)


def land_kernel(near, near_ref, *refs):
    far_refs = refs[:-7]
    _, out_ref, slot_ref, length_ref, window_ref, buffer, sems = refs[-7:]
    capacity = buffer.shape[2]
    me = lax.axis_index("inst")
    blocks = [near_ref.at[piece] for piece in range(near)] + list(far_refs)

    def store(piece):
        slot = jnp.maximum(slot_ref[piece], 0)
        return pltpu.make_async_copy(buffer.at[piece], out_ref.at[slot], sems.at[piece])

    for piece, block in enumerate(blocks):
        slot, length = read_facts(block)
        if piece < near:
            slot = jnp.where(me % near == piece, -1, slot)
        slot_ref[piece] = slot
        length_ref[piece] = length
    for piece, block in enumerate(blocks):

        @pl.when(slot_ref[piece] >= 0)
        def _():
            length = length_ref[piece]
            clean(block, length, buffer.at[piece])
            store(piece).start()
            start = window_start(length, capacity)
            window_ref[piece] = buffer[piece, :, pl.ds(start, WINDOW), :]

    for piece in range(len(blocks)):

        @pl.when(slot_ref[piece] >= 0)
        def _():
            store(piece).wait()


def land(near_got, far_got, moved):
    near = near_got.shape[0]
    pieces = near + len(far_got)
    smem = pl.BlockSpec(memory_space=pltpu.SMEM)
    vmem = pl.BlockSpec(memory_space=pltpu.VMEM)
    hbm = pl.BlockSpec(memory_space=pl.ANY)
    scalars = jax.ShapeDtypeStruct((pieces,), jnp.int32)
    return pl.pallas_call(
        functools.partial(land_kernel, near),
        out_shape=[
            jax.ShapeDtypeStruct(moved.shape, moved.dtype),
            scalars,
            scalars,
            jax.ShapeDtypeStruct((pieces, 2, WINDOW, moved.shape[3]), moved.dtype),
        ],
        in_specs=[vmem] * (1 + len(far_got)) + [hbm],
        out_specs=[hbm, smem, smem, vmem],
        scratch_shapes=[
            pltpu.VMEM((pieces,) + moved.shape[1:], moved.dtype),
            pltpu.SemaphoreType.DMA((pieces,)),
        ],
        input_output_aliases={1 + len(far_got): 0},
        compiler_params=pltpu.CompilerParams(vmem_limit_bytes=SMALL_LIMIT),
        cost_estimate=HEAVY,
        name="land",
    )(near_got, *far_got, moved)


def settle_kernel(
    count,
    near,
    group,
    slot_ref,
    length_ref,
    mixed_ref,
    small_ref,
    window_ref,
    _,
    out_ref,
    moved_ref,
    mixed,
    windows,
    sems,
):
    steps, rows, query_width = out_ref.shape
    per_row = steps * query_width // HD
    capacity, lanes = moved_ref.shape[2:]
    heads = lanes // HD
    me = lax.axis_index("inst")
    pieces = slot_ref.shape[0]

    def store(piece):
        slot = jnp.maximum(slot_ref[piece], 0)
        start = window_start(length_ref[piece], capacity)
        return pltpu.make_async_copy(
            windows.at[piece], moved_ref.at[slot, :, pl.ds(start, WINDOW), :], sems.at[piece]
        )

    def take(slot, peer):
        mixed[pl.ds(pl.multiple_of(slot * per_row, per_row), per_row), :] = small_ref[
            peer, :per_row, :
        ].astype(jnp.float32)

    for piece in range(pieces):

        @pl.when(slot_ref[piece] >= 0)
        def _():
            length = length_ref[piece]
            peer = peer_of(me, piece, near, False)
            news = small_ref[peer, per_row:, :].astype(jnp.float32)
            ahead = length - window_start(length, capacity)
            insert(window_ref.at[piece], news, ahead, steps, windows.at[piece])
            store(piece).start()

    mixed[...] = mixed_ref[...].astype(jnp.float32)
    for piece in range(count):
        peer = peer_of(me, piece, near, False)
        if piece < pieces:
            slot = slot_ref[piece]
        else:
            line = 2 * steps * heads
            facts = small_ref[peer, per_row:, :].astype(jnp.float32)[line : line + 1]
            slot = jnp.max(facts).astype(jnp.int32)
        pl.when(slot >= 0)(functools.partial(take, slot, peer))
    for step in range(steps):
        for chunk in range(query_width // HD):
            head, member = chunk // group, chunk % group
            at = head * steps * group + step * group + member
            out_ref[step, :, chunk * HD : (chunk + 1) * HD] = mixed[
                pl.ds(at, rows, stride=per_row), :
            ].astype(jnp.bfloat16)

    for piece in range(pieces):

        @pl.when(slot_ref[piece] >= 0)
        def _():
            store(piece).wait()


def settle(slots, lengths, mixed, small, windows, moved, shape, group, count, near):
    smem = pl.BlockSpec(memory_space=pltpu.SMEM)
    vmem = pl.BlockSpec(memory_space=pltpu.VMEM)
    hbm = pl.BlockSpec(memory_space=pl.ANY)
    return pl.pallas_call(
        functools.partial(settle_kernel, count, near, group),
        out_shape=[
            jax.ShapeDtypeStruct(shape, jnp.bfloat16),
            jax.ShapeDtypeStruct(moved.shape, moved.dtype),
        ],
        in_specs=[smem, smem, vmem, vmem, vmem, hbm],
        out_specs=[vmem, hbm],
        scratch_shapes=[
            pltpu.VMEM(mixed.shape, jnp.float32),
            pltpu.VMEM(windows.shape, windows.dtype),
            pltpu.SemaphoreType.DMA((slots.shape[0],)),
        ],
        input_output_aliases={5: 1},
        compiler_params=pltpu.CompilerParams(vmem_limit_bytes=SMALL_LIMIT),
        cost_estimate=LIGHT,
        name="settle",
    )(slots, lengths, mixed, small, windows, moved)


def finish_kernel(count, near, steps, late_ref, small_ref, _, out_ref, buffer, sem):
    capacity, lanes = buffer.shape[1:]
    news_rows = 2 * steps * (lanes // HD)
    slot, length = read_facts(late_ref)
    peer = peer_of(lax.axis_index("inst"), count - 1, near, False)

    @pl.when(slot >= 0)
    def _():
        clean(late_ref, length, buffer)
        start = window_start(length, capacity)
        window = buffer.at[:, pl.ds(start, WINDOW), :]
        height = small_ref.shape[1]
        tail = height - -(-(news_rows + 1) // TILE) * TILE
        news = small_ref[peer, tail:, :].astype(jnp.float32)
        insert(window, news, length - start, steps, window)
        copy = pltpu.make_async_copy(buffer, out_ref.at[slot], sem)
        copy.start()
        copy.wait()


def finish(late_got, small, moved, steps, count, near):
    vmem = pl.BlockSpec(memory_space=pltpu.VMEM)
    hbm = pl.BlockSpec(memory_space=pl.ANY)
    return pl.pallas_call(
        functools.partial(finish_kernel, count, near, steps),
        out_shape=jax.ShapeDtypeStruct(moved.shape, moved.dtype),
        in_specs=[vmem, vmem, hbm],
        out_specs=hbm,
        scratch_shapes=[
            pltpu.VMEM(late_got.shape, late_got.dtype),
            pltpu.SemaphoreType.DMA,
        ],
        input_output_aliases={2: 0},
        compiler_params=pltpu.CompilerParams(vmem_limit_bytes=SMALL_LIMIT),
        cost_estimate=LIGHT,
        name="finish",
    )(late_got, small, moved)


def local(hidden_new, queries, kv_cache, lengths, destination, key_weight, value_weight, key_gain):
    steps = queries.shape[0]
    group = queries.shape[2] // kv_cache.shape[3]
    count = lax.axis_size("inst")
    near = near_size(count)

    def send(block, piece):
        pairs = [(i, peer_to(i, piece, count)) for i in range(count)]
        return lax.ppermute(block, "inst", pairs)

    near_blocks, far_blocks, pick = pack(kv_cache, destination, lengths, count, near)
    near_got = near_blocks
    if near > 1:
        teams = [list(range(i, i + near)) for i in range(0, count, near)]
        near_got = lax.all_to_all(near_blocks, "inst", 0, 0, axis_index_groups=teams, tiled=True)
    far_got = [send(block, piece) for piece, block in enumerate(far_blocks[:-1], near)]
    own, other = project(hidden_new, key_weight, value_weight)
    got = lax.ppermute(other, "tp", [(0, 1), (1, 0)])
    moved, mixed, small, late = attend(
        kv_cache,
        queries,
        own,
        got,
        key_gain[None, :],
        lengths,
        destination,
        pick,
        far_blocks[-1],
        count,
    )
    late_got = send(late, count - 1)
    small_got = lax.all_to_all(small, "inst", 0, 0, tiled=True)
    moved, slots, arrived, windows = land(near_got, far_got, moved)
    attended, moved = settle(
        slots, arrived, mixed, small_got, windows, moved, queries.shape, group, count, near
    )
    return attended, finish(late_got, small_got, moved, steps, count, near)


def solution(mesh):
    return jax.shard_map(
        local,
        mesh=mesh,
        in_specs=(
            P(None, ("group", "inst"), "tp"),
            P(None, ("group", "inst"), "tp"),
            P(("group", "inst"), None, None, "tp"),
            P(("group", "inst")),
            P(("group", "inst")),
            P("tp", None),
            P("tp", None),
            P(),
        ),
        out_specs=(P(None, ("group", "inst"), "tp"), P(("group", "inst"), None, None, "tp")),
        check_vma=False,
    )
```

```python
import functools
import math

import jax
import jax.numpy as jnp
from jax import lax
from jax.experimental import pallas as pl
from jax.experimental.pallas import tpu as pltpu
from jax.sharding import PartitionSpec as P

HD = 128
ROPE_BASE = 1000000.0
NORM_EPS = 1e-06
VMEM_LIMIT = 62 * 1024 * 1024
ATTEND_LIMIT = 56 * 1024 * 1024
SMALL_LIMIT = 40 * 1024 * 1024
LIGHT = pl.CostEstimate(flops=1, bytes_accessed=1, transcendentals=0)
HEAVY = pl.CostEstimate(flops=1 << 36, bytes_accessed=1 << 28, transcendentals=0)
TILE = 16
WINDOW = 32


def quotient(value, divisor, bound):
    factor = -(-(1 << 16) // divisor)
    if bound * factor < 1 << 31 and all(
        (x * factor) >> 16 == x // divisor for x in range(bound)
    ):
        return (value * factor) >> 16
    return value // divisor


def peer_to(index, shift, count):
    return index ^ shift if count & (count - 1) == 0 else (index + shift) % count


def peer_from(index, shift, count):
    return index ^ shift if count & (count - 1) == 0 else (index + count - shift) % count


def prepare_kernel(
    count, chunks, dest_ref, length_ref, hidden_ref, kv_ref, key_ref, value_ref, *refs
):
    block_refs = refs[: count - 1]
    pick_ref, own_ref, other_ref, blocks, held, total = refs[count - 1 : count + 5]
    in_sems, out_sems, weight_sems = refs[count + 5 :]
    rows = dest_ref.shape[0]
    capacity, lanes = kv_ref.shape[2:]
    me = lax.axis_index("inst")
    shifts = range(1, count)

    for peer in range(count):
        pick_ref[peer] = 0
    for row in range(rows):
        pick_ref[quotient(dest_ref[row], rows, rows * count)] = row
    fetches, stores = {}, {}
    for shift in shifts:
        row = pick_ref[peer_to(me, shift, count)]
        fetches[shift] = pltpu.make_async_copy(
            kv_ref.at[row], blocks.at[shift - 1], in_sems.at[shift - 1]
        )
        fetches[shift].start()

    steps, _, depth = hidden_ref.shape
    width = key_ref.shape[1]
    part = depth // chunks
    weights = []
    for chunk in range(chunks):
        span = pl.ds(chunk * part, part)
        for which, ref in enumerate((key_ref, value_ref)):
            weights.append(
                pltpu.make_async_copy(
                    ref.at[span], held.at[which, span], weight_sems.at[chunk, which]
                )
            )
            weights[-1].start()

    tile = (TILE, lanes)
    last = lax.broadcasted_iota(jnp.int32, tile, 0) == TILE - 1
    first_lanes = lax.broadcasted_iota(jnp.int32, tile, 1) < HD
    for shift in shifts:
        peer = peer_to(me, shift, count)
        row = pick_ref[peer]
        slot = dest_ref[row] - peer * rows
        slot = jnp.where((slot >= 0) & (slot < rows), slot, -1)
        facts = jnp.where(first_lanes, slot, length_ref[row]).astype(jnp.float32)
        fetches[shift].wait()
        end = blocks[shift - 1, 0, capacity - TILE :, :].astype(jnp.float32)
        blocks[shift - 1, 0, capacity - TILE :, :] = jnp.where(last, facts, end).astype(
            jnp.bfloat16
        )
        stores[shift] = pltpu.make_async_copy(
            blocks.at[shift - 1], block_refs[shift - 1], out_sems.at[shift - 1]
        )
        stores[shift].start()

    hidden = hidden_ref[...].reshape(steps * rows, depth)
    sums = [None, None]
    for chunk in range(chunks):
        for which in range(2):
            weights[2 * chunk + which].wait()
            product = jnp.dot(
                hidden[:, chunk * part : (chunk + 1) * part],
                held[which, chunk * part : (chunk + 1) * part, :],
                preferred_element_type=jnp.float32,
            )
            sums[which] = product if chunk == 0 else sums[which] + product
    total[:, :width] = sums[0]
    total[:, width:] = sums[1]
    half = width // 2
    core = lax.axis_index("tp")
    for ref, place in ((own_ref, core), (other_ref, 1 - core)):
        at = pl.multiple_of(place * half, half)
        ref[:, :half] = total[:, pl.ds(at, half)]
        ref[:, half:] = total[:, pl.ds(pl.multiple_of(width + at, half), half)]
    for shift in shifts:
        stores[shift].wait()


def prepare(destination, lengths, hidden_new, kv_cache, key_weight, value_weight, count):
    steps, rows, depth = hidden_new.shape
    width = key_weight.shape[1]
    chunks = 5
    shape = kv_cache.shape[1:]
    part = jax.ShapeDtypeStruct((steps * rows, width), jnp.float32)
    smem = pl.BlockSpec(memory_space=pltpu.SMEM)
    vmem = pl.BlockSpec(memory_space=pltpu.VMEM)
    hbm = pl.BlockSpec(memory_space=pl.ANY)
    outs = pl.pallas_call(
        functools.partial(prepare_kernel, count, chunks),
        out_shape=[jax.ShapeDtypeStruct(shape, kv_cache.dtype)] * (count - 1)
        + [jax.ShapeDtypeStruct((count,), jnp.int32), part, part],
        in_specs=[smem, smem, vmem, hbm, hbm, hbm],
        out_specs=[hbm] * (count - 1) + [smem, vmem, vmem],
        scratch_shapes=[
            pltpu.VMEM((count - 1,) + shape, kv_cache.dtype),
            pltpu.VMEM((2, depth, width), key_weight.dtype),
            pltpu.VMEM((steps * rows, 2 * width), jnp.float32),
            pltpu.SemaphoreType.DMA((count - 1,)),
            pltpu.SemaphoreType.DMA((count - 1,)),
            pltpu.SemaphoreType.DMA((chunks, 2)),
        ],
        compiler_params=pltpu.CompilerParams(vmem_limit_bytes=VMEM_LIMIT),
        cost_estimate=LIGHT,
        name="prepare",
    )(destination, lengths, hidden_new, kv_cache, key_weight, value_weight)
    return outs[: count - 1], *outs[count - 1 :]


def rotation(length_ref, steps, rows):
    half = HD // 2
    line = lax.broadcasted_iota(jnp.int32, (steps * rows, HD), 0)
    lane = lax.broadcasted_iota(jnp.int32, (steps * rows, HD), 1)
    position = jnp.zeros((steps * rows, HD), jnp.int32)
    for step in range(steps):
        for row in range(rows):
            position = jnp.where(line == step * rows + row, length_ref[row] + step, position)
    order = (lane % half).astype(jnp.float32)
    angle = position.astype(jnp.float32) * jnp.exp(-math.log(ROPE_BASE) * 2.0 * order / HD)
    sine = jnp.sin(angle)
    return jnp.cos(angle), jnp.where(lane < half, -sine, sine)


def attend_kernel(
    count,
    block,
    length_ref,
    dest_ref,
    pick_ref,
    own_ref,
    got_ref,
    gain_ref,
    query_ref,
    kv_ref,
    *refs,
):
    late = (len(refs) - 7) // 2
    moved_ref, mixed_ref, small_ref = refs[late : late + 3]
    fresh, query_rows, query_columns, mixed = refs[-4:]
    part = pl.program_id(0)
    steps, rows, query_width = query_ref.shape
    capacity, lanes = kv_ref.shape[2:]
    heads = lanes // HD
    group = query_width // lanes
    per_head = steps * group
    per_row = heads * per_head
    team = HD // per_row

    @pl.when(part == 0)
    def _():
        raw = own_ref[...] + got_ref[...]
        cosine, sine = rotation(length_ref, steps, rows)
        gain = gain_ref[...].astype(jnp.float32)
        for head in range(heads):
            at = slice(head * HD, (head + 1) * HD)
            piece = raw[:, at]
            mean = jnp.mean(piece * piece, axis=-1, keepdims=True)
            piece = piece * lax.rsqrt(mean + NORM_EPS) * gain
            swapped = jnp.concatenate([piece[:, HD // 2 :], piece[:, : HD // 2]], axis=1)
            turned = piece * cosine + swapped * sine
            fresh[0, :, at] = turned.astype(jnp.bfloat16).astype(jnp.float32)
        fresh[1] = raw[:, lanes:].astype(jnp.bfloat16).astype(jnp.float32)
        for step in range(steps):
            for chunk in range(query_width // HD):
                head, member = chunk // group, chunk % group
                at = head * per_head + step * group + member
                query_rows[pl.ds(at, rows, stride=per_row), :] = query_ref[
                    step, :, chunk * HD : (chunk + 1) * HD
                ].astype(jnp.float32)
        for index in range(rows // team):
            query_columns[index] = query_rows[index * HD : (index + 1) * HD, :].T

    position = lax.broadcasted_iota(jnp.int32, (capacity, HD), 0)
    column = lax.broadcasted_iota(jnp.int32, (capacity, HD), 1)
    column_item = column // per_row
    column_step = (column % per_head) // group
    column_head = lax.broadcasted_iota(jnp.int32, (HD, HD), 1) % per_row // per_head
    factor = 1.0 / math.sqrt(HD)
    teams = range(block // team)
    scores = []
    for index in teams:
        queries = query_columns[part * (block // team) + index]
        queries = jnp.concatenate(
            [jnp.where(column_head == head, queries, 0.0) for head in range(heads)], axis=0
        ).astype(jnp.bfloat16)
        score, limit = None, None
        for member in range(team):
            item = index * team + member
            row = part * block + item
            length = length_ref[row]
            kept = position < length
            landing = [position == length + step for step in range(steps)]
            for which in range(2):
                news = [fresh[which, pl.ds(step * rows + row, 1), :] for step in range(steps)]
                for head in range(heads):
                    at = slice(head * HD, (head + 1) * HD)
                    stored = jnp.where(kept, kv_ref[item, which, :, at].astype(jnp.float32), 0.0)
                    for step in range(steps):
                        stored = jnp.where(landing[step], news[step][:, at], stored)
                    moved_ref[item, which, :, at] = stored.astype(jnp.bfloat16)
            one = jnp.dot(moved_ref[item, 0], queries, preferred_element_type=jnp.float32)
            score = one if member == 0 else jnp.where(column_item == member, one, score)
            limit = length if member == 0 else jnp.where(column_item == member, length, limit)
        scores.append(jnp.where(position <= limit + column_step, score * factor, -jnp.inf))
    weights = []
    for score in scores:
        raised = jnp.exp(score - jnp.max(score, axis=0, keepdims=True))
        normaliser = jnp.sum(raised, axis=0, keepdims=True)
        weights.append((raised / normaliser).T.astype(jnp.bfloat16))
    for index in teams:
        for member in range(team):
            item = index * team + member
            row = part * block + item
            result = jnp.dot(
                weights[index][member * per_row : (member + 1) * per_row],
                moved_ref[item, 1],
                preferred_element_type=jnp.float32,
            )
            for head in range(heads):
                at = pl.multiple_of(row * per_row + head * per_head, per_head)
                mixed[pl.ds(at, per_head), :] = result[
                    head * per_head : (head + 1) * per_head, head * HD : (head + 1) * HD
                ]

    @pl.when(part == pl.num_programs(0) - 1)
    def _():
        mixed_ref[...] = mixed[...].astype(jnp.bfloat16)
        for peer in range(count):
            row = pick_ref[peer]
            small_ref[peer, :per_row, :] = mixed[
                pl.ds(pl.multiple_of(row * per_row, per_row), per_row), :
            ].astype(jnp.bfloat16)
            news = []
            for which in range(2):
                for step in range(steps):
                    new = fresh[which, pl.ds(step * rows + row, 1), :]
                    news += [new[:, h * HD : (h + 1) * HD] for h in range(heads)]
            slot = dest_ref[row] - peer * rows
            slot = jnp.where((slot >= 0) & (slot < rows), slot, -1).astype(jnp.float32)
            fill = small_ref.shape[1] - per_row - len(news)
            news.append(jnp.full((fill, HD), slot))
            small_ref[peer, per_row:, :] = jnp.concatenate(news, axis=0).astype(jnp.bfloat16)


def attend(
    kv_cache, queries, own, got, gain, lengths, destination, pick, late, count
):
    late_shapes = [jax.ShapeDtypeStruct(x.shape, x.dtype) for x in late]
    steps, rows, query_width = queries.shape
    capacity, lanes = kv_cache.shape[2:]
    heads = lanes // HD
    per_row = steps * query_width // HD
    block = 8
    small_rows = per_row + -(-(2 * steps * heads + 1) // TILE) * TILE
    small = jax.ShapeDtypeStruct((count, small_rows, HD), jnp.bfloat16)
    smem = pl.BlockSpec(memory_space=pltpu.SMEM)
    vmem = pl.BlockSpec(memory_space=pltpu.VMEM)
    hbm = pl.BlockSpec(memory_space=pl.ANY)
    cache_block = pl.BlockSpec((block, 2, capacity, lanes), lambda i: (i, 0, 0, 0))
    outs = pl.pallas_call(
        functools.partial(attend_kernel, count, block),
        grid=(rows // block,),
        out_shape=[
            jax.ShapeDtypeStruct(kv_cache.shape, kv_cache.dtype),
            jax.ShapeDtypeStruct((rows * per_row, HD), jnp.bfloat16),
            small,
        ]
        + late_shapes,
        in_specs=[smem, smem, smem, vmem, vmem, vmem, vmem, cache_block] + [hbm] * len(late),
        out_specs=[cache_block, vmem, vmem] + [hbm] * len(late),
        scratch_shapes=[
            pltpu.VMEM((2, steps * rows, lanes), jnp.float32),
            pltpu.VMEM((rows * per_row, HD), jnp.float32),
            pltpu.VMEM((rows * per_row // HD, HD, HD), jnp.float32),
            pltpu.VMEM((rows * per_row, HD), jnp.float32),
        ],
        input_output_aliases={8 + i: 3 + i for i in range(len(late))},
        compiler_params=pltpu.CompilerParams(vmem_limit_bytes=ATTEND_LIMIT),
        cost_estimate=LIGHT,
        name="attend",
    )(lengths, destination, pick, own, got, gain, queries, kv_cache, *late)
    return outs[0], outs[1], outs[2], outs[3:]


def read_facts(block):
    capacity = block.shape[1]
    facts = block[0, capacity - TILE :, :].astype(jnp.float32)[TILE - 1 :]
    return (
        jnp.max(facts[:, :HD]).astype(jnp.int32),
        jnp.max(facts[:, HD : 2 * HD]).astype(jnp.int32),
    )


def window_start(length, capacity):
    return pl.multiple_of(jnp.minimum(length // TILE * TILE, capacity - WINDOW), TILE)


def clean(block, length, out):
    capacity, lanes = block.shape[1:]
    kept = lax.broadcasted_iota(jnp.int32, (capacity, HD), 0) < length
    for which in range(2):
        for at in range(0, lanes, HD):
            stored = block[which, :, at : at + HD].astype(jnp.float32)
            out[which, :, at : at + HD] = jnp.where(kept, stored, 0.0).astype(jnp.bfloat16)


def insert(window, news, ahead, steps, out):
    height, lanes = window.shape[1:]
    heads = lanes // HD
    position = lax.broadcasted_iota(jnp.int32, (height, lanes), 0)
    for which in range(2):
        stored = window[which].astype(jnp.float32)
        for step in range(steps):
            at = (which * steps + step) * heads
            new = jnp.concatenate([news[at + h : at + h + 1] for h in range(heads)], axis=1)
            stored = jnp.where(position == ahead + step, new, stored)
        out[which] = stored.astype(jnp.bfloat16)


def land_kernel(pieces, *refs):
    blocks = refs[:pieces]
    _, out_ref, slot_ref, length_ref, window_ref, buffer, sems = refs[pieces:]
    capacity = buffer.shape[2]

    def store(piece):
        slot = jnp.maximum(slot_ref[piece], 0)
        return pltpu.make_async_copy(buffer.at[piece], out_ref.at[slot], sems.at[piece])

    for piece, block in enumerate(blocks):
        slot_ref[piece], length_ref[piece] = read_facts(block)
    for piece, block in enumerate(blocks):

        @pl.when(slot_ref[piece] >= 0)
        def _():
            length = length_ref[piece]
            clean(block, length, buffer.at[piece])
            store(piece).start()
            start = window_start(length, capacity)
            window_ref[piece] = buffer[piece, :, pl.ds(start, WINDOW), :]

    for piece in range(pieces):

        @pl.when(slot_ref[piece] >= 0)
        def _():
            store(piece).wait()


def land(got, moved):
    pieces = len(got)
    smem = pl.BlockSpec(memory_space=pltpu.SMEM)
    vmem = pl.BlockSpec(memory_space=pltpu.VMEM)
    hbm = pl.BlockSpec(memory_space=pl.ANY)
    scalars = jax.ShapeDtypeStruct((pieces,), jnp.int32)
    return pl.pallas_call(
        functools.partial(land_kernel, pieces),
        out_shape=[
            jax.ShapeDtypeStruct(moved.shape, moved.dtype),
            scalars,
            scalars,
            jax.ShapeDtypeStruct((pieces, 2, WINDOW, moved.shape[3]), moved.dtype),
        ],
        in_specs=[vmem] * pieces + [hbm],
        out_specs=[hbm, smem, smem, vmem],
        scratch_shapes=[
            pltpu.VMEM((pieces,) + moved.shape[1:], moved.dtype),
            pltpu.SemaphoreType.DMA((pieces,)),
        ],
        input_output_aliases={pieces: 0},
        compiler_params=pltpu.CompilerParams(vmem_limit_bytes=SMALL_LIMIT),
        cost_estimate=HEAVY,
        name="land",
    )(*got, moved)


def settle_kernel(
    count,
    early,
    group,
    slot_ref,
    length_ref,
    mixed_ref,
    small_ref,
    window_ref,
    _,
    out_ref,
    moved_ref,
    mixed,
    windows,
    sems,
):
    steps, rows, query_width = out_ref.shape
    per_row = steps * query_width // HD
    capacity, lanes = moved_ref.shape[2:]
    heads = lanes // HD
    me = lax.axis_index("inst")
    pieces = len(early)

    def store(piece):
        slot = jnp.maximum(slot_ref[piece], 0)
        start = window_start(length_ref[piece], capacity)
        return pltpu.make_async_copy(
            windows.at[piece], moved_ref.at[slot, :, pl.ds(start, WINDOW), :], sems.at[piece]
        )

    def take(slot, peer):
        mixed[pl.ds(pl.multiple_of(slot * per_row, per_row), per_row), :] = small_ref[
            peer, :per_row, :
        ].astype(jnp.float32)

    for piece in range(pieces):

        @pl.when(slot_ref[piece] >= 0)
        def _():
            length = length_ref[piece]
            peer = peer_from(me, early[piece], count)
            news = small_ref[peer, per_row:, :].astype(jnp.float32)
            ahead = length - window_start(length, capacity)
            insert(window_ref.at[piece], news, ahead, steps, windows.at[piece])
            store(piece).start()

    mixed[...] = mixed_ref[...].astype(jnp.float32)
    for shift in range(1, count):
        peer = peer_from(me, shift, count)
        if shift in early:
            slot = slot_ref[early.index(shift)]
        else:
            line = 2 * steps * heads
            facts = small_ref[peer, per_row:, :].astype(jnp.float32)[line : line + 1]
            slot = jnp.max(facts).astype(jnp.int32)
        pl.when(slot >= 0)(functools.partial(take, slot, peer))
    for step in range(steps):
        for chunk in range(query_width // HD):
            head, member = chunk // group, chunk % group
            at = head * steps * group + step * group + member
            out_ref[step, :, chunk * HD : (chunk + 1) * HD] = mixed[
                pl.ds(at, rows, stride=per_row), :
            ].astype(jnp.bfloat16)

    for piece in range(pieces):

        @pl.when(slot_ref[piece] >= 0)
        def _():
            store(piece).wait()


def settle(slots, lengths, mixed, small, windows, moved, shape, group, count, early):
    smem = pl.BlockSpec(memory_space=pltpu.SMEM)
    vmem = pl.BlockSpec(memory_space=pltpu.VMEM)
    hbm = pl.BlockSpec(memory_space=pl.ANY)
    return pl.pallas_call(
        functools.partial(settle_kernel, count, early, group),
        out_shape=[
            jax.ShapeDtypeStruct(shape, jnp.bfloat16),
            jax.ShapeDtypeStruct(moved.shape, moved.dtype),
        ],
        in_specs=[smem, smem, vmem, vmem, vmem, hbm],
        out_specs=[vmem, hbm],
        scratch_shapes=[
            pltpu.VMEM(mixed.shape, jnp.float32),
            pltpu.VMEM(windows.shape, windows.dtype),
            pltpu.SemaphoreType.DMA((slots.shape[0],)),
        ],
        input_output_aliases={5: 1},
        compiler_params=pltpu.CompilerParams(vmem_limit_bytes=SMALL_LIMIT),
        cost_estimate=LIGHT,
        name="settle",
    )(slots, lengths, mixed, small, windows, moved)


def finish_kernel(count, late, steps, *refs):
    blocks = refs[: len(late)]
    small_ref, _, out_ref, buffer, sems, slot_ref = refs[len(late) :]
    capacity, lanes = buffer.shape[2:]
    height = small_ref.shape[1]
    tail = height - -(-(2 * steps * (lanes // HD) + 1) // TILE) * TILE
    me = lax.axis_index("inst")

    def store(piece):
        slot = jnp.maximum(slot_ref[piece], 0)
        return pltpu.make_async_copy(buffer.at[piece], out_ref.at[slot], sems.at[piece])

    facts = [read_facts(block) for block in blocks]
    for piece, (slot, length) in enumerate(facts):
        slot_ref[piece] = slot

        @pl.when(slot >= 0)
        def _():
            clean(blocks[piece], length, buffer.at[piece])
            start = window_start(length, capacity)
            window = buffer.at[piece, :, pl.ds(start, WINDOW), :]
            news = small_ref[peer_from(me, late[piece], count), tail:, :].astype(jnp.float32)
            insert(window, news, length - start, steps, window)
            store(piece).start()

    for piece in range(len(late)):

        @pl.when(slot_ref[piece] >= 0)
        def _():
            store(piece).wait()


def finish(got, small, moved, steps, count, late):
    vmem = pl.BlockSpec(memory_space=pltpu.VMEM)
    hbm = pl.BlockSpec(memory_space=pl.ANY)
    return pl.pallas_call(
        functools.partial(finish_kernel, count, late, steps),
        out_shape=jax.ShapeDtypeStruct(moved.shape, moved.dtype),
        in_specs=[vmem] * len(got) + [vmem, hbm],
        out_specs=hbm,
        scratch_shapes=[
            pltpu.VMEM((len(got),) + moved.shape[1:], moved.dtype),
            pltpu.SemaphoreType.DMA((len(got),)),
            pltpu.SMEM((len(got),), jnp.int32),
        ],
        input_output_aliases={len(got) + 1: 0},
        compiler_params=pltpu.CompilerParams(vmem_limit_bytes=SMALL_LIMIT),
        cost_estimate=LIGHT,
        name="finish",
    )(*got, small, moved)


def local(hidden_new, queries, kv_cache, lengths, destination, key_weight, value_weight, key_gain):
    steps = queries.shape[0]
    group = queries.shape[2] // kv_cache.shape[3]
    count = lax.axis_size("inst")
    early = list(range(max(count // 2, 1), count - 1))
    late = [count - 1] + list(range(1, max(count // 2, 1)))

    def send(block, shift):
        pairs = [(i, peer_to(i, shift, count)) for i in range(count)]
        return lax.ppermute(block, "inst", pairs)

    blocks, pick, own, other = prepare(
        destination, lengths, hidden_new, kv_cache, key_weight, value_weight, count
    )
    early_got = [send(blocks[shift - 1], shift) for shift in early]
    got = lax.ppermute(other, "tp", [(0, 1), (1, 0)])
    moved, mixed, small, late_blocks = attend(
        kv_cache,
        queries,
        own,
        got,
        key_gain[None, :],
        lengths,
        destination,
        pick,
        [blocks[shift - 1] for shift in late],
        count,
    )
    late_got = [send(block, shift) for block, shift in zip(late_blocks, late)]
    small_got = lax.all_to_all(small, "inst", 0, 0, tiled=True)
    moved, slots, arrived, windows = land(early_got, moved)
    attended, moved = settle(
        slots, arrived, mixed, small_got, windows, moved, queries.shape, group, count, early
    )
    return attended, finish(late_got, small_got, moved, steps, count, late)


def solution(mesh):
    return jax.shard_map(
        local,
        mesh=mesh,
        in_specs=(
            P(None, ("group", "inst"), "tp"),
            P(None, ("group", "inst"), "tp"),
            P(("group", "inst"), None, None, "tp"),
            P(("group", "inst")),
            P(("group", "inst")),
            P("tp", None),
            P("tp", None),
            P(),
        ),
        out_specs=(P(None, ("group", "inst"), "tp"), P(("group", "inst"), None, None, "tp")),
        check_vma=False,
    )
```

```python
import functools
import math

import jax
import jax.numpy as jnp
from jax import lax
from jax.experimental import pallas as pl
from jax.experimental.pallas import tpu as pltpu
from jax.sharding import PartitionSpec as P

HD = 128
ROPE_BASE = 1000000.0
NORM_EPS = 1e-06
VMEM_LIMIT = 62 * 1024 * 1024
ATTEND_LIMIT = 56 * 1024 * 1024
SMALL_LIMIT = 40 * 1024 * 1024
LIGHT = pl.CostEstimate(flops=1, bytes_accessed=1, transcendentals=0)
HEAVY = pl.CostEstimate(flops=1 << 36, bytes_accessed=1 << 28, transcendentals=0)
TILE = 16
WINDOW = 32


def quotient(value, divisor, bound):
    factor = -(-(1 << 16) // divisor)
    if bound * factor < 1 << 31 and all(
        (x * factor) >> 16 == x // divisor for x in range(bound)
    ):
        return (value * factor) >> 16
    return value // divisor


def peer_to(index, shift, count):
    return index ^ shift if count & (count - 1) == 0 else (index + shift) % count


def peer_from(index, shift, count):
    return index ^ shift if count & (count - 1) == 0 else (index + count - shift) % count


def prepare_kernel(
    count, chunks, dest_ref, length_ref, hidden_ref, kv_ref, key_ref, value_ref, *refs
):
    block_refs = refs[: count - 1]
    pick_ref, own_ref, other_ref, blocks, hidden_held, held, total = refs[count - 1 : count + 6]
    in_sems, out_sems, hidden_sem, weight_sems = refs[count + 6 :]
    rows = dest_ref.shape[0]
    capacity, lanes = kv_ref.shape[2:]
    me = lax.axis_index("inst")
    shifts = range(1, count)

    hidden_copy = pltpu.make_async_copy(hidden_ref, hidden_held, hidden_sem)
    hidden_copy.start()
    steps, _, depth = hidden_ref.shape
    width = key_ref.shape[1]
    part = depth // chunks
    weights = []
    for chunk in range(chunks):
        span = pl.ds(chunk * part, part)
        for which, ref in enumerate((key_ref, value_ref)):
            weights.append(
                pltpu.make_async_copy(
                    ref.at[span], held.at[which, span], weight_sems.at[chunk, which]
                )
            )
            weights[-1].start()

    for peer in range(count):
        pick_ref[peer] = 0
    for row in range(rows):
        pick_ref[quotient(dest_ref[row], rows, rows * count)] = row
    fetches, stores = {}, {}
    for shift in shifts:
        row = pick_ref[peer_to(me, shift, count)]
        fetches[shift] = pltpu.make_async_copy(
            kv_ref.at[row], blocks.at[shift - 1], in_sems.at[shift - 1]
        )
        fetches[shift].start()

    tile = (TILE, lanes)
    last = lax.broadcasted_iota(jnp.int32, tile, 0) == TILE - 1
    first_lanes = lax.broadcasted_iota(jnp.int32, tile, 1) < HD
    for shift in shifts:
        peer = peer_to(me, shift, count)
        row = pick_ref[peer]
        slot = dest_ref[row] - peer * rows
        slot = jnp.where((slot >= 0) & (slot < rows), slot, -1)
        facts = jnp.where(first_lanes, slot, length_ref[row]).astype(jnp.float32)
        fetches[shift].wait()
        end = blocks[shift - 1, 0, capacity - TILE :, :].astype(jnp.float32)
        blocks[shift - 1, 0, capacity - TILE :, :] = jnp.where(last, facts, end).astype(
            jnp.bfloat16
        )
        stores[shift] = pltpu.make_async_copy(
            blocks.at[shift - 1], block_refs[shift - 1], out_sems.at[shift - 1]
        )
        stores[shift].start()

    hidden_copy.wait()
    hidden = hidden_held[...].reshape(steps * rows, depth)
    sums = [None, None]
    for chunk in range(chunks):
        for which in range(2):
            weights[2 * chunk + which].wait()
            product = jnp.dot(
                hidden[:, chunk * part : (chunk + 1) * part],
                held[which, chunk * part : (chunk + 1) * part, :],
                preferred_element_type=jnp.float32,
            )
            sums[which] = product if chunk == 0 else sums[which] + product
    total[:, :width] = sums[0]
    total[:, width:] = sums[1]
    half = width // 2
    core = lax.axis_index("tp")
    for ref, place in ((own_ref, core), (other_ref, 1 - core)):
        at = pl.multiple_of(place * half, half)
        ref[:, :half] = total[:, pl.ds(at, half)]
        ref[:, half:] = total[:, pl.ds(pl.multiple_of(width + at, half), half)]
    for shift in shifts:
        stores[shift].wait()


def prepare(destination, lengths, hidden_new, kv_cache, key_weight, value_weight, count):
    steps, rows, depth = hidden_new.shape
    width = key_weight.shape[1]
    chunks = 5
    shape = kv_cache.shape[1:]
    part = jax.ShapeDtypeStruct((steps * rows, width), jnp.float32)
    smem = pl.BlockSpec(memory_space=pltpu.SMEM)
    vmem = pl.BlockSpec(memory_space=pltpu.VMEM)
    hbm = pl.BlockSpec(memory_space=pl.ANY)
    outs = pl.pallas_call(
        functools.partial(prepare_kernel, count, chunks),
        out_shape=[jax.ShapeDtypeStruct(shape, kv_cache.dtype)] * (count - 1)
        + [jax.ShapeDtypeStruct((count,), jnp.int32), part, part],
        in_specs=[smem, smem, hbm, hbm, hbm, hbm],
        out_specs=[hbm] * (count - 1) + [smem, vmem, vmem],
        scratch_shapes=[
            pltpu.VMEM((count - 1,) + shape, kv_cache.dtype),
            pltpu.VMEM(hidden_new.shape, hidden_new.dtype),
            pltpu.VMEM((2, depth, width), key_weight.dtype),
            pltpu.VMEM((steps * rows, 2 * width), jnp.float32),
            pltpu.SemaphoreType.DMA((count - 1,)),
            pltpu.SemaphoreType.DMA((count - 1,)),
            pltpu.SemaphoreType.DMA,
            pltpu.SemaphoreType.DMA((chunks, 2)),
        ],
        compiler_params=pltpu.CompilerParams(vmem_limit_bytes=VMEM_LIMIT),
        cost_estimate=LIGHT,
        name="prepare",
    )(destination, lengths, hidden_new, kv_cache, key_weight, value_weight)
    return outs[: count - 1], *outs[count - 1 :]


def rotation(length_ref, steps, rows):
    half = HD // 2
    line = lax.broadcasted_iota(jnp.int32, (steps * rows, HD), 0)
    lane = lax.broadcasted_iota(jnp.int32, (steps * rows, HD), 1)
    position = jnp.zeros((steps * rows, HD), jnp.int32)
    for step in range(steps):
        for row in range(rows):
            position = jnp.where(line == step * rows + row, length_ref[row] + step, position)
    order = (lane % half).astype(jnp.float32)
    angle = position.astype(jnp.float32) * jnp.exp(-math.log(ROPE_BASE) * 2.0 * order / HD)
    sine = jnp.sin(angle)
    return jnp.cos(angle), jnp.where(lane < half, -sine, sine)


def attend_kernel(
    count,
    block,
    length_ref,
    dest_ref,
    pick_ref,
    own_ref,
    got_ref,
    gain_ref,
    query_ref,
    kv_ref,
    *refs,
):
    late = (len(refs) - 14) // 2
    moved_ref, mixed_ref, small_ref = refs[late : late + 3]
    fresh, query_held, query_rows, query_columns, mixed, sums, held = refs[-11:-4]
    sum_sems, query_sem, in_sems, out_sems = refs[-4:]
    steps, rows, query_width = query_ref.shape
    capacity, lanes = kv_ref.shape[2:]
    heads = lanes // HD
    group = query_width // lanes
    per_head = steps * group
    per_row = heads * per_head
    team = HD // per_row

    query_copy = pltpu.make_async_copy(query_ref, query_held, query_sem)
    query_copy.start()
    sum_copies = [
        pltpu.make_async_copy(ref, sums.at[index], sum_sems.at[index])
        for index, ref in enumerate((own_ref, got_ref))
    ]
    for copy in sum_copies:
        copy.start()

    def span(index):
        return pl.ds(index * team, team)

    def fetch(index):
        return pltpu.make_async_copy(
            kv_ref.at[span(index)], held.at[span(index)], in_sems.at[index]
        )

    def store(index):
        return pltpu.make_async_copy(
            held.at[span(index)], moved_ref.at[span(index)], out_sems.at[index]
        )

    for index in range(rows // team):
        fetch(index).start()

    cosine, sine = rotation(length_ref, steps, rows)
    query_copy.wait()
    for step in range(steps):
        for chunk in range(query_width // HD):
            head, member = chunk // group, chunk % group
            at = head * per_head + step * group + member
            query_rows[pl.ds(at, rows, stride=per_row), :] = query_held[
                step, :, chunk * HD : (chunk + 1) * HD
            ].astype(jnp.float32)
    for index in range(rows // team):
        query_columns[index] = query_rows[index * HD : (index + 1) * HD, :].T
    for copy in sum_copies:
        copy.wait()
    raw = sums[0] + sums[1]
    gain = gain_ref[...].astype(jnp.float32)
    for head in range(heads):
        at = slice(head * HD, (head + 1) * HD)
        piece = raw[:, at]
        mean = jnp.mean(piece * piece, axis=-1, keepdims=True)
        piece = piece * lax.rsqrt(mean + NORM_EPS) * gain
        swapped = jnp.concatenate([piece[:, HD // 2 :], piece[:, : HD // 2]], axis=1)
        turned = piece * cosine + swapped * sine
        fresh[0, :, at] = turned.astype(jnp.bfloat16).astype(jnp.float32)
    fresh[1] = raw[:, lanes:].astype(jnp.bfloat16).astype(jnp.float32)

    position = lax.broadcasted_iota(jnp.int32, (capacity, HD), 0)
    column = lax.broadcasted_iota(jnp.int32, (capacity, HD), 1)
    column_item = column // per_row
    column_step = (column % per_head) // group
    column_head = lax.broadcasted_iota(jnp.int32, (HD, HD), 1) % per_row // per_head
    factor = 1.0 / math.sqrt(HD)
    teams = range(block // team)

    def work(part, carry):
        for index in teams:
            fetch(part * len(teams) + index).wait()
        scores = []
        for index in teams:
            queries = query_columns[part * len(teams) + index]
            queries = jnp.concatenate(
                [jnp.where(column_head == head, queries, 0.0) for head in range(heads)], axis=0
            ).astype(jnp.bfloat16)
            score, limit = None, None
            for member in range(team):
                row = part * block + index * team + member
                length = length_ref[row]
                kept = position < length
                landing = [position == length + step for step in range(steps)]
                for which in range(2):
                    news = [fresh[which, pl.ds(step * rows + row, 1), :] for step in range(steps)]
                    for head in range(heads):
                        at = slice(head * HD, (head + 1) * HD)
                        stored = held[row, which, :, at].astype(jnp.float32)
                        stored = jnp.where(kept, stored, 0.0)
                        for step in range(steps):
                            stored = jnp.where(landing[step], news[step][:, at], stored)
                        held[row, which, :, at] = stored.astype(jnp.bfloat16)
                one = jnp.dot(held[row, 0], queries, preferred_element_type=jnp.float32)
                score = one if member == 0 else jnp.where(column_item == member, one, score)
                limit = length if member == 0 else jnp.where(column_item == member, length, limit)
            scores.append(jnp.where(position <= limit + column_step, score * factor, -jnp.inf))
        weights = []
        for score in scores:
            raised = jnp.exp(score - jnp.max(score, axis=0, keepdims=True))
            normaliser = jnp.sum(raised, axis=0, keepdims=True)
            weights.append((raised / normaliser).T.astype(jnp.bfloat16))
        for index in teams:
            for member in range(team):
                row = part * block + index * team + member
                result = jnp.dot(
                    weights[index][member * per_row : (member + 1) * per_row],
                    held[row, 1],
                    preferred_element_type=jnp.float32,
                )
                for head in range(heads):
                    at = pl.multiple_of(row * per_row + head * per_head, per_head)
                    mixed[pl.ds(at, per_head), :] = result[
                        head * per_head : (head + 1) * per_head, head * HD : (head + 1) * HD
                    ]
        for index in teams:
            store(part * len(teams) + index).start()
        return carry

    lax.fori_loop(0, rows // block, work, 0)

    mixed_ref[...] = mixed[...].astype(jnp.bfloat16)
    for peer in range(count):
        row = pick_ref[peer]
        small_ref[peer, :per_row, :] = mixed[
            pl.ds(pl.multiple_of(row * per_row, per_row), per_row), :
        ].astype(jnp.bfloat16)
        news = []
        for which in range(2):
            for step in range(steps):
                new = fresh[which, pl.ds(step * rows + row, 1), :]
                news += [new[:, h * HD : (h + 1) * HD] for h in range(heads)]
        slot = dest_ref[row] - peer * rows
        slot = jnp.where((slot >= 0) & (slot < rows), slot, -1).astype(jnp.float32)
        fill = small_ref.shape[1] - per_row - len(news)
        news.append(jnp.full((fill, HD), slot))
        small_ref[peer, per_row:, :] = jnp.concatenate(news, axis=0).astype(jnp.bfloat16)
    for index in range(rows // team):
        store(index).wait()


def attend(
    kv_cache, queries, own, got, gain, lengths, destination, pick, late, count
):
    late_shapes = [jax.ShapeDtypeStruct(x.shape, x.dtype) for x in late]
    steps, rows, query_width = queries.shape
    capacity, lanes = kv_cache.shape[2:]
    heads = lanes // HD
    per_row = steps * query_width // HD
    block = 8
    teams = rows * per_row // HD
    small_rows = per_row + -(-(2 * steps * heads + 1) // TILE) * TILE
    small = jax.ShapeDtypeStruct((count, small_rows, HD), jnp.bfloat16)
    smem = pl.BlockSpec(memory_space=pltpu.SMEM)
    vmem = pl.BlockSpec(memory_space=pltpu.VMEM)
    hbm = pl.BlockSpec(memory_space=pl.ANY)
    outs = pl.pallas_call(
        functools.partial(attend_kernel, count, block),
        out_shape=[
            jax.ShapeDtypeStruct(kv_cache.shape, kv_cache.dtype),
            jax.ShapeDtypeStruct((rows * per_row, HD), jnp.bfloat16),
            small,
        ]
        + late_shapes,
        in_specs=[smem, smem, smem, hbm, hbm, vmem, hbm, hbm] + [hbm] * len(late),
        out_specs=[hbm, vmem, vmem] + [hbm] * len(late),
        scratch_shapes=[
            pltpu.VMEM((2, steps * rows, lanes), jnp.float32),
            pltpu.VMEM(queries.shape, queries.dtype),
            pltpu.VMEM((rows * per_row, HD), jnp.float32),
            pltpu.VMEM((teams, HD, HD), jnp.float32),
            pltpu.VMEM((rows * per_row, HD), jnp.float32),
            pltpu.VMEM((2,) + own.shape, own.dtype),
            pltpu.VMEM(kv_cache.shape, kv_cache.dtype),
            pltpu.SemaphoreType.DMA((2,)),
            pltpu.SemaphoreType.DMA,
            pltpu.SemaphoreType.DMA((teams,)),
            pltpu.SemaphoreType.DMA((teams,)),
        ],
        input_output_aliases={8 + i: 3 + i for i in range(len(late))},
        compiler_params=pltpu.CompilerParams(vmem_limit_bytes=ATTEND_LIMIT),
        cost_estimate=HEAVY,
        name="attend",
    )(lengths, destination, pick, own, got, gain, queries, kv_cache, *late)
    return outs[0], outs[1], outs[2], outs[3:]


def read_facts(block):
    capacity = block.shape[1]
    facts = block[0, capacity - TILE :, :].astype(jnp.float32)[TILE - 1 :]
    return (
        jnp.max(facts[:, :HD]).astype(jnp.int32),
        jnp.max(facts[:, HD : 2 * HD]).astype(jnp.int32),
    )


def window_start(length, capacity):
    return pl.multiple_of(jnp.minimum(length // TILE * TILE, capacity - WINDOW), TILE)


def clean(block, length, out):
    capacity, lanes = block.shape[1:]
    kept = lax.broadcasted_iota(jnp.int32, (capacity, HD), 0) < length
    for which in range(2):
        for at in range(0, lanes, HD):
            stored = block[which, :, at : at + HD].astype(jnp.float32)
            out[which, :, at : at + HD] = jnp.where(kept, stored, 0.0).astype(jnp.bfloat16)


def insert(window, news, ahead, steps, out):
    height, lanes = window.shape[1:]
    heads = lanes // HD
    position = lax.broadcasted_iota(jnp.int32, (height, lanes), 0)
    for which in range(2):
        stored = window[which].astype(jnp.float32)
        for step in range(steps):
            at = (which * steps + step) * heads
            new = jnp.concatenate([news[at + h : at + h + 1] for h in range(heads)], axis=1)
            stored = jnp.where(position == ahead + step, new, stored)
        out[which] = stored.astype(jnp.bfloat16)


def land_kernel(pieces, *refs):
    blocks = refs[:pieces]
    _, out_ref, slot_ref, length_ref, window_ref, buffer, sems = refs[pieces:]
    capacity = buffer.shape[2]

    def store(piece):
        slot = jnp.maximum(slot_ref[piece], 0)
        return pltpu.make_async_copy(buffer.at[piece], out_ref.at[slot], sems.at[piece])

    for piece, block in enumerate(blocks):
        slot_ref[piece], length_ref[piece] = read_facts(block)
    for piece, block in enumerate(blocks):

        @pl.when(slot_ref[piece] >= 0)
        def _():
            length = length_ref[piece]
            clean(block, length, buffer.at[piece])
            store(piece).start()
            start = window_start(length, capacity)
            window_ref[piece] = buffer[piece, :, pl.ds(start, WINDOW), :]

    for piece in range(pieces):

        @pl.when(slot_ref[piece] >= 0)
        def _():
            store(piece).wait()


def land(got, moved):
    pieces = len(got)
    smem = pl.BlockSpec(memory_space=pltpu.SMEM)
    vmem = pl.BlockSpec(memory_space=pltpu.VMEM)
    hbm = pl.BlockSpec(memory_space=pl.ANY)
    scalars = jax.ShapeDtypeStruct((pieces,), jnp.int32)
    return pl.pallas_call(
        functools.partial(land_kernel, pieces),
        out_shape=[
            jax.ShapeDtypeStruct(moved.shape, moved.dtype),
            scalars,
            scalars,
            jax.ShapeDtypeStruct((pieces, 2, WINDOW, moved.shape[3]), moved.dtype),
        ],
        in_specs=[vmem] * pieces + [hbm],
        out_specs=[hbm, smem, smem, vmem],
        scratch_shapes=[
            pltpu.VMEM((pieces,) + moved.shape[1:], moved.dtype),
            pltpu.SemaphoreType.DMA((pieces,)),
        ],
        input_output_aliases={pieces: 0},
        compiler_params=pltpu.CompilerParams(vmem_limit_bytes=SMALL_LIMIT),
        cost_estimate=HEAVY,
        name="land",
    )(*got, moved)


def settle_kernel(
    count,
    early,
    group,
    slot_ref,
    length_ref,
    mixed_ref,
    small_ref,
    window_ref,
    _,
    out_ref,
    moved_ref,
    mixed,
    windows,
    sems,
):
    steps, rows, query_width = out_ref.shape
    per_row = steps * query_width // HD
    capacity, lanes = moved_ref.shape[2:]
    heads = lanes // HD
    me = lax.axis_index("inst")
    pieces = len(early)

    def store(piece):
        slot = jnp.maximum(slot_ref[piece], 0)
        start = window_start(length_ref[piece], capacity)
        return pltpu.make_async_copy(
            windows.at[piece], moved_ref.at[slot, :, pl.ds(start, WINDOW), :], sems.at[piece]
        )

    def take(slot, peer):
        mixed[pl.ds(pl.multiple_of(slot * per_row, per_row), per_row), :] = small_ref[
            peer, :per_row, :
        ].astype(jnp.float32)

    for piece in range(pieces):

        @pl.when(slot_ref[piece] >= 0)
        def _():
            length = length_ref[piece]
            peer = peer_from(me, early[piece], count)
            news = small_ref[peer, per_row:, :].astype(jnp.float32)
            ahead = length - window_start(length, capacity)
            insert(window_ref.at[piece], news, ahead, steps, windows.at[piece])
            store(piece).start()

    mixed[...] = mixed_ref[...].astype(jnp.float32)
    for shift in range(1, count):
        peer = peer_from(me, shift, count)
        if shift in early:
            slot = slot_ref[early.index(shift)]
        else:
            line = 2 * steps * heads
            facts = small_ref[peer, per_row:, :].astype(jnp.float32)[line : line + 1]
            slot = jnp.max(facts).astype(jnp.int32)
        pl.when(slot >= 0)(functools.partial(take, slot, peer))
    for step in range(steps):
        for chunk in range(query_width // HD):
            head, member = chunk // group, chunk % group
            at = head * steps * group + step * group + member
            out_ref[step, :, chunk * HD : (chunk + 1) * HD] = mixed[
                pl.ds(at, rows, stride=per_row), :
            ].astype(jnp.bfloat16)

    for piece in range(pieces):

        @pl.when(slot_ref[piece] >= 0)
        def _():
            store(piece).wait()


def settle(slots, lengths, mixed, small, windows, moved, shape, group, count, early):
    smem = pl.BlockSpec(memory_space=pltpu.SMEM)
    vmem = pl.BlockSpec(memory_space=pltpu.VMEM)
    hbm = pl.BlockSpec(memory_space=pl.ANY)
    return pl.pallas_call(
        functools.partial(settle_kernel, count, early, group),
        out_shape=[
            jax.ShapeDtypeStruct(shape, jnp.bfloat16),
            jax.ShapeDtypeStruct(moved.shape, moved.dtype),
        ],
        in_specs=[smem, smem, vmem, vmem, vmem, hbm],
        out_specs=[vmem, hbm],
        scratch_shapes=[
            pltpu.VMEM(mixed.shape, jnp.float32),
            pltpu.VMEM(windows.shape, windows.dtype),
            pltpu.SemaphoreType.DMA((slots.shape[0],)),
        ],
        input_output_aliases={5: 1},
        compiler_params=pltpu.CompilerParams(vmem_limit_bytes=SMALL_LIMIT),
        cost_estimate=LIGHT,
        name="settle",
    )(slots, lengths, mixed, small, windows, moved)


def finish_kernel(count, late, steps, *refs):
    blocks = refs[: len(late)]
    small_ref, _, out_ref, buffer, sems, slot_ref = refs[len(late) :]
    capacity, lanes = buffer.shape[2:]
    height = small_ref.shape[1]
    tail = height - -(-(2 * steps * (lanes // HD) + 1) // TILE) * TILE
    me = lax.axis_index("inst")

    def store(piece):
        slot = jnp.maximum(slot_ref[piece], 0)
        return pltpu.make_async_copy(buffer.at[piece], out_ref.at[slot], sems.at[piece])

    facts = [read_facts(block) for block in blocks]
    for piece, (slot, length) in enumerate(facts):
        slot_ref[piece] = slot

        @pl.when(slot >= 0)
        def _():
            clean(blocks[piece], length, buffer.at[piece])
            start = window_start(length, capacity)
            window = buffer.at[piece, :, pl.ds(start, WINDOW), :]
            news = small_ref[peer_from(me, late[piece], count), tail:, :].astype(jnp.float32)
            insert(window, news, length - start, steps, window)
            store(piece).start()

    for piece in range(len(late)):

        @pl.when(slot_ref[piece] >= 0)
        def _():
            store(piece).wait()


def finish(got, small, moved, steps, count, late):
    vmem = pl.BlockSpec(memory_space=pltpu.VMEM)
    hbm = pl.BlockSpec(memory_space=pl.ANY)
    return pl.pallas_call(
        functools.partial(finish_kernel, count, late, steps),
        out_shape=jax.ShapeDtypeStruct(moved.shape, moved.dtype),
        in_specs=[vmem] * len(got) + [vmem, hbm],
        out_specs=hbm,
        scratch_shapes=[
            pltpu.VMEM((len(got),) + moved.shape[1:], moved.dtype),
            pltpu.SemaphoreType.DMA((len(got),)),
            pltpu.SMEM((len(got),), jnp.int32),
        ],
        input_output_aliases={len(got) + 1: 0},
        compiler_params=pltpu.CompilerParams(vmem_limit_bytes=SMALL_LIMIT),
        cost_estimate=LIGHT,
        name="finish",
    )(*got, small, moved)


def local(hidden_new, queries, kv_cache, lengths, destination, key_weight, value_weight, key_gain):
    steps = queries.shape[0]
    group = queries.shape[2] // kv_cache.shape[3]
    count = lax.axis_size("inst")
    half = max(count // 2, 1)
    early = list(range(half, count - 1)) + [half - 1] * (half > 1)
    late = [count - 1] + list(range(half - 2, 0, -1))

    def send(block, shift):
        pairs = [(i, peer_to(i, shift, count)) for i in range(count)]
        return lax.ppermute(block, "inst", pairs)

    blocks, pick, own, other = prepare(
        destination, lengths, hidden_new, kv_cache, key_weight, value_weight, count
    )
    early_got = [send(blocks[shift - 1], shift) for shift in early]
    got = lax.ppermute(other, "tp", [(0, 1), (1, 0)])
    moved, mixed, small, late_blocks = attend(
        kv_cache,
        queries,
        own,
        got,
        key_gain[None, :],
        lengths,
        destination,
        pick,
        [blocks[shift - 1] for shift in late],
        count,
    )
    late_got = [send(block, shift) for block, shift in zip(late_blocks, late)]
    small_got = lax.all_to_all(small, "inst", 0, 0, tiled=True)
    moved, slots, arrived, windows = land(early_got, moved)
    attended, moved = settle(
        slots, arrived, mixed, small_got, windows, moved, queries.shape, group, count, early
    )
    return attended, finish(late_got, small_got, moved, steps, count, late)


def solution(mesh):
    return jax.shard_map(
        local,
        mesh=mesh,
        in_specs=(
            P(None, ("group", "inst"), "tp"),
            P(None, ("group", "inst"), "tp"),
            P(("group", "inst"), None, None, "tp"),
            P(("group", "inst")),
            P(("group", "inst")),
            P("tp", None),
            P("tp", None),
            P(),
        ),
        out_specs=(P(None, ("group", "inst"), "tp"), P(("group", "inst"), None, None, "tp")),
        check_vma=False,
    )
```

```python
import functools
import math

import jax
import jax.numpy as jnp
from jax import lax
from jax.experimental import pallas as pl
from jax.experimental.pallas import tpu as pltpu
from jax.sharding import PartitionSpec as P

HD = 128
ROPE_BASE = 1000000.0
NORM_EPS = 1e-06
VMEM_LIMIT = 62 * 1024 * 1024
ATTEND_LIMIT = 56 * 1024 * 1024
SMALL_LIMIT = 40 * 1024 * 1024
LIGHT = pl.CostEstimate(flops=1, bytes_accessed=1, transcendentals=0)
HEAVY = pl.CostEstimate(flops=1 << 36, bytes_accessed=1 << 28, transcendentals=0)
TILE = 16
WINDOW = 32


def quotient(value, divisor, bound):
    factor = -(-(1 << 16) // divisor)
    if bound * factor < 1 << 31 and all(
        (x * factor) >> 16 == x // divisor for x in range(bound)
    ):
        return (value * factor) >> 16
    return value // divisor


def peer_to(index, shift, count):
    return index ^ shift if count & (count - 1) == 0 else (index + shift) % count


def peer_from(index, shift, count):
    return index ^ shift if count & (count - 1) == 0 else (index + count - shift) % count


def pack_kernel(count, early, dest_ref, length_ref, kv_ref, *refs):
    block_refs = refs[: len(early)]
    pick_ref, blocks, in_sems, out_sems = refs[len(early) :]
    rows = dest_ref.shape[0]
    capacity, lanes = kv_ref.shape[2:]
    me = lax.axis_index("inst")
    for peer in range(count):
        pick_ref[peer] = 0
    for row in range(rows):
        pick_ref[quotient(dest_ref[row], rows, rows * count)] = row
    fetches, stores = [], []
    for piece, shift in enumerate(early):
        row = pick_ref[peer_to(me, shift, count)]
        fetches.append(
            pltpu.make_async_copy(kv_ref.at[row], blocks.at[piece], in_sems.at[piece])
        )
        fetches[-1].start()
    tile = (TILE, lanes)
    last = lax.broadcasted_iota(jnp.int32, tile, 0) == TILE - 1
    first_lanes = lax.broadcasted_iota(jnp.int32, tile, 1) < HD
    for piece, shift in enumerate(early):
        peer = peer_to(me, shift, count)
        row = pick_ref[peer]
        slot = dest_ref[row] - peer * rows
        slot = jnp.where((slot >= 0) & (slot < rows), slot, -1)
        facts = jnp.where(first_lanes, slot, length_ref[row]).astype(jnp.float32)
        fetches[piece].wait()
        end = blocks[piece, 0, capacity - TILE :, :].astype(jnp.float32)
        blocks[piece, 0, capacity - TILE :, :] = jnp.where(last, facts, end).astype(jnp.bfloat16)
        stores.append(
            pltpu.make_async_copy(blocks.at[piece], block_refs[piece], out_sems.at[piece])
        )
        stores[-1].start()
    for copy in stores:
        copy.wait()


def pack(kv_cache, destination, lengths, count, early):
    shape = kv_cache.shape[1:]
    smem = pl.BlockSpec(memory_space=pltpu.SMEM)
    hbm = pl.BlockSpec(memory_space=pl.ANY)
    outs = pl.pallas_call(
        functools.partial(pack_kernel, count, early),
        out_shape=[jax.ShapeDtypeStruct(shape, kv_cache.dtype)] * len(early)
        + [jax.ShapeDtypeStruct((count,), jnp.int32)],
        in_specs=[smem, smem, hbm],
        out_specs=[hbm] * len(early) + [smem],
        scratch_shapes=[
            pltpu.VMEM((len(early),) + shape, kv_cache.dtype),
            pltpu.SemaphoreType.DMA((len(early),)),
            pltpu.SemaphoreType.DMA((len(early),)),
        ],
        compiler_params=pltpu.CompilerParams(vmem_limit_bytes=VMEM_LIMIT),
        cost_estimate=LIGHT,
        name="pack",
    )(destination, lengths, kv_cache)
    return outs[:-1], outs[-1]


def project_kernel(
    chunks,
    _,
    hidden_ref,
    key_ref,
    value_ref,
    own_ref,
    other_ref,
    hidden_held,
    held,
    total,
    hidden_sem,
    weight_sems,
):
    steps, rows, depth = hidden_ref.shape
    width = key_ref.shape[1]
    part = depth // chunks
    hidden_copy = pltpu.make_async_copy(hidden_ref, hidden_held, hidden_sem)
    hidden_copy.start()
    weights = []
    for chunk in range(chunks):
        span = pl.ds(chunk * part, part)
        for which, ref in enumerate((key_ref, value_ref)):
            weights.append(
                pltpu.make_async_copy(
                    ref.at[span], held.at[which, span], weight_sems.at[chunk, which]
                )
            )
            weights[-1].start()
    hidden_copy.wait()
    hidden = hidden_held[...].reshape(steps * rows, depth)
    sums = [None, None]
    for chunk in range(chunks):
        for which in range(2):
            weights[2 * chunk + which].wait()
            product = jnp.dot(
                hidden[:, chunk * part : (chunk + 1) * part],
                held[which, chunk * part : (chunk + 1) * part, :],
                preferred_element_type=jnp.float32,
            )
            sums[which] = product if chunk == 0 else sums[which] + product
    total[:, :width] = sums[0]
    total[:, width:] = sums[1]
    half = width // 2
    core = lax.axis_index("tp")
    for ref, place in ((own_ref, core), (other_ref, 1 - core)):
        at = pl.multiple_of(place * half, half)
        ref[:, :half] = total[:, pl.ds(at, half)]
        ref[:, half:] = total[:, pl.ds(pl.multiple_of(width + at, half), half)]


def project(hidden_new, key_weight, value_weight, pick):
    steps, rows, depth = hidden_new.shape
    width = key_weight.shape[1]
    chunks = 5
    part = jax.ShapeDtypeStruct((steps * rows, width), jnp.float32)
    vmem = pl.BlockSpec(memory_space=pltpu.VMEM)
    hbm = pl.BlockSpec(memory_space=pl.ANY)
    return pl.pallas_call(
        functools.partial(project_kernel, chunks),
        out_shape=[part, part],
        in_specs=[hbm, hbm, hbm, hbm],
        out_specs=[vmem, vmem],
        scratch_shapes=[
            pltpu.VMEM(hidden_new.shape, hidden_new.dtype),
            pltpu.VMEM((2, depth, width), key_weight.dtype),
            pltpu.VMEM((steps * rows, 2 * width), jnp.float32),
            pltpu.SemaphoreType.DMA,
            pltpu.SemaphoreType.DMA((chunks, 2)),
        ],
        compiler_params=pltpu.CompilerParams(vmem_limit_bytes=VMEM_LIMIT),
        cost_estimate=LIGHT,
        name="project",
    )(pick, hidden_new, key_weight, value_weight)


def rotation(length_ref, steps, rows):
    half = HD // 2
    line = lax.broadcasted_iota(jnp.int32, (steps * rows, HD), 0)
    lane = lax.broadcasted_iota(jnp.int32, (steps * rows, HD), 1)
    position = jnp.zeros((steps * rows, HD), jnp.int32)
    for step in range(steps):
        for row in range(rows):
            position = jnp.where(line == step * rows + row, length_ref[row] + step, position)
    order = (lane % half).astype(jnp.float32)
    angle = position.astype(jnp.float32) * jnp.exp(-math.log(ROPE_BASE) * 2.0 * order / HD)
    sine = jnp.sin(angle)
    return jnp.cos(angle), jnp.where(lane < half, -sine, sine)


def attend_kernel(
    count,
    late,
    block,
    length_ref,
    dest_ref,
    pick_ref,
    own_ref,
    got_ref,
    gain_ref,
    query_ref,
    kv_ref,
    *refs,
):
    moved_ref, mixed_ref, small_ref = refs[:3]
    late_refs = refs[3 : 3 + len(late)]
    fresh, query_held, query_rows, query_columns, mixed, sums, held, appended = refs[-13:-5]
    sum_sems, query_sem, in_sems, out_sems, late_sems = refs[-5:]
    steps, rows, query_width = query_ref.shape
    capacity, lanes = kv_ref.shape[2:]
    heads = lanes // HD
    group = query_width // lanes
    per_head = steps * group
    per_row = heads * per_head
    team = HD // per_row

    query_copy = pltpu.make_async_copy(query_ref, query_held, query_sem)
    query_copy.start()
    sum_copies = [
        pltpu.make_async_copy(ref, sums.at[index], sum_sems.at[index])
        for index, ref in enumerate((own_ref, got_ref))
    ]
    for copy in sum_copies:
        copy.start()

    def span(index):
        return pl.ds(index * team, team)

    def fetch(index):
        return pltpu.make_async_copy(
            kv_ref.at[span(index)], held.at[span(index)], in_sems.at[index]
        )

    def store(index):
        return pltpu.make_async_copy(
            appended.at[span(index)], moved_ref.at[span(index)], out_sems.at[index]
        )

    for index in range(rows // team):
        fetch(index).start()

    cosine, sine = rotation(length_ref, steps, rows)
    query_copy.wait()
    for step in range(steps):
        for chunk in range(query_width // HD):
            head, member = chunk // group, chunk % group
            at = head * per_head + step * group + member
            query_rows[pl.ds(at, rows, stride=per_row), :] = query_held[
                step, :, chunk * HD : (chunk + 1) * HD
            ].astype(jnp.float32)
    for index in range(rows // team):
        query_columns[index] = query_rows[index * HD : (index + 1) * HD, :].T
    for copy in sum_copies:
        copy.wait()
    raw = sums[0] + sums[1]
    gain = gain_ref[...].astype(jnp.float32)
    for head in range(heads):
        at = slice(head * HD, (head + 1) * HD)
        piece = raw[:, at]
        mean = jnp.mean(piece * piece, axis=-1, keepdims=True)
        piece = piece * lax.rsqrt(mean + NORM_EPS) * gain
        swapped = jnp.concatenate([piece[:, HD // 2 :], piece[:, : HD // 2]], axis=1)
        turned = piece * cosine + swapped * sine
        fresh[0, :, at] = turned.astype(jnp.bfloat16).astype(jnp.float32)
    fresh[1] = raw[:, lanes:].astype(jnp.bfloat16).astype(jnp.float32)

    position = lax.broadcasted_iota(jnp.int32, (capacity, HD), 0)
    column = lax.broadcasted_iota(jnp.int32, (capacity, HD), 1)
    column_item = column // per_row
    column_step = (column % per_head) // group
    column_head = lax.broadcasted_iota(jnp.int32, (HD, HD), 1) % per_row // per_head
    factor = 1.0 / math.sqrt(HD)
    teams = range(block // team)

    for part in range(rows // block):
        scores = []
        for index in teams:
            fetch(part * len(teams) + index).wait()
            queries = query_columns[part * len(teams) + index]
            queries = jnp.concatenate(
                [jnp.where(column_head == head, queries, 0.0) for head in range(heads)], axis=0
            ).astype(jnp.bfloat16)
            score, limit = None, None
            for member in range(team):
                row = part * block + index * team + member
                length = length_ref[row]
                kept = position < length
                landing = [position == length + step for step in range(steps)]
                for which in range(2):
                    for head in range(heads):
                        at = slice(head * HD, (head + 1) * HD)
                        stored = held[row, which, :, at].astype(jnp.float32)
                        stored = jnp.where(kept, stored, 0.0)
                        for step in range(steps):
                            new = fresh[which, step * rows + row : step * rows + row + 1, at]
                            stored = jnp.where(landing[step], new, stored)
                        appended[row, which, :, at] = stored.astype(jnp.bfloat16)
                one = jnp.dot(appended[row, 0], queries, preferred_element_type=jnp.float32)
                score = one if member == 0 else jnp.where(column_item == member, one, score)
                limit = length if member == 0 else jnp.where(column_item == member, length, limit)
            scores.append(jnp.where(position <= limit + column_step, score * factor, -jnp.inf))
            store(part * len(teams) + index).start()
        weights = []
        for score in scores:
            raised = jnp.exp(score - jnp.max(score, axis=0, keepdims=True))
            normaliser = jnp.sum(raised, axis=0, keepdims=True)
            weights.append((raised / normaliser).T.astype(jnp.bfloat16))
        for index in teams:
            for member in range(team):
                row = part * block + index * team + member
                result = jnp.dot(
                    weights[index][member * per_row : (member + 1) * per_row],
                    appended[row, 1],
                    preferred_element_type=jnp.float32,
                )
                for head in range(heads):
                    at = row * per_row + head * per_head
                    mixed[at : at + per_head, :] = result[
                        head * per_head : (head + 1) * per_head, head * HD : (head + 1) * HD
                    ]

    me = lax.axis_index("inst")
    sends = []
    for piece, shift in enumerate(late):
        row = pick_ref[peer_to(me, shift, count)]
        sends.append(
            pltpu.make_async_copy(appended.at[row], late_refs[piece], late_sems.at[piece])
        )
        sends[-1].start()
    mixed_ref[...] = mixed[...].astype(jnp.bfloat16)
    for peer in range(count):
        row = pick_ref[peer]
        small_ref[peer, :per_row, :] = mixed[
            pl.ds(pl.multiple_of(row * per_row, per_row), per_row), :
        ].astype(jnp.bfloat16)
        news = []
        for which in range(2):
            for step in range(steps):
                new = fresh[which, pl.ds(step * rows + row, 1), :]
                news += [new[:, h * HD : (h + 1) * HD] for h in range(heads)]
        slot = dest_ref[row] - peer * rows
        slot = jnp.where((slot >= 0) & (slot < rows), slot, -1).astype(jnp.float32)
        fill = small_ref.shape[1] - per_row - len(news)
        news.append(jnp.full((fill, HD), slot))
        small_ref[peer, per_row:, :] = jnp.concatenate(news, axis=0).astype(jnp.bfloat16)
    for index in range(rows // team):
        store(index).wait()
    for copy in sends:
        copy.wait()


def attend(kv_cache, queries, own, got, gain, lengths, destination, pick, count, late):
    steps, rows, query_width = queries.shape
    capacity, lanes = kv_cache.shape[2:]
    heads = lanes // HD
    per_row = steps * query_width // HD
    block = 8
    teams = rows * per_row // HD
    small_rows = per_row + -(-(2 * steps * heads + 1) // TILE) * TILE
    small = jax.ShapeDtypeStruct((count, small_rows, HD), jnp.bfloat16)
    smem = pl.BlockSpec(memory_space=pltpu.SMEM)
    vmem = pl.BlockSpec(memory_space=pltpu.VMEM)
    hbm = pl.BlockSpec(memory_space=pl.ANY)
    outs = pl.pallas_call(
        functools.partial(attend_kernel, count, late, block),
        out_shape=[
            jax.ShapeDtypeStruct(kv_cache.shape, kv_cache.dtype),
            jax.ShapeDtypeStruct((rows * per_row, HD), jnp.bfloat16),
            small,
        ]
        + [jax.ShapeDtypeStruct(kv_cache.shape[1:], kv_cache.dtype)] * len(late),
        in_specs=[smem, smem, smem, hbm, hbm, vmem, hbm, hbm],
        out_specs=[hbm, vmem, vmem] + [hbm] * len(late),
        scratch_shapes=[
            pltpu.VMEM((2, steps * rows, lanes), jnp.float32),
            pltpu.VMEM(queries.shape, queries.dtype),
            pltpu.VMEM((rows * per_row, HD), jnp.float32),
            pltpu.VMEM((teams, HD, HD), jnp.float32),
            pltpu.VMEM((rows * per_row, HD), jnp.float32),
            pltpu.VMEM((2,) + own.shape, own.dtype),
            pltpu.VMEM(kv_cache.shape, kv_cache.dtype),
            pltpu.VMEM(kv_cache.shape, kv_cache.dtype),
            pltpu.SemaphoreType.DMA((2,)),
            pltpu.SemaphoreType.DMA,
            pltpu.SemaphoreType.DMA((teams,)),
            pltpu.SemaphoreType.DMA((teams,)),
            pltpu.SemaphoreType.DMA((len(late),)),
        ],
        compiler_params=pltpu.CompilerParams(vmem_limit_bytes=ATTEND_LIMIT),
        cost_estimate=LIGHT,
        name="attend",
    )(lengths, destination, pick, own, got, gain, queries, kv_cache)
    return outs


def read_facts(block):
    capacity = block.shape[1]
    facts = block[0, capacity - TILE :, :].astype(jnp.float32)[TILE - 1 :]
    return (
        jnp.max(facts[:, :HD]).astype(jnp.int32),
        jnp.max(facts[:, HD : 2 * HD]).astype(jnp.int32),
    )


def window_start(length, capacity):
    return pl.multiple_of(jnp.minimum(length // TILE * TILE, capacity - WINDOW), TILE)


def clean(block, length, out):
    capacity, lanes = block.shape[1:]
    kept = lax.broadcasted_iota(jnp.int32, (capacity, HD), 0) < length
    for which in range(2):
        for at in range(0, lanes, HD):
            stored = block[which, :, at : at + HD].astype(jnp.float32)
            out[which, :, at : at + HD] = jnp.where(kept, stored, 0.0).astype(jnp.bfloat16)


def insert(window, news, ahead, steps, out):
    height, lanes = window.shape[1:]
    heads = lanes // HD
    position = lax.broadcasted_iota(jnp.int32, (height, lanes), 0)
    for which in range(2):
        stored = window[which].astype(jnp.float32)
        for step in range(steps):
            at = (which * steps + step) * heads
            new = jnp.concatenate([news[at + h : at + h + 1] for h in range(heads)], axis=1)
            stored = jnp.where(position == ahead + step, new, stored)
        out[which] = stored.astype(jnp.bfloat16)


def land_kernel(pieces, *refs):
    blocks = refs[:pieces]
    _, out_ref, slot_ref, length_ref, window_ref, buffer, sems = refs[pieces:]
    capacity = buffer.shape[2]

    def store(piece):
        slot = jnp.maximum(slot_ref[piece], 0)
        return pltpu.make_async_copy(buffer.at[piece], out_ref.at[slot], sems.at[piece])

    for piece, block in enumerate(blocks):
        slot_ref[piece], length_ref[piece] = read_facts(block)
    for piece, block in enumerate(blocks):

        @pl.when(slot_ref[piece] >= 0)
        def _():
            length = length_ref[piece]
            clean(block, length, buffer.at[piece])
            store(piece).start()
            start = window_start(length, capacity)
            window_ref[piece] = buffer[piece, :, pl.ds(start, WINDOW), :]

    for piece in range(pieces):

        @pl.when(slot_ref[piece] >= 0)
        def _():
            store(piece).wait()


def land(got, moved):
    pieces = len(got)
    smem = pl.BlockSpec(memory_space=pltpu.SMEM)
    vmem = pl.BlockSpec(memory_space=pltpu.VMEM)
    hbm = pl.BlockSpec(memory_space=pl.ANY)
    scalars = jax.ShapeDtypeStruct((pieces,), jnp.int32)
    return pl.pallas_call(
        functools.partial(land_kernel, pieces),
        out_shape=[
            jax.ShapeDtypeStruct(moved.shape, moved.dtype),
            scalars,
            scalars,
            jax.ShapeDtypeStruct((pieces, 2, WINDOW, moved.shape[3]), moved.dtype),
        ],
        in_specs=[vmem] * pieces + [hbm],
        out_specs=[hbm, smem, smem, vmem],
        scratch_shapes=[
            pltpu.VMEM((pieces,) + moved.shape[1:], moved.dtype),
            pltpu.SemaphoreType.DMA((pieces,)),
        ],
        input_output_aliases={pieces: 0},
        compiler_params=pltpu.CompilerParams(vmem_limit_bytes=SMALL_LIMIT),
        cost_estimate=HEAVY,
        name="land",
    )(*got, moved)


def settle_kernel(
    count,
    early,
    late,
    group,
    slot_ref,
    length_ref,
    mixed_ref,
    small_ref,
    window_ref,
    _,
    out_ref,
    moved_ref,
    late_slot_ref,
    mixed,
    windows,
    sems,
):
    steps, rows, query_width = out_ref.shape
    per_row = steps * query_width // HD
    capacity, lanes = moved_ref.shape[2:]
    heads = lanes // HD
    me = lax.axis_index("inst")
    pieces = len(early)

    def store(piece):
        slot = jnp.maximum(slot_ref[piece], 0)
        start = window_start(length_ref[piece], capacity)
        return pltpu.make_async_copy(
            windows.at[piece], moved_ref.at[slot, :, pl.ds(start, WINDOW), :], sems.at[piece]
        )

    def take(slot, peer):
        mixed[pl.ds(pl.multiple_of(slot * per_row, per_row), per_row), :] = small_ref[
            peer, :per_row, :
        ].astype(jnp.float32)

    for piece in range(pieces):

        @pl.when(slot_ref[piece] >= 0)
        def _():
            length = length_ref[piece]
            peer = peer_from(me, early[piece], count)
            news = small_ref[peer, per_row:, :].astype(jnp.float32)
            ahead = length - window_start(length, capacity)
            insert(window_ref.at[piece], news, ahead, steps, windows.at[piece])
            store(piece).start()

    mixed[...] = mixed_ref[...].astype(jnp.float32)
    for shift in range(1, count):
        peer = peer_from(me, shift, count)
        if shift in early:
            slot = slot_ref[early.index(shift)]
        else:
            line = 2 * steps * heads
            facts = small_ref[peer, per_row:, :].astype(jnp.float32)[line : line + 1]
            slot = jnp.max(facts).astype(jnp.int32)
            late_slot_ref[late.index(shift)] = slot
        pl.when(slot >= 0)(functools.partial(take, slot, peer))
    for step in range(steps):
        for chunk in range(query_width // HD):
            head, member = chunk // group, chunk % group
            at = head * steps * group + step * group + member
            out_ref[step, :, chunk * HD : (chunk + 1) * HD] = mixed[
                pl.ds(at, rows, stride=per_row), :
            ].astype(jnp.bfloat16)

    for piece in range(pieces):

        @pl.when(slot_ref[piece] >= 0)
        def _():
            store(piece).wait()


def settle(slots, lengths, mixed, small, windows, moved, shape, group, count, early, late):
    smem = pl.BlockSpec(memory_space=pltpu.SMEM)
    vmem = pl.BlockSpec(memory_space=pltpu.VMEM)
    hbm = pl.BlockSpec(memory_space=pl.ANY)
    return pl.pallas_call(
        functools.partial(settle_kernel, count, early, late, group),
        out_shape=[
            jax.ShapeDtypeStruct(shape, jnp.bfloat16),
            jax.ShapeDtypeStruct(moved.shape, moved.dtype),
            jax.ShapeDtypeStruct((len(late),), jnp.int32),
        ],
        in_specs=[smem, smem, vmem, vmem, vmem, hbm],
        out_specs=[vmem, hbm, smem],
        scratch_shapes=[
            pltpu.VMEM(mixed.shape, jnp.float32),
            pltpu.VMEM(windows.shape, windows.dtype),
            pltpu.SemaphoreType.DMA((slots.shape[0],)),
        ],
        input_output_aliases={5: 1},
        compiler_params=pltpu.CompilerParams(vmem_limit_bytes=SMALL_LIMIT),
        cost_estimate=LIGHT,
        name="settle",
    )(slots, lengths, mixed, small, windows, moved)


def finish_kernel(slot_ref, *refs):
    pieces = slot_ref.shape[0]
    blocks = refs[:pieces]
    _, out_ref, sems = refs[pieces:]

    def store(piece):
        slot = jnp.maximum(slot_ref[piece], 0)
        return pltpu.make_async_copy(blocks[piece], out_ref.at[slot], sems.at[piece])

    for piece in range(pieces):
        pl.when(slot_ref[piece] >= 0)(store(piece).start)
    for piece in range(pieces):
        pl.when(slot_ref[piece] >= 0)(store(piece).wait)


def finish(slots, got, moved):
    smem = pl.BlockSpec(memory_space=pltpu.SMEM)
    vmem = pl.BlockSpec(memory_space=pltpu.VMEM)
    hbm = pl.BlockSpec(memory_space=pl.ANY)
    return pl.pallas_call(
        finish_kernel,
        out_shape=jax.ShapeDtypeStruct(moved.shape, moved.dtype),
        in_specs=[smem] + [vmem] * len(got) + [hbm],
        out_specs=hbm,
        scratch_shapes=[pltpu.SemaphoreType.DMA((len(got),))],
        input_output_aliases={len(got) + 1: 0},
        compiler_params=pltpu.CompilerParams(vmem_limit_bytes=SMALL_LIMIT),
        cost_estimate=LIGHT,
        name="finish",
    )(slots, *got, moved)


def local(hidden_new, queries, kv_cache, lengths, destination, key_weight, value_weight, key_gain):
    group = queries.shape[2] // kv_cache.shape[3]
    count = lax.axis_size("inst")
    half = max(count // 2, 1)
    early = list(range(half, count))
    late = list(range(half - 1, 0, -1))

    def send(block, shift):
        pairs = [(i, peer_to(i, shift, count)) for i in range(count)]
        return lax.ppermute(block, "inst", pairs)

    blocks, pick = pack(kv_cache, destination, lengths, count, early)
    early_got = [send(block, shift) for block, shift in zip(blocks, early)]
    own, other = project(hidden_new, key_weight, value_weight, pick)
    got = lax.ppermute(other, "tp", [(0, 1), (1, 0)])
    moved, mixed, small, *late_blocks = attend(
        kv_cache, queries, own, got, key_gain[None, :], lengths, destination, pick, count, late
    )
    late_got = [send(block, shift) for block, shift in zip(late_blocks, late)]
    small_got = lax.all_to_all(small, "inst", 0, 0, tiled=True)
    moved, slots, arrived, windows = land(early_got, moved)
    attended, moved, late_slots = settle(
        slots, arrived, mixed, small_got, windows, moved, queries.shape, group, count, early, late
    )
    return attended, finish(late_slots, late_got, moved)


def solution(mesh):
    return jax.shard_map(
        local,
        mesh=mesh,
        in_specs=(
            P(None, ("group", "inst"), "tp"),
            P(None, ("group", "inst"), "tp"),
            P(("group", "inst"), None, None, "tp"),
            P(("group", "inst")),
            P(("group", "inst")),
            P("tp", None),
            P("tp", None),
            P(),
        ),
        out_specs=(P(None, ("group", "inst"), "tp"), P(("group", "inst"), None, None, "tp")),
        check_vma=False,
    )
```

```python
import functools
import math

import jax
import jax.numpy as jnp
from jax import lax
from jax.experimental import pallas as pl
from jax.experimental.pallas import tpu as pltpu
from jax.sharding import PartitionSpec as P

HD = 128
ROPE_BASE = 1000000.0
NORM_EPS = 1e-06
VMEM_LIMIT = 62 * 1024 * 1024
ATTEND_LIMIT = 56 * 1024 * 1024
SMALL_LIMIT = 40 * 1024 * 1024
LIGHT = pl.CostEstimate(flops=1, bytes_accessed=1, transcendentals=0)
HEAVY = pl.CostEstimate(flops=1 << 36, bytes_accessed=1 << 28, transcendentals=0)
TILE = 16
WINDOW = 32


def quotient(value, divisor, bound):
    factor = -(-(1 << 16) // divisor)
    if bound * factor < 1 << 31 and all(
        (x * factor) >> 16 == x // divisor for x in range(bound)
    ):
        return (value * factor) >> 16
    return value // divisor


def peer_to(index, shift, count):
    return index ^ shift if count & (count - 1) == 0 else (index + shift) % count


def peer_from(index, shift, count):
    return index ^ shift if count & (count - 1) == 0 else (index + count - shift) % count


def prepare_kernel(
    count, chunks, dest_ref, length_ref, hidden_ref, kv_ref, key_ref, value_ref, *refs
):
    block_refs = refs[: count - 1]
    pick_ref, own_ref, other_ref, blocks, hidden_held, held, total = refs[count - 1 : count + 6]
    in_sems, out_sems, hidden_sem, weight_sems = refs[count + 6 :]
    rows = dest_ref.shape[0]
    capacity, lanes = kv_ref.shape[2:]
    me = lax.axis_index("inst")
    shifts = range(1, count)

    hidden_copy = pltpu.make_async_copy(hidden_ref, hidden_held, hidden_sem)
    hidden_copy.start()
    for peer in range(count):
        pick_ref[peer] = 0
    for row in range(rows):
        pick_ref[quotient(dest_ref[row], rows, rows * count)] = row
    fetches, stores = {}, {}
    for shift in shifts:
        row = pick_ref[peer_to(me, shift, count)]
        fetches[shift] = pltpu.make_async_copy(
            kv_ref.at[row], blocks.at[shift - 1], in_sems.at[shift - 1]
        )
        fetches[shift].start()

    steps, _, depth = hidden_ref.shape
    width = key_ref.shape[1]
    part = depth // chunks

    def weight(chunk, which):
        ref = (key_ref, value_ref)[which]
        span = pl.ds(chunk * part, part)
        return pltpu.make_async_copy(
            ref.at[span], held.at[which, span], weight_sems.at[chunk, which]
        )

    def weights_start(chunk):
        for which in range(2):
            weight(chunk, which).start()

    weights_start(0)
    tile = (TILE, lanes)
    last = lax.broadcasted_iota(jnp.int32, tile, 0) == TILE - 1
    first_lanes = lax.broadcasted_iota(jnp.int32, tile, 1) < HD
    for shift in shifts:
        peer = peer_to(me, shift, count)
        row = pick_ref[peer]
        slot = dest_ref[row] - peer * rows
        slot = jnp.where((slot >= 0) & (slot < rows), slot, -1)
        facts = jnp.where(first_lanes, slot, length_ref[row]).astype(jnp.float32)
        fetches[shift].wait()
        end = blocks[shift - 1, 0, capacity - TILE :, :].astype(jnp.float32)
        blocks[shift - 1, 0, capacity - TILE :, :] = jnp.where(last, facts, end).astype(
            jnp.bfloat16
        )
        stores[shift] = pltpu.make_async_copy(
            blocks.at[shift - 1], block_refs[shift - 1], out_sems.at[shift - 1]
        )
        stores[shift].start()

    weights_start(1)
    hidden_copy.wait()
    hidden = hidden_held[...].reshape(steps * rows, depth)
    sums = [None, None]
    for chunk in range(chunks):
        for which in range(2):
            weight(chunk, which).wait()
        if chunk + 2 < chunks:
            weights_start(chunk + 2)
        for which in range(2):
            product = jnp.dot(
                hidden[:, chunk * part : (chunk + 1) * part],
                held[which, chunk * part : (chunk + 1) * part, :],
                preferred_element_type=jnp.float32,
            )
            sums[which] = product if chunk == 0 else sums[which] + product
    total[:, :width] = sums[0]
    total[:, width:] = sums[1]
    half = width // 2
    core = lax.axis_index("tp")
    for ref, place in ((own_ref, core), (other_ref, 1 - core)):
        at = pl.multiple_of(place * half, half)
        ref[:, :half] = total[:, pl.ds(at, half)]
        ref[:, half:] = total[:, pl.ds(pl.multiple_of(width + at, half), half)]
    for shift in shifts:
        stores[shift].wait()


def prepare(destination, lengths, hidden_new, kv_cache, key_weight, value_weight, count):
    steps, rows, depth = hidden_new.shape
    width = key_weight.shape[1]
    chunks = 5
    shape = kv_cache.shape[1:]
    part = jax.ShapeDtypeStruct((steps * rows, width), jnp.float32)
    smem = pl.BlockSpec(memory_space=pltpu.SMEM)
    vmem = pl.BlockSpec(memory_space=pltpu.VMEM)
    hbm = pl.BlockSpec(memory_space=pl.ANY)
    outs = pl.pallas_call(
        functools.partial(prepare_kernel, count, chunks),
        out_shape=[jax.ShapeDtypeStruct(shape, kv_cache.dtype)] * (count - 1)
        + [jax.ShapeDtypeStruct((count,), jnp.int32), part, part],
        in_specs=[smem, smem, hbm, hbm, hbm, hbm],
        out_specs=[hbm] * (count - 1) + [smem, vmem, vmem],
        scratch_shapes=[
            pltpu.VMEM((count - 1,) + shape, kv_cache.dtype),
            pltpu.VMEM(hidden_new.shape, hidden_new.dtype),
            pltpu.VMEM((2, depth, width), key_weight.dtype),
            pltpu.VMEM((steps * rows, 2 * width), jnp.float32),
            pltpu.SemaphoreType.DMA((count - 1,)),
            pltpu.SemaphoreType.DMA((count - 1,)),
            pltpu.SemaphoreType.DMA,
            pltpu.SemaphoreType.DMA((chunks, 2)),
        ],
        compiler_params=pltpu.CompilerParams(vmem_limit_bytes=VMEM_LIMIT),
        cost_estimate=LIGHT,
        name="prepare",
    )(destination, lengths, hidden_new, kv_cache, key_weight, value_weight)
    return outs[: count - 1], *outs[count - 1 :]


def rotation(length_ref, steps, rows):
    half = HD // 2
    line = lax.broadcasted_iota(jnp.int32, (steps * rows, HD), 0)
    lane = lax.broadcasted_iota(jnp.int32, (steps * rows, HD), 1)
    position = jnp.zeros((steps * rows, HD), jnp.int32)
    for step in range(steps):
        for row in range(rows):
            position = jnp.where(line == step * rows + row, length_ref[row] + step, position)
    order = (lane % half).astype(jnp.float32)
    angle = position.astype(jnp.float32) * jnp.exp(-math.log(ROPE_BASE) * 2.0 * order / HD)
    sine = jnp.sin(angle)
    return jnp.cos(angle), jnp.where(lane < half, -sine, sine)


def attend_kernel(
    count,
    block,
    length_ref,
    dest_ref,
    pick_ref,
    own_ref,
    got_ref,
    gain_ref,
    query_ref,
    kv_ref,
    *refs,
):
    late = (len(refs) - 15) // 2
    moved_ref, mixed_ref, small_ref = refs[late : late + 3]
    fresh, query_held, query_rows, query_columns, mixed, sums, held, appended = refs[-12:-4]
    sum_sems, query_sem, in_sems, out_sems = refs[-4:]
    steps, rows, query_width = query_ref.shape
    capacity, lanes = kv_ref.shape[2:]
    heads = lanes // HD
    group = query_width // lanes
    per_head = steps * group
    per_row = heads * per_head
    team = HD // per_row

    query_copy = pltpu.make_async_copy(query_ref, query_held, query_sem)
    query_copy.start()
    sum_copies = [
        pltpu.make_async_copy(ref, sums.at[index], sum_sems.at[index])
        for index, ref in enumerate((own_ref, got_ref))
    ]
    for copy in sum_copies:
        copy.start()

    def span(index):
        return pl.ds(index * team, team)

    def fetch(index):
        return pltpu.make_async_copy(
            kv_ref.at[span(index)], held.at[span(index)], in_sems.at[index]
        )

    def store(index):
        return pltpu.make_async_copy(
            appended.at[span(index)], moved_ref.at[span(index)], out_sems.at[index]
        )

    teams = range(block // team)
    for index in teams:
        fetch(index).start()

    cosine, sine = rotation(length_ref, steps, rows)
    query_copy.wait()
    for step in range(steps):
        for chunk in range(query_width // HD):
            head, member = chunk // group, chunk % group
            at = head * per_head + step * group + member
            query_rows[pl.ds(at, rows, stride=per_row), :] = query_held[
                step, :, chunk * HD : (chunk + 1) * HD
            ].astype(jnp.float32)
    for index in range(rows // team):
        query_columns[index] = query_rows[index * HD : (index + 1) * HD, :].T
    for copy in sum_copies:
        copy.wait()
    raw = sums[0] + sums[1]
    gain = gain_ref[...].astype(jnp.float32)
    for head in range(heads):
        at = slice(head * HD, (head + 1) * HD)
        piece = raw[:, at]
        mean = jnp.mean(piece * piece, axis=-1, keepdims=True)
        piece = piece * lax.rsqrt(mean + NORM_EPS) * gain
        swapped = jnp.concatenate([piece[:, HD // 2 :], piece[:, : HD // 2]], axis=1)
        turned = piece * cosine + swapped * sine
        fresh[0, :, at] = turned.astype(jnp.bfloat16).astype(jnp.float32)
    fresh[1] = raw[:, lanes:].astype(jnp.bfloat16).astype(jnp.float32)

    position = lax.broadcasted_iota(jnp.int32, (capacity, HD), 0)
    column = lax.broadcasted_iota(jnp.int32, (capacity, HD), 1)
    column_item = column // per_row
    column_step = (column % per_head) // group
    column_head = lax.broadcasted_iota(jnp.int32, (HD, HD), 1) % per_row // per_head
    factor = 1.0 / math.sqrt(HD)

    for part in range(rows // block):
        for index in teams:
            fetch(part * len(teams) + index).wait()
        if (part + 1) * block < rows:
            for index in teams:
                fetch((part + 1) * len(teams) + index).start()
        scores = []
        for index in teams:
            queries = query_columns[part * len(teams) + index]
            queries = jnp.concatenate(
                [jnp.where(column_head == head, queries, 0.0) for head in range(heads)], axis=0
            ).astype(jnp.bfloat16)
            score, limit = None, None
            for member in range(team):
                row = part * block + index * team + member
                length = length_ref[row]
                kept = position < length
                landing = [position == length + step for step in range(steps)]
                for which in range(2):
                    for head in range(heads):
                        at = slice(head * HD, (head + 1) * HD)
                        stored = held[row, which, :, at].astype(jnp.float32)
                        stored = jnp.where(kept, stored, 0.0)
                        for step in range(steps):
                            new = fresh[which, step * rows + row : step * rows + row + 1, at]
                            stored = jnp.where(landing[step], new, stored)
                        appended[row, which, :, at] = stored.astype(jnp.bfloat16)
                one = jnp.dot(appended[row, 0], queries, preferred_element_type=jnp.float32)
                score = one if member == 0 else jnp.where(column_item == member, one, score)
                limit = length if member == 0 else jnp.where(column_item == member, length, limit)
            scores.append(jnp.where(position <= limit + column_step, score * factor, -jnp.inf))
        for index in teams:
            store(part * len(teams) + index).start()
        weights = []
        for score in scores:
            raised = jnp.exp(score - jnp.max(score, axis=0, keepdims=True))
            normaliser = jnp.sum(raised, axis=0, keepdims=True)
            weights.append((raised / normaliser).T.astype(jnp.bfloat16))
        for index in teams:
            for member in range(team):
                row = part * block + index * team + member
                result = jnp.dot(
                    weights[index][member * per_row : (member + 1) * per_row],
                    appended[row, 1],
                    preferred_element_type=jnp.float32,
                )
                for head in range(heads):
                    at = row * per_row + head * per_head
                    mixed[at : at + per_head, :] = result[
                        head * per_head : (head + 1) * per_head, head * HD : (head + 1) * HD
                    ]

    mixed_ref[...] = mixed[...].astype(jnp.bfloat16)
    for peer in range(count):
        row = pick_ref[peer]
        small_ref[peer, :per_row, :] = mixed[
            pl.ds(pl.multiple_of(row * per_row, per_row), per_row), :
        ].astype(jnp.bfloat16)
        news = []
        for which in range(2):
            for step in range(steps):
                new = fresh[which, pl.ds(step * rows + row, 1), :]
                news += [new[:, h * HD : (h + 1) * HD] for h in range(heads)]
        slot = dest_ref[row] - peer * rows
        slot = jnp.where((slot >= 0) & (slot < rows), slot, -1).astype(jnp.float32)
        fill = small_ref.shape[1] - per_row - len(news)
        news.append(jnp.full((fill, HD), slot))
        small_ref[peer, per_row:, :] = jnp.concatenate(news, axis=0).astype(jnp.bfloat16)
    for index in range(rows // team):
        store(index).wait()


def attend(
    kv_cache, queries, own, got, gain, lengths, destination, pick, late, count
):
    late_shapes = [jax.ShapeDtypeStruct(x.shape, x.dtype) for x in late]
    steps, rows, query_width = queries.shape
    capacity, lanes = kv_cache.shape[2:]
    heads = lanes // HD
    per_row = steps * query_width // HD
    block = 8
    teams = rows * per_row // HD
    small_rows = per_row + -(-(2 * steps * heads + 1) // TILE) * TILE
    small = jax.ShapeDtypeStruct((count, small_rows, HD), jnp.bfloat16)
    smem = pl.BlockSpec(memory_space=pltpu.SMEM)
    vmem = pl.BlockSpec(memory_space=pltpu.VMEM)
    hbm = pl.BlockSpec(memory_space=pl.ANY)
    outs = pl.pallas_call(
        functools.partial(attend_kernel, count, block),
        out_shape=[
            jax.ShapeDtypeStruct(kv_cache.shape, kv_cache.dtype),
            jax.ShapeDtypeStruct((rows * per_row, HD), jnp.bfloat16),
            small,
        ]
        + late_shapes,
        in_specs=[smem, smem, smem, hbm, hbm, vmem, hbm, hbm] + [hbm] * len(late),
        out_specs=[hbm, vmem, vmem] + [hbm] * len(late),
        scratch_shapes=[
            pltpu.VMEM((2, steps * rows, lanes), jnp.float32),
            pltpu.VMEM(queries.shape, queries.dtype),
            pltpu.VMEM((rows * per_row, HD), jnp.float32),
            pltpu.VMEM((teams, HD, HD), jnp.float32),
            pltpu.VMEM((rows * per_row, HD), jnp.float32),
            pltpu.VMEM((2,) + own.shape, own.dtype),
            pltpu.VMEM(kv_cache.shape, kv_cache.dtype),
            pltpu.VMEM(kv_cache.shape, kv_cache.dtype),
            pltpu.SemaphoreType.DMA((2,)),
            pltpu.SemaphoreType.DMA,
            pltpu.SemaphoreType.DMA((teams,)),
            pltpu.SemaphoreType.DMA((teams,)),
        ],
        input_output_aliases={8 + i: 3 + i for i in range(len(late))},
        compiler_params=pltpu.CompilerParams(vmem_limit_bytes=ATTEND_LIMIT),
        cost_estimate=HEAVY,
        name="attend",
    )(lengths, destination, pick, own, got, gain, queries, kv_cache, *late)
    return outs[0], outs[1], outs[2], outs[3:]


def read_facts(block):
    capacity = block.shape[1]
    facts = block[0, capacity - TILE :, :].astype(jnp.float32)[TILE - 1 :]
    return (
        jnp.max(facts[:, :HD]).astype(jnp.int32),
        jnp.max(facts[:, HD : 2 * HD]).astype(jnp.int32),
    )


def window_start(length, capacity):
    return pl.multiple_of(jnp.minimum(length // TILE * TILE, capacity - WINDOW), TILE)


def clean(block, length, out):
    capacity, lanes = block.shape[1:]
    kept = lax.broadcasted_iota(jnp.int32, (capacity, HD), 0) < length
    for which in range(2):
        for at in range(0, lanes, HD):
            stored = block[which, :, at : at + HD].astype(jnp.float32)
            out[which, :, at : at + HD] = jnp.where(kept, stored, 0.0).astype(jnp.bfloat16)


def insert(window, news, ahead, steps, out):
    height, lanes = window.shape[1:]
    heads = lanes // HD
    position = lax.broadcasted_iota(jnp.int32, (height, lanes), 0)
    for which in range(2):
        stored = window[which].astype(jnp.float32)
        for step in range(steps):
            at = (which * steps + step) * heads
            new = jnp.concatenate([news[at + h : at + h + 1] for h in range(heads)], axis=1)
            stored = jnp.where(position == ahead + step, new, stored)
        out[which] = stored.astype(jnp.bfloat16)


def land_kernel(pieces, *refs):
    blocks = refs[:pieces]
    _, out_ref, slot_ref, length_ref, window_ref, buffer, sems = refs[pieces:]
    capacity = buffer.shape[2]

    def store(piece):
        slot = jnp.maximum(slot_ref[piece], 0)
        return pltpu.make_async_copy(buffer.at[piece], out_ref.at[slot], sems.at[piece])

    for piece, block in enumerate(blocks):
        slot_ref[piece], length_ref[piece] = read_facts(block)
    for piece, block in enumerate(blocks):

        @pl.when(slot_ref[piece] >= 0)
        def _():
            length = length_ref[piece]
            clean(block, length, buffer.at[piece])
            store(piece).start()
            start = window_start(length, capacity)
            window_ref[piece] = buffer[piece, :, pl.ds(start, WINDOW), :]

    for piece in range(pieces):

        @pl.when(slot_ref[piece] >= 0)
        def _():
            store(piece).wait()


def land(got, moved):
    pieces = len(got)
    smem = pl.BlockSpec(memory_space=pltpu.SMEM)
    vmem = pl.BlockSpec(memory_space=pltpu.VMEM)
    hbm = pl.BlockSpec(memory_space=pl.ANY)
    scalars = jax.ShapeDtypeStruct((pieces,), jnp.int32)
    return pl.pallas_call(
        functools.partial(land_kernel, pieces),
        out_shape=[
            jax.ShapeDtypeStruct(moved.shape, moved.dtype),
            scalars,
            scalars,
            jax.ShapeDtypeStruct((pieces, 2, WINDOW, moved.shape[3]), moved.dtype),
        ],
        in_specs=[vmem] * pieces + [hbm],
        out_specs=[hbm, smem, smem, vmem],
        scratch_shapes=[
            pltpu.VMEM((pieces,) + moved.shape[1:], moved.dtype),
            pltpu.SemaphoreType.DMA((pieces,)),
        ],
        input_output_aliases={pieces: 0},
        compiler_params=pltpu.CompilerParams(vmem_limit_bytes=SMALL_LIMIT),
        cost_estimate=HEAVY,
        name="land",
    )(*got, moved)


def settle_kernel(
    count,
    early,
    group,
    slot_ref,
    length_ref,
    mixed_ref,
    small_ref,
    window_ref,
    _,
    out_ref,
    moved_ref,
    mixed,
    windows,
    sems,
):
    steps, rows, query_width = out_ref.shape
    per_row = steps * query_width // HD
    capacity, lanes = moved_ref.shape[2:]
    heads = lanes // HD
    me = lax.axis_index("inst")
    pieces = len(early)

    def store(piece):
        slot = jnp.maximum(slot_ref[piece], 0)
        start = window_start(length_ref[piece], capacity)
        return pltpu.make_async_copy(
            windows.at[piece], moved_ref.at[slot, :, pl.ds(start, WINDOW), :], sems.at[piece]
        )

    def take(slot, peer):
        mixed[pl.ds(pl.multiple_of(slot * per_row, per_row), per_row), :] = small_ref[
            peer, :per_row, :
        ].astype(jnp.float32)

    for piece in range(pieces):

        @pl.when(slot_ref[piece] >= 0)
        def _():
            length = length_ref[piece]
            peer = peer_from(me, early[piece], count)
            news = small_ref[peer, per_row:, :].astype(jnp.float32)
            ahead = length - window_start(length, capacity)
            insert(window_ref.at[piece], news, ahead, steps, windows.at[piece])
            store(piece).start()

    mixed[...] = mixed_ref[...].astype(jnp.float32)
    for shift in range(1, count):
        peer = peer_from(me, shift, count)
        if shift in early:
            slot = slot_ref[early.index(shift)]
        else:
            line = 2 * steps * heads
            facts = small_ref[peer, per_row:, :].astype(jnp.float32)[line : line + 1]
            slot = jnp.max(facts).astype(jnp.int32)
        pl.when(slot >= 0)(functools.partial(take, slot, peer))
    for step in range(steps):
        for chunk in range(query_width // HD):
            head, member = chunk // group, chunk % group
            at = head * steps * group + step * group + member
            out_ref[step, :, chunk * HD : (chunk + 1) * HD] = mixed[
                pl.ds(at, rows, stride=per_row), :
            ].astype(jnp.bfloat16)

    for piece in range(pieces):

        @pl.when(slot_ref[piece] >= 0)
        def _():
            store(piece).wait()


def settle(slots, lengths, mixed, small, windows, moved, shape, group, count, early):
    smem = pl.BlockSpec(memory_space=pltpu.SMEM)
    vmem = pl.BlockSpec(memory_space=pltpu.VMEM)
    hbm = pl.BlockSpec(memory_space=pl.ANY)
    return pl.pallas_call(
        functools.partial(settle_kernel, count, early, group),
        out_shape=[
            jax.ShapeDtypeStruct(shape, jnp.bfloat16),
            jax.ShapeDtypeStruct(moved.shape, moved.dtype),
        ],
        in_specs=[smem, smem, vmem, vmem, vmem, hbm],
        out_specs=[vmem, hbm],
        scratch_shapes=[
            pltpu.VMEM(mixed.shape, jnp.float32),
            pltpu.VMEM(windows.shape, windows.dtype),
            pltpu.SemaphoreType.DMA((slots.shape[0],)),
        ],
        input_output_aliases={5: 1},
        compiler_params=pltpu.CompilerParams(vmem_limit_bytes=SMALL_LIMIT),
        cost_estimate=LIGHT,
        name="settle",
    )(slots, lengths, mixed, small, windows, moved)


def finish_kernel(count, late, steps, *refs):
    blocks = refs[: len(late)]
    small_ref, _, out_ref, buffer, sems, slot_ref = refs[len(late) :]
    capacity, lanes = buffer.shape[2:]
    height = small_ref.shape[1]
    tail = height - -(-(2 * steps * (lanes // HD) + 1) // TILE) * TILE
    me = lax.axis_index("inst")

    def store(piece):
        slot = jnp.maximum(slot_ref[piece], 0)
        return pltpu.make_async_copy(buffer.at[piece], out_ref.at[slot], sems.at[piece])

    facts = [read_facts(block) for block in blocks]
    for piece, (slot, length) in enumerate(facts):
        slot_ref[piece] = slot

        @pl.when(slot >= 0)
        def _():
            clean(blocks[piece], length, buffer.at[piece])
            start = window_start(length, capacity)
            window = buffer.at[piece, :, pl.ds(start, WINDOW), :]
            news = small_ref[peer_from(me, late[piece], count), tail:, :].astype(jnp.float32)
            insert(window, news, length - start, steps, window)
            store(piece).start()

    for piece in range(len(late)):

        @pl.when(slot_ref[piece] >= 0)
        def _():
            store(piece).wait()


def finish(got, small, moved, steps, count, late):
    vmem = pl.BlockSpec(memory_space=pltpu.VMEM)
    hbm = pl.BlockSpec(memory_space=pl.ANY)
    return pl.pallas_call(
        functools.partial(finish_kernel, count, late, steps),
        out_shape=jax.ShapeDtypeStruct(moved.shape, moved.dtype),
        in_specs=[vmem] * len(got) + [vmem, hbm],
        out_specs=hbm,
        scratch_shapes=[
            pltpu.VMEM((len(got),) + moved.shape[1:], moved.dtype),
            pltpu.SemaphoreType.DMA((len(got),)),
            pltpu.SMEM((len(got),), jnp.int32),
        ],
        input_output_aliases={len(got) + 1: 0},
        compiler_params=pltpu.CompilerParams(vmem_limit_bytes=SMALL_LIMIT),
        cost_estimate=LIGHT,
        name="finish",
    )(*got, small, moved)


def local(hidden_new, queries, kv_cache, lengths, destination, key_weight, value_weight, key_gain):
    steps = queries.shape[0]
    group = queries.shape[2] // kv_cache.shape[3]
    count = lax.axis_size("inst")
    half = max(count // 2, 1)
    early = list(range(half, count - 1)) + [half - 1] * (half > 1)
    late = [count - 1] + list(range(half - 2, 0, -1))

    def send(block, shift):
        pairs = [(i, peer_to(i, shift, count)) for i in range(count)]
        return lax.ppermute(block, "inst", pairs)

    blocks, pick, own, other = prepare(
        destination, lengths, hidden_new, kv_cache, key_weight, value_weight, count
    )
    early_got = [send(blocks[shift - 1], shift) for shift in early]
    got = lax.ppermute(other, "tp", [(0, 1), (1, 0)])
    moved, mixed, small, late_blocks = attend(
        kv_cache,
        queries,
        own,
        got,
        key_gain[None, :],
        lengths,
        destination,
        pick,
        [blocks[shift - 1] for shift in late],
        count,
    )
    late_got = [send(block, shift) for block, shift in zip(late_blocks, late)]
    small_got = lax.all_to_all(small, "inst", 0, 0, tiled=True)
    moved, slots, arrived, windows = land(early_got, moved)
    attended, moved = settle(
        slots, arrived, mixed, small_got, windows, moved, queries.shape, group, count, early
    )
    return attended, finish(late_got, small_got, moved, steps, count, late)


def solution(mesh):
    return jax.shard_map(
        local,
        mesh=mesh,
        in_specs=(
            P(None, ("group", "inst"), "tp"),
            P(None, ("group", "inst"), "tp"),
            P(("group", "inst"), None, None, "tp"),
            P(("group", "inst")),
            P(("group", "inst")),
            P("tp", None),
            P("tp", None),
            P(),
        ),
        out_specs=(P(None, ("group", "inst"), "tp"), P(("group", "inst"), None, None, "tp")),
        check_vma=False,
    )
```

```python
import functools
import math

import jax
import jax.numpy as jnp
from jax import lax
from jax.experimental import pallas as pl
from jax.experimental.pallas import tpu as pltpu
from jax.sharding import PartitionSpec as P

HD = 128
ROPE_BASE = 1000000.0
NORM_EPS = 1e-06
VMEM_LIMIT = 62 * 1024 * 1024
ATTEND_LIMIT = 56 * 1024 * 1024
SMALL_LIMIT = 40 * 1024 * 1024
LIGHT = pl.CostEstimate(flops=1, bytes_accessed=1, transcendentals=0)
HEAVY = pl.CostEstimate(flops=1 << 36, bytes_accessed=1 << 28, transcendentals=0)
TILE = 16
WINDOW = 32


def quotient(value, divisor, bound):
    factor = -(-(1 << 16) // divisor)
    if bound * factor < 1 << 31 and all(
        (x * factor) >> 16 == x // divisor for x in range(bound)
    ):
        return (value * factor) >> 16
    return value // divisor


def peer_to(index, shift, count):
    return index ^ shift if count & (count - 1) == 0 else (index + shift) % count


def peer_from(index, shift, count):
    return index ^ shift if count & (count - 1) == 0 else (index + count - shift) % count


def prepare_kernel(
    count, chunks, dest_ref, length_ref, hidden_ref, kv_ref, key_ref, value_ref, *refs
):
    block_refs = refs[: count - 1]
    pick_ref, own_ref, other_ref, blocks, hidden_held, held, total = refs[count - 1 : count + 6]
    in_sems, out_sems, hidden_sem, weight_sems = refs[count + 6 :]
    rows = dest_ref.shape[0]
    capacity, lanes = kv_ref.shape[2:]
    me = lax.axis_index("inst")
    shifts = range(1, count)

    hidden_copy = pltpu.make_async_copy(hidden_ref, hidden_held, hidden_sem)
    hidden_copy.start()
    steps, _, depth = hidden_ref.shape
    width = key_ref.shape[1]
    part = depth // chunks
    weights = []
    for chunk in range(chunks):
        span = pl.ds(chunk * part, part)
        for which, ref in enumerate((key_ref, value_ref)):
            weights.append(
                pltpu.make_async_copy(
                    ref.at[span], held.at[which, span], weight_sems.at[chunk, which]
                )
            )
            weights[-1].start()

    for peer in range(count):
        pick_ref[peer] = 0
    for row in range(rows):
        pick_ref[quotient(dest_ref[row], rows, rows * count)] = row
    fetches, stores = {}, {}
    for shift in shifts:
        row = pick_ref[peer_to(me, shift, count)]
        fetches[shift] = pltpu.make_async_copy(
            kv_ref.at[row], blocks.at[shift - 1], in_sems.at[shift - 1]
        )
        fetches[shift].start()

    tile = (TILE, lanes)
    last = lax.broadcasted_iota(jnp.int32, tile, 0) == TILE - 1
    first_lanes = lax.broadcasted_iota(jnp.int32, tile, 1) < HD
    for shift in shifts:
        peer = peer_to(me, shift, count)
        row = pick_ref[peer]
        slot = dest_ref[row] - peer * rows
        slot = jnp.where((slot >= 0) & (slot < rows), slot, -1)
        facts = jnp.where(first_lanes, slot, length_ref[row]).astype(jnp.float32)
        fetches[shift].wait()
        end = blocks[shift - 1, 0, capacity - TILE :, :].astype(jnp.float32)
        blocks[shift - 1, 0, capacity - TILE :, :] = jnp.where(last, facts, end).astype(
            jnp.bfloat16
        )
        stores[shift] = pltpu.make_async_copy(
            blocks.at[shift - 1], block_refs[shift - 1], out_sems.at[shift - 1]
        )
        stores[shift].start()

    hidden_copy.wait()
    hidden = hidden_held[...].reshape(steps * rows, depth)
    sums = [None, None]
    for chunk in range(chunks):
        for which in range(2):
            weights[2 * chunk + which].wait()
            product = jnp.dot(
                hidden[:, chunk * part : (chunk + 1) * part],
                held[which, chunk * part : (chunk + 1) * part, :],
                preferred_element_type=jnp.float32,
            )
            sums[which] = product if chunk == 0 else sums[which] + product
    total[:, :width] = sums[0]
    total[:, width:] = sums[1]
    half = width // 2
    core = lax.axis_index("tp")
    for ref, place in ((own_ref, core), (other_ref, 1 - core)):
        at = pl.multiple_of(place * half, half)
        ref[:, :half] = total[:, pl.ds(at, half)]
        ref[:, half:] = total[:, pl.ds(pl.multiple_of(width + at, half), half)]
    for shift in shifts:
        stores[shift].wait()


def prepare(destination, lengths, hidden_new, kv_cache, key_weight, value_weight, count):
    steps, rows, depth = hidden_new.shape
    width = key_weight.shape[1]
    chunks = 5
    shape = kv_cache.shape[1:]
    part = jax.ShapeDtypeStruct((steps * rows, width), jnp.float32)
    smem = pl.BlockSpec(memory_space=pltpu.SMEM)
    vmem = pl.BlockSpec(memory_space=pltpu.VMEM)
    hbm = pl.BlockSpec(memory_space=pl.ANY)
    outs = pl.pallas_call(
        functools.partial(prepare_kernel, count, chunks),
        out_shape=[jax.ShapeDtypeStruct(shape, kv_cache.dtype)] * (count - 1)
        + [jax.ShapeDtypeStruct((count,), jnp.int32), part, part],
        in_specs=[smem, smem, hbm, hbm, hbm, hbm],
        out_specs=[hbm] * (count - 1) + [smem, vmem, vmem],
        scratch_shapes=[
            pltpu.VMEM((count - 1,) + shape, kv_cache.dtype),
            pltpu.VMEM(hidden_new.shape, hidden_new.dtype),
            pltpu.VMEM((2, depth, width), key_weight.dtype),
            pltpu.VMEM((steps * rows, 2 * width), jnp.float32),
            pltpu.SemaphoreType.DMA((count - 1,)),
            pltpu.SemaphoreType.DMA((count - 1,)),
            pltpu.SemaphoreType.DMA,
            pltpu.SemaphoreType.DMA((chunks, 2)),
        ],
        compiler_params=pltpu.CompilerParams(vmem_limit_bytes=VMEM_LIMIT),
        cost_estimate=LIGHT,
        name="prepare",
    )(destination, lengths, hidden_new, kv_cache, key_weight, value_weight)
    return outs[: count - 1], *outs[count - 1 :]


def rotation(length_ref, steps, rows):
    half = HD // 2
    line = lax.broadcasted_iota(jnp.int32, (rows, HD), 0)
    lane = lax.broadcasted_iota(jnp.int32, (steps * rows, HD), 1)
    length = jnp.zeros((rows, HD), jnp.int32)
    for row in range(rows):
        length = jnp.where(line == row, length_ref[row], length)
    position = jnp.concatenate([length + step for step in range(steps)], axis=0)
    order = (lane % half).astype(jnp.float32)
    angle = position.astype(jnp.float32) * jnp.exp(-math.log(ROPE_BASE) * 2.0 * order / HD)
    turns = jnp.floor(angle * (1.0 / math.pi) + 0.5)
    rest = ((angle - turns * 3.140625) - turns * 9.67502593994140625e-4) - turns * 1.5099579909783e-7
    sign = 1.0 - 2.0 * (turns - 2.0 * jnp.floor(turns * 0.5))
    square = rest * rest
    cosine, sine = jnp.ones_like(rest), jnp.ones_like(rest)
    for power in range(6, 0, -1):
        cosine = 1.0 - cosine * square * (1.0 / ((2 * power - 1) * (2 * power)))
        sine = 1.0 - sine * square * (1.0 / ((2 * power) * (2 * power + 1)))
    sine = sign * rest * sine
    return sign * cosine, jnp.where(lane < half, -sine, sine)


def attend_kernel(
    count,
    block,
    length_ref,
    dest_ref,
    pick_ref,
    own_ref,
    got_ref,
    gain_ref,
    query_ref,
    kv_ref,
    *refs,
):
    late = (len(refs) - 7) // 2
    moved_ref, mixed_ref, small_ref = refs[late : late + 3]
    fresh, query_rows, query_columns, mixed = refs[-4:]
    part = pl.program_id(0)
    steps, rows, query_width = query_ref.shape
    capacity, lanes = kv_ref.shape[2:]
    heads = lanes // HD
    group = query_width // lanes
    per_head = steps * group
    per_row = heads * per_head
    team = HD // per_row

    @pl.when(part == 0)
    def _():
        raw = own_ref[...] + got_ref[...]
        cosine, sine = rotation(length_ref, steps, rows)
        gain = gain_ref[...].astype(jnp.float32)
        for head in range(heads):
            at = slice(head * HD, (head + 1) * HD)
            piece = raw[:, at]
            mean = jnp.mean(piece * piece, axis=-1, keepdims=True)
            piece = piece * lax.rsqrt(mean + NORM_EPS) * gain
            swapped = jnp.concatenate([piece[:, HD // 2 :], piece[:, : HD // 2]], axis=1)
            turned = piece * cosine + swapped * sine
            fresh[0, :, at] = turned.astype(jnp.bfloat16).astype(jnp.float32)
        fresh[1] = raw[:, lanes:].astype(jnp.bfloat16).astype(jnp.float32)
        for step in range(steps):
            for chunk in range(query_width // HD):
                head, member = chunk // group, chunk % group
                at = head * per_head + step * group + member
                query_rows[pl.ds(at, rows, stride=per_row), :] = query_ref[
                    step, :, chunk * HD : (chunk + 1) * HD
                ].astype(jnp.float32)
        for index in range(rows // team):
            query_columns[index] = query_rows[index * HD : (index + 1) * HD, :].T

    position = lax.broadcasted_iota(jnp.int32, (capacity, HD), 0)
    column = lax.broadcasted_iota(jnp.int32, (capacity, HD), 1)
    column_item = column // per_row
    column_step = (column % per_head) // group
    column_head = lax.broadcasted_iota(jnp.int32, (HD, HD), 1) % per_row // per_head
    factor = 1.0 / math.sqrt(HD)
    teams = range(block // team)
    scores = []
    for index in teams:
        queries = query_columns[part * (block // team) + index]
        queries = jnp.concatenate(
            [jnp.where(column_head == head, queries, 0.0) for head in range(heads)], axis=0
        ).astype(jnp.bfloat16)
        score, limit = None, None
        for member in range(team):
            item = index * team + member
            row = part * block + item
            length = length_ref[row]
            kept = position < length
            landing = [position == length + step for step in range(steps)]
            for which in range(2):
                news = [fresh[which, pl.ds(step * rows + row, 1), :] for step in range(steps)]
                for head in range(heads):
                    at = slice(head * HD, (head + 1) * HD)
                    stored = jnp.where(kept, kv_ref[item, which, :, at].astype(jnp.float32), 0.0)
                    for step in range(steps):
                        stored = jnp.where(landing[step], news[step][:, at], stored)
                    moved_ref[item, which, :, at] = stored.astype(jnp.bfloat16)
            one = jnp.dot(moved_ref[item, 0], queries, preferred_element_type=jnp.float32)
            score = one if member == 0 else jnp.where(column_item == member, one, score)
            limit = length if member == 0 else jnp.where(column_item == member, length, limit)
        scores.append(jnp.where(position <= limit + column_step, score * factor, -jnp.inf))
    weights = []
    for score in scores:
        raised = jnp.exp(score - jnp.max(score, axis=0, keepdims=True))
        normaliser = jnp.sum(raised, axis=0, keepdims=True)
        weights.append((raised / normaliser).T.astype(jnp.bfloat16))
    for index in teams:
        for member in range(team):
            item = index * team + member
            row = part * block + item
            result = jnp.dot(
                weights[index][member * per_row : (member + 1) * per_row],
                moved_ref[item, 1],
                preferred_element_type=jnp.float32,
            )
            for head in range(heads):
                at = pl.multiple_of(row * per_row + head * per_head, per_head)
                mixed[pl.ds(at, per_head), :] = result[
                    head * per_head : (head + 1) * per_head, head * HD : (head + 1) * HD
                ]

    @pl.when(part == pl.num_programs(0) - 1)
    def _():
        mixed_ref[...] = mixed[...].astype(jnp.bfloat16)
        for peer in range(count):
            row = pick_ref[peer]
            small_ref[peer, :per_row, :] = mixed[
                pl.ds(pl.multiple_of(row * per_row, per_row), per_row), :
            ].astype(jnp.bfloat16)
            news = []
            for which in range(2):
                for step in range(steps):
                    new = fresh[which, pl.ds(step * rows + row, 1), :]
                    news += [new[:, h * HD : (h + 1) * HD] for h in range(heads)]
            slot = dest_ref[row] - peer * rows
            slot = jnp.where((slot >= 0) & (slot < rows), slot, -1).astype(jnp.float32)
            fill = small_ref.shape[1] - per_row - len(news)
            news.append(jnp.full((fill, HD), slot))
            small_ref[peer, per_row:, :] = jnp.concatenate(news, axis=0).astype(jnp.bfloat16)


def attend(
    kv_cache, queries, own, got, gain, lengths, destination, pick, late, count
):
    late_shapes = [jax.ShapeDtypeStruct(x.shape, x.dtype) for x in late]
    steps, rows, query_width = queries.shape
    capacity, lanes = kv_cache.shape[2:]
    heads = lanes // HD
    per_row = steps * query_width // HD
    block = 8
    small_rows = per_row + -(-(2 * steps * heads + 1) // TILE) * TILE
    small = jax.ShapeDtypeStruct((count, small_rows, HD), jnp.bfloat16)
    smem = pl.BlockSpec(memory_space=pltpu.SMEM)
    vmem = pl.BlockSpec(memory_space=pltpu.VMEM)
    hbm = pl.BlockSpec(memory_space=pl.ANY)
    cache_block = pl.BlockSpec((block, 2, capacity, lanes), lambda i: (i, 0, 0, 0))
    outs = pl.pallas_call(
        functools.partial(attend_kernel, count, block),
        grid=(rows // block,),
        out_shape=[
            jax.ShapeDtypeStruct(kv_cache.shape, kv_cache.dtype),
            jax.ShapeDtypeStruct((rows * per_row, HD), jnp.bfloat16),
            small,
        ]
        + late_shapes,
        in_specs=[smem, smem, smem, vmem, vmem, vmem, vmem, cache_block] + [hbm] * len(late),
        out_specs=[cache_block, vmem, vmem] + [hbm] * len(late),
        scratch_shapes=[
            pltpu.VMEM((2, steps * rows, lanes), jnp.float32),
            pltpu.VMEM((rows * per_row, HD), jnp.float32),
            pltpu.VMEM((rows * per_row // HD, HD, HD), jnp.float32),
            pltpu.VMEM((rows * per_row, HD), jnp.float32),
        ],
        input_output_aliases={8 + i: 3 + i for i in range(len(late))},
        compiler_params=pltpu.CompilerParams(vmem_limit_bytes=ATTEND_LIMIT),
        cost_estimate=HEAVY,
        name="attend",
    )(lengths, destination, pick, own, got, gain, queries, kv_cache, *late)
    return outs[0], outs[1], outs[2], outs[3:]


def read_facts(block):
    capacity = block.shape[1]
    facts = block[0, capacity - TILE :, :].astype(jnp.float32)[TILE - 1 :]
    return (
        jnp.max(facts[:, :HD]).astype(jnp.int32),
        jnp.max(facts[:, HD : 2 * HD]).astype(jnp.int32),
    )


def window_start(length, capacity):
    return pl.multiple_of(jnp.minimum(length // TILE * TILE, capacity - WINDOW), TILE)


def clean(block, length, out):
    capacity, lanes = block.shape[1:]
    kept = lax.broadcasted_iota(jnp.int32, (capacity, HD), 0) < length
    for which in range(2):
        for at in range(0, lanes, HD):
            stored = block[which, :, at : at + HD].astype(jnp.float32)
            out[which, :, at : at + HD] = jnp.where(kept, stored, 0.0).astype(jnp.bfloat16)


def insert(window, news, ahead, steps, out):
    height, lanes = window.shape[1:]
    heads = lanes // HD
    position = lax.broadcasted_iota(jnp.int32, (height, lanes), 0)
    for which in range(2):
        stored = window[which].astype(jnp.float32)
        for step in range(steps):
            at = (which * steps + step) * heads
            new = jnp.concatenate([news[at + h : at + h + 1] for h in range(heads)], axis=1)
            stored = jnp.where(position == ahead + step, new, stored)
        out[which] = stored.astype(jnp.bfloat16)


def land_kernel(pieces, *refs):
    blocks = refs[:pieces]
    _, out_ref, slot_ref, length_ref, window_ref, buffer, sems = refs[pieces:]
    capacity = buffer.shape[2]

    def store(piece):
        slot = jnp.maximum(slot_ref[piece], 0)
        return pltpu.make_async_copy(buffer.at[piece], out_ref.at[slot], sems.at[piece])

    for piece, block in enumerate(blocks):
        slot_ref[piece], length_ref[piece] = read_facts(block)
    for piece, block in enumerate(blocks):

        @pl.when(slot_ref[piece] >= 0)
        def _():
            length = length_ref[piece]
            clean(block, length, buffer.at[piece])
            store(piece).start()
            start = window_start(length, capacity)
            window_ref[piece] = buffer[piece, :, pl.ds(start, WINDOW), :]

    for piece in range(pieces):

        @pl.when(slot_ref[piece] >= 0)
        def _():
            store(piece).wait()


def land(got, moved):
    pieces = len(got)
    smem = pl.BlockSpec(memory_space=pltpu.SMEM)
    vmem = pl.BlockSpec(memory_space=pltpu.VMEM)
    hbm = pl.BlockSpec(memory_space=pl.ANY)
    scalars = jax.ShapeDtypeStruct((pieces,), jnp.int32)
    return pl.pallas_call(
        functools.partial(land_kernel, pieces),
        out_shape=[
            jax.ShapeDtypeStruct(moved.shape, moved.dtype),
            scalars,
            scalars,
            jax.ShapeDtypeStruct((pieces, 2, WINDOW, moved.shape[3]), moved.dtype),
        ],
        in_specs=[vmem] * pieces + [hbm],
        out_specs=[hbm, smem, smem, vmem],
        scratch_shapes=[
            pltpu.VMEM((pieces,) + moved.shape[1:], moved.dtype),
            pltpu.SemaphoreType.DMA((pieces,)),
        ],
        input_output_aliases={pieces: 0},
        compiler_params=pltpu.CompilerParams(vmem_limit_bytes=SMALL_LIMIT),
        cost_estimate=HEAVY,
        name="land",
    )(*got, moved)


def settle_kernel(
    count,
    early,
    group,
    slot_ref,
    length_ref,
    mixed_ref,
    small_ref,
    window_ref,
    _,
    out_ref,
    moved_ref,
    mixed,
    windows,
    sems,
):
    steps, rows, query_width = out_ref.shape
    per_row = steps * query_width // HD
    capacity, lanes = moved_ref.shape[2:]
    heads = lanes // HD
    me = lax.axis_index("inst")
    pieces = len(early)

    def store(piece):
        slot = jnp.maximum(slot_ref[piece], 0)
        start = window_start(length_ref[piece], capacity)
        return pltpu.make_async_copy(
            windows.at[piece], moved_ref.at[slot, :, pl.ds(start, WINDOW), :], sems.at[piece]
        )

    def take(slot, peer):
        mixed[pl.ds(pl.multiple_of(slot * per_row, per_row), per_row), :] = small_ref[
            peer, :per_row, :
        ].astype(jnp.float32)

    for piece in range(pieces):

        @pl.when(slot_ref[piece] >= 0)
        def _():
            length = length_ref[piece]
            peer = peer_from(me, early[piece], count)
            news = small_ref[peer, per_row:, :].astype(jnp.float32)
            ahead = length - window_start(length, capacity)
            insert(window_ref.at[piece], news, ahead, steps, windows.at[piece])
            store(piece).start()

    mixed[...] = mixed_ref[...].astype(jnp.float32)
    for shift in range(1, count):
        peer = peer_from(me, shift, count)
        if shift in early:
            slot = slot_ref[early.index(shift)]
        else:
            line = 2 * steps * heads
            facts = small_ref[peer, per_row:, :].astype(jnp.float32)[line : line + 1]
            slot = jnp.max(facts).astype(jnp.int32)
        pl.when(slot >= 0)(functools.partial(take, slot, peer))
    for step in range(steps):
        for chunk in range(query_width // HD):
            head, member = chunk // group, chunk % group
            at = head * steps * group + step * group + member
            out_ref[step, :, chunk * HD : (chunk + 1) * HD] = mixed[
                pl.ds(at, rows, stride=per_row), :
            ].astype(jnp.bfloat16)

    for piece in range(pieces):

        @pl.when(slot_ref[piece] >= 0)
        def _():
            store(piece).wait()


def settle(slots, lengths, mixed, small, windows, moved, shape, group, count, early):
    smem = pl.BlockSpec(memory_space=pltpu.SMEM)
    vmem = pl.BlockSpec(memory_space=pltpu.VMEM)
    hbm = pl.BlockSpec(memory_space=pl.ANY)
    return pl.pallas_call(
        functools.partial(settle_kernel, count, early, group),
        out_shape=[
            jax.ShapeDtypeStruct(shape, jnp.bfloat16),
            jax.ShapeDtypeStruct(moved.shape, moved.dtype),
        ],
        in_specs=[smem, smem, vmem, vmem, vmem, hbm],
        out_specs=[vmem, hbm],
        scratch_shapes=[
            pltpu.VMEM(mixed.shape, jnp.float32),
            pltpu.VMEM(windows.shape, windows.dtype),
            pltpu.SemaphoreType.DMA((slots.shape[0],)),
        ],
        input_output_aliases={5: 1},
        compiler_params=pltpu.CompilerParams(vmem_limit_bytes=SMALL_LIMIT),
        cost_estimate=LIGHT,
        name="settle",
    )(slots, lengths, mixed, small, windows, moved)


def finish_kernel(count, late, steps, *refs):
    blocks = refs[: len(late)]
    small_ref, _, out_ref, buffer, sems, slot_ref = refs[len(late) :]
    capacity, lanes = buffer.shape[2:]
    height = small_ref.shape[1]
    tail = height - -(-(2 * steps * (lanes // HD) + 1) // TILE) * TILE
    me = lax.axis_index("inst")

    def store(piece):
        slot = jnp.maximum(slot_ref[piece], 0)
        return pltpu.make_async_copy(buffer.at[piece], out_ref.at[slot], sems.at[piece])

    facts = [read_facts(block) for block in blocks]
    for piece, (slot, length) in enumerate(facts):
        slot_ref[piece] = slot

        @pl.when(slot >= 0)
        def _():
            clean(blocks[piece], length, buffer.at[piece])
            start = window_start(length, capacity)
            window = buffer.at[piece, :, pl.ds(start, WINDOW), :]
            news = small_ref[peer_from(me, late[piece], count), tail:, :].astype(jnp.float32)
            insert(window, news, length - start, steps, window)
            store(piece).start()

    for piece in range(len(late)):

        @pl.when(slot_ref[piece] >= 0)
        def _():
            store(piece).wait()


def finish(got, small, moved, steps, count, late):
    vmem = pl.BlockSpec(memory_space=pltpu.VMEM)
    hbm = pl.BlockSpec(memory_space=pl.ANY)
    return pl.pallas_call(
        functools.partial(finish_kernel, count, late, steps),
        out_shape=jax.ShapeDtypeStruct(moved.shape, moved.dtype),
        in_specs=[vmem] * len(got) + [vmem, hbm],
        out_specs=hbm,
        scratch_shapes=[
            pltpu.VMEM((len(got),) + moved.shape[1:], moved.dtype),
            pltpu.SemaphoreType.DMA((len(got),)),
            pltpu.SMEM((len(got),), jnp.int32),
        ],
        input_output_aliases={len(got) + 1: 0},
        compiler_params=pltpu.CompilerParams(vmem_limit_bytes=SMALL_LIMIT),
        cost_estimate=LIGHT,
        name="finish",
    )(*got, small, moved)


def local(hidden_new, queries, kv_cache, lengths, destination, key_weight, value_weight, key_gain):
    steps = queries.shape[0]
    group = queries.shape[2] // kv_cache.shape[3]
    count = lax.axis_size("inst")
    half = max(count // 2, 1)
    early = list(range(half, count - 1)) + [half - 1] * (half > 1)
    late = [count - 1] + list(range(half - 2, 0, -1))

    def send(block, shift):
        pairs = [(i, peer_to(i, shift, count)) for i in range(count)]
        return lax.ppermute(block, "inst", pairs)

    blocks, pick, own, other = prepare(
        destination, lengths, hidden_new, kv_cache, key_weight, value_weight, count
    )
    early_got = [send(blocks[shift - 1], shift) for shift in early]
    got = lax.ppermute(other, "tp", [(0, 1), (1, 0)])
    moved, mixed, small, late_blocks = attend(
        kv_cache,
        queries,
        own,
        got,
        key_gain[None, :],
        lengths,
        destination,
        pick,
        [blocks[shift - 1] for shift in late],
        count,
    )
    late_got = [send(block, shift) for block, shift in zip(late_blocks, late)]
    small_got = lax.all_to_all(small, "inst", 0, 0, tiled=True)
    moved, slots, arrived, windows = land(early_got, moved)
    attended, moved = settle(
        slots, arrived, mixed, small_got, windows, moved, queries.shape, group, count, early
    )
    return attended, finish(late_got, small_got, moved, steps, count, late)


def solution(mesh):
    return jax.shard_map(
        local,
        mesh=mesh,
        in_specs=(
            P(None, ("group", "inst"), "tp"),
            P(None, ("group", "inst"), "tp"),
            P(("group", "inst"), None, None, "tp"),
            P(("group", "inst")),
            P(("group", "inst")),
            P("tp", None),
            P("tp", None),
            P(),
        ),
        out_specs=(P(None, ("group", "inst"), "tp"), P(("group", "inst"), None, None, "tp")),
        check_vma=False,
    )
```

```python
import functools
import math

import jax
import jax.numpy as jnp
from jax import lax
from jax.experimental import pallas as pl
from jax.experimental.pallas import tpu as pltpu
from jax.sharding import PartitionSpec as P

HD = 128
ROPE_BASE = 1000000.0
NORM_EPS = 1e-06
VMEM_LIMIT = 62 * 1024 * 1024
ATTEND_LIMIT = 56 * 1024 * 1024
SMALL_LIMIT = 40 * 1024 * 1024
LIGHT = pl.CostEstimate(flops=1, bytes_accessed=1, transcendentals=0)
HEAVY = pl.CostEstimate(flops=1 << 36, bytes_accessed=1 << 28, transcendentals=0)
TILE = 16
WINDOW = 32


def quotient(value, divisor, bound):
    factor = -(-(1 << 16) // divisor)
    if bound * factor < 1 << 31 and all(
        (x * factor) >> 16 == x // divisor for x in range(bound)
    ):
        return (value * factor) >> 16
    return value // divisor


def peer_to(index, shift, count):
    return index ^ shift if count & (count - 1) == 0 else (index + shift) % count


def peer_from(index, shift, count):
    return index ^ shift if count & (count - 1) == 0 else (index + count - shift) % count


def pack_kernel(count, early, dest_ref, length_ref, kv_ref, *refs):
    block_refs = refs[: len(early)]
    pick_ref, blocks, in_sems, out_sems = refs[len(early) :]
    rows = dest_ref.shape[0]
    capacity, lanes = kv_ref.shape[2:]
    me = lax.axis_index("inst")
    for peer in range(count):
        pick_ref[peer] = 0
    for row in range(rows):
        pick_ref[quotient(dest_ref[row], rows, rows * count)] = row
    fetches, stores = [], []
    for piece, shift in enumerate(early):
        row = pick_ref[peer_to(me, shift, count)]
        fetches.append(
            pltpu.make_async_copy(kv_ref.at[row], blocks.at[piece], in_sems.at[piece])
        )
        fetches[-1].start()
    tile = (TILE, lanes)
    last = lax.broadcasted_iota(jnp.int32, tile, 0) == TILE - 1
    first_lanes = lax.broadcasted_iota(jnp.int32, tile, 1) < HD
    for piece, shift in enumerate(early):
        peer = peer_to(me, shift, count)
        row = pick_ref[peer]
        slot = dest_ref[row] - peer * rows
        slot = jnp.where((slot >= 0) & (slot < rows), slot, -1)
        facts = jnp.where(first_lanes, slot, length_ref[row]).astype(jnp.float32)
        fetches[piece].wait()
        end = blocks[piece, 0, capacity - TILE :, :].astype(jnp.float32)
        blocks[piece, 0, capacity - TILE :, :] = jnp.where(last, facts, end).astype(jnp.bfloat16)
        stores.append(
            pltpu.make_async_copy(blocks.at[piece], block_refs[piece], out_sems.at[piece])
        )
        stores[-1].start()
    for copy in stores:
        copy.wait()


def pack(kv_cache, destination, lengths, count, early):
    shape = kv_cache.shape[1:]
    smem = pl.BlockSpec(memory_space=pltpu.SMEM)
    hbm = pl.BlockSpec(memory_space=pl.ANY)
    outs = pl.pallas_call(
        functools.partial(pack_kernel, count, early),
        out_shape=[jax.ShapeDtypeStruct(shape, kv_cache.dtype)] * len(early)
        + [jax.ShapeDtypeStruct((count,), jnp.int32)],
        in_specs=[smem, smem, hbm],
        out_specs=[hbm] * len(early) + [smem],
        scratch_shapes=[
            pltpu.VMEM((len(early),) + shape, kv_cache.dtype),
            pltpu.SemaphoreType.DMA((len(early),)),
            pltpu.SemaphoreType.DMA((len(early),)),
        ],
        compiler_params=pltpu.CompilerParams(vmem_limit_bytes=VMEM_LIMIT),
        cost_estimate=LIGHT,
        name="pack",
    )(destination, lengths, kv_cache)
    return outs[:-1], outs[-1]


def project_kernel(
    chunks,
    _,
    hidden_ref,
    key_ref,
    value_ref,
    own_ref,
    other_ref,
    hidden_held,
    held,
    total,
    hidden_sem,
    weight_sems,
):
    steps, rows, depth = hidden_ref.shape
    width = key_ref.shape[1]
    part = depth // chunks
    hidden_copy = pltpu.make_async_copy(hidden_ref, hidden_held, hidden_sem)
    hidden_copy.start()
    weights = []
    for chunk in range(chunks):
        span = pl.ds(chunk * part, part)
        for which, ref in enumerate((key_ref, value_ref)):
            weights.append(
                pltpu.make_async_copy(
                    ref.at[span], held.at[which, span], weight_sems.at[chunk, which]
                )
            )
            weights[-1].start()
    hidden_copy.wait()
    hidden = hidden_held[...].reshape(steps * rows, depth)
    sums = [None, None]
    for chunk in range(chunks):
        for which in range(2):
            weights[2 * chunk + which].wait()
            product = jnp.dot(
                hidden[:, chunk * part : (chunk + 1) * part],
                held[which, chunk * part : (chunk + 1) * part, :],
                preferred_element_type=jnp.float32,
            )
            sums[which] = product if chunk == 0 else sums[which] + product
    total[:, :width] = sums[0]
    total[:, width:] = sums[1]
    half = width // 2
    core = lax.axis_index("tp")
    for ref, place in ((own_ref, core), (other_ref, 1 - core)):
        at = pl.multiple_of(place * half, half)
        ref[:, :half] = total[:, pl.ds(at, half)]
        ref[:, half:] = total[:, pl.ds(pl.multiple_of(width + at, half), half)]


def project(hidden_new, key_weight, value_weight, pick):
    steps, rows, depth = hidden_new.shape
    width = key_weight.shape[1]
    chunks = 5
    part = jax.ShapeDtypeStruct((steps * rows, width), jnp.float32)
    vmem = pl.BlockSpec(memory_space=pltpu.VMEM)
    hbm = pl.BlockSpec(memory_space=pl.ANY)
    return pl.pallas_call(
        functools.partial(project_kernel, chunks),
        out_shape=[part, part],
        in_specs=[hbm, hbm, hbm, hbm],
        out_specs=[vmem, vmem],
        scratch_shapes=[
            pltpu.VMEM(hidden_new.shape, hidden_new.dtype),
            pltpu.VMEM((2, depth, width), key_weight.dtype),
            pltpu.VMEM((steps * rows, 2 * width), jnp.float32),
            pltpu.SemaphoreType.DMA,
            pltpu.SemaphoreType.DMA((chunks, 2)),
        ],
        compiler_params=pltpu.CompilerParams(vmem_limit_bytes=VMEM_LIMIT),
        cost_estimate=LIGHT,
        name="project",
    )(pick, hidden_new, key_weight, value_weight)


def rotation(length_ref, steps, rows):
    half = HD // 2
    line = lax.broadcasted_iota(jnp.int32, (rows, HD), 0)
    lane = lax.broadcasted_iota(jnp.int32, (steps * rows, HD), 1)
    length = jnp.zeros((rows, HD), jnp.int32)
    for row in range(rows):
        length = jnp.where(line == row, length_ref[row], length)
    position = jnp.concatenate([length + step for step in range(steps)], axis=0)
    order = (lane % half).astype(jnp.float32)
    angle = position.astype(jnp.float32) * jnp.exp(-math.log(ROPE_BASE) * 2.0 * order / HD)
    turns = jnp.floor(angle * (1.0 / math.pi) + 0.5)
    rest = ((angle - turns * 3.140625) - turns * 9.67502593994140625e-4) - turns * 1.5099579909783e-7
    sign = 1.0 - 2.0 * (turns - 2.0 * jnp.floor(turns * 0.5))
    square = rest * rest
    cosine, sine = jnp.ones_like(rest), jnp.ones_like(rest)
    for power in range(6, 0, -1):
        cosine = 1.0 - cosine * square * (1.0 / ((2 * power - 1) * (2 * power)))
        sine = 1.0 - sine * square * (1.0 / ((2 * power) * (2 * power + 1)))
    sine = sign * rest * sine
    return sign * cosine, jnp.where(lane < half, -sine, sine)


def attend_kernel(
    count,
    late,
    block,
    length_ref,
    dest_ref,
    pick_ref,
    own_ref,
    got_ref,
    gain_ref,
    query_ref,
    kv_ref,
    *refs,
):
    moved_ref, mixed_ref, small_ref = refs[:3]
    late_refs = refs[3:-4]
    fresh, query_rows, query_columns, mixed = refs[-4:]
    part = pl.program_id(0)
    steps, rows, query_width = query_ref.shape
    capacity, lanes = kv_ref.shape[2:]
    heads = lanes // HD
    group = query_width // lanes
    per_head = steps * group
    per_row = heads * per_head
    team = HD // per_row

    @pl.when(part == 0)
    def _():
        raw = own_ref[...] + got_ref[...]
        cosine, sine = rotation(length_ref, steps, rows)
        gain = gain_ref[...].astype(jnp.float32)
        for head in range(heads):
            at = slice(head * HD, (head + 1) * HD)
            piece = raw[:, at]
            mean = jnp.mean(piece * piece, axis=-1, keepdims=True)
            piece = piece * lax.rsqrt(mean + NORM_EPS) * gain
            swapped = jnp.concatenate([piece[:, HD // 2 :], piece[:, : HD // 2]], axis=1)
            turned = piece * cosine + swapped * sine
            fresh[0, :, at] = turned.astype(jnp.bfloat16).astype(jnp.float32)
        fresh[1] = raw[:, lanes:].astype(jnp.bfloat16).astype(jnp.float32)
        for step in range(steps):
            for chunk in range(query_width // HD):
                head, member = chunk // group, chunk % group
                at = head * per_head + step * group + member
                query_rows[pl.ds(at, rows, stride=per_row), :] = query_ref[
                    step, :, chunk * HD : (chunk + 1) * HD
                ].astype(jnp.float32)
        for index in range(rows // team):
            query_columns[index] = query_rows[index * HD : (index + 1) * HD, :].T

    position = lax.broadcasted_iota(jnp.int32, (capacity, HD), 0)
    column = lax.broadcasted_iota(jnp.int32, (capacity, HD), 1)
    column_item = column // per_row
    column_step = (column % per_head) // group
    column_head = lax.broadcasted_iota(jnp.int32, (HD, HD), 1) % per_row // per_head
    factor = 1.0 / math.sqrt(HD)
    teams = range(block // team)
    scores = []
    for index in teams:
        queries = query_columns[part * (block // team) + index]
        queries = jnp.concatenate(
            [jnp.where(column_head == head, queries, 0.0) for head in range(heads)], axis=0
        ).astype(jnp.bfloat16)
        score, limit = None, None
        for member in range(team):
            item = index * team + member
            row = part * block + item
            length = length_ref[row]
            kept = position < length
            landing = [position == length + step for step in range(steps)]
            for which in range(2):
                news = [fresh[which, pl.ds(step * rows + row, 1), :] for step in range(steps)]
                for head in range(heads):
                    at = slice(head * HD, (head + 1) * HD)
                    stored = jnp.where(kept, kv_ref[item, which, :, at].astype(jnp.float32), 0.0)
                    for step in range(steps):
                        stored = jnp.where(landing[step], news[step][:, at], stored)
                    moved_ref[item, which, :, at] = stored.astype(jnp.bfloat16)
            one = jnp.dot(moved_ref[item, 0], queries, preferred_element_type=jnp.float32)
            score = one if member == 0 else jnp.where(column_item == member, one, score)
            limit = length if member == 0 else jnp.where(column_item == member, length, limit)
        scores.append(jnp.where(position <= limit + column_step, score * factor, -jnp.inf))
    weights = []
    for score in scores:
        raised = jnp.exp(score - jnp.max(score, axis=0, keepdims=True))
        normaliser = jnp.sum(raised, axis=0, keepdims=True)
        weights.append((raised / normaliser).T.astype(jnp.bfloat16))
    for index in teams:
        for member in range(team):
            item = index * team + member
            row = part * block + item
            result = jnp.dot(
                weights[index][member * per_row : (member + 1) * per_row],
                moved_ref[item, 1],
                preferred_element_type=jnp.float32,
            )
            for head in range(heads):
                at = pl.multiple_of(row * per_row + head * per_head, per_head)
                mixed[pl.ds(at, per_head), :] = result[
                    head * per_head : (head + 1) * per_head, head * HD : (head + 1) * HD
                ]

    me = lax.axis_index("inst")
    for late_ref, shift in zip(late_refs, late):
        item = pick_ref[peer_to(me, shift, count)] - part * block

        @pl.when((item >= 0) & (item < block))
        def _():
            late_ref[...] = moved_ref[item]

    @pl.when(part == pl.num_programs(0) - 1)
    def _():
        mixed_ref[...] = mixed[...].astype(jnp.bfloat16)
        for peer in range(count):
            row = pick_ref[peer]
            small_ref[peer, :per_row, :] = mixed[
                pl.ds(pl.multiple_of(row * per_row, per_row), per_row), :
            ].astype(jnp.bfloat16)
            news = []
            for which in range(2):
                for step in range(steps):
                    new = fresh[which, pl.ds(step * rows + row, 1), :]
                    news += [new[:, h * HD : (h + 1) * HD] for h in range(heads)]
            slot = dest_ref[row] - peer * rows
            slot = jnp.where((slot >= 0) & (slot < rows), slot, -1).astype(jnp.float32)
            news.append(jnp.full((1, HD), slot))
            fill = small_ref.shape[1] - per_row - 2 * steps * heads - 1
            news.append(jnp.full((fill, HD), length_ref[row].astype(jnp.float32)))
            small_ref[peer, per_row:, :] = jnp.concatenate(news, axis=0).astype(jnp.bfloat16)


def attend(kv_cache, queries, own, got, gain, lengths, destination, pick, count, late):
    steps, rows, query_width = queries.shape
    capacity, lanes = kv_cache.shape[2:]
    heads = lanes // HD
    per_row = steps * query_width // HD
    block = 8
    small_rows = per_row + -(-(2 * steps * heads + 2) // TILE) * TILE
    small = jax.ShapeDtypeStruct((count, small_rows, HD), jnp.bfloat16)
    smem = pl.BlockSpec(memory_space=pltpu.SMEM)
    vmem = pl.BlockSpec(memory_space=pltpu.VMEM)
    cache_block = pl.BlockSpec((block, 2, capacity, lanes), lambda i: (i, 0, 0, 0))
    return pl.pallas_call(
        functools.partial(attend_kernel, count, late, block),
        grid=(rows // block,),
        out_shape=[
            jax.ShapeDtypeStruct(kv_cache.shape, kv_cache.dtype),
            jax.ShapeDtypeStruct((rows * per_row, HD), jnp.bfloat16),
            small,
        ]
        + [jax.ShapeDtypeStruct(kv_cache.shape[1:], kv_cache.dtype)] * len(late),
        in_specs=[smem, smem, smem, vmem, vmem, vmem, vmem, cache_block],
        out_specs=[cache_block, vmem, vmem] + [vmem] * len(late),
        scratch_shapes=[
            pltpu.VMEM((2, steps * rows, lanes), jnp.float32),
            pltpu.VMEM((rows * per_row, HD), jnp.float32),
            pltpu.VMEM((rows * per_row // HD, HD, HD), jnp.float32),
            pltpu.VMEM((rows * per_row, HD), jnp.float32),
        ],
        compiler_params=pltpu.CompilerParams(vmem_limit_bytes=ATTEND_LIMIT),
        cost_estimate=LIGHT,
        name="attend",
    )(lengths, destination, pick, own, got, gain, queries, kv_cache)


def read_facts(block):
    capacity = block.shape[1]
    facts = block[0, capacity - TILE :, :].astype(jnp.float32)[TILE - 1 :]
    return (
        jnp.max(facts[:, :HD]).astype(jnp.int32),
        jnp.max(facts[:, HD : 2 * HD]).astype(jnp.int32),
    )


def window_start(length, capacity):
    return pl.multiple_of(jnp.minimum(length // TILE * TILE, capacity - WINDOW), TILE)


def clean(block, length, out):
    capacity, lanes = block.shape[1:]
    kept = lax.broadcasted_iota(jnp.int32, (capacity, HD), 0) < length
    for which in range(2):
        for at in range(0, lanes, HD):
            stored = block[which, :, at : at + HD].astype(jnp.float32)
            out[which, :, at : at + HD] = jnp.where(kept, stored, 0.0).astype(jnp.bfloat16)


def insert(window, news, ahead, steps, out):
    height, lanes = window.shape[1:]
    heads = lanes // HD
    position = lax.broadcasted_iota(jnp.int32, (height, lanes), 0)
    for which in range(2):
        stored = window[which].astype(jnp.float32)
        for step in range(steps):
            at = (which * steps + step) * heads
            new = jnp.concatenate([news[at + h : at + h + 1] for h in range(heads)], axis=1)
            stored = jnp.where(position == ahead + step, new, stored)
        out[which] = stored.astype(jnp.bfloat16)


def land_kernel(pieces, *refs):
    blocks = refs[:pieces]
    _, out_ref, window_ref, buffer, sems, slots = refs[pieces:]
    capacity = buffer.shape[2]

    def store(piece):
        slot = jnp.maximum(slots[piece], 0)
        return pltpu.make_async_copy(buffer.at[piece], out_ref.at[slot], sems.at[piece])

    facts = [read_facts(block) for block in blocks]
    for piece, (slot, length) in enumerate(facts):
        slots[piece] = slot

        @pl.when(slot >= 0)
        def _():
            clean(blocks[piece], length, buffer.at[piece])
            store(piece).start()
            start = window_start(length, capacity)
            window_ref[piece] = buffer[piece, :, pl.ds(start, WINDOW), :]

    for piece in range(pieces):

        @pl.when(slots[piece] >= 0)
        def _():
            store(piece).wait()


def land(got, moved):
    pieces = len(got)
    vmem = pl.BlockSpec(memory_space=pltpu.VMEM)
    hbm = pl.BlockSpec(memory_space=pl.ANY)
    return pl.pallas_call(
        functools.partial(land_kernel, pieces),
        out_shape=[
            jax.ShapeDtypeStruct(moved.shape, moved.dtype),
            jax.ShapeDtypeStruct((pieces, 2, WINDOW, moved.shape[3]), moved.dtype),
        ],
        in_specs=[vmem] * pieces + [hbm],
        out_specs=[hbm, vmem],
        scratch_shapes=[
            pltpu.VMEM((pieces,) + moved.shape[1:], moved.dtype),
            pltpu.SemaphoreType.DMA((pieces,)),
            pltpu.SMEM((pieces,), jnp.int32),
        ],
        input_output_aliases={pieces: 0},
        compiler_params=pltpu.CompilerParams(vmem_limit_bytes=SMALL_LIMIT),
        cost_estimate=HEAVY,
        name="land",
    )(*got, moved)


def read_small(small_ref, peer, per_row, line):
    rows = small_ref[peer, per_row:, :].astype(jnp.float32)
    return jnp.max(rows[line : line + 1]).astype(jnp.int32)


def settle_kernel(
    count,
    early,
    group,
    mixed_ref,
    small_ref,
    window_ref,
    _,
    out_ref,
    moved_ref,
    mixed,
    windows,
    sems,
    slots,
    lengths,
):
    steps, rows, query_width = out_ref.shape
    per_row = steps * query_width // HD
    capacity, lanes = moved_ref.shape[2:]
    line = 2 * steps * (lanes // HD)
    me = lax.axis_index("inst")

    def store(piece):
        slot = jnp.maximum(slots[early[piece]], 0)
        start = window_start(lengths[early[piece]], capacity)
        return pltpu.make_async_copy(
            windows.at[piece], moved_ref.at[slot, :, pl.ds(start, WINDOW), :], sems.at[piece]
        )

    for shift in range(1, count):
        peer = peer_from(me, shift, count)
        slots[shift] = read_small(small_ref, peer, per_row, line)
        lengths[shift] = read_small(small_ref, peer, per_row, line + 1)

    for piece, shift in enumerate(early):

        @pl.when(slots[shift] >= 0)
        def _():
            peer = peer_from(me, shift, count)
            news = small_ref[peer, per_row:, :].astype(jnp.float32)
            ahead = lengths[shift] - window_start(lengths[shift], capacity)
            insert(window_ref.at[piece], news, ahead, steps, windows.at[piece])
            store(piece).start()

    mixed[...] = mixed_ref[...].astype(jnp.float32)
    for shift in range(1, count):

        @pl.when(slots[shift] >= 0)
        def _():
            mixed[pl.ds(pl.multiple_of(slots[shift] * per_row, per_row), per_row), :] = small_ref[
                peer_from(me, shift, count), :per_row, :
            ].astype(jnp.float32)

    for step in range(steps):
        for chunk in range(query_width // HD):
            head, member = chunk // group, chunk % group
            at = head * steps * group + step * group + member
            out_ref[step, :, chunk * HD : (chunk + 1) * HD] = mixed[
                pl.ds(at, rows, stride=per_row), :
            ].astype(jnp.bfloat16)

    for piece, shift in enumerate(early):

        @pl.when(slots[shift] >= 0)
        def _():
            store(piece).wait()


def settle(mixed, small, windows, moved, shape, group, count, early):
    vmem = pl.BlockSpec(memory_space=pltpu.VMEM)
    hbm = pl.BlockSpec(memory_space=pl.ANY)
    return pl.pallas_call(
        functools.partial(settle_kernel, count, early, group),
        out_shape=[
            jax.ShapeDtypeStruct(shape, jnp.bfloat16),
            jax.ShapeDtypeStruct(moved.shape, moved.dtype),
        ],
        in_specs=[vmem, vmem, vmem, hbm],
        out_specs=[vmem, hbm],
        scratch_shapes=[
            pltpu.VMEM(mixed.shape, jnp.float32),
            pltpu.VMEM(windows.shape, windows.dtype),
            pltpu.SemaphoreType.DMA((len(early),)),
            pltpu.SMEM((count,), jnp.int32),
            pltpu.SMEM((count,), jnp.int32),
        ],
        input_output_aliases={3: 1},
        compiler_params=pltpu.CompilerParams(vmem_limit_bytes=SMALL_LIMIT),
        cost_estimate=LIGHT,
        name="settle",
    )(mixed, small, windows, moved)


def finish_kernel(count, late, steps, *refs):
    blocks = refs[: len(late)]
    small_ref, _, out_ref, sems, slots = refs[len(late) :]
    line = 2 * steps * (out_ref.shape[3] // HD)
    facts = -(-(line + 2) // TILE) * TILE
    me = lax.axis_index("inst")

    def store(piece):
        slot = jnp.maximum(slots[piece], 0)
        return pltpu.make_async_copy(blocks[piece], out_ref.at[slot], sems.at[piece])

    for piece, shift in enumerate(late):
        peer = peer_from(me, shift, count)
        slots[piece] = read_small(small_ref, peer, small_ref.shape[1] - facts, line)
    for piece in range(len(late)):
        pl.when(slots[piece] >= 0)(store(piece).start)
    for piece in range(len(late)):
        pl.when(slots[piece] >= 0)(store(piece).wait)


def finish(got, small, moved, steps, count, late):
    vmem = pl.BlockSpec(memory_space=pltpu.VMEM)
    hbm = pl.BlockSpec(memory_space=pl.ANY)
    return pl.pallas_call(
        functools.partial(finish_kernel, count, late, steps),
        out_shape=jax.ShapeDtypeStruct(moved.shape, moved.dtype),
        in_specs=[vmem] * len(got) + [vmem, hbm],
        out_specs=hbm,
        scratch_shapes=[
            pltpu.SemaphoreType.DMA((len(got),)),
            pltpu.SMEM((len(got),), jnp.int32),
        ],
        input_output_aliases={len(got) + 1: 0},
        compiler_params=pltpu.CompilerParams(vmem_limit_bytes=SMALL_LIMIT),
        cost_estimate=LIGHT,
        name="finish",
    )(*got, small, moved)


def local(hidden_new, queries, kv_cache, lengths, destination, key_weight, value_weight, key_gain):
    steps = queries.shape[0]
    group = queries.shape[2] // kv_cache.shape[3]
    count = lax.axis_size("inst")
    half = max(count // 2, 1)
    early = list(range(half, count - 1)) + [half - 1] * (half > 1)
    late = [count - 1] + list(range(half - 2, 0, -1))

    def send(block, shift):
        pairs = [(i, peer_to(i, shift, count)) for i in range(count)]
        return lax.ppermute(block, "inst", pairs)

    blocks, pick = pack(kv_cache, destination, lengths, count, early)
    early_got = [send(block, shift) for block, shift in zip(blocks, early)]
    own, other = project(hidden_new, key_weight, value_weight, pick)
    got = lax.ppermute(other, "tp", [(0, 1), (1, 0)])
    moved, mixed, small, *late_blocks = attend(
        kv_cache, queries, own, got, key_gain[None, :], lengths, destination, pick, count, late
    )
    late_got = [send(block, shift) for block, shift in zip(late_blocks, late)]
    small_got = lax.all_to_all(small, "inst", 0, 0, tiled=True)
    moved, windows = land(early_got, moved)
    attended, moved = settle(mixed, small_got, windows, moved, queries.shape, group, count, early)
    return attended, finish(late_got, small_got, moved, steps, count, late)


def solution(mesh):
    return jax.shard_map(
        local,
        mesh=mesh,
        in_specs=(
            P(None, ("group", "inst"), "tp"),
            P(None, ("group", "inst"), "tp"),
            P(("group", "inst"), None, None, "tp"),
            P(("group", "inst")),
            P(("group", "inst")),
            P("tp", None),
            P("tp", None),
            P(),
        ),
        out_specs=(P(None, ("group", "inst"), "tp"), P(("group", "inst"), None, None, "tp")),
        check_vma=False,
    )
```

```python
import functools
import math

import jax
import jax.numpy as jnp
from jax import lax
from jax.experimental import pallas as pl
from jax.experimental.pallas import tpu as pltpu
from jax.sharding import PartitionSpec as P

HD = 128
ROPE_BASE = 1000000.0
NORM_EPS = 1e-06
VMEM_LIMIT = 54 * 1024 * 1024
ATTEND_LIMIT = 50 * 1024 * 1024
SMALL_LIMIT = 40 * 1024 * 1024
LIGHT = pl.CostEstimate(flops=1, bytes_accessed=1, transcendentals=0)
HEAVY = pl.CostEstimate(flops=1 << 36, bytes_accessed=1 << 28, transcendentals=0)
TILE = 16
WINDOW = 32


def quotient(value, divisor, bound):
    factor = -(-(1 << 16) // divisor)
    if bound * factor < 1 << 31 and all(
        (x * factor) >> 16 == x // divisor for x in range(bound)
    ):
        return (value * factor) >> 16
    return value // divisor


def peer_to(index, shift, count):
    return index ^ shift if count & (count - 1) == 0 else (index + shift) % count


def peer_from(index, shift, count):
    return index ^ shift if count & (count - 1) == 0 else (index + count - shift) % count


def prepare_kernel(
    count, early, chunks, dest_ref, length_ref, hidden_ref, kv_ref, key_ref, value_ref, *refs
):
    block_refs = refs[: len(early)]
    pick_ref, own_ref, other_ref, hidden_held, held, total = refs[len(early) : len(early) + 6]
    block_sems, hidden_sem, weight_sems = refs[len(early) + 6 :]
    rows = dest_ref.shape[0]
    capacity, lanes = kv_ref.shape[2:]
    steps, _, depth = hidden_ref.shape
    width = key_ref.shape[1]
    part = depth // chunks
    me = lax.axis_index("inst")

    def weights(chunk):
        span = pl.ds(chunk * part, part)
        return [
            pltpu.make_async_copy(ref.at[span], held.at[which, span], weight_sems.at[chunk, which])
            for which, ref in enumerate((key_ref, value_ref))
        ]

    hidden_copy = pltpu.make_async_copy(hidden_ref, hidden_held, hidden_sem)
    hidden_copy.start()
    for copy in weights(0):
        copy.start()
    for peer in range(count):
        pick_ref[peer] = 0
    for row in range(rows):
        pick_ref[quotient(dest_ref[row], rows, rows * count)] = row
    fetches = []
    for piece, shift in enumerate(early):
        row = pick_ref[peer_to(me, shift, count)]
        fetches.append(
            pltpu.make_async_copy(kv_ref.at[row], block_refs[piece], block_sems.at[piece])
        )
        fetches[-1].start()
    for chunk in range(1, chunks):
        for copy in weights(chunk):
            copy.start()

    hidden_copy.wait()
    hidden = hidden_held[...].reshape(steps * rows, depth)
    sums = [None, None]
    for chunk in range(chunks):
        for which, copy in enumerate(weights(chunk)):
            copy.wait()
            product = jnp.dot(
                hidden[:, chunk * part : (chunk + 1) * part],
                held[which, chunk * part : (chunk + 1) * part, :],
                preferred_element_type=jnp.float32,
            )
            sums[which] = product if chunk == 0 else sums[which] + product
    total[:, :width] = sums[0]
    total[:, width:] = sums[1]
    half = width // 2
    core = lax.axis_index("tp")
    for ref, place in ((own_ref, core), (other_ref, 1 - core)):
        at = pl.multiple_of(place * half, half)
        ref[:, :half] = total[:, pl.ds(at, half)]
        ref[:, half:] = total[:, pl.ds(pl.multiple_of(width + at, half), half)]

    tile = (TILE, lanes)
    last = lax.broadcasted_iota(jnp.int32, tile, 0) == TILE - 1
    first_lanes = lax.broadcasted_iota(jnp.int32, tile, 1) < HD
    for piece, shift in enumerate(early):
        peer = peer_to(me, shift, count)
        row = pick_ref[peer]
        slot = dest_ref[row] - peer * rows
        slot = jnp.where((slot >= 0) & (slot < rows), slot, -1)
        facts = jnp.where(first_lanes, slot, length_ref[row]).astype(jnp.float32)
        fetches[piece].wait()
        block = block_refs[piece]
        end = block[0, capacity - TILE :, :].astype(jnp.float32)
        block[0, capacity - TILE :, :] = jnp.where(last, facts, end).astype(jnp.bfloat16)


def prepare(destination, lengths, hidden_new, kv_cache, key_weight, value_weight, count, early):
    steps, rows, depth = hidden_new.shape
    width = key_weight.shape[1]
    chunks = 5
    part = jax.ShapeDtypeStruct((steps * rows, width), jnp.float32)
    smem = pl.BlockSpec(memory_space=pltpu.SMEM)
    vmem = pl.BlockSpec(memory_space=pltpu.VMEM)
    hbm = pl.BlockSpec(memory_space=pl.ANY)
    outs = pl.pallas_call(
        functools.partial(prepare_kernel, count, early, chunks),
        out_shape=[jax.ShapeDtypeStruct(kv_cache.shape[1:], kv_cache.dtype)] * len(early)
        + [jax.ShapeDtypeStruct((count,), jnp.int32), part, part],
        in_specs=[smem, smem, hbm, hbm, hbm, hbm],
        out_specs=[vmem] * len(early) + [smem, vmem, vmem],
        scratch_shapes=[
            pltpu.VMEM(hidden_new.shape, hidden_new.dtype),
            pltpu.VMEM((2, depth, width), key_weight.dtype),
            pltpu.VMEM((steps * rows, 2 * width), jnp.float32),
            pltpu.SemaphoreType.DMA((len(early),)),
            pltpu.SemaphoreType.DMA,
            pltpu.SemaphoreType.DMA((chunks, 2)),
        ],
        compiler_params=pltpu.CompilerParams(vmem_limit_bytes=VMEM_LIMIT),
        cost_estimate=LIGHT,
        name="prepare",
    )(destination, lengths, hidden_new, kv_cache, key_weight, value_weight)
    return outs[: len(early)], *outs[len(early) :]


def rotation(length_ref, steps, rows):
    half = HD // 2
    line = lax.broadcasted_iota(jnp.int32, (rows, HD), 0)
    lane = lax.broadcasted_iota(jnp.int32, (steps * rows, HD), 1)
    length = jnp.zeros((rows, HD), jnp.int32)
    for row in range(rows):
        length = jnp.where(line == row, length_ref[row], length)
    position = jnp.concatenate([length + step for step in range(steps)], axis=0)
    order = (lane % half).astype(jnp.float32)
    angle = position.astype(jnp.float32) * jnp.exp(-math.log(ROPE_BASE) * 2.0 * order / HD)
    turns = jnp.floor(angle * (1.0 / math.pi) + 0.5)
    rest = ((angle - turns * 3.140625) - turns * 9.67502593994140625e-4) - turns * 1.5099579909783e-7
    sign = 1.0 - 2.0 * (turns - 2.0 * jnp.floor(turns * 0.5))
    square = rest * rest
    cosine, sine = jnp.ones_like(rest), jnp.ones_like(rest)
    for power in range(6, 0, -1):
        cosine = 1.0 - cosine * square * (1.0 / ((2 * power - 1) * (2 * power)))
        sine = 1.0 - sine * square * (1.0 / ((2 * power) * (2 * power + 1)))
    sine = sign * rest * sine
    return sign * cosine, jnp.where(lane < half, -sine, sine)


def attend_kernel(
    count,
    late,
    block,
    length_ref,
    dest_ref,
    pick_ref,
    own_ref,
    got_ref,
    gain_ref,
    query_ref,
    kv_ref,
    *refs,
):
    moved_ref, mixed_ref, small_ref = refs[:3]
    late_refs = refs[3:-4]
    fresh, query_rows, query_columns, mixed = refs[-4:]
    part = pl.program_id(0)
    steps, rows, query_width = query_ref.shape
    capacity, lanes = kv_ref.shape[2:]
    heads = lanes // HD
    group = query_width // lanes
    per_head = steps * group
    per_row = heads * per_head
    team = HD // per_row

    @pl.when(part == 0)
    def _():
        raw = own_ref[...] + got_ref[...]
        cosine, sine = rotation(length_ref, steps, rows)
        gain = gain_ref[...].astype(jnp.float32)
        for head in range(heads):
            at = slice(head * HD, (head + 1) * HD)
            piece = raw[:, at]
            mean = jnp.mean(piece * piece, axis=-1, keepdims=True)
            piece = piece * lax.rsqrt(mean + NORM_EPS) * gain
            swapped = jnp.concatenate([piece[:, HD // 2 :], piece[:, : HD // 2]], axis=1)
            turned = piece * cosine + swapped * sine
            fresh[0, :, at] = turned.astype(jnp.bfloat16).astype(jnp.float32)
        fresh[1] = raw[:, lanes:].astype(jnp.bfloat16).astype(jnp.float32)
        for step in range(steps):
            for chunk in range(query_width // HD):
                head, member = chunk // group, chunk % group
                at = head * per_head + step * group + member
                query_rows[pl.ds(at, rows, stride=per_row), :] = query_ref[
                    step, :, chunk * HD : (chunk + 1) * HD
                ].astype(jnp.float32)
        for index in range(rows // team):
            query_columns[index] = query_rows[index * HD : (index + 1) * HD, :].T

    position = lax.broadcasted_iota(jnp.int32, (capacity, HD), 0)
    column = lax.broadcasted_iota(jnp.int32, (capacity, HD), 1)
    column_item = column // per_row
    column_step = (column % per_head) // group
    column_head = lax.broadcasted_iota(jnp.int32, (HD, HD), 1) % per_row // per_head
    factor = 1.0 / math.sqrt(HD)
    teams = range(block // team)
    scores = []
    for index in teams:
        queries = query_columns[part * (block // team) + index]
        queries = jnp.concatenate(
            [jnp.where(column_head == head, queries, 0.0) for head in range(heads)], axis=0
        ).astype(jnp.bfloat16)
        score, limit = None, None
        for member in range(team):
            item = index * team + member
            row = part * block + item
            length = length_ref[row]
            kept = position < length
            landing = [position == length + step for step in range(steps)]
            for which in range(2):
                news = [fresh[which, pl.ds(step * rows + row, 1), :] for step in range(steps)]
                for head in range(heads):
                    at = slice(head * HD, (head + 1) * HD)
                    stored = jnp.where(kept, kv_ref[item, which, :, at].astype(jnp.float32), 0.0)
                    for step in range(steps):
                        stored = jnp.where(landing[step], news[step][:, at], stored)
                    moved_ref[item, which, :, at] = stored.astype(jnp.bfloat16)
            one = jnp.dot(moved_ref[item, 0], queries, preferred_element_type=jnp.float32)
            score = one if member == 0 else jnp.where(column_item == member, one, score)
            limit = length if member == 0 else jnp.where(column_item == member, length, limit)
        scores.append(jnp.where(position <= limit + column_step, score * factor, -jnp.inf))
    weights = []
    for score in scores:
        raised = jnp.exp(score - jnp.max(score, axis=0, keepdims=True))
        normaliser = jnp.sum(raised, axis=0, keepdims=True)
        weights.append((raised / normaliser).T.astype(jnp.bfloat16))
    for index in teams:
        for member in range(team):
            item = index * team + member
            row = part * block + item
            result = jnp.dot(
                weights[index][member * per_row : (member + 1) * per_row],
                moved_ref[item, 1],
                preferred_element_type=jnp.float32,
            )
            for head in range(heads):
                at = pl.multiple_of(row * per_row + head * per_head, per_head)
                mixed[pl.ds(at, per_head), :] = result[
                    head * per_head : (head + 1) * per_head, head * HD : (head + 1) * HD
                ]

    me = lax.axis_index("inst")
    for late_ref, shift in zip(late_refs, late):
        item = pick_ref[peer_to(me, shift, count)] - part * block

        @pl.when((item >= 0) & (item < block))
        def _():
            late_ref[...] = moved_ref[item]

    @pl.when(part == pl.num_programs(0) - 1)
    def _():
        mixed_ref[...] = mixed[...].astype(jnp.bfloat16)
        for peer in range(count):
            row = pick_ref[peer]
            small_ref[peer, :per_row, :] = mixed[
                pl.ds(pl.multiple_of(row * per_row, per_row), per_row), :
            ].astype(jnp.bfloat16)
            news = []
            for which in range(2):
                for step in range(steps):
                    new = fresh[which, pl.ds(step * rows + row, 1), :]
                    news += [new[:, h * HD : (h + 1) * HD] for h in range(heads)]
            slot = dest_ref[row] - peer * rows
            slot = jnp.where((slot >= 0) & (slot < rows), slot, -1).astype(jnp.float32)
            news.append(jnp.full((1, HD), slot))
            fill = small_ref.shape[1] - per_row - 2 * steps * heads - 1
            news.append(jnp.full((fill, HD), length_ref[row].astype(jnp.float32)))
            small_ref[peer, per_row:, :] = jnp.concatenate(news, axis=0).astype(jnp.bfloat16)


def attend(kv_cache, queries, own, got, gain, lengths, destination, pick, count, late):
    steps, rows, query_width = queries.shape
    capacity, lanes = kv_cache.shape[2:]
    heads = lanes // HD
    per_row = steps * query_width // HD
    block = 8
    small_rows = per_row + -(-(2 * steps * heads + 2) // TILE) * TILE
    small = jax.ShapeDtypeStruct((count, small_rows, HD), jnp.bfloat16)
    smem = pl.BlockSpec(memory_space=pltpu.SMEM)
    vmem = pl.BlockSpec(memory_space=pltpu.VMEM)
    cache_block = pl.BlockSpec((block, 2, capacity, lanes), lambda i: (i, 0, 0, 0))
    return pl.pallas_call(
        functools.partial(attend_kernel, count, late, block),
        grid=(rows // block,),
        out_shape=[
            jax.ShapeDtypeStruct(kv_cache.shape, kv_cache.dtype),
            jax.ShapeDtypeStruct((rows * per_row, HD), jnp.bfloat16),
            small,
        ]
        + [jax.ShapeDtypeStruct(kv_cache.shape[1:], kv_cache.dtype)] * len(late),
        in_specs=[smem, smem, smem, vmem, vmem, vmem, vmem, cache_block],
        out_specs=[cache_block, vmem, vmem] + [vmem] * len(late),
        scratch_shapes=[
            pltpu.VMEM((2, steps * rows, lanes), jnp.float32),
            pltpu.VMEM((rows * per_row, HD), jnp.float32),
            pltpu.VMEM((rows * per_row // HD, HD, HD), jnp.float32),
            pltpu.VMEM((rows * per_row, HD), jnp.float32),
        ],
        compiler_params=pltpu.CompilerParams(vmem_limit_bytes=ATTEND_LIMIT),
        cost_estimate=HEAVY,
        name="attend",
    )(lengths, destination, pick, own, got, gain, queries, kv_cache)


def read_facts(block):
    capacity = block.shape[1]
    facts = block[0, capacity - TILE :, :].astype(jnp.float32)[TILE - 1 :]
    return (
        jnp.max(facts[:, :HD]).astype(jnp.int32),
        jnp.max(facts[:, HD : 2 * HD]).astype(jnp.int32),
    )


def window_start(length, capacity):
    return pl.multiple_of(jnp.minimum(length // TILE * TILE, capacity - WINDOW), TILE)


def clean(block, length, out):
    capacity, lanes = block.shape[1:]
    kept = lax.broadcasted_iota(jnp.int32, (capacity, HD), 0) < length
    for which in range(2):
        for at in range(0, lanes, HD):
            stored = block[which, :, at : at + HD].astype(jnp.float32)
            out[which, :, at : at + HD] = jnp.where(kept, stored, 0.0).astype(jnp.bfloat16)


def insert(window, news, ahead, steps, out):
    height, lanes = window.shape[1:]
    heads = lanes // HD
    position = lax.broadcasted_iota(jnp.int32, (height, lanes), 0)
    for which in range(2):
        stored = window[which].astype(jnp.float32)
        for step in range(steps):
            at = (which * steps + step) * heads
            new = jnp.concatenate([news[at + h : at + h + 1] for h in range(heads)], axis=1)
            stored = jnp.where(position == ahead + step, new, stored)
        out[which] = stored.astype(jnp.bfloat16)


def land_kernel(pieces, *refs):
    blocks = refs[:pieces]
    _, out_ref, window_ref, buffer, sems, slots = refs[pieces:]
    capacity = buffer.shape[2]

    def store(piece):
        slot = jnp.maximum(slots[piece], 0)
        return pltpu.make_async_copy(buffer.at[piece], out_ref.at[slot], sems.at[piece])

    facts = [read_facts(block) for block in blocks]
    for piece, (slot, length) in enumerate(facts):
        slots[piece] = slot

        @pl.when(slot >= 0)
        def _():
            clean(blocks[piece], length, buffer.at[piece])
            store(piece).start()
            start = window_start(length, capacity)
            window_ref[piece] = buffer[piece, :, pl.ds(start, WINDOW), :]

    for piece in range(pieces):

        @pl.when(slots[piece] >= 0)
        def _():
            store(piece).wait()


def land(got, moved):
    pieces = len(got)
    vmem = pl.BlockSpec(memory_space=pltpu.VMEM)
    hbm = pl.BlockSpec(memory_space=pl.ANY)
    return pl.pallas_call(
        functools.partial(land_kernel, pieces),
        out_shape=[
            jax.ShapeDtypeStruct(moved.shape, moved.dtype),
            jax.ShapeDtypeStruct((pieces, 2, WINDOW, moved.shape[3]), moved.dtype),
        ],
        in_specs=[vmem] * pieces + [hbm],
        out_specs=[hbm, vmem],
        scratch_shapes=[
            pltpu.VMEM((pieces,) + moved.shape[1:], moved.dtype),
            pltpu.SemaphoreType.DMA((pieces,)),
            pltpu.SMEM((pieces,), jnp.int32),
        ],
        input_output_aliases={pieces: 0},
        compiler_params=pltpu.CompilerParams(vmem_limit_bytes=SMALL_LIMIT),
        cost_estimate=HEAVY,
        name="land",
    )(*got, moved)


def read_small(small_ref, peer, per_row, line):
    rows = small_ref[peer, per_row:, :].astype(jnp.float32)
    return jnp.max(rows[line : line + 1]).astype(jnp.int32)


def settle_kernel(
    count,
    early,
    group,
    mixed_ref,
    small_ref,
    window_ref,
    _,
    out_ref,
    moved_ref,
    mixed,
    windows,
    sems,
    slots,
    lengths,
):
    steps, rows, query_width = out_ref.shape
    per_row = steps * query_width // HD
    capacity, lanes = moved_ref.shape[2:]
    line = 2 * steps * (lanes // HD)
    me = lax.axis_index("inst")

    def store(piece):
        slot = jnp.maximum(slots[early[piece]], 0)
        start = window_start(lengths[early[piece]], capacity)
        return pltpu.make_async_copy(
            windows.at[piece], moved_ref.at[slot, :, pl.ds(start, WINDOW), :], sems.at[piece]
        )

    for shift in range(1, count):
        peer = peer_from(me, shift, count)
        slots[shift] = read_small(small_ref, peer, per_row, line)
        lengths[shift] = read_small(small_ref, peer, per_row, line + 1)

    for piece, shift in enumerate(early):

        @pl.when(slots[shift] >= 0)
        def _():
            peer = peer_from(me, shift, count)
            news = small_ref[peer, per_row:, :].astype(jnp.float32)
            ahead = lengths[shift] - window_start(lengths[shift], capacity)
            insert(window_ref.at[piece], news, ahead, steps, windows.at[piece])
            store(piece).start()

    mixed[...] = mixed_ref[...].astype(jnp.float32)
    for shift in range(1, count):

        @pl.when(slots[shift] >= 0)
        def _():
            mixed[pl.ds(pl.multiple_of(slots[shift] * per_row, per_row), per_row), :] = small_ref[
                peer_from(me, shift, count), :per_row, :
            ].astype(jnp.float32)

    for step in range(steps):
        for chunk in range(query_width // HD):
            head, member = chunk // group, chunk % group
            at = head * steps * group + step * group + member
            out_ref[step, :, chunk * HD : (chunk + 1) * HD] = mixed[
                pl.ds(at, rows, stride=per_row), :
            ].astype(jnp.bfloat16)

    for piece, shift in enumerate(early):

        @pl.when(slots[shift] >= 0)
        def _():
            store(piece).wait()


def settle(mixed, small, windows, moved, shape, group, count, early):
    vmem = pl.BlockSpec(memory_space=pltpu.VMEM)
    hbm = pl.BlockSpec(memory_space=pl.ANY)
    return pl.pallas_call(
        functools.partial(settle_kernel, count, early, group),
        out_shape=[
            jax.ShapeDtypeStruct(shape, jnp.bfloat16),
            jax.ShapeDtypeStruct(moved.shape, moved.dtype),
        ],
        in_specs=[vmem, vmem, vmem, hbm],
        out_specs=[vmem, hbm],
        scratch_shapes=[
            pltpu.VMEM(mixed.shape, jnp.float32),
            pltpu.VMEM(windows.shape, windows.dtype),
            pltpu.SemaphoreType.DMA((len(early),)),
            pltpu.SMEM((count,), jnp.int32),
            pltpu.SMEM((count,), jnp.int32),
        ],
        input_output_aliases={3: 1},
        compiler_params=pltpu.CompilerParams(vmem_limit_bytes=SMALL_LIMIT),
        cost_estimate=LIGHT,
        name="settle",
    )(mixed, small, windows, moved)


def finish_kernel(count, late, steps, *refs):
    blocks = refs[: len(late)]
    small_ref, _, out_ref, sems, slots = refs[len(late) :]
    line = 2 * steps * (out_ref.shape[3] // HD)
    facts = -(-(line + 2) // TILE) * TILE
    me = lax.axis_index("inst")

    def store(piece):
        slot = jnp.maximum(slots[piece], 0)
        return pltpu.make_async_copy(blocks[piece], out_ref.at[slot], sems.at[piece])

    for piece, shift in enumerate(late):
        peer = peer_from(me, shift, count)
        slots[piece] = read_small(small_ref, peer, small_ref.shape[1] - facts, line)
    for piece in range(len(late)):
        pl.when(slots[piece] >= 0)(store(piece).start)
    for piece in range(len(late)):
        pl.when(slots[piece] >= 0)(store(piece).wait)


def finish(got, small, moved, steps, count, late):
    vmem = pl.BlockSpec(memory_space=pltpu.VMEM)
    hbm = pl.BlockSpec(memory_space=pl.ANY)
    return pl.pallas_call(
        functools.partial(finish_kernel, count, late, steps),
        out_shape=jax.ShapeDtypeStruct(moved.shape, moved.dtype),
        in_specs=[vmem] * len(got) + [vmem, hbm],
        out_specs=hbm,
        scratch_shapes=[
            pltpu.SemaphoreType.DMA((len(got),)),
            pltpu.SMEM((len(got),), jnp.int32),
        ],
        input_output_aliases={len(got) + 1: 0},
        compiler_params=pltpu.CompilerParams(vmem_limit_bytes=SMALL_LIMIT),
        cost_estimate=LIGHT,
        name="finish",
    )(*got, small, moved)


def local(hidden_new, queries, kv_cache, lengths, destination, key_weight, value_weight, key_gain):
    steps = queries.shape[0]
    group = queries.shape[2] // kv_cache.shape[3]
    count = lax.axis_size("inst")
    half = max(count // 2, 1)
    early = list(range(half, count - 1)) + [half - 1] * (half > 1)
    late = [count - 1] + list(range(half - 2, 0, -1))

    def send(block, shift):
        pairs = [(i, peer_to(i, shift, count)) for i in range(count)]
        return lax.ppermute(block, "inst", pairs)

    blocks, pick, own, other = prepare(
        destination, lengths, hidden_new, kv_cache, key_weight, value_weight, count, early
    )
    early_got = [send(block, shift) for block, shift in zip(blocks, early)]
    got = lax.ppermute(other, "tp", [(0, 1), (1, 0)])
    moved, mixed, small, *late_blocks = attend(
        kv_cache, queries, own, got, key_gain[None, :], lengths, destination, pick, count, late
    )
    late_got = [send(block, shift) for block, shift in zip(late_blocks, late)]
    small_got = lax.all_to_all(small, "inst", 0, 0, tiled=True)
    moved, windows = land(early_got, moved)
    attended, moved = settle(mixed, small_got, windows, moved, queries.shape, group, count, early)
    return attended, finish(late_got, small_got, moved, steps, count, late)


def solution(mesh):
    return jax.shard_map(
        local,
        mesh=mesh,
        in_specs=(
            P(None, ("group", "inst"), "tp"),
            P(None, ("group", "inst"), "tp"),
            P(("group", "inst"), None, None, "tp"),
            P(("group", "inst")),
            P(("group", "inst")),
            P("tp", None),
            P("tp", None),
            P(),
        ),
        out_specs=(P(None, ("group", "inst"), "tp"), P(("group", "inst"), None, None, "tp")),
        check_vma=False,
    )
```

```python
import functools
import math

import jax
import jax.numpy as jnp
from jax import lax
from jax.experimental import pallas as pl
from jax.experimental.pallas import tpu as pltpu
from jax.sharding import PartitionSpec as P

HD = 128
ROPE_BASE = 1000000.0
NORM_EPS = 1e-06
VMEM_LIMIT = 62 * 1024 * 1024
ATTEND_LIMIT = 56 * 1024 * 1024
SMALL_LIMIT = 40 * 1024 * 1024
LIGHT = pl.CostEstimate(flops=1, bytes_accessed=1, transcendentals=0)
HEAVY = pl.CostEstimate(flops=1 << 36, bytes_accessed=1 << 28, transcendentals=0)
TILE = 16
WINDOW = 32


def quotient(value, divisor, bound):
    factor = -(-(1 << 16) // divisor)
    if bound * factor < 1 << 31 and all(
        (x * factor) >> 16 == x // divisor for x in range(bound)
    ):
        return (value * factor) >> 16
    return value // divisor


def peer_to(index, shift, count):
    return index ^ shift if count & (count - 1) == 0 else (index + shift) % count


def peer_from(index, shift, count):
    return index ^ shift if count & (count - 1) == 0 else (index + count - shift) % count


def pick_rows(count, dest_ref, pick_ref):
    rows = dest_ref.shape[0]
    for peer in range(count):
        pick_ref[peer] = 0
    for row in range(rows):
        pick_ref[quotient(dest_ref[row], rows, rows * count)] = row


def add_facts(block, peer, row, dest_ref, length_ref):
    capacity, lanes = block.shape[1:]
    rows = dest_ref.shape[0]
    slot = dest_ref[row] - peer * rows
    slot = jnp.where((slot >= 0) & (slot < rows), slot, -1)
    last = lax.broadcasted_iota(jnp.int32, (TILE, lanes), 0) == TILE - 1
    first_lanes = lax.broadcasted_iota(jnp.int32, (TILE, lanes), 1) < HD
    facts = jnp.where(first_lanes, slot, length_ref[row]).astype(jnp.float32)
    end = block[0, capacity - TILE :, :].astype(jnp.float32)
    block[0, capacity - TILE :, :] = jnp.where(last, facts, end).astype(jnp.bfloat16)


def pack_kernel(count, shift, dest_ref, length_ref, kv_ref, block_ref, block, sem, pick):
    pick_rows(count, dest_ref, pick)
    peer = peer_to(lax.axis_index("inst"), shift, count)
    row = pick[peer]
    fetch = pltpu.make_async_copy(kv_ref.at[row], block, sem)
    fetch.start()
    fetch.wait()
    add_facts(block, peer, row, dest_ref, length_ref)
    store = pltpu.make_async_copy(block, block_ref, sem)
    store.start()
    store.wait()


def pack(kv_cache, destination, lengths, count, shift):
    smem = pl.BlockSpec(memory_space=pltpu.SMEM)
    hbm = pl.BlockSpec(memory_space=pl.ANY)
    return pl.pallas_call(
        functools.partial(pack_kernel, count, shift),
        out_shape=jax.ShapeDtypeStruct(kv_cache.shape[1:], kv_cache.dtype),
        in_specs=[smem, smem, hbm],
        out_specs=hbm,
        scratch_shapes=[
            pltpu.VMEM(kv_cache.shape[1:], kv_cache.dtype),
            pltpu.SemaphoreType.DMA,
            pltpu.SMEM((count,), jnp.int32),
        ],
        compiler_params=pltpu.CompilerParams(vmem_limit_bytes=VMEM_LIMIT),
        cost_estimate=LIGHT,
        name="pack",
    )(destination, lengths, kv_cache)


def prepare_kernel(
    count, early, chunks, dest_ref, length_ref, hidden_ref, kv_ref, key_ref, value_ref, *refs
):
    block_refs = refs[1 : len(early) + 1]
    pick_ref, own_ref, other_ref, blocks, hidden_held, held, total = refs[
        len(early) + 1 : len(early) + 8
    ]
    in_sems, out_sems, hidden_sem, weight_sems = refs[len(early) + 8 :]
    steps, rows, depth = hidden_ref.shape
    width = key_ref.shape[1]
    part = depth // chunks
    me = lax.axis_index("inst")

    def weights(chunk):
        span = pl.ds(chunk * part, part)
        return [
            pltpu.make_async_copy(ref.at[span], held.at[which, span], weight_sems.at[chunk, which])
            for which, ref in enumerate((key_ref, value_ref))
        ]

    hidden_copy = pltpu.make_async_copy(hidden_ref, hidden_held, hidden_sem)
    hidden_copy.start()
    for copy in weights(0):
        copy.start()
    pick_rows(count, dest_ref, pick_ref)
    fetches, stores = [], []
    for piece, shift in enumerate(early):
        row = pick_ref[peer_to(me, shift, count)]
        fetches.append(
            pltpu.make_async_copy(kv_ref.at[row], blocks.at[piece], in_sems.at[piece])
        )
        fetches[-1].start()
    for chunk in range(1, chunks):
        for copy in weights(chunk):
            copy.start()

    for piece, shift in enumerate(early):
        peer = peer_to(me, shift, count)
        fetches[piece].wait()
        add_facts(blocks.at[piece], peer, pick_ref[peer], dest_ref, length_ref)
        stores.append(
            pltpu.make_async_copy(blocks.at[piece], block_refs[piece], out_sems.at[piece])
        )
        stores[-1].start()
    hidden_copy.wait()
    hidden = hidden_held[...].reshape(steps * rows, depth)
    sums = [None, None]
    for chunk in range(chunks):
        for which, copy in enumerate(weights(chunk)):
            copy.wait()
            product = jnp.dot(
                hidden[:, chunk * part : (chunk + 1) * part],
                held[which, chunk * part : (chunk + 1) * part, :],
                preferred_element_type=jnp.float32,
            )
            sums[which] = product if chunk == 0 else sums[which] + product
    total[:, :width] = sums[0]
    total[:, width:] = sums[1]
    half = width // 2
    core = lax.axis_index("tp")
    for ref, place in ((own_ref, core), (other_ref, 1 - core)):
        at = pl.multiple_of(place * half, half)
        ref[:, :half] = total[:, pl.ds(at, half)]
        ref[:, half:] = total[:, pl.ds(pl.multiple_of(width + at, half), half)]

    for copy in stores:
        copy.wait()


def prepare(destination, lengths, hidden_new, kv_cache, key_weight, value_weight, count, early, first):
    steps, rows, depth = hidden_new.shape
    width = key_weight.shape[1]
    chunks = 5
    part = jax.ShapeDtypeStruct((steps * rows, width), jnp.float32)
    smem = pl.BlockSpec(memory_space=pltpu.SMEM)
    vmem = pl.BlockSpec(memory_space=pltpu.VMEM)
    hbm = pl.BlockSpec(memory_space=pl.ANY)
    outs = pl.pallas_call(
        functools.partial(prepare_kernel, count, early, chunks),
        out_shape=[jax.ShapeDtypeStruct(kv_cache.shape[1:], kv_cache.dtype)] * len(early)
        + [jax.ShapeDtypeStruct((count,), jnp.int32), part, part],
        in_specs=[smem, smem, hbm, hbm, hbm, hbm, hbm],
        out_specs=[hbm] * len(early) + [smem, vmem, vmem],
        scratch_shapes=[
            pltpu.VMEM((len(early),) + kv_cache.shape[1:], kv_cache.dtype),
            pltpu.VMEM(hidden_new.shape, hidden_new.dtype),
            pltpu.VMEM((2, depth, width), key_weight.dtype),
            pltpu.VMEM((steps * rows, 2 * width), jnp.float32),
            pltpu.SemaphoreType.DMA((len(early),)),
            pltpu.SemaphoreType.DMA((len(early),)),
            pltpu.SemaphoreType.DMA,
            pltpu.SemaphoreType.DMA((chunks, 2)),
        ],
        compiler_params=pltpu.CompilerParams(vmem_limit_bytes=VMEM_LIMIT),
        cost_estimate=LIGHT,
        name="prepare",
    )(destination, lengths, hidden_new, kv_cache, key_weight, value_weight, first)
    return outs[: len(early)], *outs[len(early) :]


def rotation(length_ref, steps, rows):
    half = HD // 2
    line = lax.broadcasted_iota(jnp.int32, (rows, HD), 0)
    lane = lax.broadcasted_iota(jnp.int32, (steps * rows, HD), 1)
    length = jnp.zeros((rows, HD), jnp.int32)
    for row in range(rows):
        length = jnp.where(line == row, length_ref[row], length)
    position = jnp.concatenate([length + step for step in range(steps)], axis=0)
    order = (lane % half).astype(jnp.float32)
    angle = position.astype(jnp.float32) * jnp.exp(-math.log(ROPE_BASE) * 2.0 * order / HD)
    turns = jnp.floor(angle * (1.0 / math.pi) + 0.5)
    rest = ((angle - turns * 3.140625) - turns * 9.67502593994140625e-4) - turns * 1.5099579909783e-7
    sign = 1.0 - 2.0 * (turns - 2.0 * jnp.floor(turns * 0.5))
    square = rest * rest
    cosine, sine = jnp.ones_like(rest), jnp.ones_like(rest)
    for power in range(6, 0, -1):
        cosine = 1.0 - cosine * square * (1.0 / ((2 * power - 1) * (2 * power)))
        sine = 1.0 - sine * square * (1.0 / ((2 * power) * (2 * power + 1)))
    sine = sign * rest * sine
    return sign * cosine, jnp.where(lane < half, -sine, sine)


def attend_kernel(
    count,
    late,
    block,
    length_ref,
    dest_ref,
    pick_ref,
    own_ref,
    got_ref,
    gain_ref,
    query_ref,
    kv_ref,
    *refs,
):
    moved_ref, mixed_ref, small_ref = refs[1:4]
    late_refs = refs[4:-4]
    fresh, query_rows, query_columns, mixed = refs[-4:]
    part = pl.program_id(0)
    steps, rows, query_width = query_ref.shape
    capacity, lanes = kv_ref.shape[2:]
    heads = lanes // HD
    group = query_width // lanes
    per_head = steps * group
    per_row = heads * per_head
    team = HD // per_row

    @pl.when(part == 0)
    def _():
        raw = own_ref[...] + got_ref[...]
        cosine, sine = rotation(length_ref, steps, rows)
        gain = gain_ref[...].astype(jnp.float32)
        for head in range(heads):
            at = slice(head * HD, (head + 1) * HD)
            piece = raw[:, at]
            mean = jnp.mean(piece * piece, axis=-1, keepdims=True)
            piece = piece * lax.rsqrt(mean + NORM_EPS) * gain
            swapped = jnp.concatenate([piece[:, HD // 2 :], piece[:, : HD // 2]], axis=1)
            turned = piece * cosine + swapped * sine
            fresh[0, :, at] = turned.astype(jnp.bfloat16).astype(jnp.float32)
        fresh[1] = raw[:, lanes:].astype(jnp.bfloat16).astype(jnp.float32)
        for step in range(steps):
            for chunk in range(query_width // HD):
                head, member = chunk // group, chunk % group
                at = head * per_head + step * group + member
                query_rows[pl.ds(at, rows, stride=per_row), :] = query_ref[
                    step, :, chunk * HD : (chunk + 1) * HD
                ].astype(jnp.float32)
        for index in range(rows // team):
            query_columns[index] = query_rows[index * HD : (index + 1) * HD, :].T

    position = lax.broadcasted_iota(jnp.int32, (capacity, HD), 0)
    column = lax.broadcasted_iota(jnp.int32, (capacity, HD), 1)
    column_item = column // per_row
    column_step = (column % per_head) // group
    column_head = lax.broadcasted_iota(jnp.int32, (HD, HD), 1) % per_row // per_head
    factor = 1.0 / math.sqrt(HD)
    teams = range(block // team)
    scores = []
    for index in teams:
        queries = query_columns[part * (block // team) + index]
        queries = jnp.concatenate(
            [jnp.where(column_head == head, queries, 0.0) for head in range(heads)], axis=0
        ).astype(jnp.bfloat16)
        score, limit = None, None
        for member in range(team):
            item = index * team + member
            row = part * block + item
            length = length_ref[row]
            kept = position < length
            landing = [position == length + step for step in range(steps)]
            for which in range(2):
                news = [fresh[which, pl.ds(step * rows + row, 1), :] for step in range(steps)]
                for head in range(heads):
                    at = slice(head * HD, (head + 1) * HD)
                    stored = jnp.where(kept, kv_ref[item, which, :, at].astype(jnp.float32), 0.0)
                    for step in range(steps):
                        stored = jnp.where(landing[step], news[step][:, at], stored)
                    moved_ref[item, which, :, at] = stored.astype(jnp.bfloat16)
            one = jnp.dot(moved_ref[item, 0], queries, preferred_element_type=jnp.float32)
            score = one if member == 0 else jnp.where(column_item == member, one, score)
            limit = length if member == 0 else jnp.where(column_item == member, length, limit)
        scores.append(jnp.where(position <= limit + column_step, score * factor, -jnp.inf))
    weights = []
    for score in scores:
        raised = jnp.exp(score - jnp.max(score, axis=0, keepdims=True))
        normaliser = jnp.sum(raised, axis=0, keepdims=True)
        weights.append((raised / normaliser).T.astype(jnp.bfloat16))
    for index in teams:
        for member in range(team):
            item = index * team + member
            row = part * block + item
            result = jnp.dot(
                weights[index][member * per_row : (member + 1) * per_row],
                moved_ref[item, 1],
                preferred_element_type=jnp.float32,
            )
            for head in range(heads):
                at = pl.multiple_of(row * per_row + head * per_head, per_head)
                mixed[pl.ds(at, per_head), :] = result[
                    head * per_head : (head + 1) * per_head, head * HD : (head + 1) * HD
                ]

    me = lax.axis_index("inst")
    for late_ref, shift in zip(late_refs, late):
        item = pick_ref[peer_to(me, shift, count)] - part * block

        @pl.when((item >= 0) & (item < block))
        def _():
            late_ref[...] = moved_ref[item]

    @pl.when(part == pl.num_programs(0) - 1)
    def _():
        mixed_ref[...] = mixed[...].astype(jnp.bfloat16)
        for peer in range(count):
            row = pick_ref[peer]
            small_ref[peer, :per_row, :] = mixed[
                pl.ds(pl.multiple_of(row * per_row, per_row), per_row), :
            ].astype(jnp.bfloat16)
            news = []
            for which in range(2):
                for step in range(steps):
                    new = fresh[which, pl.ds(step * rows + row, 1), :]
                    news += [new[:, h * HD : (h + 1) * HD] for h in range(heads)]
            slot = dest_ref[row] - peer * rows
            slot = jnp.where((slot >= 0) & (slot < rows), slot, -1).astype(jnp.float32)
            news.append(jnp.full((1, HD), slot))
            fill = small_ref.shape[1] - per_row - 2 * steps * heads - 1
            news.append(jnp.full((fill, HD), length_ref[row].astype(jnp.float32)))
            small_ref[peer, per_row:, :] = jnp.concatenate(news, axis=0).astype(jnp.bfloat16)


def attend(kv_cache, queries, own, got, gain, lengths, destination, pick, count, late, arrived):
    steps, rows, query_width = queries.shape
    capacity, lanes = kv_cache.shape[2:]
    heads = lanes // HD
    per_row = steps * query_width // HD
    block = 8
    small_rows = per_row + -(-(2 * steps * heads + 2) // TILE) * TILE
    small = jax.ShapeDtypeStruct((count, small_rows, HD), jnp.bfloat16)
    smem = pl.BlockSpec(memory_space=pltpu.SMEM)
    vmem = pl.BlockSpec(memory_space=pltpu.VMEM)
    hbm = pl.BlockSpec(memory_space=pl.ANY)
    cache_block = pl.BlockSpec((block, 2, capacity, lanes), lambda i: (i, 0, 0, 0))
    return pl.pallas_call(
        functools.partial(attend_kernel, count, late, block),
        grid=(rows // block,),
        out_shape=[
            jax.ShapeDtypeStruct(kv_cache.shape, kv_cache.dtype),
            jax.ShapeDtypeStruct((rows * per_row, HD), jnp.bfloat16),
            small,
        ]
        + [jax.ShapeDtypeStruct(kv_cache.shape[1:], kv_cache.dtype)] * len(late),
        in_specs=[smem, smem, smem, vmem, vmem, vmem, vmem, cache_block, hbm],
        out_specs=[cache_block, vmem, vmem] + [vmem] * len(late),
        scratch_shapes=[
            pltpu.VMEM((2, steps * rows, lanes), jnp.float32),
            pltpu.VMEM((rows * per_row, HD), jnp.float32),
            pltpu.VMEM((rows * per_row // HD, HD, HD), jnp.float32),
            pltpu.VMEM((rows * per_row, HD), jnp.float32),
        ],
        compiler_params=pltpu.CompilerParams(vmem_limit_bytes=ATTEND_LIMIT),
        cost_estimate=HEAVY,
        name="attend",
    )(lengths, destination, pick, own, got, gain, queries, kv_cache, arrived)


def read_facts(block):
    capacity = block.shape[1]
    facts = block[0, capacity - TILE :, :].astype(jnp.float32)[TILE - 1 :]
    return (
        jnp.max(facts[:, :HD]).astype(jnp.int32),
        jnp.max(facts[:, HD : 2 * HD]).astype(jnp.int32),
    )


def window_start(length, capacity):
    return pl.multiple_of(jnp.minimum(length // TILE * TILE, capacity - WINDOW), TILE)


def clean(block, length, out):
    capacity, lanes = block.shape[1:]
    kept = lax.broadcasted_iota(jnp.int32, (capacity, HD), 0) < length
    for which in range(2):
        for at in range(0, lanes, HD):
            stored = block[which, :, at : at + HD].astype(jnp.float32)
            out[which, :, at : at + HD] = jnp.where(kept, stored, 0.0).astype(jnp.bfloat16)


def insert(window, news, ahead, steps, out):
    height, lanes = window.shape[1:]
    heads = lanes // HD
    position = lax.broadcasted_iota(jnp.int32, (height, lanes), 0)
    for which in range(2):
        stored = window[which].astype(jnp.float32)
        for step in range(steps):
            at = (which * steps + step) * heads
            new = jnp.concatenate([news[at + h : at + h + 1] for h in range(heads)], axis=1)
            stored = jnp.where(position == ahead + step, new, stored)
        out[which] = stored.astype(jnp.bfloat16)


def land_kernel(pieces, *refs):
    blocks = refs[:pieces]
    _, out_ref, window_ref, buffer, sems, slots = refs[pieces:]
    capacity = buffer.shape[2]

    def store(piece):
        slot = jnp.maximum(slots[piece], 0)
        return pltpu.make_async_copy(buffer.at[piece], out_ref.at[slot], sems.at[piece])

    facts = [read_facts(block) for block in blocks]
    for piece, (slot, length) in enumerate(facts):
        slots[piece] = slot

        @pl.when(slot >= 0)
        def _():
            clean(blocks[piece], length, buffer.at[piece])
            store(piece).start()
            start = window_start(length, capacity)
            window_ref[piece] = buffer[piece, :, pl.ds(start, WINDOW), :]

    for piece in range(pieces):

        @pl.when(slots[piece] >= 0)
        def _():
            store(piece).wait()


def land(got, moved):
    pieces = len(got)
    vmem = pl.BlockSpec(memory_space=pltpu.VMEM)
    hbm = pl.BlockSpec(memory_space=pl.ANY)
    return pl.pallas_call(
        functools.partial(land_kernel, pieces),
        out_shape=[
            jax.ShapeDtypeStruct(moved.shape, moved.dtype),
            jax.ShapeDtypeStruct((pieces, 2, WINDOW, moved.shape[3]), moved.dtype),
        ],
        in_specs=[vmem] * pieces + [hbm],
        out_specs=[hbm, vmem],
        scratch_shapes=[
            pltpu.VMEM((pieces,) + moved.shape[1:], moved.dtype),
            pltpu.SemaphoreType.DMA((pieces,)),
            pltpu.SMEM((pieces,), jnp.int32),
        ],
        input_output_aliases={pieces: 0},
        compiler_params=pltpu.CompilerParams(vmem_limit_bytes=SMALL_LIMIT),
        cost_estimate=HEAVY,
        name="land",
    )(*got, moved)


def read_small(small_ref, peer, per_row, line):
    rows = small_ref[peer, per_row:, :].astype(jnp.float32)
    return jnp.max(rows[line : line + 1]).astype(jnp.int32)


def settle_kernel(
    count,
    early,
    group,
    mixed_ref,
    small_ref,
    window_ref,
    _,
    out_ref,
    moved_ref,
    mixed,
    windows,
    sems,
    slots,
    lengths,
):
    steps, rows, query_width = out_ref.shape
    per_row = steps * query_width // HD
    capacity, lanes = moved_ref.shape[2:]
    line = 2 * steps * (lanes // HD)
    me = lax.axis_index("inst")

    def store(piece):
        slot = jnp.maximum(slots[early[piece]], 0)
        start = window_start(lengths[early[piece]], capacity)
        return pltpu.make_async_copy(
            windows.at[piece], moved_ref.at[slot, :, pl.ds(start, WINDOW), :], sems.at[piece]
        )

    for shift in range(1, count):
        peer = peer_from(me, shift, count)
        slots[shift] = read_small(small_ref, peer, per_row, line)
        lengths[shift] = read_small(small_ref, peer, per_row, line + 1)

    for piece, shift in enumerate(early):

        @pl.when(slots[shift] >= 0)
        def _():
            peer = peer_from(me, shift, count)
            news = small_ref[peer, per_row:, :].astype(jnp.float32)
            ahead = lengths[shift] - window_start(lengths[shift], capacity)
            insert(window_ref.at[piece], news, ahead, steps, windows.at[piece])
            store(piece).start()

    mixed[...] = mixed_ref[...].astype(jnp.float32)
    for shift in range(1, count):

        @pl.when(slots[shift] >= 0)
        def _():
            mixed[pl.ds(pl.multiple_of(slots[shift] * per_row, per_row), per_row), :] = small_ref[
                peer_from(me, shift, count), :per_row, :
            ].astype(jnp.float32)

    for step in range(steps):
        for chunk in range(query_width // HD):
            head, member = chunk // group, chunk % group
            at = head * steps * group + step * group + member
            out_ref[step, :, chunk * HD : (chunk + 1) * HD] = mixed[
                pl.ds(at, rows, stride=per_row), :
            ].astype(jnp.bfloat16)

    for piece, shift in enumerate(early):

        @pl.when(slots[shift] >= 0)
        def _():
            store(piece).wait()


def settle(mixed, small, windows, moved, shape, group, count, early):
    vmem = pl.BlockSpec(memory_space=pltpu.VMEM)
    hbm = pl.BlockSpec(memory_space=pl.ANY)
    return pl.pallas_call(
        functools.partial(settle_kernel, count, early, group),
        out_shape=[
            jax.ShapeDtypeStruct(shape, jnp.bfloat16),
            jax.ShapeDtypeStruct(moved.shape, moved.dtype),
        ],
        in_specs=[vmem, vmem, vmem, hbm],
        out_specs=[vmem, hbm],
        scratch_shapes=[
            pltpu.VMEM(mixed.shape, jnp.float32),
            pltpu.VMEM(windows.shape, windows.dtype),
            pltpu.SemaphoreType.DMA((len(early),)),
            pltpu.SMEM((count,), jnp.int32),
            pltpu.SMEM((count,), jnp.int32),
        ],
        input_output_aliases={3: 1},
        compiler_params=pltpu.CompilerParams(vmem_limit_bytes=SMALL_LIMIT),
        cost_estimate=LIGHT,
        name="settle",
    )(mixed, small, windows, moved)


def finish_kernel(count, late, steps, *refs):
    blocks = refs[: len(late)]
    small_ref, _, out_ref, sems, slots = refs[len(late) :]
    line = 2 * steps * (out_ref.shape[3] // HD)
    facts = -(-(line + 2) // TILE) * TILE
    me = lax.axis_index("inst")

    def store(piece):
        slot = jnp.maximum(slots[piece], 0)
        return pltpu.make_async_copy(blocks[piece], out_ref.at[slot], sems.at[piece])

    for piece, shift in enumerate(late):
        peer = peer_from(me, shift, count)
        slots[piece] = read_small(small_ref, peer, small_ref.shape[1] - facts, line)
    for piece in range(len(late)):
        pl.when(slots[piece] >= 0)(store(piece).start)
    for piece in range(len(late)):
        pl.when(slots[piece] >= 0)(store(piece).wait)


def finish(got, small, moved, steps, count, late):
    vmem = pl.BlockSpec(memory_space=pltpu.VMEM)
    hbm = pl.BlockSpec(memory_space=pl.ANY)
    return pl.pallas_call(
        functools.partial(finish_kernel, count, late, steps),
        out_shape=jax.ShapeDtypeStruct(moved.shape, moved.dtype),
        in_specs=[vmem] * len(got) + [vmem, hbm],
        out_specs=hbm,
        scratch_shapes=[
            pltpu.SemaphoreType.DMA((len(got),)),
            pltpu.SMEM((len(got),), jnp.int32),
        ],
        input_output_aliases={len(got) + 1: 0},
        compiler_params=pltpu.CompilerParams(vmem_limit_bytes=SMALL_LIMIT),
        cost_estimate=LIGHT,
        name="finish",
    )(*got, small, moved)


def local(hidden_new, queries, kv_cache, lengths, destination, key_weight, value_weight, key_gain):
    steps = queries.shape[0]
    group = queries.shape[2] // kv_cache.shape[3]
    count = lax.axis_size("inst")
    half = max(count // 2, 1)
    early = list(range(half, count - 1)) + [half - 1] * (half > 1)
    late = [count - 1] + list(range(half - 2, 0, -1))

    def send(block, shift):
        pairs = [(i, peer_to(i, shift, count)) for i in range(count)]
        return lax.ppermute(block, "inst", pairs)

    first = pack(kv_cache, destination, lengths, count, early[0])
    first_got = send(first, early[0])
    blocks, pick, own, other = prepare(
        destination,
        lengths,
        hidden_new,
        kv_cache,
        key_weight,
        value_weight,
        count,
        early[1:],
        first,
    )
    early_got = [first_got] + [send(block, shift) for block, shift in zip(blocks, early[1:])]
    got = lax.ppermute(other, "tp", [(0, 1), (1, 0)])
    moved, mixed, small, *late_blocks = attend(
        kv_cache,
        queries,
        own,
        got,
        key_gain[None, :],
        lengths,
        destination,
        pick,
        count,
        late,
        first_got,
    )
    late_got = [send(block, shift) for block, shift in zip(late_blocks, late)]
    small_got = lax.all_to_all(small, "inst", 0, 0, tiled=True)
    moved, windows = land(early_got, moved)
    attended, moved = settle(mixed, small_got, windows, moved, queries.shape, group, count, early)
    return attended, finish(late_got, small_got, moved, steps, count, late)


def solution(mesh):
    return jax.shard_map(
        local,
        mesh=mesh,
        in_specs=(
            P(None, ("group", "inst"), "tp"),
            P(None, ("group", "inst"), "tp"),
            P(("group", "inst"), None, None, "tp"),
            P(("group", "inst")),
            P(("group", "inst")),
            P("tp", None),
            P("tp", None),
            P(),
        ),
        out_specs=(P(None, ("group", "inst"), "tp"), P(("group", "inst"), None, None, "tp")),
        check_vma=False,
    )
```

```python
import functools
import math

import jax
import jax.numpy as jnp
from jax import lax
from jax.experimental import pallas as pl
from jax.experimental.pallas import tpu as pltpu
from jax.sharding import PartitionSpec as P

HD = 128
ROPE_BASE = 1000000.0
NORM_EPS = 1e-06
VMEM_LIMIT = 62 * 1024 * 1024
ATTEND_LIMIT = 56 * 1024 * 1024
SMALL_LIMIT = 40 * 1024 * 1024
LAND_LIMIT = 52 * 1024 * 1024
LIGHT = pl.CostEstimate(flops=1, bytes_accessed=1, transcendentals=0)
HEAVY = pl.CostEstimate(flops=1 << 36, bytes_accessed=1 << 28, transcendentals=0)
TILE = 16
WINDOW = 32


def quotient(value, divisor, bound):
    factor = -(-(1 << 16) // divisor)
    if bound * factor < 1 << 31 and all(
        (x * factor) >> 16 == x // divisor for x in range(bound)
    ):
        return (value * factor) >> 16
    return value // divisor


def near_size(count):
    return 4 if count >= 8 and count & (count - 1) == 0 else 1


def peer_to(index, shift, count):
    return index ^ shift if count & (count - 1) == 0 else (index + shift) % count


def peer_from(index, shift, count):
    return index ^ shift if count & (count - 1) == 0 else (index + count - shift) % count


def pick_rows(count, dest_ref, pick_ref):
    rows = dest_ref.shape[0]
    for peer in range(count):
        pick_ref[peer] = 0
    for row in range(rows):
        pick_ref[quotient(dest_ref[row], rows, rows * count)] = row


def add_facts(block, peer, row, dest_ref, length_ref):
    capacity, lanes = block.shape[1:]
    rows = dest_ref.shape[0]
    slot = dest_ref[row] - peer * rows
    slot = jnp.where((slot >= 0) & (slot < rows), slot, -1)
    last = lax.broadcasted_iota(jnp.int32, (TILE, lanes), 0) == TILE - 1
    first_lanes = lax.broadcasted_iota(jnp.int32, (TILE, lanes), 1) < HD
    facts = jnp.where(first_lanes, slot, length_ref[row]).astype(jnp.float32)
    end = block[0, capacity - TILE :, :].astype(jnp.float32)
    block[0, capacity - TILE :, :] = jnp.where(last, facts, end).astype(jnp.bfloat16)


def prepare_kernel(
    count, early, near, chunks, dest_ref, length_ref, hidden_ref, kv_ref, key_ref, value_ref, *refs
):
    outs = len(early) + (near > 1)
    block_refs = list(refs[: len(early)]) + [refs[len(early)].at[i] for i in range(near - 1)]
    early = list(early) + list(range(1, near))
    pick_ref, own_ref, other_ref, blocks, hidden_held, held, total = refs[outs : outs + 7]
    in_sems, out_sems, hidden_sem, weight_sems = refs[outs + 7 :]
    steps, rows, depth = hidden_ref.shape
    width = key_ref.shape[1]
    part = depth // chunks
    me = lax.axis_index("inst")

    def weights(chunk):
        span = pl.ds(chunk * part, part)
        return [
            pltpu.make_async_copy(ref.at[span], held.at[which, span], weight_sems.at[chunk, which])
            for which, ref in enumerate((key_ref, value_ref))
        ]

    hidden_copy = pltpu.make_async_copy(hidden_ref, hidden_held, hidden_sem)
    hidden_copy.start()
    for copy in weights(0):
        copy.start()
    pick_rows(count, dest_ref, pick_ref)
    fetches, stores = [], []
    for piece, shift in enumerate(early):
        row = pick_ref[peer_to(me, shift, count)]
        fetches.append(
            pltpu.make_async_copy(kv_ref.at[row], blocks.at[piece], in_sems.at[piece])
        )
        fetches[-1].start()
    for chunk in range(1, chunks):
        for copy in weights(chunk):
            copy.start()

    for piece, shift in enumerate(early):
        peer = peer_to(me, shift, count)
        fetches[piece].wait()
        add_facts(blocks.at[piece], peer, pick_ref[peer], dest_ref, length_ref)
        stores.append(
            pltpu.make_async_copy(blocks.at[piece], block_refs[piece], out_sems.at[piece])
        )
        stores[-1].start()
    hidden_copy.wait()
    hidden = hidden_held[...].reshape(steps * rows, depth)
    sums = [None, None]
    for chunk in range(chunks):
        for which, copy in enumerate(weights(chunk)):
            copy.wait()
            product = jnp.dot(
                hidden[:, chunk * part : (chunk + 1) * part],
                held[which, chunk * part : (chunk + 1) * part, :],
                preferred_element_type=jnp.float32,
            )
            sums[which] = product if chunk == 0 else sums[which] + product
    total[:, :width] = sums[0]
    total[:, width:] = sums[1]
    half = width // 2
    core = lax.axis_index("tp")
    for ref, place in ((own_ref, core), (other_ref, 1 - core)):
        at = pl.multiple_of(place * half, half)
        ref[:, :half] = total[:, pl.ds(at, half)]
        ref[:, half:] = total[:, pl.ds(pl.multiple_of(width + at, half), half)]

    for copy in stores:
        copy.wait()


def prepare(destination, lengths, hidden_new, kv_cache, key_weight, value_weight, count, early, near):
    steps, rows, depth = hidden_new.shape
    width = key_weight.shape[1]
    chunks = 5
    part = jax.ShapeDtypeStruct((steps * rows, width), jnp.float32)
    smem = pl.BlockSpec(memory_space=pltpu.SMEM)
    vmem = pl.BlockSpec(memory_space=pltpu.VMEM)
    hbm = pl.BlockSpec(memory_space=pl.ANY)
    block = kv_cache.shape[1:]
    shapes = [jax.ShapeDtypeStruct(block, kv_cache.dtype)] * len(early)
    if near > 1:
        shapes.append(jax.ShapeDtypeStruct((near - 1,) + block, kv_cache.dtype))
    pieces = len(early) + near - 1
    outs = pl.pallas_call(
        functools.partial(prepare_kernel, count, early, near, chunks),
        out_shape=shapes
        + [jax.ShapeDtypeStruct((count,), jnp.int32), part, part],
        in_specs=[smem, smem, hbm, hbm, hbm, hbm],
        out_specs=[hbm] * len(shapes) + [smem, vmem, vmem],
        scratch_shapes=[
            pltpu.VMEM((pieces,) + block, kv_cache.dtype),
            pltpu.VMEM(hidden_new.shape, hidden_new.dtype),
            pltpu.VMEM((2, depth, width), key_weight.dtype),
            pltpu.VMEM((steps * rows, 2 * width), jnp.float32),
            pltpu.SemaphoreType.DMA((pieces,)),
            pltpu.SemaphoreType.DMA((pieces,)),
            pltpu.SemaphoreType.DMA,
            pltpu.SemaphoreType.DMA((chunks, 2)),
        ],
        compiler_params=pltpu.CompilerParams(vmem_limit_bytes=VMEM_LIMIT),
        cost_estimate=LIGHT,
        name="prepare",
    )(destination, lengths, hidden_new, kv_cache, key_weight, value_weight)
    return outs[: len(shapes)], *outs[len(shapes) :]


def rotation(length_ref, steps, rows):
    half = HD // 2
    line = lax.broadcasted_iota(jnp.int32, (rows, HD), 0)
    lane = lax.broadcasted_iota(jnp.int32, (steps * rows, HD), 1)
    length = jnp.zeros((rows, HD), jnp.int32)
    for row in range(rows):
        length = jnp.where(line == row, length_ref[row], length)
    position = jnp.concatenate([length + step for step in range(steps)], axis=0)
    order = (lane % half).astype(jnp.float32)
    angle = position.astype(jnp.float32) * jnp.exp(-math.log(ROPE_BASE) * 2.0 * order / HD)
    turns = jnp.floor(angle * (1.0 / math.pi) + 0.5)
    rest = ((angle - turns * 3.140625) - turns * 9.67502593994140625e-4) - turns * 1.5099579909783e-7
    sign = 1.0 - 2.0 * (turns - 2.0 * jnp.floor(turns * 0.5))
    square = rest * rest
    cosine, sine = jnp.ones_like(rest), jnp.ones_like(rest)
    for power in range(6, 0, -1):
        cosine = 1.0 - cosine * square * (1.0 / ((2 * power - 1) * (2 * power)))
        sine = 1.0 - sine * square * (1.0 / ((2 * power) * (2 * power + 1)))
    sine = sign * rest * sine
    return sign * cosine, jnp.where(lane < half, -sine, sine)


def attend_kernel(
    count,
    late,
    block,
    length_ref,
    dest_ref,
    pick_ref,
    own_ref,
    got_ref,
    gain_ref,
    query_ref,
    kv_ref,
    *refs,
):
    moved_ref, mixed_ref, small_ref = refs[:3]
    late_refs = refs[3:-4]
    fresh, query_rows, query_columns, mixed = refs[-4:]
    part = pl.program_id(0)
    steps, rows, query_width = query_ref.shape
    capacity, lanes = kv_ref.shape[2:]
    heads = lanes // HD
    group = query_width // lanes
    per_head = steps * group
    per_row = heads * per_head
    team = HD // per_row

    @pl.when(part == 0)
    def _():
        raw = own_ref[...] + got_ref[...]
        cosine, sine = rotation(length_ref, steps, rows)
        gain = gain_ref[...].astype(jnp.float32)
        for head in range(heads):
            at = slice(head * HD, (head + 1) * HD)
            piece = raw[:, at]
            mean = jnp.mean(piece * piece, axis=-1, keepdims=True)
            piece = piece * lax.rsqrt(mean + NORM_EPS) * gain
            swapped = jnp.concatenate([piece[:, HD // 2 :], piece[:, : HD // 2]], axis=1)
            turned = piece * cosine + swapped * sine
            fresh[0, :, at] = turned.astype(jnp.bfloat16).astype(jnp.float32)
        fresh[1] = raw[:, lanes:].astype(jnp.bfloat16).astype(jnp.float32)
        for step in range(steps):
            for chunk in range(query_width // HD):
                head, member = chunk // group, chunk % group
                at = head * per_head + step * group + member
                query_rows[pl.ds(at, rows, stride=per_row), :] = query_ref[
                    step, :, chunk * HD : (chunk + 1) * HD
                ].astype(jnp.float32)
        for index in range(rows // team):
            query_columns[index] = query_rows[index * HD : (index + 1) * HD, :].T

    position = lax.broadcasted_iota(jnp.int32, (capacity, HD), 0)
    column = lax.broadcasted_iota(jnp.int32, (capacity, HD), 1)
    column_item = column // per_row
    column_step = (column % per_head) // group
    column_head = lax.broadcasted_iota(jnp.int32, (HD, HD), 1) % per_row // per_head
    factor = 1.0 / math.sqrt(HD)
    teams = range(block // team)
    scores = []
    for index in teams:
        queries = query_columns[part * (block // team) + index]
        queries = jnp.concatenate(
            [jnp.where(column_head == head, queries, 0.0) for head in range(heads)], axis=0
        ).astype(jnp.bfloat16)
        score, limit = None, None
        for member in range(team):
            item = index * team + member
            row = part * block + item
            length = length_ref[row]
            kept = position < length
            landing = [position == length + step for step in range(steps)]
            for which in range(2):
                news = [fresh[which, pl.ds(step * rows + row, 1), :] for step in range(steps)]
                for head in range(heads):
                    at = slice(head * HD, (head + 1) * HD)
                    stored = jnp.where(kept, kv_ref[item, which, :, at].astype(jnp.float32), 0.0)
                    for step in range(steps):
                        stored = jnp.where(landing[step], news[step][:, at], stored)
                    moved_ref[item, which, :, at] = stored.astype(jnp.bfloat16)
            one = jnp.dot(moved_ref[item, 0], queries, preferred_element_type=jnp.float32)
            score = one if member == 0 else jnp.where(column_item == member, one, score)
            limit = length if member == 0 else jnp.where(column_item == member, length, limit)
        scores.append(jnp.where(position <= limit + column_step, score * factor, -jnp.inf))
    weights = []
    for score in scores:
        raised = jnp.exp(score - jnp.max(score, axis=0, keepdims=True))
        normaliser = jnp.sum(raised, axis=0, keepdims=True)
        weights.append((raised / normaliser).T.astype(jnp.bfloat16))
    for index in teams:
        for member in range(team):
            item = index * team + member
            row = part * block + item
            result = jnp.dot(
                weights[index][member * per_row : (member + 1) * per_row],
                moved_ref[item, 1],
                preferred_element_type=jnp.float32,
            )
            for head in range(heads):
                at = pl.multiple_of(row * per_row + head * per_head, per_head)
                mixed[pl.ds(at, per_head), :] = result[
                    head * per_head : (head + 1) * per_head, head * HD : (head + 1) * HD
                ]

    me = lax.axis_index("inst")
    for late_ref, shift in zip(late_refs, late):
        item = pick_ref[peer_to(me, shift, count)] - part * block

        @pl.when((item >= 0) & (item < block))
        def _():
            late_ref[...] = moved_ref[item]

    @pl.when(part == pl.num_programs(0) - 1)
    def _():
        mixed_ref[...] = mixed[...].astype(jnp.bfloat16)
        for peer in range(count):
            row = pick_ref[peer]
            small_ref[peer, :per_row, :] = mixed[
                pl.ds(pl.multiple_of(row * per_row, per_row), per_row), :
            ].astype(jnp.bfloat16)
            news = []
            for which in range(2):
                for step in range(steps):
                    new = fresh[which, pl.ds(step * rows + row, 1), :]
                    news += [new[:, h * HD : (h + 1) * HD] for h in range(heads)]
            slot = dest_ref[row] - peer * rows
            slot = jnp.where((slot >= 0) & (slot < rows), slot, -1).astype(jnp.float32)
            news.append(jnp.full((1, HD), slot))
            fill = small_ref.shape[1] - per_row - 2 * steps * heads - 1
            news.append(jnp.full((fill, HD), length_ref[row].astype(jnp.float32)))
            small_ref[peer, per_row:, :] = jnp.concatenate(news, axis=0).astype(jnp.bfloat16)


def attend(kv_cache, queries, own, got, gain, lengths, destination, pick, count, late):
    steps, rows, query_width = queries.shape
    capacity, lanes = kv_cache.shape[2:]
    heads = lanes // HD
    per_row = steps * query_width // HD
    block = 8
    small_rows = per_row + -(-(2 * steps * heads + 2) // TILE) * TILE
    small = jax.ShapeDtypeStruct((count, small_rows, HD), jnp.bfloat16)
    smem = pl.BlockSpec(memory_space=pltpu.SMEM)
    vmem = pl.BlockSpec(memory_space=pltpu.VMEM)
    cache_block = pl.BlockSpec((block, 2, capacity, lanes), lambda i: (i, 0, 0, 0))
    return pl.pallas_call(
        functools.partial(attend_kernel, count, late, block),
        grid=(rows // block,),
        out_shape=[
            jax.ShapeDtypeStruct(kv_cache.shape, kv_cache.dtype),
            jax.ShapeDtypeStruct((rows * per_row, HD), jnp.bfloat16),
            small,
        ]
        + [jax.ShapeDtypeStruct(kv_cache.shape[1:], kv_cache.dtype)] * len(late),
        in_specs=[smem, smem, smem, vmem, vmem, vmem, vmem, cache_block],
        out_specs=[cache_block, vmem, vmem] + [vmem] * len(late),
        scratch_shapes=[
            pltpu.VMEM((2, steps * rows, lanes), jnp.float32),
            pltpu.VMEM((rows * per_row, HD), jnp.float32),
            pltpu.VMEM((rows * per_row // HD, HD, HD), jnp.float32),
            pltpu.VMEM((rows * per_row, HD), jnp.float32),
        ],
        compiler_params=pltpu.CompilerParams(vmem_limit_bytes=ATTEND_LIMIT),
        cost_estimate=HEAVY,
        name="attend",
    )(lengths, destination, pick, own, got, gain, queries, kv_cache)


def read_facts(block):
    capacity = block.shape[1]
    facts = block[0, capacity - TILE :, :].astype(jnp.float32)[TILE - 1 :]
    return (
        jnp.max(facts[:, :HD]).astype(jnp.int32),
        jnp.max(facts[:, HD : 2 * HD]).astype(jnp.int32),
    )


def window_start(length, capacity):
    return pl.multiple_of(jnp.minimum(length // TILE * TILE, capacity - WINDOW), TILE)


def clean(block, length, out):
    capacity, lanes = block.shape[1:]
    kept = lax.broadcasted_iota(jnp.int32, (capacity, HD), 0) < length
    for which in range(2):
        for at in range(0, lanes, HD):
            stored = block[which, :, at : at + HD].astype(jnp.float32)
            out[which, :, at : at + HD] = jnp.where(kept, stored, 0.0).astype(jnp.bfloat16)


def insert(window, news, ahead, steps, out):
    height, lanes = window.shape[1:]
    heads = lanes // HD
    position = lax.broadcasted_iota(jnp.int32, (height, lanes), 0)
    for which in range(2):
        stored = window[which].astype(jnp.float32)
        for step in range(steps):
            at = (which * steps + step) * heads
            new = jnp.concatenate([news[at + h : at + h + 1] for h in range(heads)], axis=1)
            stored = jnp.where(position == ahead + step, new, stored)
        out[which] = stored.astype(jnp.bfloat16)


def land_kernel(early, near, *refs):
    blocks = list(refs[:early])
    if near > 1:
        gathered_ref = refs[early]
        held, held_sems = refs[-2:]
        me = lax.axis_index("inst") % near
        fetches = [
            pltpu.make_async_copy(
                gathered_ref.at[me ^ shift, shift - 1], held.at[shift - 1], held_sems.at[shift - 1]
            )
            for shift in range(1, near)
        ]
        for copy in fetches:
            copy.start()
        blocks += [held.at[i] for i in range(near - 1)]
    _, out_ref, window_ref, buffer, sems, slots = refs[early + (near > 1) :][:6]
    capacity = buffer.shape[2]

    def store(piece):
        slot = jnp.maximum(slots[piece], 0)
        return pltpu.make_async_copy(buffer.at[piece], out_ref.at[slot], sems.at[piece])

    def take(piece):
        slot, length = read_facts(blocks[piece])
        slots[piece] = slot

        @pl.when(slot >= 0)
        def _():
            clean(blocks[piece], length, buffer.at[piece])
            store(piece).start()
            start = window_start(length, capacity)
            window_ref[piece] = buffer[piece, :, pl.ds(start, WINDOW), :]

    for piece in range(len(blocks)):
        if piece >= early:
            fetches[piece - early].wait()
        take(piece)
    for piece in range(len(blocks)):

        @pl.when(slots[piece] >= 0)
        def _():
            store(piece).wait()


def land(got, gathered, moved):
    near = gathered[0].shape[0] if gathered else 1
    pieces = len(got) + near - 1
    vmem = pl.BlockSpec(memory_space=pltpu.VMEM)
    hbm = pl.BlockSpec(memory_space=pl.ANY)
    extra = []
    if near > 1:
        extra = [
            pltpu.VMEM((near - 1,) + moved.shape[1:], moved.dtype),
            pltpu.SemaphoreType.DMA((near - 1,)),
        ]
    return pl.pallas_call(
        functools.partial(land_kernel, len(got), near),
        out_shape=[
            jax.ShapeDtypeStruct(moved.shape, moved.dtype),
            jax.ShapeDtypeStruct((pieces, 2, WINDOW, moved.shape[3]), moved.dtype),
        ],
        in_specs=[vmem] * len(got) + [hbm] * len(gathered) + [hbm],
        out_specs=[hbm, vmem],
        scratch_shapes=[
            pltpu.VMEM((pieces,) + moved.shape[1:], moved.dtype),
            pltpu.SemaphoreType.DMA((pieces,)),
            pltpu.SMEM((pieces,), jnp.int32),
        ]
        + extra,
        input_output_aliases={len(got) + len(gathered): 0},
        compiler_params=pltpu.CompilerParams(vmem_limit_bytes=LAND_LIMIT),
        cost_estimate=HEAVY,
        name="land",
    )(*got, *gathered, moved)


def read_small(small_ref, peer, per_row, line):
    rows = small_ref[peer, per_row:, :].astype(jnp.float32)
    return jnp.max(rows[line : line + 1]).astype(jnp.int32)


def settle_kernel(
    count,
    early,
    group,
    mixed_ref,
    small_ref,
    window_ref,
    _,
    out_ref,
    moved_ref,
    mixed,
    windows,
    sems,
    slots,
    lengths,
):
    steps, rows, query_width = out_ref.shape
    per_row = steps * query_width // HD
    capacity, lanes = moved_ref.shape[2:]
    line = 2 * steps * (lanes // HD)
    me = lax.axis_index("inst")

    def store(piece):
        slot = jnp.maximum(slots[early[piece]], 0)
        start = window_start(lengths[early[piece]], capacity)
        return pltpu.make_async_copy(
            windows.at[piece], moved_ref.at[slot, :, pl.ds(start, WINDOW), :], sems.at[piece]
        )

    for shift in range(1, count):
        peer = peer_from(me, shift, count)
        slots[shift] = read_small(small_ref, peer, per_row, line)
        lengths[shift] = read_small(small_ref, peer, per_row, line + 1)

    for piece, shift in enumerate(early):

        @pl.when(slots[shift] >= 0)
        def _():
            peer = peer_from(me, shift, count)
            news = small_ref[peer, per_row:, :].astype(jnp.float32)
            ahead = lengths[shift] - window_start(lengths[shift], capacity)
            insert(window_ref.at[piece], news, ahead, steps, windows.at[piece])
            store(piece).start()

    mixed[...] = mixed_ref[...].astype(jnp.float32)
    for shift in range(1, count):

        @pl.when(slots[shift] >= 0)
        def _():
            mixed[pl.ds(pl.multiple_of(slots[shift] * per_row, per_row), per_row), :] = small_ref[
                peer_from(me, shift, count), :per_row, :
            ].astype(jnp.float32)

    for step in range(steps):
        for chunk in range(query_width // HD):
            head, member = chunk // group, chunk % group
            at = head * steps * group + step * group + member
            out_ref[step, :, chunk * HD : (chunk + 1) * HD] = mixed[
                pl.ds(at, rows, stride=per_row), :
            ].astype(jnp.bfloat16)

    for piece, shift in enumerate(early):

        @pl.when(slots[shift] >= 0)
        def _():
            store(piece).wait()


def settle(mixed, small, windows, moved, shape, group, count, early):
    vmem = pl.BlockSpec(memory_space=pltpu.VMEM)
    hbm = pl.BlockSpec(memory_space=pl.ANY)
    return pl.pallas_call(
        functools.partial(settle_kernel, count, early, group),
        out_shape=[
            jax.ShapeDtypeStruct(shape, jnp.bfloat16),
            jax.ShapeDtypeStruct(moved.shape, moved.dtype),
        ],
        in_specs=[vmem, vmem, vmem, hbm],
        out_specs=[vmem, hbm],
        scratch_shapes=[
            pltpu.VMEM(mixed.shape, jnp.float32),
            pltpu.VMEM(windows.shape, windows.dtype),
            pltpu.SemaphoreType.DMA((len(early),)),
            pltpu.SMEM((count,), jnp.int32),
            pltpu.SMEM((count,), jnp.int32),
        ],
        input_output_aliases={3: 1},
        compiler_params=pltpu.CompilerParams(vmem_limit_bytes=SMALL_LIMIT),
        cost_estimate=LIGHT,
        name="settle",
    )(mixed, small, windows, moved)


def finish_kernel(count, late, steps, *refs):
    blocks = refs[: len(late)]
    small_ref, _, out_ref, sems, slots = refs[len(late) :]
    line = 2 * steps * (out_ref.shape[3] // HD)
    facts = -(-(line + 2) // TILE) * TILE
    me = lax.axis_index("inst")

    def store(piece):
        slot = jnp.maximum(slots[piece], 0)
        return pltpu.make_async_copy(blocks[piece], out_ref.at[slot], sems.at[piece])

    for piece, shift in enumerate(late):
        peer = peer_from(me, shift, count)
        slots[piece] = read_small(small_ref, peer, small_ref.shape[1] - facts, line)
    for piece in range(len(late)):
        pl.when(slots[piece] >= 0)(store(piece).start)
    for piece in range(len(late)):
        pl.when(slots[piece] >= 0)(store(piece).wait)


def finish(got, small, moved, steps, count, late):
    vmem = pl.BlockSpec(memory_space=pltpu.VMEM)
    hbm = pl.BlockSpec(memory_space=pl.ANY)
    return pl.pallas_call(
        functools.partial(finish_kernel, count, late, steps),
        out_shape=jax.ShapeDtypeStruct(moved.shape, moved.dtype),
        in_specs=[vmem] * len(got) + [vmem, hbm],
        out_specs=hbm,
        scratch_shapes=[
            pltpu.SemaphoreType.DMA((len(got),)),
            pltpu.SMEM((len(got),), jnp.int32),
        ],
        input_output_aliases={len(got) + 1: 0},
        compiler_params=pltpu.CompilerParams(vmem_limit_bytes=SMALL_LIMIT),
        cost_estimate=LIGHT,
        name="finish",
    )(*got, small, moved)


def local(hidden_new, queries, kv_cache, lengths, destination, key_weight, value_weight, key_gain):
    steps = queries.shape[0]
    group = queries.shape[2] // kv_cache.shape[3]
    count = lax.axis_size("inst")
    near = near_size(count)
    early = list(range(near, count - 1))
    late = [count - 1]

    def send(block, shift):
        pairs = [(i, peer_to(i, shift, count)) for i in range(count)]
        return lax.ppermute(block, "inst", pairs)

    blocks, pick, own, other = prepare(
        destination, lengths, hidden_new, kv_cache, key_weight, value_weight, count, early, near
    )
    early_got = [send(block, shift) for block, shift in zip(blocks, early)]
    gathered = []
    if near > 1:
        teams = [list(range(i, i + near)) for i in range(0, count, near)]
        gathered = [lax.all_gather(blocks[-1], "inst", axis_index_groups=teams)]
    got = lax.ppermute(other, "tp", [(0, 1), (1, 0)])
    moved, mixed, small, *late_blocks = attend(
        kv_cache,
        queries,
        own,
        got,
        key_gain[None, :],
        lengths,
        destination,
        pick,
        count,
        late,
    )
    late_got = [send(block, shift) for block, shift in zip(late_blocks, late)]
    small_got = lax.all_to_all(small, "inst", 0, 0, tiled=True)
    moved, windows = land(early_got, gathered, moved)
    landed = early + list(range(1, near))
    attended, moved = settle(mixed, small_got, windows, moved, queries.shape, group, count, landed)
    return attended, finish(late_got, small_got, moved, steps, count, late)


def solution(mesh):
    return jax.shard_map(
        local,
        mesh=mesh,
        in_specs=(
            P(None, ("group", "inst"), "tp"),
            P(None, ("group", "inst"), "tp"),
            P(("group", "inst"), None, None, "tp"),
            P(("group", "inst")),
            P(("group", "inst")),
            P("tp", None),
            P("tp", None),
            P(),
        ),
        out_specs=(P(None, ("group", "inst"), "tp"), P(("group", "inst"), None, None, "tp")),
        check_vma=False,
    )
```

```python
import functools
import math

import jax
import jax.numpy as jnp
from jax import lax
from jax.experimental import pallas as pl
from jax.experimental.pallas import tpu as pltpu
from jax.sharding import PartitionSpec as P

HD = 128
ROPE_BASE = 1000000.0
NORM_EPS = 1e-06
VMEM_LIMIT = 62 * 1024 * 1024
ATTEND_LIMIT = 50 * 1024 * 1024
PREPARE_LIMIT = 53 * 1024 * 1024
SMALL_LIMIT = 40 * 1024 * 1024
LIGHT = pl.CostEstimate(flops=1, bytes_accessed=1, transcendentals=0)
HEAVY = pl.CostEstimate(flops=1 << 36, bytes_accessed=1 << 28, transcendentals=0)
TILE = 16
WINDOW = 32


def quotient(value, divisor, bound):
    factor = -(-(1 << 16) // divisor)
    if bound * factor < 1 << 31 and all(
        (x * factor) >> 16 == x // divisor for x in range(bound)
    ):
        return (value * factor) >> 16
    return value // divisor


def peer_to(index, shift, count):
    return index ^ shift if count & (count - 1) == 0 else (index + shift) % count


def peer_from(index, shift, count):
    return index ^ shift if count & (count - 1) == 0 else (index + count - shift) % count


def pick_rows(count, dest_ref, pick_ref):
    rows = dest_ref.shape[0]
    for peer in range(count):
        pick_ref[peer] = 0
    for row in range(rows):
        pick_ref[quotient(dest_ref[row], rows, rows * count)] = row


def add_facts(block, peer, row, dest_ref, length_ref):
    capacity, lanes = block.shape[1:]
    rows = dest_ref.shape[0]
    slot = dest_ref[row] - peer * rows
    slot = jnp.where((slot >= 0) & (slot < rows), slot, -1)
    last = lax.broadcasted_iota(jnp.int32, (TILE, lanes), 0) == TILE - 1
    first_lanes = lax.broadcasted_iota(jnp.int32, (TILE, lanes), 1) < HD
    facts = jnp.where(first_lanes, slot, length_ref[row]).astype(jnp.float32)
    end = block[0, capacity - TILE :, :].astype(jnp.float32)
    block[0, capacity - TILE :, :] = jnp.where(last, facts, end).astype(jnp.bfloat16)


def pack_kernel(count, shift, dest_ref, length_ref, kv_ref, block_ref, block, sem, pick):
    pick_rows(count, dest_ref, pick)
    peer = peer_to(lax.axis_index("inst"), shift, count)
    row = pick[peer]
    fetch = pltpu.make_async_copy(kv_ref.at[row], block, sem)
    fetch.start()
    fetch.wait()
    add_facts(block, peer, row, dest_ref, length_ref)
    store = pltpu.make_async_copy(block, block_ref, sem)
    store.start()
    store.wait()


def pack(kv_cache, destination, lengths, count, shift):
    smem = pl.BlockSpec(memory_space=pltpu.SMEM)
    hbm = pl.BlockSpec(memory_space=pl.ANY)
    return pl.pallas_call(
        functools.partial(pack_kernel, count, shift),
        out_shape=jax.ShapeDtypeStruct(kv_cache.shape[1:], kv_cache.dtype),
        in_specs=[smem, smem, hbm],
        out_specs=hbm,
        scratch_shapes=[
            pltpu.VMEM(kv_cache.shape[1:], kv_cache.dtype),
            pltpu.SemaphoreType.DMA,
            pltpu.SMEM((count,), jnp.int32),
        ],
        compiler_params=pltpu.CompilerParams(vmem_limit_bytes=VMEM_LIMIT),
        cost_estimate=LIGHT,
        name="pack",
    )(destination, lengths, kv_cache)


def prepare_kernel(
    count, early, chunks, dest_ref, length_ref, hidden_ref, kv_ref, key_ref, value_ref, *refs
):
    block_refs = refs[: len(early)]
    own_ref, other_ref, blocks, hidden_held, held, total = refs[len(early) : len(early) + 6]
    in_sems, out_sems, hidden_sem, weight_sems, pick_ref = refs[len(early) + 6 :]
    steps, rows, depth = hidden_ref.shape
    width = key_ref.shape[1]
    part = depth // chunks
    me = lax.axis_index("inst")

    def weights(chunk):
        span = pl.ds(chunk * part, part)
        return [
            pltpu.make_async_copy(ref.at[span], held.at[which, span], weight_sems.at[chunk, which])
            for which, ref in enumerate((key_ref, value_ref))
        ]

    hidden_copy = pltpu.make_async_copy(hidden_ref, hidden_held, hidden_sem)
    hidden_copy.start()
    for copy in weights(0):
        copy.start()
    pick_rows(count, dest_ref, pick_ref)
    fetches, stores = [], []
    for piece, shift in enumerate(early):
        row = pick_ref[peer_to(me, shift, count)]
        fetches.append(
            pltpu.make_async_copy(kv_ref.at[row], blocks.at[piece], in_sems.at[piece])
        )
        fetches[-1].start()
    for chunk in range(1, chunks):
        for copy in weights(chunk):
            copy.start()

    for piece, shift in enumerate(early):
        peer = peer_to(me, shift, count)
        fetches[piece].wait()
        add_facts(blocks.at[piece], peer, pick_ref[peer], dest_ref, length_ref)
        stores.append(
            pltpu.make_async_copy(blocks.at[piece], block_refs[piece], out_sems.at[piece])
        )
        stores[-1].start()
    hidden_copy.wait()
    hidden = hidden_held[...].reshape(steps * rows, depth)
    sums = [None, None]
    for chunk in range(chunks):
        for which, copy in enumerate(weights(chunk)):
            copy.wait()
            product = jnp.dot(
                hidden[:, chunk * part : (chunk + 1) * part],
                held[which, chunk * part : (chunk + 1) * part, :],
                preferred_element_type=jnp.float32,
            )
            sums[which] = product if chunk == 0 else sums[which] + product
    total[:, :width] = sums[0]
    total[:, width:] = sums[1]
    half = width // 2
    core = lax.axis_index("tp")
    for ref, place in ((own_ref, core), (other_ref, 1 - core)):
        at = pl.multiple_of(place * half, half)
        ref[:, :half] = total[:, pl.ds(at, half)]
        ref[:, half:] = total[:, pl.ds(pl.multiple_of(width + at, half), half)]

    for copy in stores:
        copy.wait()


def prepare(destination, lengths, hidden_new, kv_cache, key_weight, value_weight, count, early):
    steps, rows, depth = hidden_new.shape
    width = key_weight.shape[1]
    chunks = 5
    part = jax.ShapeDtypeStruct((steps * rows, width), jnp.float32)
    smem = pl.BlockSpec(memory_space=pltpu.SMEM)
    vmem = pl.BlockSpec(memory_space=pltpu.VMEM)
    hbm = pl.BlockSpec(memory_space=pl.ANY)
    outs = pl.pallas_call(
        functools.partial(prepare_kernel, count, early, chunks),
        out_shape=[jax.ShapeDtypeStruct(kv_cache.shape[1:], kv_cache.dtype)] * len(early)
        + [part, part],
        in_specs=[smem, smem, hbm, hbm, hbm, hbm],
        out_specs=[hbm] * len(early) + [vmem, vmem],
        scratch_shapes=[
            pltpu.VMEM((len(early),) + kv_cache.shape[1:], kv_cache.dtype),
            pltpu.VMEM(hidden_new.shape, hidden_new.dtype),
            pltpu.VMEM((2, depth, width), key_weight.dtype),
            pltpu.VMEM((steps * rows, 2 * width), jnp.float32),
            pltpu.SemaphoreType.DMA((len(early),)),
            pltpu.SemaphoreType.DMA((len(early),)),
            pltpu.SemaphoreType.DMA,
            pltpu.SemaphoreType.DMA((chunks, 2)),
            pltpu.SMEM((count,), jnp.int32),
        ],
        compiler_params=pltpu.CompilerParams(vmem_limit_bytes=PREPARE_LIMIT),
        cost_estimate=LIGHT,
        name="prepare",
    )(destination, lengths, hidden_new, kv_cache, key_weight, value_weight)
    return outs[: len(early)], *outs[len(early) :]


def rotation(length_ref, steps, rows):
    half = HD // 2
    line = lax.broadcasted_iota(jnp.int32, (rows, HD), 0)
    lane = lax.broadcasted_iota(jnp.int32, (steps * rows, HD), 1)
    length = jnp.zeros((rows, HD), jnp.int32)
    for row in range(rows):
        length = jnp.where(line == row, length_ref[row], length)
    position = jnp.concatenate([length + step for step in range(steps)], axis=0)
    order = (lane % half).astype(jnp.float32)
    angle = position.astype(jnp.float32) * jnp.exp(-math.log(ROPE_BASE) * 2.0 * order / HD)
    turns = jnp.floor(angle * (1.0 / math.pi) + 0.5)
    rest = ((angle - turns * 3.140625) - turns * 9.67502593994140625e-4) - turns * 1.5099579909783e-7
    sign = 1.0 - 2.0 * (turns - 2.0 * jnp.floor(turns * 0.5))
    square = rest * rest
    cosine, sine = jnp.ones_like(rest), jnp.ones_like(rest)
    for power in range(6, 0, -1):
        cosine = 1.0 - cosine * square * (1.0 / ((2 * power - 1) * (2 * power)))
        sine = 1.0 - sine * square * (1.0 / ((2 * power) * (2 * power + 1)))
    sine = sign * rest * sine
    return sign * cosine, jnp.where(lane < half, -sine, sine)


def attend_kernel(
    count,
    late,
    block,
    length_ref,
    dest_ref,
    own_ref,
    got_ref,
    gain_ref,
    query_ref,
    kv_ref,
    *refs,
):
    moved_ref, mixed_ref, small_ref = refs[1:4]
    late_refs = refs[4:-5]
    fresh, query_rows, query_columns, mixed, pick_ref = refs[-5:]
    part = pl.program_id(0)
    steps, rows, query_width = query_ref.shape
    capacity, lanes = kv_ref.shape[2:]
    heads = lanes // HD
    group = query_width // lanes
    per_head = steps * group
    per_row = heads * per_head
    team = HD // per_row

    @pl.when(part == 0)
    def _():
        pick_rows(count, dest_ref, pick_ref)
        raw = own_ref[...] + got_ref[...]
        cosine, sine = rotation(length_ref, steps, rows)
        gain = gain_ref[...].astype(jnp.float32)
        for head in range(heads):
            at = slice(head * HD, (head + 1) * HD)
            piece = raw[:, at]
            mean = jnp.mean(piece * piece, axis=-1, keepdims=True)
            piece = piece * lax.rsqrt(mean + NORM_EPS) * gain
            swapped = jnp.concatenate([piece[:, HD // 2 :], piece[:, : HD // 2]], axis=1)
            turned = piece * cosine + swapped * sine
            fresh[0, :, at] = turned.astype(jnp.bfloat16).astype(jnp.float32)
        fresh[1] = raw[:, lanes:].astype(jnp.bfloat16).astype(jnp.float32)
        for step in range(steps):
            for chunk in range(query_width // HD):
                head, member = chunk // group, chunk % group
                at = head * per_head + step * group + member
                query_rows[pl.ds(at, rows, stride=per_row), :] = query_ref[
                    step, :, chunk * HD : (chunk + 1) * HD
                ].astype(jnp.float32)
        for index in range(rows // team):
            query_columns[index] = query_rows[index * HD : (index + 1) * HD, :].T

    position = lax.broadcasted_iota(jnp.int32, (capacity, HD), 0)
    column = lax.broadcasted_iota(jnp.int32, (capacity, HD), 1)
    column_item = column // per_row
    column_step = (column % per_head) // group
    column_head = lax.broadcasted_iota(jnp.int32, (HD, HD), 1) % per_row // per_head
    factor = 1.0 / math.sqrt(HD)
    teams = range(block // team)
    scores = []
    for index in teams:
        queries = query_columns[part * (block // team) + index]
        queries = jnp.concatenate(
            [jnp.where(column_head == head, queries, 0.0) for head in range(heads)], axis=0
        ).astype(jnp.bfloat16)
        score, limit = None, None
        for member in range(team):
            item = index * team + member
            row = part * block + item
            length = length_ref[row]
            kept = position < length
            landing = [position == length + step for step in range(steps)]
            for which in range(2):
                news = [fresh[which, pl.ds(step * rows + row, 1), :] for step in range(steps)]
                for head in range(heads):
                    at = slice(head * HD, (head + 1) * HD)
                    stored = jnp.where(kept, kv_ref[item, which, :, at].astype(jnp.float32), 0.0)
                    for step in range(steps):
                        stored = jnp.where(landing[step], news[step][:, at], stored)
                    moved_ref[item, which, :, at] = stored.astype(jnp.bfloat16)
            one = jnp.dot(moved_ref[item, 0], queries, preferred_element_type=jnp.float32)
            score = one if member == 0 else jnp.where(column_item == member, one, score)
            limit = length if member == 0 else jnp.where(column_item == member, length, limit)
        scores.append(jnp.where(position <= limit + column_step, score * factor, -jnp.inf))
    weights = []
    for score in scores:
        raised = jnp.exp(score - jnp.max(score, axis=0, keepdims=True))
        normaliser = jnp.sum(raised, axis=0, keepdims=True)
        weights.append((raised / normaliser).T.astype(jnp.bfloat16))
    for index in teams:
        for member in range(team):
            item = index * team + member
            row = part * block + item
            result = jnp.dot(
                weights[index][member * per_row : (member + 1) * per_row],
                moved_ref[item, 1],
                preferred_element_type=jnp.float32,
            )
            for head in range(heads):
                at = pl.multiple_of(row * per_row + head * per_head, per_head)
                mixed[pl.ds(at, per_head), :] = result[
                    head * per_head : (head + 1) * per_head, head * HD : (head + 1) * HD
                ]

    me = lax.axis_index("inst")
    for late_ref, shift in zip(late_refs, late):
        item = pick_ref[peer_to(me, shift, count)] - part * block

        @pl.when((item >= 0) & (item < block))
        def _():
            late_ref[...] = moved_ref[item]

    @pl.when(part == pl.num_programs(0) - 1)
    def _():
        mixed_ref[...] = mixed[...].astype(jnp.bfloat16)
        for peer in range(count):
            row = pick_ref[peer]
            small_ref[peer, :per_row, :] = mixed[
                pl.ds(pl.multiple_of(row * per_row, per_row), per_row), :
            ].astype(jnp.bfloat16)
            news = []
            for which in range(2):
                for step in range(steps):
                    new = fresh[which, pl.ds(step * rows + row, 1), :]
                    news += [new[:, h * HD : (h + 1) * HD] for h in range(heads)]
            slot = dest_ref[row] - peer * rows
            slot = jnp.where((slot >= 0) & (slot < rows), slot, -1).astype(jnp.float32)
            news.append(jnp.full((1, HD), slot))
            fill = small_ref.shape[1] - per_row - 2 * steps * heads - 1
            news.append(jnp.full((fill, HD), length_ref[row].astype(jnp.float32)))
            small_ref[peer, per_row:, :] = jnp.concatenate(news, axis=0).astype(jnp.bfloat16)


def attend(kv_cache, queries, own, got, gain, lengths, destination, count, late, arrived):
    steps, rows, query_width = queries.shape
    capacity, lanes = kv_cache.shape[2:]
    heads = lanes // HD
    per_row = steps * query_width // HD
    block = 8
    small_rows = per_row + -(-(2 * steps * heads + 2) // TILE) * TILE
    small = jax.ShapeDtypeStruct((count, small_rows, HD), jnp.bfloat16)
    smem = pl.BlockSpec(memory_space=pltpu.SMEM)
    vmem = pl.BlockSpec(memory_space=pltpu.VMEM)
    hbm = pl.BlockSpec(memory_space=pl.ANY)
    cache_block = pl.BlockSpec((block, 2, capacity, lanes), lambda i: (i, 0, 0, 0))
    return pl.pallas_call(
        functools.partial(attend_kernel, count, late, block),
        grid=(rows // block,),
        out_shape=[
            jax.ShapeDtypeStruct(kv_cache.shape, kv_cache.dtype),
            jax.ShapeDtypeStruct((rows * per_row, HD), jnp.bfloat16),
            small,
        ]
        + [jax.ShapeDtypeStruct(kv_cache.shape[1:], kv_cache.dtype)] * len(late),
        in_specs=[smem, smem, vmem, vmem, vmem, vmem, cache_block, hbm],
        out_specs=[cache_block, vmem, vmem] + [vmem] * len(late),
        scratch_shapes=[
            pltpu.VMEM((2, steps * rows, lanes), jnp.float32),
            pltpu.VMEM((rows * per_row, HD), jnp.float32),
            pltpu.VMEM((rows * per_row // HD, HD, HD), jnp.float32),
            pltpu.VMEM((rows * per_row, HD), jnp.float32),
            pltpu.SMEM((count,), jnp.int32),
        ],
        compiler_params=pltpu.CompilerParams(vmem_limit_bytes=ATTEND_LIMIT),
        cost_estimate=HEAVY,
        name="attend",
    )(lengths, destination, own, got, gain, queries, kv_cache, arrived)


def read_facts(block):
    capacity = block.shape[1]
    facts = block[0, capacity - TILE :, :].astype(jnp.float32)[TILE - 1 :]
    return (
        jnp.max(facts[:, :HD]).astype(jnp.int32),
        jnp.max(facts[:, HD : 2 * HD]).astype(jnp.int32),
    )


def window_start(length, capacity):
    return pl.multiple_of(jnp.minimum(length // TILE * TILE, capacity - WINDOW), TILE)


def clean(block, length, out):
    capacity, lanes = block.shape[1:]
    kept = lax.broadcasted_iota(jnp.int32, (capacity, HD), 0) < length
    for which in range(2):
        for at in range(0, lanes, HD):
            stored = block[which, :, at : at + HD].astype(jnp.float32)
            out[which, :, at : at + HD] = jnp.where(kept, stored, 0.0).astype(jnp.bfloat16)


def insert(window, news, ahead, steps, out):
    height, lanes = window.shape[1:]
    heads = lanes // HD
    position = lax.broadcasted_iota(jnp.int32, (height, lanes), 0)
    for which in range(2):
        stored = window[which].astype(jnp.float32)
        for step in range(steps):
            at = (which * steps + step) * heads
            new = jnp.concatenate([news[at + h : at + h + 1] for h in range(heads)], axis=1)
            stored = jnp.where(position == ahead + step, new, stored)
        out[which] = stored.astype(jnp.bfloat16)


def land_kernel(pieces, *refs):
    blocks = refs[:pieces]
    _, out_ref, window_ref, buffer, sems, slots = refs[pieces:]
    capacity = buffer.shape[2]

    def store(piece):
        slot = jnp.maximum(slots[piece], 0)
        return pltpu.make_async_copy(buffer.at[piece], out_ref.at[slot], sems.at[piece])

    facts = [read_facts(block) for block in blocks]
    for piece, (slot, length) in enumerate(facts):
        slots[piece] = slot

        @pl.when(slot >= 0)
        def _():
            clean(blocks[piece], length, buffer.at[piece])
            store(piece).start()
            start = window_start(length, capacity)
            window_ref[piece] = buffer[piece, :, pl.ds(start, WINDOW), :]

    for piece in range(pieces):

        @pl.when(slots[piece] >= 0)
        def _():
            store(piece).wait()


def land(got, moved):
    pieces = len(got)
    vmem = pl.BlockSpec(memory_space=pltpu.VMEM)
    hbm = pl.BlockSpec(memory_space=pl.ANY)
    return pl.pallas_call(
        functools.partial(land_kernel, pieces),
        out_shape=[
            jax.ShapeDtypeStruct(moved.shape, moved.dtype),
            jax.ShapeDtypeStruct((pieces, 2, WINDOW, moved.shape[3]), moved.dtype),
        ],
        in_specs=[vmem] * pieces + [hbm],
        out_specs=[hbm, vmem],
        scratch_shapes=[
            pltpu.VMEM((pieces,) + moved.shape[1:], moved.dtype),
            pltpu.SemaphoreType.DMA((pieces,)),
            pltpu.SMEM((pieces,), jnp.int32),
        ],
        input_output_aliases={pieces: 0},
        compiler_params=pltpu.CompilerParams(vmem_limit_bytes=SMALL_LIMIT),
        cost_estimate=HEAVY,
        name="land",
    )(*got, moved)


def read_small(small_ref, peer, per_row, line):
    rows = small_ref[peer, per_row:, :].astype(jnp.float32)
    return jnp.max(rows[line : line + 1]).astype(jnp.int32)


def settle_kernel(
    count,
    early,
    group,
    mixed_ref,
    small_ref,
    window_ref,
    _,
    out_ref,
    moved_ref,
    mixed,
    windows,
    sems,
    slots,
    lengths,
):
    steps, rows, query_width = out_ref.shape
    per_row = steps * query_width // HD
    capacity, lanes = moved_ref.shape[2:]
    line = 2 * steps * (lanes // HD)
    me = lax.axis_index("inst")

    def store(piece):
        slot = jnp.maximum(slots[early[piece]], 0)
        start = window_start(lengths[early[piece]], capacity)
        return pltpu.make_async_copy(
            windows.at[piece], moved_ref.at[slot, :, pl.ds(start, WINDOW), :], sems.at[piece]
        )

    for shift in range(1, count):
        peer = peer_from(me, shift, count)
        slots[shift] = read_small(small_ref, peer, per_row, line)
        lengths[shift] = read_small(small_ref, peer, per_row, line + 1)

    for piece, shift in enumerate(early):

        @pl.when(slots[shift] >= 0)
        def _():
            peer = peer_from(me, shift, count)
            news = small_ref[peer, per_row:, :].astype(jnp.float32)
            ahead = lengths[shift] - window_start(lengths[shift], capacity)
            insert(window_ref.at[piece], news, ahead, steps, windows.at[piece])
            store(piece).start()

    mixed[...] = mixed_ref[...].astype(jnp.float32)
    for shift in range(1, count):

        @pl.when(slots[shift] >= 0)
        def _():
            mixed[pl.ds(pl.multiple_of(slots[shift] * per_row, per_row), per_row), :] = small_ref[
                peer_from(me, shift, count), :per_row, :
            ].astype(jnp.float32)

    for step in range(steps):
        for chunk in range(query_width // HD):
            head, member = chunk // group, chunk % group
            at = head * steps * group + step * group + member
            out_ref[step, :, chunk * HD : (chunk + 1) * HD] = mixed[
                pl.ds(at, rows, stride=per_row), :
            ].astype(jnp.bfloat16)

    for piece, shift in enumerate(early):

        @pl.when(slots[shift] >= 0)
        def _():
            store(piece).wait()


def settle(mixed, small, windows, moved, shape, group, count, early):
    vmem = pl.BlockSpec(memory_space=pltpu.VMEM)
    hbm = pl.BlockSpec(memory_space=pl.ANY)
    return pl.pallas_call(
        functools.partial(settle_kernel, count, early, group),
        out_shape=[
            jax.ShapeDtypeStruct(shape, jnp.bfloat16),
            jax.ShapeDtypeStruct(moved.shape, moved.dtype),
        ],
        in_specs=[vmem, vmem, vmem, hbm],
        out_specs=[vmem, hbm],
        scratch_shapes=[
            pltpu.VMEM(mixed.shape, jnp.float32),
            pltpu.VMEM(windows.shape, windows.dtype),
            pltpu.SemaphoreType.DMA((len(early),)),
            pltpu.SMEM((count,), jnp.int32),
            pltpu.SMEM((count,), jnp.int32),
        ],
        input_output_aliases={3: 1},
        compiler_params=pltpu.CompilerParams(vmem_limit_bytes=SMALL_LIMIT),
        cost_estimate=LIGHT,
        name="settle",
    )(mixed, small, windows, moved)


def finish_kernel(count, late, steps, *refs):
    blocks = refs[: len(late)]
    small_ref, _, out_ref, sems, slots = refs[len(late) :]
    line = 2 * steps * (out_ref.shape[3] // HD)
    facts = -(-(line + 2) // TILE) * TILE
    me = lax.axis_index("inst")

    def store(piece):
        slot = jnp.maximum(slots[piece], 0)
        return pltpu.make_async_copy(blocks[piece], out_ref.at[slot], sems.at[piece])

    for piece, shift in enumerate(late):
        peer = peer_from(me, shift, count)
        slots[piece] = read_small(small_ref, peer, small_ref.shape[1] - facts, line)
    for piece in range(len(late)):
        pl.when(slots[piece] >= 0)(store(piece).start)
    for piece in range(len(late)):
        pl.when(slots[piece] >= 0)(store(piece).wait)


def finish(got, small, moved, steps, count, late):
    vmem = pl.BlockSpec(memory_space=pltpu.VMEM)
    hbm = pl.BlockSpec(memory_space=pl.ANY)
    return pl.pallas_call(
        functools.partial(finish_kernel, count, late, steps),
        out_shape=jax.ShapeDtypeStruct(moved.shape, moved.dtype),
        in_specs=[vmem] * len(got) + [vmem, hbm],
        out_specs=hbm,
        scratch_shapes=[
            pltpu.SemaphoreType.DMA((len(got),)),
            pltpu.SMEM((len(got),), jnp.int32),
        ],
        input_output_aliases={len(got) + 1: 0},
        compiler_params=pltpu.CompilerParams(vmem_limit_bytes=SMALL_LIMIT),
        cost_estimate=LIGHT,
        name="finish",
    )(*got, small, moved)


def local(hidden_new, queries, kv_cache, lengths, destination, key_weight, value_weight, key_gain):
    steps = queries.shape[0]
    group = queries.shape[2] // kv_cache.shape[3]
    count = lax.axis_size("inst")
    half = max(count // 2, 1)
    early = list(range(half, count))
    late = list(range(half - 1, 0, -1))

    def send(block, shift):
        pairs = [(i, peer_to(i, shift, count)) for i in range(count)]
        return lax.ppermute(block, "inst", pairs)

    first = pack(kv_cache, destination, lengths, count, early[0])
    first_got = send(first, early[0])
    blocks, own, other = prepare(
        destination,
        lengths,
        hidden_new,
        kv_cache,
        key_weight,
        value_weight,
        count,
        early[1:],
    )
    early_got = [first_got] + [send(block, shift) for block, shift in zip(blocks, early[1:])]
    got = lax.ppermute(other, "tp", [(0, 1), (1, 0)])
    moved, mixed, small, *late_blocks = attend(
        kv_cache,
        queries,
        own,
        got,
        key_gain[None, :],
        lengths,
        destination,
        count,
        late,
        first_got,
    )
    late_got = [send(block, shift) for block, shift in zip(late_blocks, late)]
    small_got = lax.all_to_all(small, "inst", 0, 0, tiled=True)
    moved, windows = land(early_got, moved)
    attended, moved = settle(mixed, small_got, windows, moved, queries.shape, group, count, early)
    return attended, finish(late_got, small_got, moved, steps, count, late)


def solution(mesh):
    return jax.shard_map(
        local,
        mesh=mesh,
        in_specs=(
            P(None, ("group", "inst"), "tp"),
            P(None, ("group", "inst"), "tp"),
            P(("group", "inst"), None, None, "tp"),
            P(("group", "inst")),
            P(("group", "inst")),
            P("tp", None),
            P("tp", None),
            P(),
        ),
        out_specs=(P(None, ("group", "inst"), "tp"), P(("group", "inst"), None, None, "tp")),
        check_vma=False,
    )
```

```python
import functools
import math

import jax
import jax.numpy as jnp
from jax import lax
from jax.experimental import pallas as pl
from jax.experimental.pallas import tpu as pltpu
from jax.sharding import PartitionSpec as P

HD = 128
ROPE_BASE = 1000000.0
NORM_EPS = 1e-06
VMEM_LIMIT = 62 * 1024 * 1024
ATTEND_LIMIT = 50 * 1024 * 1024
PREPARE_LIMIT = 62 * 1024 * 1024
SMALL_LIMIT = 40 * 1024 * 1024
LIGHT = pl.CostEstimate(flops=1, bytes_accessed=1, transcendentals=0)
HEAVY = pl.CostEstimate(flops=1 << 36, bytes_accessed=1 << 28, transcendentals=0)
TILE = 16
WINDOW = 32


def quotient(value, divisor, bound):
    factor = -(-(1 << 16) // divisor)
    if bound * factor < 1 << 31 and all(
        (x * factor) >> 16 == x // divisor for x in range(bound)
    ):
        return (value * factor) >> 16
    return value // divisor


def peer_to(index, shift, count):
    return index ^ shift if count & (count - 1) == 0 else (index + shift) % count


def peer_from(index, shift, count):
    return index ^ shift if count & (count - 1) == 0 else (index + count - shift) % count


def pick_rows(count, dest_ref, pick_ref):
    rows = dest_ref.shape[0]
    for peer in range(count):
        pick_ref[peer] = 0
    for row in range(rows):
        pick_ref[quotient(dest_ref[row], rows, rows * count)] = row


def add_facts(block, peer, row, dest_ref, length_ref):
    capacity, lanes = block.shape[1:]
    rows = dest_ref.shape[0]
    slot = dest_ref[row] - peer * rows
    slot = jnp.where((slot >= 0) & (slot < rows), slot, -1)
    last = lax.broadcasted_iota(jnp.int32, (TILE, lanes), 0) == TILE - 1
    first_lanes = lax.broadcasted_iota(jnp.int32, (TILE, lanes), 1) < HD
    facts = jnp.where(first_lanes, slot, length_ref[row]).astype(jnp.float32)
    end = block[0, capacity - TILE :, :].astype(jnp.float32)
    block[0, capacity - TILE :, :] = jnp.where(last, facts, end).astype(jnp.bfloat16)


def prepare_kernel(
    count, early, chunks, dest_ref, length_ref, hidden_ref, kv_ref, key_ref, value_ref, *refs
):
    block_refs = refs[: len(early)]
    own_ref, other_ref, blocks, hidden_held, held, total = refs[len(early) : len(early) + 6]
    in_sems, out_sems, hidden_sem, weight_sems, pick_ref = refs[len(early) + 6 :]
    steps, rows, depth = hidden_ref.shape
    width = key_ref.shape[1]
    part = depth // chunks
    me = lax.axis_index("inst")

    def weights(chunk):
        span = pl.ds(chunk * part, part)
        return [
            pltpu.make_async_copy(ref.at[span], held.at[which, span], weight_sems.at[chunk, which])
            for which, ref in enumerate((key_ref, value_ref))
        ]

    hidden_copy = pltpu.make_async_copy(hidden_ref, hidden_held, hidden_sem)
    hidden_copy.start()
    for copy in weights(0):
        copy.start()
    pick_rows(count, dest_ref, pick_ref)
    fetches, stores = [], []
    for piece, shift in enumerate(early):
        row = pick_ref[peer_to(me, shift, count)]
        fetches.append(
            pltpu.make_async_copy(kv_ref.at[row], blocks.at[piece], in_sems.at[piece])
        )
        fetches[-1].start()
    for chunk in range(1, chunks):
        for copy in weights(chunk):
            copy.start()

    for piece, shift in enumerate(early):
        peer = peer_to(me, shift, count)
        fetches[piece].wait()
        add_facts(blocks.at[piece], peer, pick_ref[peer], dest_ref, length_ref)
        stores.append(
            pltpu.make_async_copy(blocks.at[piece], block_refs[piece], out_sems.at[piece])
        )
        stores[-1].start()
    hidden_copy.wait()
    hidden = hidden_held[...].reshape(steps * rows, depth)
    sums = [None, None]
    for chunk in range(chunks):
        for which, copy in enumerate(weights(chunk)):
            copy.wait()
            product = jnp.dot(
                hidden[:, chunk * part : (chunk + 1) * part],
                held[which, chunk * part : (chunk + 1) * part, :],
                preferred_element_type=jnp.float32,
            )
            sums[which] = product if chunk == 0 else sums[which] + product
    total[:, :width] = sums[0]
    total[:, width:] = sums[1]
    half = width // 2
    core = lax.axis_index("tp")
    for ref, place in ((own_ref, core), (other_ref, 1 - core)):
        at = pl.multiple_of(place * half, half)
        ref[:, :half] = total[:, pl.ds(at, half)]
        ref[:, half:] = total[:, pl.ds(pl.multiple_of(width + at, half), half)]

    for copy in stores:
        copy.wait()


def prepare(destination, lengths, hidden_new, kv_cache, key_weight, value_weight, count, early):
    steps, rows, depth = hidden_new.shape
    width = key_weight.shape[1]
    chunks = 5
    part = jax.ShapeDtypeStruct((steps * rows, width), jnp.float32)
    smem = pl.BlockSpec(memory_space=pltpu.SMEM)
    vmem = pl.BlockSpec(memory_space=pltpu.VMEM)
    hbm = pl.BlockSpec(memory_space=pl.ANY)
    outs = pl.pallas_call(
        functools.partial(prepare_kernel, count, early, chunks),
        out_shape=[jax.ShapeDtypeStruct(kv_cache.shape[1:], kv_cache.dtype)] * len(early)
        + [part, part],
        in_specs=[smem, smem, hbm, hbm, hbm, hbm],
        out_specs=[hbm] * len(early) + [vmem, vmem],
        scratch_shapes=[
            pltpu.VMEM((len(early),) + kv_cache.shape[1:], kv_cache.dtype),
            pltpu.VMEM(hidden_new.shape, hidden_new.dtype),
            pltpu.VMEM((2, depth, width), key_weight.dtype),
            pltpu.VMEM((steps * rows, 2 * width), jnp.float32),
            pltpu.SemaphoreType.DMA((len(early),)),
            pltpu.SemaphoreType.DMA((len(early),)),
            pltpu.SemaphoreType.DMA,
            pltpu.SemaphoreType.DMA((chunks, 2)),
            pltpu.SMEM((count,), jnp.int32),
        ],
        compiler_params=pltpu.CompilerParams(vmem_limit_bytes=PREPARE_LIMIT),
        cost_estimate=LIGHT,
        name="prepare",
    )(destination, lengths, hidden_new, kv_cache, key_weight, value_weight)
    return outs[: len(early)], *outs[len(early) :]


def rotation(length_ref, steps, rows):
    half = HD // 2
    line = lax.broadcasted_iota(jnp.int32, (rows, HD), 0)
    lane = lax.broadcasted_iota(jnp.int32, (steps * rows, HD), 1)
    length = jnp.zeros((rows, HD), jnp.int32)
    for row in range(rows):
        length = jnp.where(line == row, length_ref[row], length)
    position = jnp.concatenate([length + step for step in range(steps)], axis=0)
    order = (lane % half).astype(jnp.float32)
    angle = position.astype(jnp.float32) * jnp.exp(-math.log(ROPE_BASE) * 2.0 * order / HD)
    turns = jnp.floor(angle * (1.0 / math.pi) + 0.5)
    rest = ((angle - turns * 3.140625) - turns * 9.67502593994140625e-4) - turns * 1.5099579909783e-7
    sign = 1.0 - 2.0 * (turns - 2.0 * jnp.floor(turns * 0.5))
    square = rest * rest
    cosine, sine = jnp.ones_like(rest), jnp.ones_like(rest)
    for power in range(6, 0, -1):
        cosine = 1.0 - cosine * square * (1.0 / ((2 * power - 1) * (2 * power)))
        sine = 1.0 - sine * square * (1.0 / ((2 * power) * (2 * power + 1)))
    sine = sign * rest * sine
    return sign * cosine, jnp.where(lane < half, -sine, sine)


def attend_kernel(
    count,
    late,
    block,
    length_ref,
    dest_ref,
    own_ref,
    got_ref,
    gain_ref,
    query_ref,
    kv_ref,
    *refs,
):
    moved_ref, mixed_ref, small_ref = refs[:3]
    late_refs = refs[3:-5]
    fresh, query_rows, query_columns, mixed, pick_ref = refs[-5:]
    part = pl.program_id(0)
    steps, rows, query_width = query_ref.shape
    capacity, lanes = kv_ref.shape[2:]
    heads = lanes // HD
    group = query_width // lanes
    per_head = steps * group
    per_row = heads * per_head
    team = HD // per_row

    @pl.when(part == 0)
    def _():
        pick_rows(count, dest_ref, pick_ref)
        raw = own_ref[...] + got_ref[...]
        cosine, sine = rotation(length_ref, steps, rows)
        gain = gain_ref[...].astype(jnp.float32)
        for head in range(heads):
            at = slice(head * HD, (head + 1) * HD)
            piece = raw[:, at]
            mean = jnp.mean(piece * piece, axis=-1, keepdims=True)
            piece = piece * lax.rsqrt(mean + NORM_EPS) * gain
            swapped = jnp.concatenate([piece[:, HD // 2 :], piece[:, : HD // 2]], axis=1)
            turned = piece * cosine + swapped * sine
            fresh[0, :, at] = turned.astype(jnp.bfloat16).astype(jnp.float32)
        fresh[1] = raw[:, lanes:].astype(jnp.bfloat16).astype(jnp.float32)
        for step in range(steps):
            for chunk in range(query_width // HD):
                head, member = chunk // group, chunk % group
                at = head * per_head + step * group + member
                query_rows[pl.ds(at, rows, stride=per_row), :] = query_ref[
                    step, :, chunk * HD : (chunk + 1) * HD
                ].astype(jnp.float32)
        for index in range(rows // team):
            query_columns[index] = query_rows[index * HD : (index + 1) * HD, :].T

    position = lax.broadcasted_iota(jnp.int32, (capacity, HD), 0)
    column = lax.broadcasted_iota(jnp.int32, (capacity, HD), 1)
    column_item = column // per_row
    column_step = (column % per_head) // group
    column_head = lax.broadcasted_iota(jnp.int32, (HD, HD), 1) % per_row // per_head
    factor = 1.0 / math.sqrt(HD)
    teams = range(block // team)
    scores = []
    for index in teams:
        queries = query_columns[part * (block // team) + index]
        queries = jnp.concatenate(
            [jnp.where(column_head == head, queries, 0.0) for head in range(heads)], axis=0
        ).astype(jnp.bfloat16)
        score, limit = None, None
        for member in range(team):
            item = index * team + member
            row = part * block + item
            length = length_ref[row]
            kept = position < length
            landing = [position == length + step for step in range(steps)]
            for which in range(2):
                news = [fresh[which, pl.ds(step * rows + row, 1), :] for step in range(steps)]
                for head in range(heads):
                    at = slice(head * HD, (head + 1) * HD)
                    stored = jnp.where(kept, kv_ref[item, which, :, at].astype(jnp.float32), 0.0)
                    for step in range(steps):
                        stored = jnp.where(landing[step], news[step][:, at], stored)
                    moved_ref[item, which, :, at] = stored.astype(jnp.bfloat16)
            one = jnp.dot(moved_ref[item, 0], queries, preferred_element_type=jnp.float32)
            score = one if member == 0 else jnp.where(column_item == member, one, score)
            limit = length if member == 0 else jnp.where(column_item == member, length, limit)
        scores.append(jnp.where(position <= limit + column_step, score * factor, -jnp.inf))
    weights = []
    for score in scores:
        raised = jnp.exp(score - jnp.max(score, axis=0, keepdims=True))
        normaliser = jnp.sum(raised, axis=0, keepdims=True)
        weights.append((raised / normaliser).T.astype(jnp.bfloat16))
    for index in teams:
        for member in range(team):
            item = index * team + member
            row = part * block + item
            result = jnp.dot(
                weights[index][member * per_row : (member + 1) * per_row],
                moved_ref[item, 1],
                preferred_element_type=jnp.float32,
            )
            for head in range(heads):
                at = pl.multiple_of(row * per_row + head * per_head, per_head)
                mixed[pl.ds(at, per_head), :] = result[
                    head * per_head : (head + 1) * per_head, head * HD : (head + 1) * HD
                ]

    me = lax.axis_index("inst")
    for late_ref, shift in zip(late_refs, late):
        item = pick_ref[peer_to(me, shift, count)] - part * block

        @pl.when((item >= 0) & (item < block))
        def _():
            late_ref[...] = moved_ref[item]

    @pl.when(part == pl.num_programs(0) - 1)
    def _():
        mixed_ref[...] = mixed[...].astype(jnp.bfloat16)
        for peer in range(count):
            row = pick_ref[peer]
            small_ref[peer, :per_row, :] = mixed[
                pl.ds(pl.multiple_of(row * per_row, per_row), per_row), :
            ].astype(jnp.bfloat16)
            news = []
            for which in range(2):
                for step in range(steps):
                    new = fresh[which, pl.ds(step * rows + row, 1), :]
                    news += [new[:, h * HD : (h + 1) * HD] for h in range(heads)]
            slot = dest_ref[row] - peer * rows
            slot = jnp.where((slot >= 0) & (slot < rows), slot, -1).astype(jnp.float32)
            news.append(jnp.full((1, HD), slot))
            fill = small_ref.shape[1] - per_row - 2 * steps * heads - 1
            news.append(jnp.full((fill, HD), length_ref[row].astype(jnp.float32)))
            small_ref[peer, per_row:, :] = jnp.concatenate(news, axis=0).astype(jnp.bfloat16)


def attend(kv_cache, queries, own, got, gain, lengths, destination, count, late):
    steps, rows, query_width = queries.shape
    capacity, lanes = kv_cache.shape[2:]
    heads = lanes // HD
    per_row = steps * query_width // HD
    block = 8
    small_rows = per_row + -(-(2 * steps * heads + 2) // TILE) * TILE
    small = jax.ShapeDtypeStruct((count, small_rows, HD), jnp.bfloat16)
    smem = pl.BlockSpec(memory_space=pltpu.SMEM)
    vmem = pl.BlockSpec(memory_space=pltpu.VMEM)
    cache_block = pl.BlockSpec((block, 2, capacity, lanes), lambda i: (i, 0, 0, 0))
    return pl.pallas_call(
        functools.partial(attend_kernel, count, late, block),
        grid=(rows // block,),
        out_shape=[
            jax.ShapeDtypeStruct(kv_cache.shape, kv_cache.dtype),
            jax.ShapeDtypeStruct((rows * per_row, HD), jnp.bfloat16),
            small,
        ]
        + [jax.ShapeDtypeStruct(kv_cache.shape[1:], kv_cache.dtype)] * len(late),
        in_specs=[smem, smem, vmem, vmem, vmem, vmem, cache_block],
        out_specs=[cache_block, vmem, vmem] + [vmem] * len(late),
        scratch_shapes=[
            pltpu.VMEM((2, steps * rows, lanes), jnp.float32),
            pltpu.VMEM((rows * per_row, HD), jnp.float32),
            pltpu.VMEM((rows * per_row // HD, HD, HD), jnp.float32),
            pltpu.VMEM((rows * per_row, HD), jnp.float32),
            pltpu.SMEM((count,), jnp.int32),
        ],
        compiler_params=pltpu.CompilerParams(vmem_limit_bytes=ATTEND_LIMIT),
        cost_estimate=HEAVY,
        name="attend",
    )(lengths, destination, own, got, gain, queries, kv_cache)


def read_facts(block):
    capacity = block.shape[1]
    facts = block[0, capacity - TILE :, :].astype(jnp.float32)[TILE - 1 :]
    return (
        jnp.max(facts[:, :HD]).astype(jnp.int32),
        jnp.max(facts[:, HD : 2 * HD]).astype(jnp.int32),
    )


def window_start(length, capacity):
    return pl.multiple_of(jnp.minimum(length // TILE * TILE, capacity - WINDOW), TILE)


def clean(block, length, out):
    capacity, lanes = block.shape[1:]
    kept = lax.broadcasted_iota(jnp.int32, (capacity, HD), 0) < length
    for which in range(2):
        for at in range(0, lanes, HD):
            stored = block[which, :, at : at + HD].astype(jnp.float32)
            out[which, :, at : at + HD] = jnp.where(kept, stored, 0.0).astype(jnp.bfloat16)


def insert(window, news, ahead, steps, out):
    height, lanes = window.shape[1:]
    heads = lanes // HD
    position = lax.broadcasted_iota(jnp.int32, (height, lanes), 0)
    for which in range(2):
        stored = window[which].astype(jnp.float32)
        for step in range(steps):
            at = (which * steps + step) * heads
            new = jnp.concatenate([news[at + h : at + h + 1] for h in range(heads)], axis=1)
            stored = jnp.where(position == ahead + step, new, stored)
        out[which] = stored.astype(jnp.bfloat16)


def land_kernel(pieces, *refs):
    blocks = refs[:pieces]
    _, out_ref, window_ref, buffer, sems, slots = refs[pieces:]
    capacity = buffer.shape[2]

    def store(piece):
        slot = jnp.maximum(slots[piece], 0)
        return pltpu.make_async_copy(buffer.at[piece], out_ref.at[slot], sems.at[piece])

    facts = [read_facts(block) for block in blocks]
    for piece, (slot, length) in enumerate(facts):
        slots[piece] = slot

        @pl.when(slot >= 0)
        def _():
            clean(blocks[piece], length, buffer.at[piece])
            store(piece).start()
            start = window_start(length, capacity)
            window_ref[piece] = buffer[piece, :, pl.ds(start, WINDOW), :]

    for piece in range(pieces):

        @pl.when(slots[piece] >= 0)
        def _():
            store(piece).wait()


def land(got, moved):
    pieces = len(got)
    vmem = pl.BlockSpec(memory_space=pltpu.VMEM)
    hbm = pl.BlockSpec(memory_space=pl.ANY)
    return pl.pallas_call(
        functools.partial(land_kernel, pieces),
        out_shape=[
            jax.ShapeDtypeStruct(moved.shape, moved.dtype),
            jax.ShapeDtypeStruct((pieces, 2, WINDOW, moved.shape[3]), moved.dtype),
        ],
        in_specs=[vmem] * pieces + [hbm],
        out_specs=[hbm, vmem],
        scratch_shapes=[
            pltpu.VMEM((pieces,) + moved.shape[1:], moved.dtype),
            pltpu.SemaphoreType.DMA((pieces,)),
            pltpu.SMEM((pieces,), jnp.int32),
        ],
        input_output_aliases={pieces: 0},
        compiler_params=pltpu.CompilerParams(vmem_limit_bytes=SMALL_LIMIT),
        cost_estimate=HEAVY,
        name="land",
    )(*got, moved)


def read_small(small_ref, peer, per_row, line):
    rows = small_ref[peer, per_row:, :].astype(jnp.float32)
    return jnp.max(rows[line : line + 1]).astype(jnp.int32)


def settle_kernel(
    count,
    early,
    group,
    mixed_ref,
    small_ref,
    window_ref,
    _,
    out_ref,
    moved_ref,
    mixed,
    windows,
    sems,
    slots,
    lengths,
):
    steps, rows, query_width = out_ref.shape
    per_row = steps * query_width // HD
    capacity, lanes = moved_ref.shape[2:]
    line = 2 * steps * (lanes // HD)
    me = lax.axis_index("inst")

    def store(piece):
        slot = jnp.maximum(slots[early[piece]], 0)
        start = window_start(lengths[early[piece]], capacity)
        return pltpu.make_async_copy(
            windows.at[piece], moved_ref.at[slot, :, pl.ds(start, WINDOW), :], sems.at[piece]
        )

    for shift in range(1, count):
        peer = peer_from(me, shift, count)
        slots[shift] = read_small(small_ref, peer, per_row, line)
        lengths[shift] = read_small(small_ref, peer, per_row, line + 1)

    for piece, shift in enumerate(early):

        @pl.when(slots[shift] >= 0)
        def _():
            peer = peer_from(me, shift, count)
            news = small_ref[peer, per_row:, :].astype(jnp.float32)
            ahead = lengths[shift] - window_start(lengths[shift], capacity)
            insert(window_ref.at[piece], news, ahead, steps, windows.at[piece])
            store(piece).start()

    mixed[...] = mixed_ref[...].astype(jnp.float32)
    for shift in range(1, count):

        @pl.when(slots[shift] >= 0)
        def _():
            mixed[pl.ds(pl.multiple_of(slots[shift] * per_row, per_row), per_row), :] = small_ref[
                peer_from(me, shift, count), :per_row, :
            ].astype(jnp.float32)

    for step in range(steps):
        for chunk in range(query_width // HD):
            head, member = chunk // group, chunk % group
            at = head * steps * group + step * group + member
            out_ref[step, :, chunk * HD : (chunk + 1) * HD] = mixed[
                pl.ds(at, rows, stride=per_row), :
            ].astype(jnp.bfloat16)

    for piece, shift in enumerate(early):

        @pl.when(slots[shift] >= 0)
        def _():
            store(piece).wait()


def settle(mixed, small, windows, moved, shape, group, count, early):
    vmem = pl.BlockSpec(memory_space=pltpu.VMEM)
    hbm = pl.BlockSpec(memory_space=pl.ANY)
    return pl.pallas_call(
        functools.partial(settle_kernel, count, early, group),
        out_shape=[
            jax.ShapeDtypeStruct(shape, jnp.bfloat16),
            jax.ShapeDtypeStruct(moved.shape, moved.dtype),
        ],
        in_specs=[vmem, vmem, vmem, hbm],
        out_specs=[vmem, hbm],
        scratch_shapes=[
            pltpu.VMEM(mixed.shape, jnp.float32),
            pltpu.VMEM(windows.shape, windows.dtype),
            pltpu.SemaphoreType.DMA((len(early),)),
            pltpu.SMEM((count,), jnp.int32),
            pltpu.SMEM((count,), jnp.int32),
        ],
        input_output_aliases={3: 1},
        compiler_params=pltpu.CompilerParams(vmem_limit_bytes=SMALL_LIMIT),
        cost_estimate=LIGHT,
        name="settle",
    )(mixed, small, windows, moved)


def finish_kernel(count, late, steps, *refs):
    blocks = refs[: len(late)]
    small_ref, _, out_ref, sems, slots = refs[len(late) :]
    line = 2 * steps * (out_ref.shape[3] // HD)
    facts = -(-(line + 2) // TILE) * TILE
    me = lax.axis_index("inst")

    def store(piece):
        slot = jnp.maximum(slots[piece], 0)
        return pltpu.make_async_copy(blocks[piece], out_ref.at[slot], sems.at[piece])

    for piece, shift in enumerate(late):
        peer = peer_from(me, shift, count)
        slots[piece] = read_small(small_ref, peer, small_ref.shape[1] - facts, line)
    for piece in range(len(late)):
        pl.when(slots[piece] >= 0)(store(piece).start)
    for piece in range(len(late)):
        pl.when(slots[piece] >= 0)(store(piece).wait)


def finish(got, small, moved, steps, count, late):
    vmem = pl.BlockSpec(memory_space=pltpu.VMEM)
    hbm = pl.BlockSpec(memory_space=pl.ANY)
    return pl.pallas_call(
        functools.partial(finish_kernel, count, late, steps),
        out_shape=jax.ShapeDtypeStruct(moved.shape, moved.dtype),
        in_specs=[vmem] * len(got) + [vmem, hbm],
        out_specs=hbm,
        scratch_shapes=[
            pltpu.SemaphoreType.DMA((len(got),)),
            pltpu.SMEM((len(got),), jnp.int32),
        ],
        input_output_aliases={len(got) + 1: 0},
        compiler_params=pltpu.CompilerParams(vmem_limit_bytes=SMALL_LIMIT),
        cost_estimate=LIGHT,
        name="finish",
    )(*got, small, moved)


def local(hidden_new, queries, kv_cache, lengths, destination, key_weight, value_weight, key_gain):
    steps = queries.shape[0]
    group = queries.shape[2] // kv_cache.shape[3]
    count = lax.axis_size("inst")
    half = max(count // 2, 1)
    early = list(range(half, count - 1)) + [half - 1] * (half > 1)
    late = [count - 1] + list(range(half - 2, 0, -1))

    def send(block, shift):
        pairs = [(i, peer_to(i, shift, count)) for i in range(count)]
        return lax.ppermute(block, "inst", pairs)

    blocks, own, other = prepare(
        destination, lengths, hidden_new, kv_cache, key_weight, value_weight, count, early
    )
    early_got = [send(block, shift) for block, shift in zip(blocks, early)]
    got = lax.ppermute(other, "tp", [(0, 1), (1, 0)])
    moved, mixed, small, *late_blocks = attend(
        kv_cache,
        queries,
        own,
        got,
        key_gain[None, :],
        lengths,
        destination,
        count,
        late,
    )
    late_got = [send(block, shift) for block, shift in zip(late_blocks, late)]
    small_got = lax.all_to_all(small, "inst", 0, 0, tiled=True)
    moved, windows = land(early_got, moved)
    attended, moved = settle(mixed, small_got, windows, moved, queries.shape, group, count, early)
    return attended, finish(late_got, small_got, moved, steps, count, late)


def solution(mesh):
    return jax.shard_map(
        local,
        mesh=mesh,
        in_specs=(
            P(None, ("group", "inst"), "tp"),
            P(None, ("group", "inst"), "tp"),
            P(("group", "inst"), None, None, "tp"),
            P(("group", "inst")),
            P(("group", "inst")),
            P("tp", None),
            P("tp", None),
            P(),
        ),
        out_specs=(P(None, ("group", "inst"), "tp"), P(("group", "inst"), None, None, "tp")),
        check_vma=False,
    )
```

```python
import functools
import math

import jax
import jax.numpy as jnp
from jax import lax
from jax.experimental import pallas as pl
from jax.experimental.pallas import tpu as pltpu
from jax.sharding import PartitionSpec as P

HD = 128
ROPE_BASE = 1000000.0
NORM_EPS = 1e-06
VMEM_LIMIT = 62 * 1024 * 1024
ATTEND_LIMIT = 50 * 1024 * 1024
PREPARE_LIMIT = 62 * 1024 * 1024
SMALL_LIMIT = 40 * 1024 * 1024
LIGHT = pl.CostEstimate(flops=1, bytes_accessed=1, transcendentals=0)
HEAVY = pl.CostEstimate(flops=1 << 36, bytes_accessed=1 << 28, transcendentals=0)
TILE = 16
WINDOW = 32


def quotient(value, divisor, bound):
    factor = -(-(1 << 16) // divisor)
    if bound * factor < 1 << 31 and all(
        (x * factor) >> 16 == x // divisor for x in range(bound)
    ):
        return (value * factor) >> 16
    return value // divisor


def peer_to(index, shift, count):
    return index ^ shift if count & (count - 1) == 0 else (index + shift) % count


def peer_from(index, shift, count):
    return index ^ shift if count & (count - 1) == 0 else (index + count - shift) % count


def pick_rows(count, dest_ref, pick_ref):
    rows = dest_ref.shape[0]
    for peer in range(count):
        pick_ref[peer] = 0
    for row in range(rows):
        pick_ref[quotient(dest_ref[row], rows, rows * count)] = row


def add_facts(block, peer, row, dest_ref, length_ref):
    capacity, lanes = block.shape[1:]
    rows = dest_ref.shape[0]
    slot = dest_ref[row] - peer * rows
    slot = jnp.where((slot >= 0) & (slot < rows), slot, -1)
    last = lax.broadcasted_iota(jnp.int32, (TILE, lanes), 0) == TILE - 1
    first_lanes = lax.broadcasted_iota(jnp.int32, (TILE, lanes), 1) < HD
    facts = jnp.where(first_lanes, slot, length_ref[row]).astype(jnp.float32)
    end = block[0, capacity - TILE :, :].astype(jnp.float32)
    block[0, capacity - TILE :, :] = jnp.where(last, facts, end).astype(jnp.bfloat16)


def prepare_kernel(
    count, early, chunks, dest_ref, length_ref, hidden_ref, kv_ref, key_ref, value_ref, *refs
):
    block_refs = refs[: len(early)]
    own_ref, other_ref, blocks, hidden_held, held, total = refs[len(early) : len(early) + 6]
    in_sems, out_sems, hidden_sem, weight_sems, pick_ref = refs[len(early) + 6 :]
    steps, rows, depth = hidden_ref.shape
    width = key_ref.shape[1]
    part = depth // chunks
    me = lax.axis_index("inst")

    def weights(chunk):
        span = pl.ds(chunk * part, part)
        return [
            pltpu.make_async_copy(ref.at[span], held.at[which, span], weight_sems.at[chunk, which])
            for which, ref in enumerate((key_ref, value_ref))
        ]

    hidden_copy = pltpu.make_async_copy(hidden_ref, hidden_held, hidden_sem)
    hidden_copy.start()
    for copy in weights(0):
        copy.start()
    pick_rows(count, dest_ref, pick_ref)
    fetches, stores = [], []
    for piece, shift in enumerate(early):
        row = pick_ref[peer_to(me, shift, count)]
        fetches.append(
            pltpu.make_async_copy(kv_ref.at[row], blocks.at[piece], in_sems.at[piece])
        )
        fetches[-1].start()
    for chunk in range(1, chunks):
        for copy in weights(chunk):
            copy.start()

    for piece, shift in enumerate(early):
        peer = peer_to(me, shift, count)
        fetches[piece].wait()
        add_facts(blocks.at[piece], peer, pick_ref[peer], dest_ref, length_ref)
        stores.append(
            pltpu.make_async_copy(blocks.at[piece], block_refs[piece], out_sems.at[piece])
        )
        stores[-1].start()
    hidden_copy.wait()
    hidden = hidden_held[...].reshape(steps * rows, depth)
    sums = [None, None]
    for chunk in range(chunks):
        for which, copy in enumerate(weights(chunk)):
            copy.wait()
            product = jnp.dot(
                hidden[:, chunk * part : (chunk + 1) * part],
                held[which, chunk * part : (chunk + 1) * part, :],
                preferred_element_type=jnp.float32,
            )
            sums[which] = product if chunk == 0 else sums[which] + product
    total[:, :width] = sums[0]
    total[:, width:] = sums[1]
    half = width // 2
    core = lax.axis_index("tp")
    for ref, place in ((own_ref, core), (other_ref, 1 - core)):
        at = pl.multiple_of(place * half, half)
        ref[:, :half] = total[:, pl.ds(at, half)]
        ref[:, half:] = total[:, pl.ds(pl.multiple_of(width + at, half), half)]

    for copy in stores:
        copy.wait()


def prepare(destination, lengths, hidden_new, kv_cache, key_weight, value_weight, count, early):
    steps, rows, depth = hidden_new.shape
    width = key_weight.shape[1]
    chunks = 5
    part = jax.ShapeDtypeStruct((steps * rows, width), jnp.float32)
    smem = pl.BlockSpec(memory_space=pltpu.SMEM)
    vmem = pl.BlockSpec(memory_space=pltpu.VMEM)
    hbm = pl.BlockSpec(memory_space=pl.ANY)
    outs = pl.pallas_call(
        functools.partial(prepare_kernel, count, early, chunks),
        out_shape=[jax.ShapeDtypeStruct(kv_cache.shape[1:], kv_cache.dtype)] * len(early)
        + [part, part],
        in_specs=[smem, smem, hbm, hbm, hbm, hbm],
        out_specs=[hbm] * len(early) + [vmem, vmem],
        scratch_shapes=[
            pltpu.VMEM((len(early),) + kv_cache.shape[1:], kv_cache.dtype),
            pltpu.VMEM(hidden_new.shape, hidden_new.dtype),
            pltpu.VMEM((2, depth, width), key_weight.dtype),
            pltpu.VMEM((steps * rows, 2 * width), jnp.float32),
            pltpu.SemaphoreType.DMA((len(early),)),
            pltpu.SemaphoreType.DMA((len(early),)),
            pltpu.SemaphoreType.DMA,
            pltpu.SemaphoreType.DMA((chunks, 2)),
            pltpu.SMEM((count,), jnp.int32),
        ],
        compiler_params=pltpu.CompilerParams(vmem_limit_bytes=PREPARE_LIMIT),
        cost_estimate=LIGHT,
        name="prepare",
    )(destination, lengths, hidden_new, kv_cache, key_weight, value_weight)
    return outs[: len(early)], *outs[len(early) :]


def rotation(length_ref, steps, rows):
    half = HD // 2
    line = lax.broadcasted_iota(jnp.int32, (rows, HD), 0)
    lane = lax.broadcasted_iota(jnp.int32, (steps * rows, HD), 1)
    length = jnp.zeros((rows, HD), jnp.int32)
    for row in range(rows):
        length = jnp.where(line == row, length_ref[row], length)
    position = jnp.concatenate([length + step for step in range(steps)], axis=0)
    order = (lane % half).astype(jnp.float32)
    angle = position.astype(jnp.float32) * jnp.exp(-math.log(ROPE_BASE) * 2.0 * order / HD)
    turns = jnp.floor(angle * (1.0 / math.pi) + 0.5)
    rest = ((angle - turns * 3.140625) - turns * 9.67502593994140625e-4) - turns * 1.5099579909783e-7
    sign = 1.0 - 2.0 * (turns - 2.0 * jnp.floor(turns * 0.5))
    square = rest * rest
    cosine, sine = jnp.ones_like(rest), jnp.ones_like(rest)
    for power in range(6, 0, -1):
        cosine = 1.0 - cosine * square * (1.0 / ((2 * power - 1) * (2 * power)))
        sine = 1.0 - sine * square * (1.0 / ((2 * power) * (2 * power + 1)))
    sine = sign * rest * sine
    return sign * cosine, jnp.where(lane < half, -sine, sine)


def attend_kernel(
    count,
    late,
    block,
    length_ref,
    dest_ref,
    own_ref,
    got_ref,
    gain_ref,
    query_ref,
    kv_ref,
    *refs,
):
    moved_ref, mixed_ref, small_ref = refs[:3]
    late_refs = refs[3:-5]
    fresh, query_rows, query_columns, mixed, pick_ref = refs[-5:]
    part = pl.program_id(0)
    steps, rows, query_width = query_ref.shape
    capacity, lanes = kv_ref.shape[2:]
    heads = lanes // HD
    group = query_width // lanes
    per_head = steps * group
    per_row = heads * per_head
    team = HD // per_row

    @pl.when(part == 0)
    def _():
        pick_rows(count, dest_ref, pick_ref)
        raw = own_ref[...] + got_ref[...]
        cosine, sine = rotation(length_ref, steps, rows)
        gain = gain_ref[...].astype(jnp.float32)
        for head in range(heads):
            at = slice(head * HD, (head + 1) * HD)
            piece = raw[:, at]
            mean = jnp.mean(piece * piece, axis=-1, keepdims=True)
            piece = piece * lax.rsqrt(mean + NORM_EPS) * gain
            swapped = jnp.concatenate([piece[:, HD // 2 :], piece[:, : HD // 2]], axis=1)
            turned = piece * cosine + swapped * sine
            fresh[0, :, at] = turned.astype(jnp.bfloat16).astype(jnp.float32)
        fresh[1] = raw[:, lanes:].astype(jnp.bfloat16).astype(jnp.float32)
        for step in range(steps):
            for chunk in range(query_width // HD):
                head, member = chunk // group, chunk % group
                at = head * per_head + step * group + member
                query_rows[pl.ds(at, rows, stride=per_row), :] = query_ref[
                    step, :, chunk * HD : (chunk + 1) * HD
                ].astype(jnp.float32)
        for index in range(rows // team):
            query_columns[index] = query_rows[index * HD : (index + 1) * HD, :].T

    position = lax.broadcasted_iota(jnp.int32, (capacity, HD), 0)
    column = lax.broadcasted_iota(jnp.int32, (capacity, HD), 1)
    column_item = column // per_row
    column_step = (column % per_head) // group
    column_head = lax.broadcasted_iota(jnp.int32, (HD, HD), 1) % per_row // per_head
    factor = 1.0 / math.sqrt(HD)
    teams = range(block // team)
    scores = []
    for index in teams:
        queries = query_columns[part * (block // team) + index]
        queries = jnp.concatenate(
            [jnp.where(column_head == head, queries, 0.0) for head in range(heads)], axis=0
        ).astype(jnp.bfloat16)
        score, limit = None, None
        for member in range(team):
            item = index * team + member
            row = part * block + item
            length = length_ref[row]
            kept = position < length
            landing = [position == length + step for step in range(steps)]
            for which in range(2):
                news = [fresh[which, pl.ds(step * rows + row, 1), :] for step in range(steps)]
                for head in range(heads):
                    at = slice(head * HD, (head + 1) * HD)
                    stored = jnp.where(kept, kv_ref[item, which, :, at].astype(jnp.float32), 0.0)
                    for step in range(steps):
                        stored = jnp.where(landing[step], news[step][:, at], stored)
                    moved_ref[item, which, :, at] = stored.astype(jnp.bfloat16)
            one = jnp.dot(moved_ref[item, 0], queries, preferred_element_type=jnp.float32)
            score = one if member == 0 else jnp.where(column_item == member, one, score)
            limit = length if member == 0 else jnp.where(column_item == member, length, limit)
        scores.append(jnp.where(position <= limit + column_step, score * factor, -jnp.inf))
    weights = []
    for score in scores:
        raised = jnp.exp(score - jnp.max(score, axis=0, keepdims=True))
        normaliser = jnp.sum(raised, axis=0, keepdims=True)
        weights.append((raised / normaliser).T.astype(jnp.bfloat16))
    for index in teams:
        for member in range(team):
            item = index * team + member
            row = part * block + item
            result = jnp.dot(
                weights[index][member * per_row : (member + 1) * per_row],
                moved_ref[item, 1],
                preferred_element_type=jnp.float32,
            )
            for head in range(heads):
                at = pl.multiple_of(row * per_row + head * per_head, per_head)
                mixed[pl.ds(at, per_head), :] = result[
                    head * per_head : (head + 1) * per_head, head * HD : (head + 1) * HD
                ]

    me = lax.axis_index("inst")
    for late_ref, shift in zip(late_refs, late):
        item = pick_ref[peer_to(me, shift, count)] - part * block

        @pl.when((item >= 0) & (item < block))
        def _():
            late_ref[...] = moved_ref[item]

    @pl.when(part == pl.num_programs(0) - 1)
    def _():
        mixed_ref[...] = mixed[...].astype(jnp.bfloat16)
        for peer in range(count):
            row = pick_ref[peer]
            small_ref[peer, :per_row, :] = mixed[
                pl.ds(pl.multiple_of(row * per_row, per_row), per_row), :
            ].astype(jnp.bfloat16)
            news = []
            for which in range(2):
                for step in range(steps):
                    new = fresh[which, pl.ds(step * rows + row, 1), :]
                    news += [new[:, h * HD : (h + 1) * HD] for h in range(heads)]
            slot = dest_ref[row] - peer * rows
            slot = jnp.where((slot >= 0) & (slot < rows), slot, -1).astype(jnp.float32)
            news.append(jnp.full((1, HD), slot))
            fill = small_ref.shape[1] - per_row - 2 * steps * heads - 1
            news.append(jnp.full((fill, HD), length_ref[row].astype(jnp.float32)))
            small_ref[peer, per_row:, :] = jnp.concatenate(news, axis=0).astype(jnp.bfloat16)


def attend(kv_cache, queries, own, got, gain, lengths, destination, count, late):
    steps, rows, query_width = queries.shape
    capacity, lanes = kv_cache.shape[2:]
    heads = lanes // HD
    per_row = steps * query_width // HD
    block = 8
    small_rows = per_row + -(-(2 * steps * heads + 2) // TILE) * TILE
    small = jax.ShapeDtypeStruct((count, small_rows, HD), jnp.bfloat16)
    smem = pl.BlockSpec(memory_space=pltpu.SMEM)
    vmem = pl.BlockSpec(memory_space=pltpu.VMEM)
    cache_block = pl.BlockSpec((block, 2, capacity, lanes), lambda i: (i, 0, 0, 0))
    return pl.pallas_call(
        functools.partial(attend_kernel, count, late, block),
        grid=(rows // block,),
        out_shape=[
            jax.ShapeDtypeStruct(kv_cache.shape, kv_cache.dtype),
            jax.ShapeDtypeStruct((rows * per_row, HD), jnp.bfloat16),
            small,
        ]
        + [jax.ShapeDtypeStruct(kv_cache.shape[1:], kv_cache.dtype)] * len(late),
        in_specs=[smem, smem, vmem, vmem, vmem, vmem, cache_block],
        out_specs=[cache_block, vmem, vmem] + [vmem] * len(late),
        scratch_shapes=[
            pltpu.VMEM((2, steps * rows, lanes), jnp.float32),
            pltpu.VMEM((rows * per_row, HD), jnp.float32),
            pltpu.VMEM((rows * per_row // HD, HD, HD), jnp.float32),
            pltpu.VMEM((rows * per_row, HD), jnp.float32),
            pltpu.SMEM((count,), jnp.int32),
        ],
        compiler_params=pltpu.CompilerParams(vmem_limit_bytes=ATTEND_LIMIT),
        cost_estimate=HEAVY,
        name="attend",
    )(lengths, destination, own, got, gain, queries, kv_cache)


def read_facts(block):
    capacity = block.shape[1]
    facts = block[0, capacity - TILE :, :].astype(jnp.float32)[TILE - 1 :]
    return (
        jnp.max(facts[:, :HD]).astype(jnp.int32),
        jnp.max(facts[:, HD : 2 * HD]).astype(jnp.int32),
    )


def window_start(length, capacity):
    return pl.multiple_of(jnp.minimum(length // TILE * TILE, capacity - WINDOW), TILE)


def clean(block, length, out):
    capacity, lanes = block.shape[1:]
    kept = lax.broadcasted_iota(jnp.int32, (capacity, HD), 0) < length
    for which in range(2):
        for at in range(0, lanes, HD):
            stored = block[which, :, at : at + HD].astype(jnp.float32)
            out[which, :, at : at + HD] = jnp.where(kept, stored, 0.0).astype(jnp.bfloat16)


def insert(window, news, ahead, steps, out):
    height, lanes = window.shape[1:]
    heads = lanes // HD
    position = lax.broadcasted_iota(jnp.int32, (height, lanes), 0)
    for which in range(2):
        stored = window[which].astype(jnp.float32)
        for step in range(steps):
            at = (which * steps + step) * heads
            new = jnp.concatenate([news[at + h : at + h + 1] for h in range(heads)], axis=1)
            stored = jnp.where(position == ahead + step, new, stored)
        out[which] = stored.astype(jnp.bfloat16)


def land_kernel(pieces, *refs):
    blocks = refs[:pieces]
    _, out_ref, window_ref, buffer, sems, slots = refs[pieces:]
    capacity = buffer.shape[2]

    def store(piece):
        slot = jnp.maximum(slots[piece], 0)
        return pltpu.make_async_copy(buffer.at[piece], out_ref.at[slot], sems.at[piece])

    facts = [read_facts(block) for block in blocks]
    for piece, (slot, length) in enumerate(facts):
        slots[piece] = slot

        @pl.when(slot >= 0)
        def _():
            clean(blocks[piece], length, buffer.at[piece])
            store(piece).start()
            start = window_start(length, capacity)
            window_ref[piece] = buffer[piece, :, pl.ds(start, WINDOW), :]

    for piece in range(pieces):

        @pl.when(slots[piece] >= 0)
        def _():
            store(piece).wait()


def land(got, moved):
    pieces = len(got)
    vmem = pl.BlockSpec(memory_space=pltpu.VMEM)
    hbm = pl.BlockSpec(memory_space=pl.ANY)
    return pl.pallas_call(
        functools.partial(land_kernel, pieces),
        out_shape=[
            jax.ShapeDtypeStruct(moved.shape, moved.dtype),
            jax.ShapeDtypeStruct((pieces, 2, WINDOW, moved.shape[3]), moved.dtype),
        ],
        in_specs=[vmem] * pieces + [hbm],
        out_specs=[hbm, vmem],
        scratch_shapes=[
            pltpu.VMEM((pieces,) + moved.shape[1:], moved.dtype),
            pltpu.SemaphoreType.DMA((pieces,)),
            pltpu.SMEM((pieces,), jnp.int32),
        ],
        input_output_aliases={pieces: 0},
        compiler_params=pltpu.CompilerParams(vmem_limit_bytes=SMALL_LIMIT),
        cost_estimate=HEAVY,
        name="land",
    )(*got, moved)


def read_small(small_ref, peer, per_row, line):
    rows = small_ref[peer, per_row:, :].astype(jnp.float32)
    return jnp.max(rows[line : line + 1]).astype(jnp.int32)


def settle_kernel(
    count,
    early,
    group,
    mixed_ref,
    small_ref,
    window_ref,
    _,
    out_ref,
    moved_ref,
    mixed,
    windows,
    sems,
    slots,
    lengths,
):
    steps, rows, query_width = out_ref.shape
    per_row = steps * query_width // HD
    capacity, lanes = moved_ref.shape[2:]
    line = 2 * steps * (lanes // HD)
    me = lax.axis_index("inst")

    def store(piece):
        slot = jnp.maximum(slots[early[piece]], 0)
        start = window_start(lengths[early[piece]], capacity)
        return pltpu.make_async_copy(
            windows.at[piece], moved_ref.at[slot, :, pl.ds(start, WINDOW), :], sems.at[piece]
        )

    for shift in range(1, count):
        peer = peer_from(me, shift, count)
        slots[shift] = read_small(small_ref, peer, per_row, line)
        lengths[shift] = read_small(small_ref, peer, per_row, line + 1)

    for piece, shift in enumerate(early):

        @pl.when(slots[shift] >= 0)
        def _():
            peer = peer_from(me, shift, count)
            news = small_ref[peer, per_row:, :].astype(jnp.float32)
            ahead = lengths[shift] - window_start(lengths[shift], capacity)
            insert(window_ref.at[piece], news, ahead, steps, windows.at[piece])
            store(piece).start()

    mixed[...] = mixed_ref[...].astype(jnp.float32)
    for shift in range(1, count):

        @pl.when(slots[shift] >= 0)
        def _():
            mixed[pl.ds(pl.multiple_of(slots[shift] * per_row, per_row), per_row), :] = small_ref[
                peer_from(me, shift, count), :per_row, :
            ].astype(jnp.float32)

    for step in range(steps):
        for chunk in range(query_width // HD):
            head, member = chunk // group, chunk % group
            at = head * steps * group + step * group + member
            out_ref[step, :, chunk * HD : (chunk + 1) * HD] = mixed[
                pl.ds(at, rows, stride=per_row), :
            ].astype(jnp.bfloat16)

    for piece, shift in enumerate(early):

        @pl.when(slots[shift] >= 0)
        def _():
            store(piece).wait()


def settle(mixed, small, windows, moved, shape, group, count, early):
    vmem = pl.BlockSpec(memory_space=pltpu.VMEM)
    hbm = pl.BlockSpec(memory_space=pl.ANY)
    return pl.pallas_call(
        functools.partial(settle_kernel, count, early, group),
        out_shape=[
            jax.ShapeDtypeStruct(shape, jnp.bfloat16),
            jax.ShapeDtypeStruct(moved.shape, moved.dtype),
        ],
        in_specs=[vmem, vmem, vmem, hbm],
        out_specs=[vmem, hbm],
        scratch_shapes=[
            pltpu.VMEM(mixed.shape, jnp.float32),
            pltpu.VMEM(windows.shape, windows.dtype),
            pltpu.SemaphoreType.DMA((len(early),)),
            pltpu.SMEM((count,), jnp.int32),
            pltpu.SMEM((count,), jnp.int32),
        ],
        input_output_aliases={3: 1},
        compiler_params=pltpu.CompilerParams(vmem_limit_bytes=SMALL_LIMIT),
        cost_estimate=LIGHT,
        name="settle",
    )(mixed, small, windows, moved)


def finish_kernel(count, late, steps, *refs):
    blocks = refs[: len(late)]
    small_ref, _, out_ref, sems, slots = refs[len(late) :]
    line = 2 * steps * (out_ref.shape[3] // HD)
    facts = -(-(line + 2) // TILE) * TILE
    me = lax.axis_index("inst")

    def store(piece):
        slot = jnp.maximum(slots[piece], 0)
        return pltpu.make_async_copy(blocks[piece], out_ref.at[slot], sems.at[piece])

    for piece, shift in enumerate(late):
        peer = peer_from(me, shift, count)
        slots[piece] = read_small(small_ref, peer, small_ref.shape[1] - facts, line)
    for piece in range(len(late)):
        pl.when(slots[piece] >= 0)(store(piece).start)
    for piece in range(len(late)):
        pl.when(slots[piece] >= 0)(store(piece).wait)


def finish(got, small, moved, steps, count, late):
    vmem = pl.BlockSpec(memory_space=pltpu.VMEM)
    hbm = pl.BlockSpec(memory_space=pl.ANY)
    return pl.pallas_call(
        functools.partial(finish_kernel, count, late, steps),
        out_shape=jax.ShapeDtypeStruct(moved.shape, moved.dtype),
        in_specs=[vmem] * len(got) + [vmem, hbm],
        out_specs=hbm,
        scratch_shapes=[
            pltpu.SemaphoreType.DMA((len(got),)),
            pltpu.SMEM((len(got),), jnp.int32),
        ],
        input_output_aliases={len(got) + 1: 0},
        compiler_params=pltpu.CompilerParams(vmem_limit_bytes=SMALL_LIMIT),
        cost_estimate=LIGHT,
        name="finish",
    )(*got, small, moved)


def local(hidden_new, queries, kv_cache, lengths, destination, key_weight, value_weight, key_gain):
    steps = queries.shape[0]
    group = queries.shape[2] // kv_cache.shape[3]
    count = lax.axis_size("inst")
    half = max(count // 2, 1)
    early = list(range(count - 1, half, -1)) + [half - 1] * (half > 1)
    late = [half] + list(range(half - 2, 0, -1))

    def send(block, shift):
        pairs = [(i, peer_to(i, shift, count)) for i in range(count)]
        return lax.ppermute(block, "inst", pairs)

    blocks, own, other = prepare(
        destination, lengths, hidden_new, kv_cache, key_weight, value_weight, count, early
    )
    early_got = [send(block, shift) for block, shift in zip(blocks, early)]
    got = lax.ppermute(other, "tp", [(0, 1), (1, 0)])
    moved, mixed, small, *late_blocks = attend(
        kv_cache,
        queries,
        own,
        got,
        key_gain[None, :],
        lengths,
        destination,
        count,
        late,
    )
    late_got = [send(block, shift) for block, shift in zip(late_blocks, late)]
    small_got = lax.all_to_all(small, "inst", 0, 0, tiled=True)
    moved, windows = land(early_got, moved)
    attended, moved = settle(mixed, small_got, windows, moved, queries.shape, group, count, early)
    return attended, finish(late_got, small_got, moved, steps, count, late)


def solution(mesh):
    return jax.shard_map(
        local,
        mesh=mesh,
        in_specs=(
            P(None, ("group", "inst"), "tp"),
            P(None, ("group", "inst"), "tp"),
            P(("group", "inst"), None, None, "tp"),
            P(("group", "inst")),
            P(("group", "inst")),
            P("tp", None),
            P("tp", None),
            P(),
        ),
        out_specs=(P(None, ("group", "inst"), "tp"), P(("group", "inst"), None, None, "tp")),
        check_vma=False,
    )
```

```python
import functools
import math

import jax
import jax.numpy as jnp
from jax import lax
from jax.experimental import pallas as pl
from jax.experimental.pallas import tpu as pltpu
from jax.sharding import PartitionSpec as P

HD = 128
ROPE_BASE = 1000000.0
NORM_EPS = 1e-06
VMEM_LIMIT = 62 * 1024 * 1024
ATTEND_LIMIT = 50 * 1024 * 1024
PREPARE_LIMIT = 62 * 1024 * 1024
SMALL_LIMIT = 40 * 1024 * 1024
LIGHT = pl.CostEstimate(flops=1, bytes_accessed=1, transcendentals=0)
HEAVY = pl.CostEstimate(flops=1 << 36, bytes_accessed=1 << 28, transcendentals=0)
TILE = 16
WINDOW = 32


def quotient(value, divisor, bound):
    factor = -(-(1 << 16) // divisor)
    if bound * factor < 1 << 31 and all(
        (x * factor) >> 16 == x // divisor for x in range(bound)
    ):
        return (value * factor) >> 16
    return value // divisor


def peer_to(index, shift, count):
    return index ^ shift if count & (count - 1) == 0 else (index + shift) % count


def peer_from(index, shift, count):
    return index ^ shift if count & (count - 1) == 0 else (index + count - shift) % count


def pick_rows(count, dest_ref, pick_ref):
    rows = dest_ref.shape[0]
    for peer in range(count):
        pick_ref[peer] = 0
    for row in range(rows):
        pick_ref[quotient(dest_ref[row], rows, rows * count)] = row


def add_facts(block, peer, row, dest_ref, length_ref):
    capacity, lanes = block.shape[1:]
    rows = dest_ref.shape[0]
    slot = dest_ref[row] - peer * rows
    slot = jnp.where((slot >= 0) & (slot < rows), slot, -1)
    last = lax.broadcasted_iota(jnp.int32, (TILE, lanes), 0) == TILE - 1
    first_lanes = lax.broadcasted_iota(jnp.int32, (TILE, lanes), 1) < HD
    facts = jnp.where(first_lanes, slot, length_ref[row]).astype(jnp.float32)
    end = block[0, capacity - TILE :, :].astype(jnp.float32)
    block[0, capacity - TILE :, :] = jnp.where(last, facts, end).astype(jnp.bfloat16)


def prepare_kernel(
    count, early, chunks, dest_ref, length_ref, hidden_ref, kv_ref, key_ref, value_ref, *refs
):
    block_refs = refs[: len(early)]
    own_ref, other_ref, blocks, hidden_held, held, total = refs[len(early) : len(early) + 6]
    in_sems, out_sems, hidden_sem, weight_sems, pick_ref = refs[len(early) + 6 :]
    steps, rows, depth = hidden_ref.shape
    width = key_ref.shape[1]
    part = depth // chunks
    me = lax.axis_index("inst")

    def weights(chunk):
        span = pl.ds(chunk * part, part)
        return [
            pltpu.make_async_copy(ref.at[span], held.at[which, span], weight_sems.at[chunk, which])
            for which, ref in enumerate((key_ref, value_ref))
        ]

    hidden_copy = pltpu.make_async_copy(hidden_ref, hidden_held, hidden_sem)
    hidden_copy.start()
    for copy in weights(0):
        copy.start()
    pick_rows(count, dest_ref, pick_ref)
    fetches, stores = [], []
    for piece, shift in enumerate(early):
        row = pick_ref[peer_to(me, shift, count)]
        fetches.append(
            pltpu.make_async_copy(kv_ref.at[row], blocks.at[piece], in_sems.at[piece])
        )
        fetches[-1].start()
    for chunk in range(1, chunks):
        for copy in weights(chunk):
            copy.start()

    for piece, shift in enumerate(early):
        peer = peer_to(me, shift, count)
        fetches[piece].wait()
        add_facts(blocks.at[piece], peer, pick_ref[peer], dest_ref, length_ref)
        stores.append(
            pltpu.make_async_copy(blocks.at[piece], block_refs[piece], out_sems.at[piece])
        )
        stores[-1].start()
    hidden_copy.wait()
    hidden = hidden_held[...].reshape(steps * rows, depth)
    sums = [None, None]
    for chunk in range(chunks):
        for which, copy in enumerate(weights(chunk)):
            copy.wait()
            product = jnp.dot(
                hidden[:, chunk * part : (chunk + 1) * part],
                held[which, chunk * part : (chunk + 1) * part, :],
                preferred_element_type=jnp.float32,
            )
            sums[which] = product if chunk == 0 else sums[which] + product
    total[:, :width] = sums[0]
    total[:, width:] = sums[1]
    half = width // 2
    core = lax.axis_index("tp")
    for ref, place in ((own_ref, core), (other_ref, 1 - core)):
        at = pl.multiple_of(place * half, half)
        ref[:, :half] = total[:, pl.ds(at, half)]
        ref[:, half:] = total[:, pl.ds(pl.multiple_of(width + at, half), half)]

    for copy in stores:
        copy.wait()


def prepare(destination, lengths, hidden_new, kv_cache, key_weight, value_weight, count, early):
    steps, rows, depth = hidden_new.shape
    width = key_weight.shape[1]
    chunks = 5
    part = jax.ShapeDtypeStruct((steps * rows, width), jnp.float32)
    smem = pl.BlockSpec(memory_space=pltpu.SMEM)
    vmem = pl.BlockSpec(memory_space=pltpu.VMEM)
    hbm = pl.BlockSpec(memory_space=pl.ANY)
    outs = pl.pallas_call(
        functools.partial(prepare_kernel, count, early, chunks),
        out_shape=[jax.ShapeDtypeStruct(kv_cache.shape[1:], kv_cache.dtype)] * len(early)
        + [part, part],
        in_specs=[smem, smem, hbm, hbm, hbm, hbm],
        out_specs=[hbm] * len(early) + [vmem, vmem],
        scratch_shapes=[
            pltpu.VMEM((len(early),) + kv_cache.shape[1:], kv_cache.dtype),
            pltpu.VMEM(hidden_new.shape, hidden_new.dtype),
            pltpu.VMEM((2, depth, width), key_weight.dtype),
            pltpu.VMEM((steps * rows, 2 * width), jnp.float32),
            pltpu.SemaphoreType.DMA((len(early),)),
            pltpu.SemaphoreType.DMA((len(early),)),
            pltpu.SemaphoreType.DMA,
            pltpu.SemaphoreType.DMA((chunks, 2)),
            pltpu.SMEM((count,), jnp.int32),
        ],
        compiler_params=pltpu.CompilerParams(vmem_limit_bytes=PREPARE_LIMIT),
        cost_estimate=LIGHT,
        name="prepare",
    )(destination, lengths, hidden_new, kv_cache, key_weight, value_weight)
    return outs[: len(early)], *outs[len(early) :]


def rotation(length_ref, steps, rows):
    half = HD // 2
    line = lax.broadcasted_iota(jnp.int32, (rows, HD), 0)
    lane = lax.broadcasted_iota(jnp.int32, (steps * rows, HD), 1)
    length = jnp.zeros((rows, HD), jnp.int32)
    for row in range(rows):
        length = jnp.where(line == row, length_ref[row], length)
    position = jnp.concatenate([length + step for step in range(steps)], axis=0)
    order = (lane % half).astype(jnp.float32)
    angle = position.astype(jnp.float32) * jnp.exp(-math.log(ROPE_BASE) * 2.0 * order / HD)
    turns = jnp.floor(angle * (1.0 / math.pi) + 0.5)
    rest = ((angle - turns * 3.140625) - turns * 9.67502593994140625e-4) - turns * 1.5099579909783e-7
    sign = 1.0 - 2.0 * (turns - 2.0 * jnp.floor(turns * 0.5))
    square = rest * rest
    cosine, sine = jnp.ones_like(rest), jnp.ones_like(rest)
    for power in range(6, 0, -1):
        cosine = 1.0 - cosine * square * (1.0 / ((2 * power - 1) * (2 * power)))
        sine = 1.0 - sine * square * (1.0 / ((2 * power) * (2 * power + 1)))
    sine = sign * rest * sine
    return sign * cosine, jnp.where(lane < half, -sine, sine)


def attend_kernel(
    count,
    late,
    block,
    length_ref,
    dest_ref,
    own_ref,
    got_ref,
    gain_ref,
    query_ref,
    kv_ref,
    *refs,
):
    moved_ref, mixed_ref, small_ref = refs[:3]
    late_refs = refs[3:-5]
    fresh, query_rows, query_columns, mixed, pick_ref = refs[-5:]
    part = pl.program_id(0)
    steps, rows, query_width = query_ref.shape
    capacity, lanes = kv_ref.shape[2:]
    heads = lanes // HD
    group = query_width // lanes
    per_head = steps * group
    per_row = heads * per_head
    team = HD // per_row

    @pl.when(part == 0)
    def _():
        pick_rows(count, dest_ref, pick_ref)
        raw = own_ref[...] + got_ref[...]
        cosine, sine = rotation(length_ref, steps, rows)
        gain = gain_ref[...].astype(jnp.float32)
        for head in range(heads):
            at = slice(head * HD, (head + 1) * HD)
            piece = raw[:, at]
            mean = jnp.mean(piece * piece, axis=-1, keepdims=True)
            piece = piece * lax.rsqrt(mean + NORM_EPS) * gain
            swapped = jnp.concatenate([piece[:, HD // 2 :], piece[:, : HD // 2]], axis=1)
            turned = piece * cosine + swapped * sine
            fresh[0, :, at] = turned.astype(jnp.bfloat16).astype(jnp.float32)
        fresh[1] = raw[:, lanes:].astype(jnp.bfloat16).astype(jnp.float32)
        for step in range(steps):
            for chunk in range(query_width // HD):
                head, member = chunk // group, chunk % group
                at = head * per_head + step * group + member
                query_rows[pl.ds(at, rows, stride=per_row), :] = query_ref[
                    step, :, chunk * HD : (chunk + 1) * HD
                ].astype(jnp.float32)
        for index in range(rows // team):
            query_columns[index] = query_rows[index * HD : (index + 1) * HD, :].T

    position = lax.broadcasted_iota(jnp.int32, (capacity, HD), 0)
    column = lax.broadcasted_iota(jnp.int32, (capacity, HD), 1)
    column_item = column // per_row
    column_step = (column % per_head) // group
    column_head = lax.broadcasted_iota(jnp.int32, (HD, HD), 1) % per_row // per_head
    factor = 1.0 / math.sqrt(HD)
    teams = range(block // team)
    scores = []
    for index in teams:
        queries = query_columns[part * (block // team) + index]
        queries = jnp.concatenate(
            [jnp.where(column_head == head, queries, 0.0) for head in range(heads)], axis=0
        ).astype(jnp.bfloat16)
        score, limit = None, None
        for member in range(team):
            item = index * team + member
            row = part * block + item
            length = length_ref[row]
            kept = position < length
            landing = [position == length + step for step in range(steps)]
            for which in range(2):
                news = [fresh[which, pl.ds(step * rows + row, 1), :] for step in range(steps)]
                for head in range(heads):
                    at = slice(head * HD, (head + 1) * HD)
                    stored = jnp.where(kept, kv_ref[item, which, :, at].astype(jnp.float32), 0.0)
                    for step in range(steps):
                        stored = jnp.where(landing[step], news[step][:, at], stored)
                    moved_ref[item, which, :, at] = stored.astype(jnp.bfloat16)
            one = jnp.dot(moved_ref[item, 0], queries, preferred_element_type=jnp.float32)
            score = one if member == 0 else jnp.where(column_item == member, one, score)
            limit = length if member == 0 else jnp.where(column_item == member, length, limit)
        scores.append(jnp.where(position <= limit + column_step, score * factor, -jnp.inf))
    weights = []
    for score in scores:
        raised = jnp.exp(score - jnp.max(score, axis=0, keepdims=True))
        normaliser = jnp.sum(raised, axis=0, keepdims=True)
        weights.append((raised / normaliser).T.astype(jnp.bfloat16))
    for index in teams:
        for member in range(team):
            item = index * team + member
            row = part * block + item
            result = jnp.dot(
                weights[index][member * per_row : (member + 1) * per_row],
                moved_ref[item, 1],
                preferred_element_type=jnp.float32,
            )
            for head in range(heads):
                at = pl.multiple_of(row * per_row + head * per_head, per_head)
                mixed[pl.ds(at, per_head), :] = result[
                    head * per_head : (head + 1) * per_head, head * HD : (head + 1) * HD
                ]

    me = lax.axis_index("inst")
    for late_ref, shift in zip(late_refs, late):
        item = pick_ref[peer_to(me, shift, count)] - part * block

        @pl.when((item >= 0) & (item < block))
        def _():
            late_ref[...] = moved_ref[item]

    @pl.when(part == pl.num_programs(0) - 1)
    def _():
        mixed_ref[...] = mixed[...].astype(jnp.bfloat16)
        for peer in range(count):
            row = pick_ref[peer]
            small_ref[peer, :per_row, :] = mixed[
                pl.ds(pl.multiple_of(row * per_row, per_row), per_row), :
            ].astype(jnp.bfloat16)
            news = []
            for which in range(2):
                for step in range(steps):
                    new = fresh[which, pl.ds(step * rows + row, 1), :]
                    news += [new[:, h * HD : (h + 1) * HD] for h in range(heads)]
            slot = dest_ref[row] - peer * rows
            slot = jnp.where((slot >= 0) & (slot < rows), slot, -1).astype(jnp.float32)
            news.append(jnp.full((1, HD), slot))
            fill = small_ref.shape[1] - per_row - 2 * steps * heads - 1
            news.append(jnp.full((fill, HD), length_ref[row].astype(jnp.float32)))
            small_ref[peer, per_row:, :] = jnp.concatenate(news, axis=0).astype(jnp.bfloat16)


def attend(kv_cache, queries, own, got, gain, lengths, destination, count, late):
    steps, rows, query_width = queries.shape
    capacity, lanes = kv_cache.shape[2:]
    heads = lanes // HD
    per_row = steps * query_width // HD
    block = 8
    small_rows = per_row + -(-(2 * steps * heads + 2) // TILE) * TILE
    small = jax.ShapeDtypeStruct((count, small_rows, HD), jnp.bfloat16)
    smem = pl.BlockSpec(memory_space=pltpu.SMEM)
    vmem = pl.BlockSpec(memory_space=pltpu.VMEM)
    cache_block = pl.BlockSpec((block, 2, capacity, lanes), lambda i: (i, 0, 0, 0))
    return pl.pallas_call(
        functools.partial(attend_kernel, count, late, block),
        grid=(rows // block,),
        out_shape=[
            jax.ShapeDtypeStruct(kv_cache.shape, kv_cache.dtype),
            jax.ShapeDtypeStruct((rows * per_row, HD), jnp.bfloat16),
            small,
        ]
        + [jax.ShapeDtypeStruct(kv_cache.shape[1:], kv_cache.dtype)] * len(late),
        in_specs=[smem, smem, vmem, vmem, vmem, vmem, cache_block],
        out_specs=[cache_block, vmem, vmem] + [vmem] * len(late),
        scratch_shapes=[
            pltpu.VMEM((2, steps * rows, lanes), jnp.float32),
            pltpu.VMEM((rows * per_row, HD), jnp.float32),
            pltpu.VMEM((rows * per_row // HD, HD, HD), jnp.float32),
            pltpu.VMEM((rows * per_row, HD), jnp.float32),
            pltpu.SMEM((count,), jnp.int32),
        ],
        compiler_params=pltpu.CompilerParams(vmem_limit_bytes=ATTEND_LIMIT),
        cost_estimate=HEAVY,
        name="attend",
    )(lengths, destination, own, got, gain, queries, kv_cache)


def read_facts(block):
    capacity = block.shape[1]
    facts = block[0, capacity - TILE :, :].astype(jnp.float32)[TILE - 1 :]
    return (
        jnp.max(facts[:, :HD]).astype(jnp.int32),
        jnp.max(facts[:, HD : 2 * HD]).astype(jnp.int32),
    )


def window_start(length, capacity):
    return pl.multiple_of(jnp.minimum(length // TILE * TILE, capacity - WINDOW), TILE)


def clean(block, length, out):
    capacity, lanes = block.shape[1:]
    kept = lax.broadcasted_iota(jnp.int32, (capacity, HD), 0) < length
    for which in range(2):
        for at in range(0, lanes, HD):
            stored = block[which, :, at : at + HD].astype(jnp.float32)
            out[which, :, at : at + HD] = jnp.where(kept, stored, 0.0).astype(jnp.bfloat16)


def insert(window, news, ahead, steps, out):
    height, lanes = window.shape[1:]
    heads = lanes // HD
    position = lax.broadcasted_iota(jnp.int32, (height, lanes), 0)
    for which in range(2):
        stored = window[which].astype(jnp.float32)
        for step in range(steps):
            at = (which * steps + step) * heads
            new = jnp.concatenate([news[at + h : at + h + 1] for h in range(heads)], axis=1)
            stored = jnp.where(position == ahead + step, new, stored)
        out[which] = stored.astype(jnp.bfloat16)


def land_kernel(pieces, *refs):
    blocks = refs[:pieces]
    _, out_ref, window_ref, buffer, sems, slots = refs[pieces:]
    capacity = buffer.shape[2]

    def store(piece):
        slot = jnp.maximum(slots[piece], 0)
        return pltpu.make_async_copy(buffer.at[piece], out_ref.at[slot], sems.at[piece])

    facts = [read_facts(block) for block in blocks]
    for piece, (slot, length) in enumerate(facts):
        slots[piece] = slot

        @pl.when(slot >= 0)
        def _():
            clean(blocks[piece], length, buffer.at[piece])
            store(piece).start()
            start = window_start(length, capacity)
            window_ref[piece] = buffer[piece, :, pl.ds(start, WINDOW), :]

    for piece in range(pieces):

        @pl.when(slots[piece] >= 0)
        def _():
            store(piece).wait()


def land(got, moved):
    pieces = len(got)
    vmem = pl.BlockSpec(memory_space=pltpu.VMEM)
    hbm = pl.BlockSpec(memory_space=pl.ANY)
    return pl.pallas_call(
        functools.partial(land_kernel, pieces),
        out_shape=[
            jax.ShapeDtypeStruct(moved.shape, moved.dtype),
            jax.ShapeDtypeStruct((pieces, 2, WINDOW, moved.shape[3]), moved.dtype),
        ],
        in_specs=[vmem] * pieces + [hbm],
        out_specs=[hbm, vmem],
        scratch_shapes=[
            pltpu.VMEM((pieces,) + moved.shape[1:], moved.dtype),
            pltpu.SemaphoreType.DMA((pieces,)),
            pltpu.SMEM((pieces,), jnp.int32),
        ],
        input_output_aliases={pieces: 0},
        compiler_params=pltpu.CompilerParams(vmem_limit_bytes=SMALL_LIMIT),
        cost_estimate=HEAVY,
        name="land",
    )(*got, moved)


def read_small(small_ref, peer, per_row, line):
    rows = small_ref[peer, per_row:, :].astype(jnp.float32)
    return jnp.max(rows[line : line + 1]).astype(jnp.int32)


def settle_kernel(
    count,
    early,
    group,
    mixed_ref,
    small_ref,
    window_ref,
    _,
    out_ref,
    moved_ref,
    mixed,
    windows,
    sems,
    slots,
    lengths,
):
    steps, rows, query_width = out_ref.shape
    per_row = steps * query_width // HD
    capacity, lanes = moved_ref.shape[2:]
    line = 2 * steps * (lanes // HD)
    me = lax.axis_index("inst")

    def store(piece):
        slot = jnp.maximum(slots[early[piece]], 0)
        start = window_start(lengths[early[piece]], capacity)
        return pltpu.make_async_copy(
            windows.at[piece], moved_ref.at[slot, :, pl.ds(start, WINDOW), :], sems.at[piece]
        )

    for shift in range(1, count):
        peer = peer_from(me, shift, count)
        slots[shift] = read_small(small_ref, peer, per_row, line)
        lengths[shift] = read_small(small_ref, peer, per_row, line + 1)

    for piece, shift in enumerate(early):

        @pl.when(slots[shift] >= 0)
        def _():
            peer = peer_from(me, shift, count)
            news = small_ref[peer, per_row:, :].astype(jnp.float32)
            ahead = lengths[shift] - window_start(lengths[shift], capacity)
            insert(window_ref.at[piece], news, ahead, steps, windows.at[piece])
            store(piece).start()

    mixed[...] = mixed_ref[...].astype(jnp.float32)
    for shift in range(1, count):

        @pl.when(slots[shift] >= 0)
        def _():
            mixed[pl.ds(pl.multiple_of(slots[shift] * per_row, per_row), per_row), :] = small_ref[
                peer_from(me, shift, count), :per_row, :
            ].astype(jnp.float32)

    for step in range(steps):
        for chunk in range(query_width // HD):
            head, member = chunk // group, chunk % group
            at = head * steps * group + step * group + member
            out_ref[step, :, chunk * HD : (chunk + 1) * HD] = mixed[
                pl.ds(at, rows, stride=per_row), :
            ].astype(jnp.bfloat16)

    for piece, shift in enumerate(early):

        @pl.when(slots[shift] >= 0)
        def _():
            store(piece).wait()


def settle(mixed, small, windows, moved, shape, group, count, early):
    vmem = pl.BlockSpec(memory_space=pltpu.VMEM)
    hbm = pl.BlockSpec(memory_space=pl.ANY)
    return pl.pallas_call(
        functools.partial(settle_kernel, count, early, group),
        out_shape=[
            jax.ShapeDtypeStruct(shape, jnp.bfloat16),
            jax.ShapeDtypeStruct(moved.shape, moved.dtype),
        ],
        in_specs=[vmem, vmem, vmem, hbm],
        out_specs=[vmem, hbm],
        scratch_shapes=[
            pltpu.VMEM(mixed.shape, jnp.float32),
            pltpu.VMEM(windows.shape, windows.dtype),
            pltpu.SemaphoreType.DMA((len(early),)),
            pltpu.SMEM((count,), jnp.int32),
            pltpu.SMEM((count,), jnp.int32),
        ],
        input_output_aliases={3: 1},
        compiler_params=pltpu.CompilerParams(vmem_limit_bytes=SMALL_LIMIT),
        cost_estimate=LIGHT,
        name="settle",
    )(mixed, small, windows, moved)


def finish_kernel(count, late, steps, *refs):
    blocks = refs[: len(late)]
    small_ref, _, out_ref, sems, slots = refs[len(late) :]
    line = 2 * steps * (out_ref.shape[3] // HD)
    facts = -(-(line + 2) // TILE) * TILE
    me = lax.axis_index("inst")

    def store(piece):
        slot = jnp.maximum(slots[piece], 0)
        return pltpu.make_async_copy(blocks[piece], out_ref.at[slot], sems.at[piece])

    for piece, shift in enumerate(late):
        peer = peer_from(me, shift, count)
        slots[piece] = read_small(small_ref, peer, small_ref.shape[1] - facts, line)
    for piece in range(len(late)):
        pl.when(slots[piece] >= 0)(store(piece).start)
    for piece in range(len(late)):
        pl.when(slots[piece] >= 0)(store(piece).wait)


def finish(got, small, moved, steps, count, late):
    vmem = pl.BlockSpec(memory_space=pltpu.VMEM)
    hbm = pl.BlockSpec(memory_space=pl.ANY)
    return pl.pallas_call(
        functools.partial(finish_kernel, count, late, steps),
        out_shape=jax.ShapeDtypeStruct(moved.shape, moved.dtype),
        in_specs=[vmem] * len(got) + [vmem, hbm],
        out_specs=hbm,
        scratch_shapes=[
            pltpu.SemaphoreType.DMA((len(got),)),
            pltpu.SMEM((len(got),), jnp.int32),
        ],
        input_output_aliases={len(got) + 1: 0},
        compiler_params=pltpu.CompilerParams(vmem_limit_bytes=SMALL_LIMIT),
        cost_estimate=LIGHT,
        name="finish",
    )(*got, small, moved)


def local(hidden_new, queries, kv_cache, lengths, destination, key_weight, value_weight, key_gain):
    steps = queries.shape[0]
    group = queries.shape[2] // kv_cache.shape[3]
    count = lax.axis_size("inst")
    half = max(count // 2, 1)
    inner = list(range(half - 1, 0, -1))
    early = list(range(half, count - 1)) + inner[:2]
    late = [count - 1] + inner[2:]

    def send(block, shift):
        pairs = [(i, peer_to(i, shift, count)) for i in range(count)]
        return lax.ppermute(block, "inst", pairs)

    blocks, own, other = prepare(
        destination, lengths, hidden_new, kv_cache, key_weight, value_weight, count, early
    )
    early_got = [send(block, shift) for block, shift in zip(blocks, early)]
    got = lax.ppermute(other, "tp", [(0, 1), (1, 0)])
    moved, mixed, small, *late_blocks = attend(
        kv_cache,
        queries,
        own,
        got,
        key_gain[None, :],
        lengths,
        destination,
        count,
        late,
    )
    late_got = [send(block, shift) for block, shift in zip(late_blocks, late)]
    small_got = lax.all_to_all(small, "inst", 0, 0, tiled=True)
    moved, windows = land(early_got, moved)
    attended, moved = settle(mixed, small_got, windows, moved, queries.shape, group, count, early)
    return attended, finish(late_got, small_got, moved, steps, count, late)


def solution(mesh):
    return jax.shard_map(
        local,
        mesh=mesh,
        in_specs=(
            P(None, ("group", "inst"), "tp"),
            P(None, ("group", "inst"), "tp"),
            P(("group", "inst"), None, None, "tp"),
            P(("group", "inst")),
            P(("group", "inst")),
            P("tp", None),
            P("tp", None),
            P(),
        ),
        out_specs=(P(None, ("group", "inst"), "tp"), P(("group", "inst"), None, None, "tp")),
        check_vma=False,
    )
```

```python
import functools
import math

import jax
import jax.numpy as jnp
from jax import lax
from jax.experimental import pallas as pl
from jax.experimental.pallas import tpu as pltpu
from jax.sharding import PartitionSpec as P

HD = 128
ROPE_BASE = 1000000.0
NORM_EPS = 1e-06
VMEM_LIMIT = 62 * 1024 * 1024
ATTEND_LIMIT = 50 * 1024 * 1024
PREPARE_LIMIT = 62 * 1024 * 1024
SMALL_LIMIT = 40 * 1024 * 1024
LIGHT = pl.CostEstimate(flops=1, bytes_accessed=1, transcendentals=0)
HEAVY = pl.CostEstimate(flops=1 << 36, bytes_accessed=1 << 28, transcendentals=0)
TILE = 16
WINDOW = 32


def quotient(value, divisor, bound):
    factor = -(-(1 << 16) // divisor)
    if bound * factor < 1 << 31 and all(
        (x * factor) >> 16 == x // divisor for x in range(bound)
    ):
        return (value * factor) >> 16
    return value // divisor


def peer_to(index, shift, count):
    return index ^ shift if count & (count - 1) == 0 else (index + shift) % count


def peer_from(index, shift, count):
    return index ^ shift if count & (count - 1) == 0 else (index + count - shift) % count


def pick_rows(count, dest_ref, pick_ref):
    rows = dest_ref.shape[0]
    for peer in range(count):
        pick_ref[peer] = 0
    for row in range(rows):
        pick_ref[quotient(dest_ref[row], rows, rows * count)] = row


def add_facts(block, peer, row, dest_ref, length_ref):
    capacity, lanes = block.shape[1:]
    rows = dest_ref.shape[0]
    slot = dest_ref[row] - peer * rows
    slot = jnp.where((slot >= 0) & (slot < rows), slot, -1)
    last = lax.broadcasted_iota(jnp.int32, (TILE, lanes), 0) == TILE - 1
    first_lanes = lax.broadcasted_iota(jnp.int32, (TILE, lanes), 1) < HD
    facts = jnp.where(first_lanes, slot, length_ref[row]).astype(jnp.float32)
    end = block[0, capacity - TILE :, :].astype(jnp.float32)
    block[0, capacity - TILE :, :] = jnp.where(last, facts, end).astype(jnp.bfloat16)


def prepare_kernel(
    count, early, chunks, dest_ref, length_ref, hidden_ref, kv_ref, key_ref, value_ref, *refs
):
    block_refs = refs[: len(early)]
    own_ref, other_ref, blocks, hidden_held, held, total = refs[len(early) : len(early) + 6]
    in_sems, out_sems, hidden_sem, weight_sems, pick_ref = refs[len(early) + 6 :]
    steps, rows, depth = hidden_ref.shape
    width = key_ref.shape[1]
    part = depth // chunks
    me = lax.axis_index("inst")

    def weights(chunk):
        span = pl.ds(chunk * part, part)
        return [
            pltpu.make_async_copy(ref.at[span], held.at[which, span], weight_sems.at[chunk, which])
            for which, ref in enumerate((key_ref, value_ref))
        ]

    hidden_copy = pltpu.make_async_copy(hidden_ref, hidden_held, hidden_sem)
    hidden_copy.start()
    for copy in weights(0):
        copy.start()
    pick_rows(count, dest_ref, pick_ref)
    fetches, stores = [], []
    for piece, shift in enumerate(early):
        row = pick_ref[peer_to(me, shift, count)]
        fetches.append(
            pltpu.make_async_copy(kv_ref.at[row], blocks.at[piece], in_sems.at[piece])
        )
        fetches[-1].start()
    for chunk in range(1, chunks):
        for copy in weights(chunk):
            copy.start()

    for piece, shift in enumerate(early):
        peer = peer_to(me, shift, count)
        fetches[piece].wait()
        add_facts(blocks.at[piece], peer, pick_ref[peer], dest_ref, length_ref)
        stores.append(
            pltpu.make_async_copy(blocks.at[piece], block_refs[piece], out_sems.at[piece])
        )
        stores[-1].start()
    hidden_copy.wait()
    hidden = hidden_held[...].reshape(steps * rows, depth)
    sums = [None, None]
    for chunk in range(chunks):
        for which, copy in enumerate(weights(chunk)):
            copy.wait()
            product = jnp.dot(
                hidden[:, chunk * part : (chunk + 1) * part],
                held[which, chunk * part : (chunk + 1) * part, :],
                preferred_element_type=jnp.float32,
            )
            sums[which] = product if chunk == 0 else sums[which] + product
    total[:, :width] = sums[0]
    total[:, width:] = sums[1]
    half = width // 2
    core = lax.axis_index("tp")
    for ref, place in ((own_ref, core), (other_ref, 1 - core)):
        at = pl.multiple_of(place * half, half)
        ref[:, :half] = total[:, pl.ds(at, half)]
        ref[:, half:] = total[:, pl.ds(pl.multiple_of(width + at, half), half)]

    for copy in stores:
        copy.wait()


def prepare(destination, lengths, hidden_new, kv_cache, key_weight, value_weight, count, early):
    steps, rows, depth = hidden_new.shape
    width = key_weight.shape[1]
    chunks = 5
    part = jax.ShapeDtypeStruct((steps * rows, width), jnp.float32)
    smem = pl.BlockSpec(memory_space=pltpu.SMEM)
    vmem = pl.BlockSpec(memory_space=pltpu.VMEM)
    hbm = pl.BlockSpec(memory_space=pl.ANY)
    outs = pl.pallas_call(
        functools.partial(prepare_kernel, count, early, chunks),
        out_shape=[jax.ShapeDtypeStruct(kv_cache.shape[1:], kv_cache.dtype)] * len(early)
        + [part, part],
        in_specs=[smem, smem, hbm, hbm, hbm, hbm],
        out_specs=[hbm] * len(early) + [vmem, vmem],
        scratch_shapes=[
            pltpu.VMEM((len(early),) + kv_cache.shape[1:], kv_cache.dtype),
            pltpu.VMEM(hidden_new.shape, hidden_new.dtype),
            pltpu.VMEM((2, depth, width), key_weight.dtype),
            pltpu.VMEM((steps * rows, 2 * width), jnp.float32),
            pltpu.SemaphoreType.DMA((len(early),)),
            pltpu.SemaphoreType.DMA((len(early),)),
            pltpu.SemaphoreType.DMA,
            pltpu.SemaphoreType.DMA((chunks, 2)),
            pltpu.SMEM((count,), jnp.int32),
        ],
        compiler_params=pltpu.CompilerParams(vmem_limit_bytes=PREPARE_LIMIT),
        cost_estimate=LIGHT,
        name="prepare",
    )(destination, lengths, hidden_new, kv_cache, key_weight, value_weight)
    return outs[: len(early)], *outs[len(early) :]


def rotation(length_ref, steps, rows):
    half = HD // 2
    line = lax.broadcasted_iota(jnp.int32, (rows, HD), 0)
    lane = lax.broadcasted_iota(jnp.int32, (steps * rows, HD), 1)
    length = jnp.zeros((rows, HD), jnp.int32)
    for row in range(rows):
        length = jnp.where(line == row, length_ref[row], length)
    position = jnp.concatenate([length + step for step in range(steps)], axis=0)
    order = (lane % half).astype(jnp.float32)
    angle = position.astype(jnp.float32) * jnp.exp(-math.log(ROPE_BASE) * 2.0 * order / HD)
    turns = jnp.floor(angle * (1.0 / math.pi) + 0.5)
    rest = ((angle - turns * 3.140625) - turns * 9.67502593994140625e-4) - turns * 1.5099579909783e-7
    sign = 1.0 - 2.0 * (turns - 2.0 * jnp.floor(turns * 0.5))
    square = rest * rest
    cosine, sine = jnp.ones_like(rest), jnp.ones_like(rest)
    for power in range(6, 0, -1):
        cosine = 1.0 - cosine * square * (1.0 / ((2 * power - 1) * (2 * power)))
        sine = 1.0 - sine * square * (1.0 / ((2 * power) * (2 * power + 1)))
    sine = sign * rest * sine
    return sign * cosine, jnp.where(lane < half, -sine, sine)


def attend_kernel(
    count,
    late,
    block,
    length_ref,
    dest_ref,
    own_ref,
    got_ref,
    gain_ref,
    query_ref,
    kv_ref,
    *refs,
):
    moved_ref, mixed_ref, small_ref = refs[:3]
    late_refs = refs[3:-5]
    fresh, query_rows, query_columns, mixed, pick_ref = refs[-5:]
    part = pl.program_id(0)
    steps, rows, query_width = query_ref.shape
    capacity, lanes = kv_ref.shape[2:]
    heads = lanes // HD
    group = query_width // lanes
    per_head = steps * group
    per_row = heads * per_head
    team = HD // per_row

    @pl.when(part == 0)
    def _():
        pick_rows(count, dest_ref, pick_ref)
        raw = own_ref[...] + got_ref[...]
        cosine, sine = rotation(length_ref, steps, rows)
        gain = gain_ref[...].astype(jnp.float32)
        for head in range(heads):
            at = slice(head * HD, (head + 1) * HD)
            piece = raw[:, at]
            mean = jnp.mean(piece * piece, axis=-1, keepdims=True)
            piece = piece * lax.rsqrt(mean + NORM_EPS) * gain
            swapped = jnp.concatenate([piece[:, HD // 2 :], piece[:, : HD // 2]], axis=1)
            turned = piece * cosine + swapped * sine
            fresh[0, :, at] = turned.astype(jnp.bfloat16).astype(jnp.float32)
        fresh[1] = raw[:, lanes:].astype(jnp.bfloat16).astype(jnp.float32)
        for step in range(steps):
            for chunk in range(query_width // HD):
                head, member = chunk // group, chunk % group
                at = head * per_head + step * group + member
                query_rows[pl.ds(at, rows, stride=per_row), :] = query_ref[
                    step, :, chunk * HD : (chunk + 1) * HD
                ].astype(jnp.float32)
        for index in range(rows // team):
            query_columns[index] = query_rows[index * HD : (index + 1) * HD, :].T

    position = lax.broadcasted_iota(jnp.int32, (capacity, HD), 0)
    column = lax.broadcasted_iota(jnp.int32, (capacity, HD), 1)
    column_item = column // per_row
    column_step = (column % per_head) // group
    column_head = lax.broadcasted_iota(jnp.int32, (HD, HD), 1) % per_row // per_head
    factor = 1.0 / math.sqrt(HD)
    teams = range(block // team)
    scores = []
    for index in teams:
        queries = query_columns[part * (block // team) + index]
        queries = jnp.concatenate(
            [jnp.where(column_head == head, queries, 0.0) for head in range(heads)], axis=0
        ).astype(jnp.bfloat16)
        score, limit = None, None
        for member in range(team):
            item = index * team + member
            row = part * block + item
            length = length_ref[row]
            kept = position < length
            landing = [position == length + step for step in range(steps)]
            for which in range(2):
                news = [fresh[which, pl.ds(step * rows + row, 1), :] for step in range(steps)]
                for head in range(heads):
                    at = slice(head * HD, (head + 1) * HD)
                    stored = jnp.where(kept, kv_ref[item, which, :, at].astype(jnp.float32), 0.0)
                    for step in range(steps):
                        stored = jnp.where(landing[step], news[step][:, at], stored)
                    moved_ref[item, which, :, at] = stored.astype(jnp.bfloat16)
            one = jnp.dot(moved_ref[item, 0], queries, preferred_element_type=jnp.float32)
            score = one if member == 0 else jnp.where(column_item == member, one, score)
            limit = length if member == 0 else jnp.where(column_item == member, length, limit)
        scores.append(jnp.where(position <= limit + column_step, score * factor, -jnp.inf))
    weights = []
    for score in scores:
        raised = jnp.exp(score - jnp.max(score, axis=0, keepdims=True))
        normaliser = jnp.sum(raised, axis=0, keepdims=True)
        weights.append((raised / normaliser).T.astype(jnp.bfloat16))
    for index in teams:
        for member in range(team):
            item = index * team + member
            row = part * block + item
            result = jnp.dot(
                weights[index][member * per_row : (member + 1) * per_row],
                moved_ref[item, 1],
                preferred_element_type=jnp.float32,
            )
            for head in range(heads):
                at = pl.multiple_of(row * per_row + head * per_head, per_head)
                mixed[pl.ds(at, per_head), :] = result[
                    head * per_head : (head + 1) * per_head, head * HD : (head + 1) * HD
                ]

    me = lax.axis_index("inst")
    for late_ref, shift in zip(late_refs, late):
        item = pick_ref[peer_to(me, shift, count)] - part * block

        @pl.when((item >= 0) & (item < block))
        def _():
            late_ref[...] = moved_ref[item]

    @pl.when(part == pl.num_programs(0) - 1)
    def _():
        mixed_ref[...] = mixed[...].astype(jnp.bfloat16)
        for peer in range(count):
            row = pick_ref[peer]
            small_ref[peer, :per_row, :] = mixed[
                pl.ds(pl.multiple_of(row * per_row, per_row), per_row), :
            ].astype(jnp.bfloat16)
            news = []
            for which in range(2):
                for step in range(steps):
                    new = fresh[which, pl.ds(step * rows + row, 1), :]
                    news += [new[:, h * HD : (h + 1) * HD] for h in range(heads)]
            slot = dest_ref[row] - peer * rows
            slot = jnp.where((slot >= 0) & (slot < rows), slot, -1).astype(jnp.float32)
            news.append(jnp.full((1, HD), slot))
            fill = small_ref.shape[1] - per_row - 2 * steps * heads - 1
            news.append(jnp.full((fill, HD), length_ref[row].astype(jnp.float32)))
            small_ref[peer, per_row:, :] = jnp.concatenate(news, axis=0).astype(jnp.bfloat16)


def attend(kv_cache, queries, own, got, gain, lengths, destination, count, late):
    steps, rows, query_width = queries.shape
    capacity, lanes = kv_cache.shape[2:]
    heads = lanes // HD
    per_row = steps * query_width // HD
    block = 8
    small_rows = per_row + -(-(2 * steps * heads + 2) // TILE) * TILE
    small = jax.ShapeDtypeStruct((count, small_rows, HD), jnp.bfloat16)
    smem = pl.BlockSpec(memory_space=pltpu.SMEM)
    vmem = pl.BlockSpec(memory_space=pltpu.VMEM)
    cache_block = pl.BlockSpec((block, 2, capacity, lanes), lambda i: (i, 0, 0, 0))
    return pl.pallas_call(
        functools.partial(attend_kernel, count, late, block),
        grid=(rows // block,),
        out_shape=[
            jax.ShapeDtypeStruct(kv_cache.shape, kv_cache.dtype),
            jax.ShapeDtypeStruct((rows * per_row, HD), jnp.bfloat16),
            small,
        ]
        + [jax.ShapeDtypeStruct(kv_cache.shape[1:], kv_cache.dtype)] * len(late),
        in_specs=[smem, smem, vmem, vmem, vmem, vmem, cache_block],
        out_specs=[cache_block, vmem, vmem] + [vmem] * len(late),
        scratch_shapes=[
            pltpu.VMEM((2, steps * rows, lanes), jnp.float32),
            pltpu.VMEM((rows * per_row, HD), jnp.float32),
            pltpu.VMEM((rows * per_row // HD, HD, HD), jnp.float32),
            pltpu.VMEM((rows * per_row, HD), jnp.float32),
            pltpu.SMEM((count,), jnp.int32),
        ],
        compiler_params=pltpu.CompilerParams(vmem_limit_bytes=ATTEND_LIMIT),
        cost_estimate=HEAVY,
        name="attend",
    )(lengths, destination, own, got, gain, queries, kv_cache)


def read_facts(block):
    capacity = block.shape[1]
    facts = block[0, capacity - TILE :, :].astype(jnp.float32)[TILE - 1 :]
    return (
        jnp.max(facts[:, :HD]).astype(jnp.int32),
        jnp.max(facts[:, HD : 2 * HD]).astype(jnp.int32),
    )


def window_start(length, capacity):
    return pl.multiple_of(jnp.minimum(length // TILE * TILE, capacity - WINDOW), TILE)


def clean(block, length, out):
    capacity, lanes = block.shape[1:]
    kept = lax.broadcasted_iota(jnp.int32, (capacity, HD), 0) < length
    for which in range(2):
        for at in range(0, lanes, HD):
            stored = block[which, :, at : at + HD].astype(jnp.float32)
            out[which, :, at : at + HD] = jnp.where(kept, stored, 0.0).astype(jnp.bfloat16)


def insert(window, news, ahead, steps, out):
    height, lanes = window.shape[1:]
    heads = lanes // HD
    position = lax.broadcasted_iota(jnp.int32, (height, lanes), 0)
    for which in range(2):
        stored = window[which].astype(jnp.float32)
        for step in range(steps):
            at = (which * steps + step) * heads
            new = jnp.concatenate([news[at + h : at + h + 1] for h in range(heads)], axis=1)
            stored = jnp.where(position == ahead + step, new, stored)
        out[which] = stored.astype(jnp.bfloat16)


def land_kernel(pieces, *refs):
    blocks = refs[:pieces]
    _, out_ref, window_ref, buffer, sems, slots = refs[pieces:]
    capacity = buffer.shape[2]

    def store(piece):
        slot = jnp.maximum(slots[piece], 0)
        return pltpu.make_async_copy(buffer.at[piece], out_ref.at[slot], sems.at[piece])

    facts = [read_facts(block) for block in blocks]
    for piece, (slot, length) in enumerate(facts):
        slots[piece] = slot

        @pl.when(slot >= 0)
        def _():
            clean(blocks[piece], length, buffer.at[piece])
            store(piece).start()
            start = window_start(length, capacity)
            window_ref[piece] = buffer[piece, :, pl.ds(start, WINDOW), :]

    for piece in range(pieces):

        @pl.when(slots[piece] >= 0)
        def _():
            store(piece).wait()


def land(got, moved):
    pieces = len(got)
    vmem = pl.BlockSpec(memory_space=pltpu.VMEM)
    hbm = pl.BlockSpec(memory_space=pl.ANY)
    return pl.pallas_call(
        functools.partial(land_kernel, pieces),
        out_shape=[
            jax.ShapeDtypeStruct(moved.shape, moved.dtype),
            jax.ShapeDtypeStruct((pieces, 2, WINDOW, moved.shape[3]), moved.dtype),
        ],
        in_specs=[vmem] * pieces + [hbm],
        out_specs=[hbm, vmem],
        scratch_shapes=[
            pltpu.VMEM((pieces,) + moved.shape[1:], moved.dtype),
            pltpu.SemaphoreType.DMA((pieces,)),
            pltpu.SMEM((pieces,), jnp.int32),
        ],
        input_output_aliases={pieces: 0},
        compiler_params=pltpu.CompilerParams(vmem_limit_bytes=SMALL_LIMIT),
        cost_estimate=HEAVY,
        name="land",
    )(*got, moved)


def read_small(small_ref, peer, per_row, line):
    rows = small_ref[peer, per_row:, :].astype(jnp.float32)
    return jnp.max(rows[line : line + 1]).astype(jnp.int32)


def settle_kernel(
    count,
    early,
    group,
    mixed_ref,
    small_ref,
    window_ref,
    _,
    out_ref,
    moved_ref,
    mixed,
    windows,
    sems,
    slots,
    lengths,
):
    steps, rows, query_width = out_ref.shape
    per_row = steps * query_width // HD
    capacity, lanes = moved_ref.shape[2:]
    line = 2 * steps * (lanes // HD)
    me = lax.axis_index("inst")

    def store(piece):
        slot = jnp.maximum(slots[early[piece]], 0)
        start = window_start(lengths[early[piece]], capacity)
        return pltpu.make_async_copy(
            windows.at[piece], moved_ref.at[slot, :, pl.ds(start, WINDOW), :], sems.at[piece]
        )

    for shift in range(1, count):
        peer = peer_from(me, shift, count)
        slots[shift] = read_small(small_ref, peer, per_row, line)
        lengths[shift] = read_small(small_ref, peer, per_row, line + 1)

    for piece, shift in enumerate(early):

        @pl.when(slots[shift] >= 0)
        def _():
            peer = peer_from(me, shift, count)
            news = small_ref[peer, per_row:, :].astype(jnp.float32)
            ahead = lengths[shift] - window_start(lengths[shift], capacity)
            insert(window_ref.at[piece], news, ahead, steps, windows.at[piece])
            store(piece).start()

    mixed[...] = mixed_ref[...].astype(jnp.float32)
    for shift in range(1, count):

        @pl.when(slots[shift] >= 0)
        def _():
            mixed[pl.ds(pl.multiple_of(slots[shift] * per_row, per_row), per_row), :] = small_ref[
                peer_from(me, shift, count), :per_row, :
            ].astype(jnp.float32)

    for step in range(steps):
        for chunk in range(query_width // HD):
            head, member = chunk // group, chunk % group
            at = head * steps * group + step * group + member
            out_ref[step, :, chunk * HD : (chunk + 1) * HD] = mixed[
                pl.ds(at, rows, stride=per_row), :
            ].astype(jnp.bfloat16)

    for piece, shift in enumerate(early):

        @pl.when(slots[shift] >= 0)
        def _():
            store(piece).wait()


def settle(mixed, small, windows, moved, shape, group, count, early):
    vmem = pl.BlockSpec(memory_space=pltpu.VMEM)
    hbm = pl.BlockSpec(memory_space=pl.ANY)
    return pl.pallas_call(
        functools.partial(settle_kernel, count, early, group),
        out_shape=[
            jax.ShapeDtypeStruct(shape, jnp.bfloat16),
            jax.ShapeDtypeStruct(moved.shape, moved.dtype),
        ],
        in_specs=[vmem, vmem, vmem, hbm],
        out_specs=[vmem, hbm],
        scratch_shapes=[
            pltpu.VMEM(mixed.shape, jnp.float32),
            pltpu.VMEM(windows.shape, windows.dtype),
            pltpu.SemaphoreType.DMA((len(early),)),
            pltpu.SMEM((count,), jnp.int32),
            pltpu.SMEM((count,), jnp.int32),
        ],
        input_output_aliases={3: 1},
        compiler_params=pltpu.CompilerParams(vmem_limit_bytes=SMALL_LIMIT),
        cost_estimate=LIGHT,
        name="settle",
    )(mixed, small, windows, moved)


def finish_kernel(count, late, steps, *refs):
    blocks = refs[: len(late)]
    small_ref, _, out_ref, sems, slots = refs[len(late) :]
    line = 2 * steps * (out_ref.shape[3] // HD)
    facts = -(-(line + 2) // TILE) * TILE
    me = lax.axis_index("inst")

    def store(piece):
        slot = jnp.maximum(slots[piece], 0)
        return pltpu.make_async_copy(blocks[piece], out_ref.at[slot], sems.at[piece])

    for piece, shift in enumerate(late):
        peer = peer_from(me, shift, count)
        slots[piece] = read_small(small_ref, peer, small_ref.shape[1] - facts, line)
    for piece in range(len(late)):
        pl.when(slots[piece] >= 0)(store(piece).start)
    for piece in range(len(late)):
        pl.when(slots[piece] >= 0)(store(piece).wait)


def finish(got, small, moved, steps, count, late):
    vmem = pl.BlockSpec(memory_space=pltpu.VMEM)
    hbm = pl.BlockSpec(memory_space=pl.ANY)
    return pl.pallas_call(
        functools.partial(finish_kernel, count, late, steps),
        out_shape=jax.ShapeDtypeStruct(moved.shape, moved.dtype),
        in_specs=[vmem] * len(got) + [vmem, hbm],
        out_specs=hbm,
        scratch_shapes=[
            pltpu.SemaphoreType.DMA((len(got),)),
            pltpu.SMEM((len(got),), jnp.int32),
        ],
        input_output_aliases={len(got) + 1: 0},
        compiler_params=pltpu.CompilerParams(vmem_limit_bytes=SMALL_LIMIT),
        cost_estimate=LIGHT,
        name="finish",
    )(*got, small, moved)


def local(hidden_new, queries, kv_cache, lengths, destination, key_weight, value_weight, key_gain):
    steps = queries.shape[0]
    group = queries.shape[2] // kv_cache.shape[3]
    count = lax.axis_size("inst")
    half = max(count // 2, 1)
    early = list(range(half, count - 1)) + [half - 1] * (half > 1)
    inner = list(range(half - 2, 0, -1))
    late = inner[:1] + [count - 1] + inner[1:]

    def send(block, shift):
        pairs = [(i, peer_to(i, shift, count)) for i in range(count)]
        return lax.ppermute(block, "inst", pairs)

    blocks, own, other = prepare(
        destination, lengths, hidden_new, kv_cache, key_weight, value_weight, count, early
    )
    early_got = [send(block, shift) for block, shift in zip(blocks, early)]
    got = lax.ppermute(other, "tp", [(0, 1), (1, 0)])
    moved, mixed, small, *late_blocks = attend(
        kv_cache,
        queries,
        own,
        got,
        key_gain[None, :],
        lengths,
        destination,
        count,
        late,
    )
    late_got = [send(block, shift) for block, shift in zip(late_blocks, late)]
    small_got = lax.all_to_all(small, "inst", 0, 0, tiled=True)
    moved, windows = land(early_got, moved)
    attended, moved = settle(mixed, small_got, windows, moved, queries.shape, group, count, early)
    return attended, finish(late_got, small_got, moved, steps, count, late)


def solution(mesh):
    return jax.shard_map(
        local,
        mesh=mesh,
        in_specs=(
            P(None, ("group", "inst"), "tp"),
            P(None, ("group", "inst"), "tp"),
            P(("group", "inst"), None, None, "tp"),
            P(("group", "inst")),
            P(("group", "inst")),
            P("tp", None),
            P("tp", None),
            P(),
        ),
        out_specs=(P(None, ("group", "inst"), "tp"), P(("group", "inst"), None, None, "tp")),
        check_vma=False,
    )
```

```python
import functools
import math

import jax
import jax.numpy as jnp
from jax import lax
from jax.experimental import pallas as pl
from jax.experimental.pallas import tpu as pltpu
from jax.sharding import PartitionSpec as P

HD = 128
ROPE_BASE = 1000000.0
NORM_EPS = 1e-06
VMEM_LIMIT = 62 * 1024 * 1024
ATTEND_LIMIT = 50 * 1024 * 1024
PREPARE_LIMIT = 62 * 1024 * 1024
SMALL_LIMIT = 40 * 1024 * 1024
LIGHT = pl.CostEstimate(flops=1, bytes_accessed=1, transcendentals=0)
HEAVY = pl.CostEstimate(flops=1 << 36, bytes_accessed=1 << 28, transcendentals=0)
TILE = 16
WINDOW = 32


def quotient(value, divisor, bound):
    factor = -(-(1 << 16) // divisor)
    if bound * factor < 1 << 31 and all(
        (x * factor) >> 16 == x // divisor for x in range(bound)
    ):
        return (value * factor) >> 16
    return value // divisor


def peer_to(index, shift, count):
    return index ^ shift if count & (count - 1) == 0 else (index + shift) % count


def peer_from(index, shift, count):
    return index ^ shift if count & (count - 1) == 0 else (index + count - shift) % count


def pick_rows(count, dest_ref, pick_ref):
    rows = dest_ref.shape[0]
    for peer in range(count):
        pick_ref[peer] = 0
    for row in range(rows):
        pick_ref[quotient(dest_ref[row], rows, rows * count)] = row


def add_facts(block, peer, row, dest_ref, length_ref):
    capacity, lanes = block.shape[1:]
    rows = dest_ref.shape[0]
    slot = dest_ref[row] - peer * rows
    slot = jnp.where((slot >= 0) & (slot < rows), slot, -1)
    last = lax.broadcasted_iota(jnp.int32, (TILE, lanes), 0) == TILE - 1
    first_lanes = lax.broadcasted_iota(jnp.int32, (TILE, lanes), 1) < HD
    facts = jnp.where(first_lanes, slot, length_ref[row]).astype(jnp.float32)
    end = block[0, capacity - TILE :, :].astype(jnp.float32)
    block[0, capacity - TILE :, :] = jnp.where(last, facts, end).astype(jnp.bfloat16)


def prepare_kernel(
    count, early, chunks, dest_ref, length_ref, hidden_ref, kv_ref, key_ref, value_ref, *refs
):
    block_refs = refs[: len(early)]
    own_ref, other_ref, blocks, hidden_held, held, total = refs[len(early) : len(early) + 6]
    in_sems, out_sems, hidden_sem, weight_sems, pick_ref = refs[len(early) + 6 :]
    steps, rows, depth = hidden_ref.shape
    width = key_ref.shape[1]
    part = depth // chunks
    me = lax.axis_index("inst")

    def weights(chunk):
        span = pl.ds(chunk * part, part)
        return [
            pltpu.make_async_copy(ref.at[span], held.at[which, span], weight_sems.at[chunk, which])
            for which, ref in enumerate((key_ref, value_ref))
        ]

    hidden_copy = pltpu.make_async_copy(hidden_ref, hidden_held, hidden_sem)
    hidden_copy.start()
    for copy in weights(0):
        copy.start()
    pick_rows(count, dest_ref, pick_ref)
    fetches, stores = [], []
    for piece, shift in enumerate(early):
        row = pick_ref[peer_to(me, shift, count)]
        fetches.append(
            pltpu.make_async_copy(kv_ref.at[row], blocks.at[piece], in_sems.at[piece])
        )
        fetches[-1].start()
    for chunk in range(1, chunks):
        for copy in weights(chunk):
            copy.start()

    for piece, shift in enumerate(early):
        peer = peer_to(me, shift, count)
        fetches[piece].wait()
        add_facts(blocks.at[piece], peer, pick_ref[peer], dest_ref, length_ref)
        stores.append(
            pltpu.make_async_copy(blocks.at[piece], block_refs[piece], out_sems.at[piece])
        )
        stores[-1].start()
    hidden_copy.wait()
    hidden = hidden_held[...].reshape(steps * rows, depth)
    sums = [None, None]
    for chunk in range(chunks):
        for which, copy in enumerate(weights(chunk)):
            copy.wait()
            product = jnp.dot(
                hidden[:, chunk * part : (chunk + 1) * part],
                held[which, chunk * part : (chunk + 1) * part, :],
                preferred_element_type=jnp.float32,
            )
            sums[which] = product if chunk == 0 else sums[which] + product
    total[:, :width] = sums[0]
    total[:, width:] = sums[1]
    half = width // 2
    core = lax.axis_index("tp")
    for ref, place in ((own_ref, core), (other_ref, 1 - core)):
        at = pl.multiple_of(place * half, half)
        ref[:, :half] = total[:, pl.ds(at, half)]
        ref[:, half:] = total[:, pl.ds(pl.multiple_of(width + at, half), half)]

    for copy in stores:
        copy.wait()


def prepare(destination, lengths, hidden_new, kv_cache, key_weight, value_weight, count, early):
    steps, rows, depth = hidden_new.shape
    width = key_weight.shape[1]
    chunks = 10
    part = jax.ShapeDtypeStruct((steps * rows, width), jnp.float32)
    smem = pl.BlockSpec(memory_space=pltpu.SMEM)
    vmem = pl.BlockSpec(memory_space=pltpu.VMEM)
    hbm = pl.BlockSpec(memory_space=pl.ANY)
    outs = pl.pallas_call(
        functools.partial(prepare_kernel, count, early, chunks),
        out_shape=[jax.ShapeDtypeStruct(kv_cache.shape[1:], kv_cache.dtype)] * len(early)
        + [part, part],
        in_specs=[smem, smem, hbm, hbm, hbm, hbm],
        out_specs=[hbm] * len(early) + [vmem, vmem],
        scratch_shapes=[
            pltpu.VMEM((len(early),) + kv_cache.shape[1:], kv_cache.dtype),
            pltpu.VMEM(hidden_new.shape, hidden_new.dtype),
            pltpu.VMEM((2, depth, width), key_weight.dtype),
            pltpu.VMEM((steps * rows, 2 * width), jnp.float32),
            pltpu.SemaphoreType.DMA((len(early),)),
            pltpu.SemaphoreType.DMA((len(early),)),
            pltpu.SemaphoreType.DMA,
            pltpu.SemaphoreType.DMA((chunks, 2)),
            pltpu.SMEM((count,), jnp.int32),
        ],
        compiler_params=pltpu.CompilerParams(vmem_limit_bytes=PREPARE_LIMIT),
        cost_estimate=LIGHT,
        name="prepare",
    )(destination, lengths, hidden_new, kv_cache, key_weight, value_weight)
    return outs[: len(early)], *outs[len(early) :]


def rotation(length_ref, steps, rows):
    half = HD // 2
    line = lax.broadcasted_iota(jnp.int32, (rows, HD), 0)
    lane = lax.broadcasted_iota(jnp.int32, (steps * rows, HD), 1)
    length = jnp.zeros((rows, HD), jnp.int32)
    for row in range(rows):
        length = jnp.where(line == row, length_ref[row], length)
    position = jnp.concatenate([length + step for step in range(steps)], axis=0)
    order = (lane % half).astype(jnp.float32)
    angle = position.astype(jnp.float32) * jnp.exp(-math.log(ROPE_BASE) * 2.0 * order / HD)
    turns = jnp.floor(angle * (1.0 / math.pi) + 0.5)
    rest = ((angle - turns * 3.140625) - turns * 9.67502593994140625e-4) - turns * 1.5099579909783e-7
    sign = 1.0 - 2.0 * (turns - 2.0 * jnp.floor(turns * 0.5))
    square = rest * rest
    cosine, sine = jnp.ones_like(rest), jnp.ones_like(rest)
    for power in range(6, 0, -1):
        cosine = 1.0 - cosine * square * (1.0 / ((2 * power - 1) * (2 * power)))
        sine = 1.0 - sine * square * (1.0 / ((2 * power) * (2 * power + 1)))
    sine = sign * rest * sine
    return sign * cosine, jnp.where(lane < half, -sine, sine)


def attend_kernel(
    count,
    late,
    block,
    length_ref,
    dest_ref,
    own_ref,
    got_ref,
    gain_ref,
    query_ref,
    kv_ref,
    *refs,
):
    moved_ref, mixed_ref, small_ref = refs[:3]
    late_refs = refs[3:-5]
    fresh, query_rows, query_columns, mixed, pick_ref = refs[-5:]
    part = pl.program_id(0)
    steps, rows, query_width = query_ref.shape
    capacity, lanes = kv_ref.shape[2:]
    heads = lanes // HD
    group = query_width // lanes
    per_head = steps * group
    per_row = heads * per_head
    team = HD // per_row

    @pl.when(part == 0)
    def _():
        pick_rows(count, dest_ref, pick_ref)
        raw = own_ref[...] + got_ref[...]
        cosine, sine = rotation(length_ref, steps, rows)
        gain = gain_ref[...].astype(jnp.float32)
        for head in range(heads):
            at = slice(head * HD, (head + 1) * HD)
            piece = raw[:, at]
            mean = jnp.mean(piece * piece, axis=-1, keepdims=True)
            piece = piece * lax.rsqrt(mean + NORM_EPS) * gain
            swapped = jnp.concatenate([piece[:, HD // 2 :], piece[:, : HD // 2]], axis=1)
            turned = piece * cosine + swapped * sine
            fresh[0, :, at] = turned.astype(jnp.bfloat16).astype(jnp.float32)
        fresh[1] = raw[:, lanes:].astype(jnp.bfloat16).astype(jnp.float32)
        for step in range(steps):
            for chunk in range(query_width // HD):
                head, member = chunk // group, chunk % group
                at = head * per_head + step * group + member
                query_rows[pl.ds(at, rows, stride=per_row), :] = query_ref[
                    step, :, chunk * HD : (chunk + 1) * HD
                ].astype(jnp.float32)
        for index in range(rows // team):
            query_columns[index] = query_rows[index * HD : (index + 1) * HD, :].T

    position = lax.broadcasted_iota(jnp.int32, (capacity, HD), 0)
    column = lax.broadcasted_iota(jnp.int32, (capacity, HD), 1)
    column_item = column // per_row
    column_step = (column % per_head) // group
    column_head = lax.broadcasted_iota(jnp.int32, (HD, HD), 1) % per_row // per_head
    factor = 1.0 / math.sqrt(HD)
    teams = range(block // team)
    scores = []
    for index in teams:
        queries = query_columns[part * (block // team) + index]
        queries = jnp.concatenate(
            [jnp.where(column_head == head, queries, 0.0) for head in range(heads)], axis=0
        ).astype(jnp.bfloat16)
        score, limit = None, None
        for member in range(team):
            item = index * team + member
            row = part * block + item
            length = length_ref[row]
            kept = position < length
            landing = [position == length + step for step in range(steps)]
            for which in range(2):
                news = [fresh[which, pl.ds(step * rows + row, 1), :] for step in range(steps)]
                for head in range(heads):
                    at = slice(head * HD, (head + 1) * HD)
                    stored = jnp.where(kept, kv_ref[item, which, :, at].astype(jnp.float32), 0.0)
                    for step in range(steps):
                        stored = jnp.where(landing[step], news[step][:, at], stored)
                    moved_ref[item, which, :, at] = stored.astype(jnp.bfloat16)
            one = jnp.dot(moved_ref[item, 0], queries, preferred_element_type=jnp.float32)
            score = one if member == 0 else jnp.where(column_item == member, one, score)
            limit = length if member == 0 else jnp.where(column_item == member, length, limit)
        scores.append(jnp.where(position <= limit + column_step, score * factor, -jnp.inf))
    weights = []
    for score in scores:
        raised = jnp.exp(score - jnp.max(score, axis=0, keepdims=True))
        normaliser = jnp.sum(raised, axis=0, keepdims=True)
        weights.append((raised / normaliser).T.astype(jnp.bfloat16))
    for index in teams:
        for member in range(team):
            item = index * team + member
            row = part * block + item
            result = jnp.dot(
                weights[index][member * per_row : (member + 1) * per_row],
                moved_ref[item, 1],
                preferred_element_type=jnp.float32,
            )
            for head in range(heads):
                at = pl.multiple_of(row * per_row + head * per_head, per_head)
                mixed[pl.ds(at, per_head), :] = result[
                    head * per_head : (head + 1) * per_head, head * HD : (head + 1) * HD
                ]

    me = lax.axis_index("inst")
    for late_ref, shift in zip(late_refs, late):
        item = pick_ref[peer_to(me, shift, count)] - part * block

        @pl.when((item >= 0) & (item < block))
        def _():
            late_ref[...] = moved_ref[item]

    @pl.when(part == pl.num_programs(0) - 1)
    def _():
        mixed_ref[...] = mixed[...].astype(jnp.bfloat16)
        for peer in range(count):
            row = pick_ref[peer]
            small_ref[peer, :per_row, :] = mixed[
                pl.ds(pl.multiple_of(row * per_row, per_row), per_row), :
            ].astype(jnp.bfloat16)
            news = []
            for which in range(2):
                for step in range(steps):
                    new = fresh[which, pl.ds(step * rows + row, 1), :]
                    news += [new[:, h * HD : (h + 1) * HD] for h in range(heads)]
            slot = dest_ref[row] - peer * rows
            slot = jnp.where((slot >= 0) & (slot < rows), slot, -1).astype(jnp.float32)
            news.append(jnp.full((1, HD), slot))
            fill = small_ref.shape[1] - per_row - 2 * steps * heads - 1
            news.append(jnp.full((fill, HD), length_ref[row].astype(jnp.float32)))
            small_ref[peer, per_row:, :] = jnp.concatenate(news, axis=0).astype(jnp.bfloat16)


def attend(kv_cache, queries, own, got, gain, lengths, destination, count, late):
    steps, rows, query_width = queries.shape
    capacity, lanes = kv_cache.shape[2:]
    heads = lanes // HD
    per_row = steps * query_width // HD
    block = 8
    small_rows = per_row + -(-(2 * steps * heads + 2) // TILE) * TILE
    small = jax.ShapeDtypeStruct((count, small_rows, HD), jnp.bfloat16)
    smem = pl.BlockSpec(memory_space=pltpu.SMEM)
    vmem = pl.BlockSpec(memory_space=pltpu.VMEM)
    cache_block = pl.BlockSpec((block, 2, capacity, lanes), lambda i: (i, 0, 0, 0))
    return pl.pallas_call(
        functools.partial(attend_kernel, count, late, block),
        grid=(rows // block,),
        out_shape=[
            jax.ShapeDtypeStruct(kv_cache.shape, kv_cache.dtype),
            jax.ShapeDtypeStruct((rows * per_row, HD), jnp.bfloat16),
            small,
        ]
        + [jax.ShapeDtypeStruct(kv_cache.shape[1:], kv_cache.dtype)] * len(late),
        in_specs=[smem, smem, vmem, vmem, vmem, vmem, cache_block],
        out_specs=[cache_block, vmem, vmem] + [vmem] * len(late),
        scratch_shapes=[
            pltpu.VMEM((2, steps * rows, lanes), jnp.float32),
            pltpu.VMEM((rows * per_row, HD), jnp.float32),
            pltpu.VMEM((rows * per_row // HD, HD, HD), jnp.float32),
            pltpu.VMEM((rows * per_row, HD), jnp.float32),
            pltpu.SMEM((count,), jnp.int32),
        ],
        compiler_params=pltpu.CompilerParams(vmem_limit_bytes=ATTEND_LIMIT),
        cost_estimate=HEAVY,
        name="attend",
    )(lengths, destination, own, got, gain, queries, kv_cache)


def read_facts(block):
    capacity = block.shape[1]
    facts = block[0, capacity - TILE :, :].astype(jnp.float32)[TILE - 1 :]
    return (
        jnp.max(facts[:, :HD]).astype(jnp.int32),
        jnp.max(facts[:, HD : 2 * HD]).astype(jnp.int32),
    )


def window_start(length, capacity):
    return pl.multiple_of(jnp.minimum(length // TILE * TILE, capacity - WINDOW), TILE)


def clean(block, length, out):
    capacity, lanes = block.shape[1:]
    kept = lax.broadcasted_iota(jnp.int32, (capacity, HD), 0) < length
    for which in range(2):
        for at in range(0, lanes, HD):
            stored = block[which, :, at : at + HD].astype(jnp.float32)
            out[which, :, at : at + HD] = jnp.where(kept, stored, 0.0).astype(jnp.bfloat16)


def insert(window, news, ahead, steps, out):
    height, lanes = window.shape[1:]
    heads = lanes // HD
    position = lax.broadcasted_iota(jnp.int32, (height, lanes), 0)
    for which in range(2):
        stored = window[which].astype(jnp.float32)
        for step in range(steps):
            at = (which * steps + step) * heads
            new = jnp.concatenate([news[at + h : at + h + 1] for h in range(heads)], axis=1)
            stored = jnp.where(position == ahead + step, new, stored)
        out[which] = stored.astype(jnp.bfloat16)


def land_kernel(pieces, *refs):
    blocks = refs[:pieces]
    _, out_ref, window_ref, buffer, sems, slots = refs[pieces:]
    capacity = buffer.shape[2]

    def store(piece):
        slot = jnp.maximum(slots[piece], 0)
        return pltpu.make_async_copy(buffer.at[piece], out_ref.at[slot], sems.at[piece])

    facts = [read_facts(block) for block in blocks]
    for piece, (slot, length) in enumerate(facts):
        slots[piece] = slot

        @pl.when(slot >= 0)
        def _():
            clean(blocks[piece], length, buffer.at[piece])
            store(piece).start()
            start = window_start(length, capacity)
            window_ref[piece] = buffer[piece, :, pl.ds(start, WINDOW), :]

    for piece in range(pieces):

        @pl.when(slots[piece] >= 0)
        def _():
            store(piece).wait()


def land(got, moved):
    pieces = len(got)
    vmem = pl.BlockSpec(memory_space=pltpu.VMEM)
    hbm = pl.BlockSpec(memory_space=pl.ANY)
    return pl.pallas_call(
        functools.partial(land_kernel, pieces),
        out_shape=[
            jax.ShapeDtypeStruct(moved.shape, moved.dtype),
            jax.ShapeDtypeStruct((pieces, 2, WINDOW, moved.shape[3]), moved.dtype),
        ],
        in_specs=[vmem] * pieces + [hbm],
        out_specs=[hbm, vmem],
        scratch_shapes=[
            pltpu.VMEM((pieces,) + moved.shape[1:], moved.dtype),
            pltpu.SemaphoreType.DMA((pieces,)),
            pltpu.SMEM((pieces,), jnp.int32),
        ],
        input_output_aliases={pieces: 0},
        compiler_params=pltpu.CompilerParams(vmem_limit_bytes=SMALL_LIMIT),
        cost_estimate=HEAVY,
        name="land",
    )(*got, moved)


def read_small(small_ref, peer, per_row, line):
    rows = small_ref[peer, per_row:, :].astype(jnp.float32)
    return jnp.max(rows[line : line + 1]).astype(jnp.int32)


def settle_kernel(
    count,
    early,
    group,
    mixed_ref,
    small_ref,
    window_ref,
    _,
    out_ref,
    moved_ref,
    mixed,
    windows,
    sems,
    slots,
    lengths,
):
    steps, rows, query_width = out_ref.shape
    per_row = steps * query_width // HD
    capacity, lanes = moved_ref.shape[2:]
    line = 2 * steps * (lanes // HD)
    me = lax.axis_index("inst")

    def store(piece):
        slot = jnp.maximum(slots[early[piece]], 0)
        start = window_start(lengths[early[piece]], capacity)
        return pltpu.make_async_copy(
            windows.at[piece], moved_ref.at[slot, :, pl.ds(start, WINDOW), :], sems.at[piece]
        )

    for shift in range(1, count):
        peer = peer_from(me, shift, count)
        slots[shift] = read_small(small_ref, peer, per_row, line)
        lengths[shift] = read_small(small_ref, peer, per_row, line + 1)

    for piece, shift in enumerate(early):

        @pl.when(slots[shift] >= 0)
        def _():
            peer = peer_from(me, shift, count)
            news = small_ref[peer, per_row:, :].astype(jnp.float32)
            ahead = lengths[shift] - window_start(lengths[shift], capacity)
            insert(window_ref.at[piece], news, ahead, steps, windows.at[piece])
            store(piece).start()

    mixed[...] = mixed_ref[...].astype(jnp.float32)
    for shift in range(1, count):

        @pl.when(slots[shift] >= 0)
        def _():
            mixed[pl.ds(pl.multiple_of(slots[shift] * per_row, per_row), per_row), :] = small_ref[
                peer_from(me, shift, count), :per_row, :
            ].astype(jnp.float32)

    for step in range(steps):
        for chunk in range(query_width // HD):
            head, member = chunk // group, chunk % group
            at = head * steps * group + step * group + member
            out_ref[step, :, chunk * HD : (chunk + 1) * HD] = mixed[
                pl.ds(at, rows, stride=per_row), :
            ].astype(jnp.bfloat16)

    for piece, shift in enumerate(early):

        @pl.when(slots[shift] >= 0)
        def _():
            store(piece).wait()


def settle(mixed, small, windows, moved, shape, group, count, early):
    vmem = pl.BlockSpec(memory_space=pltpu.VMEM)
    hbm = pl.BlockSpec(memory_space=pl.ANY)
    return pl.pallas_call(
        functools.partial(settle_kernel, count, early, group),
        out_shape=[
            jax.ShapeDtypeStruct(shape, jnp.bfloat16),
            jax.ShapeDtypeStruct(moved.shape, moved.dtype),
        ],
        in_specs=[vmem, vmem, vmem, hbm],
        out_specs=[vmem, hbm],
        scratch_shapes=[
            pltpu.VMEM(mixed.shape, jnp.float32),
            pltpu.VMEM(windows.shape, windows.dtype),
            pltpu.SemaphoreType.DMA((len(early),)),
            pltpu.SMEM((count,), jnp.int32),
            pltpu.SMEM((count,), jnp.int32),
        ],
        input_output_aliases={3: 1},
        compiler_params=pltpu.CompilerParams(vmem_limit_bytes=SMALL_LIMIT),
        cost_estimate=LIGHT,
        name="settle",
    )(mixed, small, windows, moved)


def finish_kernel(count, late, steps, *refs):
    blocks = refs[: len(late)]
    small_ref, _, out_ref, sems, slots = refs[len(late) :]
    line = 2 * steps * (out_ref.shape[3] // HD)
    facts = -(-(line + 2) // TILE) * TILE
    me = lax.axis_index("inst")

    def store(piece):
        slot = jnp.maximum(slots[piece], 0)
        return pltpu.make_async_copy(blocks[piece], out_ref.at[slot], sems.at[piece])

    for piece, shift in enumerate(late):
        peer = peer_from(me, shift, count)
        slots[piece] = read_small(small_ref, peer, small_ref.shape[1] - facts, line)
    for piece in range(len(late)):
        pl.when(slots[piece] >= 0)(store(piece).start)
    for piece in range(len(late)):
        pl.when(slots[piece] >= 0)(store(piece).wait)


def finish(got, small, moved, steps, count, late):
    vmem = pl.BlockSpec(memory_space=pltpu.VMEM)
    hbm = pl.BlockSpec(memory_space=pl.ANY)
    return pl.pallas_call(
        functools.partial(finish_kernel, count, late, steps),
        out_shape=jax.ShapeDtypeStruct(moved.shape, moved.dtype),
        in_specs=[vmem] * len(got) + [vmem, hbm],
        out_specs=hbm,
        scratch_shapes=[
            pltpu.SemaphoreType.DMA((len(got),)),
            pltpu.SMEM((len(got),), jnp.int32),
        ],
        input_output_aliases={len(got) + 1: 0},
        compiler_params=pltpu.CompilerParams(vmem_limit_bytes=SMALL_LIMIT),
        cost_estimate=LIGHT,
        name="finish",
    )(*got, small, moved)


def local(hidden_new, queries, kv_cache, lengths, destination, key_weight, value_weight, key_gain):
    steps = queries.shape[0]
    group = queries.shape[2] // kv_cache.shape[3]
    count = lax.axis_size("inst")
    half = max(count // 2, 1)
    early = list(range(half, count - 1)) + [half - 1] * (half > 1)
    late = [count - 1] + list(range(half - 2, 0, -1))

    def send(block, shift):
        pairs = [(i, peer_to(i, shift, count)) for i in range(count)]
        return lax.ppermute(block, "inst", pairs)

    blocks, own, other = prepare(
        destination, lengths, hidden_new, kv_cache, key_weight, value_weight, count, early
    )
    early_got = [send(block, shift) for block, shift in zip(blocks, early)]
    got = lax.ppermute(other, "tp", [(0, 1), (1, 0)])
    moved, mixed, small, *late_blocks = attend(
        kv_cache,
        queries,
        own,
        got,
        key_gain[None, :],
        lengths,
        destination,
        count,
        late,
    )
    late_got = [send(block, shift) for block, shift in zip(late_blocks, late)]
    small_got = lax.all_to_all(small, "inst", 0, 0, tiled=True)
    moved, windows = land(early_got, moved)
    attended, moved = settle(mixed, small_got, windows, moved, queries.shape, group, count, early)
    return attended, finish(late_got, small_got, moved, steps, count, late)


def solution(mesh):
    return jax.shard_map(
        local,
        mesh=mesh,
        in_specs=(
            P(None, ("group", "inst"), "tp"),
            P(None, ("group", "inst"), "tp"),
            P(("group", "inst"), None, None, "tp"),
            P(("group", "inst")),
            P(("group", "inst")),
            P("tp", None),
            P("tp", None),
            P(),
        ),
        out_specs=(P(None, ("group", "inst"), "tp"), P(("group", "inst"), None, None, "tp")),
        check_vma=False,
    )
```

```python
import functools
import math

import jax
import jax.numpy as jnp
from jax import lax
from jax.experimental import pallas as pl
from jax.experimental.pallas import tpu as pltpu
from jax.sharding import PartitionSpec as P

HD = 128
ROPE_BASE = 1000000.0
NORM_EPS = 1e-06
VMEM_LIMIT = 62 * 1024 * 1024
ATTEND_LIMIT = 50 * 1024 * 1024
PREPARE_LIMIT = 62 * 1024 * 1024
SMALL_LIMIT = 40 * 1024 * 1024
LIGHT = pl.CostEstimate(flops=1, bytes_accessed=1, transcendentals=0)
HEAVY = pl.CostEstimate(flops=1 << 36, bytes_accessed=1 << 28, transcendentals=0)
TILE = 16
WINDOW = 32


def quotient(value, divisor, bound):
    factor = -(-(1 << 16) // divisor)
    if bound * factor < 1 << 31 and all(
        (x * factor) >> 16 == x // divisor for x in range(bound)
    ):
        return (value * factor) >> 16
    return value // divisor


def peer_to(index, shift, count):
    return index ^ shift if count & (count - 1) == 0 else (index + shift) % count


def peer_from(index, shift, count):
    return index ^ shift if count & (count - 1) == 0 else (index + count - shift) % count


def pick_rows(count, dest_ref, pick_ref):
    rows = dest_ref.shape[0]
    for peer in range(count):
        pick_ref[peer] = 0
    for row in range(rows):
        pick_ref[quotient(dest_ref[row], rows, rows * count)] = row


def add_facts(block, peer, row, dest_ref, length_ref):
    capacity, lanes = block.shape[1:]
    rows = dest_ref.shape[0]
    slot = dest_ref[row] - peer * rows
    slot = jnp.where((slot >= 0) & (slot < rows), slot, -1)
    last = lax.broadcasted_iota(jnp.int32, (TILE, lanes), 0) == TILE - 1
    first_lanes = lax.broadcasted_iota(jnp.int32, (TILE, lanes), 1) < HD
    facts = jnp.where(first_lanes, slot, length_ref[row]).astype(jnp.float32)
    end = block[0, capacity - TILE :, :].astype(jnp.float32)
    block[0, capacity - TILE :, :] = jnp.where(last, facts, end).astype(jnp.bfloat16)


def prepare_kernel(
    count, early, chunks, dest_ref, length_ref, hidden_ref, kv_ref, key_ref, value_ref, *refs
):
    block_refs = refs[: len(early)]
    own_ref, other_ref, blocks, hidden_held, held, total = refs[len(early) : len(early) + 6]
    in_sems, out_sems, hidden_sem, weight_sems, pick_ref = refs[len(early) + 6 :]
    steps, rows, depth = hidden_ref.shape
    width = key_ref.shape[1]
    part = depth // chunks
    me = lax.axis_index("inst")

    def weights(chunk):
        span = pl.ds(chunk * part, part)
        return [
            pltpu.make_async_copy(ref.at[span], held.at[which, span], weight_sems.at[chunk, which])
            for which, ref in enumerate((key_ref, value_ref))
        ]

    hidden_copy = pltpu.make_async_copy(hidden_ref, hidden_held, hidden_sem)
    hidden_copy.start()
    for chunk in range(chunks):
        for copy in weights(chunk):
            copy.start()
    pick_rows(count, dest_ref, pick_ref)
    fetches, stores = [], []
    for piece, shift in enumerate(early):
        row = pick_ref[peer_to(me, shift, count)]
        fetches.append(
            pltpu.make_async_copy(kv_ref.at[row], blocks.at[piece], in_sems.at[piece])
        )
        fetches[-1].start()

    for piece, shift in enumerate(early):
        peer = peer_to(me, shift, count)
        fetches[piece].wait()
        add_facts(blocks.at[piece], peer, pick_ref[peer], dest_ref, length_ref)
        stores.append(
            pltpu.make_async_copy(blocks.at[piece], block_refs[piece], out_sems.at[piece])
        )
        stores[-1].start()
    hidden_copy.wait()
    hidden = hidden_held[...].reshape(steps * rows, depth)
    sums = [None, None]
    for chunk in range(chunks):
        for which, copy in enumerate(weights(chunk)):
            copy.wait()
            product = jnp.dot(
                hidden[:, chunk * part : (chunk + 1) * part],
                held[which, chunk * part : (chunk + 1) * part, :],
                preferred_element_type=jnp.float32,
            )
            sums[which] = product if chunk == 0 else sums[which] + product
    total[:, :width] = sums[0]
    total[:, width:] = sums[1]
    half = width // 2
    core = lax.axis_index("tp")
    for ref, place in ((own_ref, core), (other_ref, 1 - core)):
        at = pl.multiple_of(place * half, half)
        ref[:, :half] = total[:, pl.ds(at, half)]
        ref[:, half:] = total[:, pl.ds(pl.multiple_of(width + at, half), half)]

    for copy in stores:
        copy.wait()


def prepare(destination, lengths, hidden_new, kv_cache, key_weight, value_weight, count, early):
    steps, rows, depth = hidden_new.shape
    width = key_weight.shape[1]
    chunks = 5
    part = jax.ShapeDtypeStruct((steps * rows, width), jnp.float32)
    smem = pl.BlockSpec(memory_space=pltpu.SMEM)
    vmem = pl.BlockSpec(memory_space=pltpu.VMEM)
    hbm = pl.BlockSpec(memory_space=pl.ANY)
    outs = pl.pallas_call(
        functools.partial(prepare_kernel, count, early, chunks),
        out_shape=[jax.ShapeDtypeStruct(kv_cache.shape[1:], kv_cache.dtype)] * len(early)
        + [part, part],
        in_specs=[smem, smem, hbm, hbm, hbm, hbm],
        out_specs=[hbm] * len(early) + [vmem, vmem],
        scratch_shapes=[
            pltpu.VMEM((len(early),) + kv_cache.shape[1:], kv_cache.dtype),
            pltpu.VMEM(hidden_new.shape, hidden_new.dtype),
            pltpu.VMEM((2, depth, width), key_weight.dtype),
            pltpu.VMEM((steps * rows, 2 * width), jnp.float32),
            pltpu.SemaphoreType.DMA((len(early),)),
            pltpu.SemaphoreType.DMA((len(early),)),
            pltpu.SemaphoreType.DMA,
            pltpu.SemaphoreType.DMA((chunks, 2)),
            pltpu.SMEM((count,), jnp.int32),
        ],
        compiler_params=pltpu.CompilerParams(vmem_limit_bytes=PREPARE_LIMIT),
        cost_estimate=LIGHT,
        name="prepare",
    )(destination, lengths, hidden_new, kv_cache, key_weight, value_weight)
    return outs[: len(early)], *outs[len(early) :]


def rotation(length_ref, steps, rows):
    half = HD // 2
    line = lax.broadcasted_iota(jnp.int32, (rows, HD), 0)
    lane = lax.broadcasted_iota(jnp.int32, (steps * rows, HD), 1)
    length = jnp.zeros((rows, HD), jnp.int32)
    for row in range(rows):
        length = jnp.where(line == row, length_ref[row], length)
    position = jnp.concatenate([length + step for step in range(steps)], axis=0)
    order = (lane % half).astype(jnp.float32)
    angle = position.astype(jnp.float32) * jnp.exp(-math.log(ROPE_BASE) * 2.0 * order / HD)
    turns = jnp.floor(angle * (1.0 / math.pi) + 0.5)
    rest = ((angle - turns * 3.140625) - turns * 9.67502593994140625e-4) - turns * 1.5099579909783e-7
    sign = 1.0 - 2.0 * (turns - 2.0 * jnp.floor(turns * 0.5))
    square = rest * rest
    cosine, sine = jnp.ones_like(rest), jnp.ones_like(rest)
    for power in range(6, 0, -1):
        cosine = 1.0 - cosine * square * (1.0 / ((2 * power - 1) * (2 * power)))
        sine = 1.0 - sine * square * (1.0 / ((2 * power) * (2 * power + 1)))
    sine = sign * rest * sine
    return sign * cosine, jnp.where(lane < half, -sine, sine)


def attend_kernel(
    count,
    late,
    block,
    length_ref,
    dest_ref,
    own_ref,
    got_ref,
    gain_ref,
    query_ref,
    kv_ref,
    *refs,
):
    moved_ref, mixed_ref, small_ref = refs[:3]
    late_refs = refs[3:-5]
    fresh, query_rows, query_columns, mixed, pick_ref = refs[-5:]
    part = pl.program_id(0)
    steps, rows, query_width = query_ref.shape
    capacity, lanes = kv_ref.shape[2:]
    heads = lanes // HD
    group = query_width // lanes
    per_head = steps * group
    per_row = heads * per_head
    team = HD // per_row

    @pl.when(part == 0)
    def _():
        pick_rows(count, dest_ref, pick_ref)
        raw = own_ref[...] + got_ref[...]
        cosine, sine = rotation(length_ref, steps, rows)
        gain = gain_ref[...].astype(jnp.float32)
        for head in range(heads):
            at = slice(head * HD, (head + 1) * HD)
            piece = raw[:, at]
            mean = jnp.mean(piece * piece, axis=-1, keepdims=True)
            piece = piece * lax.rsqrt(mean + NORM_EPS) * gain
            swapped = jnp.concatenate([piece[:, HD // 2 :], piece[:, : HD // 2]], axis=1)
            turned = piece * cosine + swapped * sine
            fresh[0, :, at] = turned.astype(jnp.bfloat16).astype(jnp.float32)
        fresh[1] = raw[:, lanes:].astype(jnp.bfloat16).astype(jnp.float32)
        for step in range(steps):
            for chunk in range(query_width // HD):
                head, member = chunk // group, chunk % group
                at = head * per_head + step * group + member
                query_rows[pl.ds(at, rows, stride=per_row), :] = query_ref[
                    step, :, chunk * HD : (chunk + 1) * HD
                ].astype(jnp.float32)
        for index in range(rows // team):
            query_columns[index] = query_rows[index * HD : (index + 1) * HD, :].T

    position = lax.broadcasted_iota(jnp.int32, (capacity, HD), 0)
    column = lax.broadcasted_iota(jnp.int32, (capacity, HD), 1)
    column_item = column // per_row
    column_step = (column % per_head) // group
    column_head = lax.broadcasted_iota(jnp.int32, (HD, HD), 1) % per_row // per_head
    factor = 1.0 / math.sqrt(HD)
    teams = range(block // team)
    scores = []
    for index in teams:
        queries = query_columns[part * (block // team) + index]
        queries = jnp.concatenate(
            [jnp.where(column_head == head, queries, 0.0) for head in range(heads)], axis=0
        ).astype(jnp.bfloat16)
        score, limit = None, None
        for member in range(team):
            item = index * team + member
            row = part * block + item
            length = length_ref[row]
            kept = position < length
            landing = [position == length + step for step in range(steps)]
            for which in range(2):
                news = [fresh[which, pl.ds(step * rows + row, 1), :] for step in range(steps)]
                for head in range(heads):
                    at = slice(head * HD, (head + 1) * HD)
                    stored = jnp.where(kept, kv_ref[item, which, :, at].astype(jnp.float32), 0.0)
                    for step in range(steps):
                        stored = jnp.where(landing[step], news[step][:, at], stored)
                    moved_ref[item, which, :, at] = stored.astype(jnp.bfloat16)
            one = jnp.dot(moved_ref[item, 0], queries, preferred_element_type=jnp.float32)
            score = one if member == 0 else jnp.where(column_item == member, one, score)
            limit = length if member == 0 else jnp.where(column_item == member, length, limit)
        scores.append(jnp.where(position <= limit + column_step, score * factor, -jnp.inf))
    weights = []
    for score in scores:
        raised = jnp.exp(score - jnp.max(score, axis=0, keepdims=True))
        normaliser = jnp.sum(raised, axis=0, keepdims=True)
        weights.append((raised / normaliser).T.astype(jnp.bfloat16))
    for index in teams:
        for member in range(team):
            item = index * team + member
            row = part * block + item
            result = jnp.dot(
                weights[index][member * per_row : (member + 1) * per_row],
                moved_ref[item, 1],
                preferred_element_type=jnp.float32,
            )
            for head in range(heads):
                at = pl.multiple_of(row * per_row + head * per_head, per_head)
                mixed[pl.ds(at, per_head), :] = result[
                    head * per_head : (head + 1) * per_head, head * HD : (head + 1) * HD
                ]

    me = lax.axis_index("inst")
    for late_ref, shift in zip(late_refs, late):
        item = pick_ref[peer_to(me, shift, count)] - part * block

        @pl.when((item >= 0) & (item < block))
        def _():
            late_ref[...] = moved_ref[item]

    @pl.when(part == pl.num_programs(0) - 1)
    def _():
        mixed_ref[...] = mixed[...].astype(jnp.bfloat16)
        for peer in range(count):
            row = pick_ref[peer]
            small_ref[peer, :per_row, :] = mixed[
                pl.ds(pl.multiple_of(row * per_row, per_row), per_row), :
            ].astype(jnp.bfloat16)
            news = []
            for which in range(2):
                for step in range(steps):
                    new = fresh[which, pl.ds(step * rows + row, 1), :]
                    news += [new[:, h * HD : (h + 1) * HD] for h in range(heads)]
            slot = dest_ref[row] - peer * rows
            slot = jnp.where((slot >= 0) & (slot < rows), slot, -1).astype(jnp.float32)
            news.append(jnp.full((1, HD), slot))
            fill = small_ref.shape[1] - per_row - 2 * steps * heads - 1
            news.append(jnp.full((fill, HD), length_ref[row].astype(jnp.float32)))
            small_ref[peer, per_row:, :] = jnp.concatenate(news, axis=0).astype(jnp.bfloat16)


def attend(kv_cache, queries, own, got, gain, lengths, destination, count, late):
    steps, rows, query_width = queries.shape
    capacity, lanes = kv_cache.shape[2:]
    heads = lanes // HD
    per_row = steps * query_width // HD
    block = 8
    small_rows = per_row + -(-(2 * steps * heads + 2) // TILE) * TILE
    small = jax.ShapeDtypeStruct((count, small_rows, HD), jnp.bfloat16)
    smem = pl.BlockSpec(memory_space=pltpu.SMEM)
    vmem = pl.BlockSpec(memory_space=pltpu.VMEM)
    cache_block = pl.BlockSpec((block, 2, capacity, lanes), lambda i: (i, 0, 0, 0))
    return pl.pallas_call(
        functools.partial(attend_kernel, count, late, block),
        grid=(rows // block,),
        out_shape=[
            jax.ShapeDtypeStruct(kv_cache.shape, kv_cache.dtype),
            jax.ShapeDtypeStruct((rows * per_row, HD), jnp.bfloat16),
            small,
        ]
        + [jax.ShapeDtypeStruct(kv_cache.shape[1:], kv_cache.dtype)] * len(late),
        in_specs=[smem, smem, vmem, vmem, vmem, vmem, cache_block],
        out_specs=[cache_block, vmem, vmem] + [vmem] * len(late),
        scratch_shapes=[
            pltpu.VMEM((2, steps * rows, lanes), jnp.float32),
            pltpu.VMEM((rows * per_row, HD), jnp.float32),
            pltpu.VMEM((rows * per_row // HD, HD, HD), jnp.float32),
            pltpu.VMEM((rows * per_row, HD), jnp.float32),
            pltpu.SMEM((count,), jnp.int32),
        ],
        compiler_params=pltpu.CompilerParams(vmem_limit_bytes=ATTEND_LIMIT),
        cost_estimate=HEAVY,
        name="attend",
    )(lengths, destination, own, got, gain, queries, kv_cache)


def read_facts(block):
    capacity = block.shape[1]
    facts = block[0, capacity - TILE :, :].astype(jnp.float32)[TILE - 1 :]
    return (
        jnp.max(facts[:, :HD]).astype(jnp.int32),
        jnp.max(facts[:, HD : 2 * HD]).astype(jnp.int32),
    )


def window_start(length, capacity):
    return pl.multiple_of(jnp.minimum(length // TILE * TILE, capacity - WINDOW), TILE)


def clean(block, length, out):
    capacity, lanes = block.shape[1:]
    kept = lax.broadcasted_iota(jnp.int32, (capacity, HD), 0) < length
    for which in range(2):
        for at in range(0, lanes, HD):
            stored = block[which, :, at : at + HD].astype(jnp.float32)
            out[which, :, at : at + HD] = jnp.where(kept, stored, 0.0).astype(jnp.bfloat16)


def insert(window, news, ahead, steps, out):
    height, lanes = window.shape[1:]
    heads = lanes // HD
    position = lax.broadcasted_iota(jnp.int32, (height, lanes), 0)
    for which in range(2):
        stored = window[which].astype(jnp.float32)
        for step in range(steps):
            at = (which * steps + step) * heads
            new = jnp.concatenate([news[at + h : at + h + 1] for h in range(heads)], axis=1)
            stored = jnp.where(position == ahead + step, new, stored)
        out[which] = stored.astype(jnp.bfloat16)


def land_kernel(pieces, *refs):
    blocks = refs[:pieces]
    _, out_ref, window_ref, buffer, sems, slots = refs[pieces:]
    capacity = buffer.shape[2]

    def store(piece):
        slot = jnp.maximum(slots[piece], 0)
        return pltpu.make_async_copy(buffer.at[piece], out_ref.at[slot], sems.at[piece])

    facts = [read_facts(block) for block in blocks]
    for piece, (slot, length) in enumerate(facts):
        slots[piece] = slot

        @pl.when(slot >= 0)
        def _():
            clean(blocks[piece], length, buffer.at[piece])
            store(piece).start()
            start = window_start(length, capacity)
            window_ref[piece] = buffer[piece, :, pl.ds(start, WINDOW), :]

    for piece in range(pieces):

        @pl.when(slots[piece] >= 0)
        def _():
            store(piece).wait()


def land(got, moved):
    pieces = len(got)
    vmem = pl.BlockSpec(memory_space=pltpu.VMEM)
    hbm = pl.BlockSpec(memory_space=pl.ANY)
    return pl.pallas_call(
        functools.partial(land_kernel, pieces),
        out_shape=[
            jax.ShapeDtypeStruct(moved.shape, moved.dtype),
            jax.ShapeDtypeStruct((pieces, 2, WINDOW, moved.shape[3]), moved.dtype),
        ],
        in_specs=[vmem] * pieces + [hbm],
        out_specs=[hbm, vmem],
        scratch_shapes=[
            pltpu.VMEM((pieces,) + moved.shape[1:], moved.dtype),
            pltpu.SemaphoreType.DMA((pieces,)),
            pltpu.SMEM((pieces,), jnp.int32),
        ],
        input_output_aliases={pieces: 0},
        compiler_params=pltpu.CompilerParams(vmem_limit_bytes=SMALL_LIMIT),
        cost_estimate=HEAVY,
        name="land",
    )(*got, moved)


def read_small(small_ref, peer, per_row, line):
    rows = small_ref[peer, per_row:, :].astype(jnp.float32)
    return jnp.max(rows[line : line + 1]).astype(jnp.int32)


def settle_kernel(
    count,
    early,
    group,
    mixed_ref,
    small_ref,
    window_ref,
    _,
    out_ref,
    moved_ref,
    mixed,
    windows,
    sems,
    slots,
    lengths,
):
    steps, rows, query_width = out_ref.shape
    per_row = steps * query_width // HD
    capacity, lanes = moved_ref.shape[2:]
    line = 2 * steps * (lanes // HD)
    me = lax.axis_index("inst")

    def store(piece):
        slot = jnp.maximum(slots[early[piece]], 0)
        start = window_start(lengths[early[piece]], capacity)
        return pltpu.make_async_copy(
            windows.at[piece], moved_ref.at[slot, :, pl.ds(start, WINDOW), :], sems.at[piece]
        )

    for shift in range(1, count):
        peer = peer_from(me, shift, count)
        slots[shift] = read_small(small_ref, peer, per_row, line)
        lengths[shift] = read_small(small_ref, peer, per_row, line + 1)

    for piece, shift in enumerate(early):

        @pl.when(slots[shift] >= 0)
        def _():
            peer = peer_from(me, shift, count)
            news = small_ref[peer, per_row:, :].astype(jnp.float32)
            ahead = lengths[shift] - window_start(lengths[shift], capacity)
            insert(window_ref.at[piece], news, ahead, steps, windows.at[piece])
            store(piece).start()

    mixed[...] = mixed_ref[...].astype(jnp.float32)
    for shift in range(1, count):

        @pl.when(slots[shift] >= 0)
        def _():
            mixed[pl.ds(pl.multiple_of(slots[shift] * per_row, per_row), per_row), :] = small_ref[
                peer_from(me, shift, count), :per_row, :
            ].astype(jnp.float32)

    for step in range(steps):
        for chunk in range(query_width // HD):
            head, member = chunk // group, chunk % group
            at = head * steps * group + step * group + member
            out_ref[step, :, chunk * HD : (chunk + 1) * HD] = mixed[
                pl.ds(at, rows, stride=per_row), :
            ].astype(jnp.bfloat16)

    for piece, shift in enumerate(early):

        @pl.when(slots[shift] >= 0)
        def _():
            store(piece).wait()


def settle(mixed, small, windows, moved, shape, group, count, early):
    vmem = pl.BlockSpec(memory_space=pltpu.VMEM)
    hbm = pl.BlockSpec(memory_space=pl.ANY)
    return pl.pallas_call(
        functools.partial(settle_kernel, count, early, group),
        out_shape=[
            jax.ShapeDtypeStruct(shape, jnp.bfloat16),
            jax.ShapeDtypeStruct(moved.shape, moved.dtype),
        ],
        in_specs=[vmem, vmem, vmem, hbm],
        out_specs=[vmem, hbm],
        scratch_shapes=[
            pltpu.VMEM(mixed.shape, jnp.float32),
            pltpu.VMEM(windows.shape, windows.dtype),
            pltpu.SemaphoreType.DMA((len(early),)),
            pltpu.SMEM((count,), jnp.int32),
            pltpu.SMEM((count,), jnp.int32),
        ],
        input_output_aliases={3: 1},
        compiler_params=pltpu.CompilerParams(vmem_limit_bytes=SMALL_LIMIT),
        cost_estimate=LIGHT,
        name="settle",
    )(mixed, small, windows, moved)


def finish_kernel(count, late, steps, *refs):
    blocks = refs[: len(late)]
    small_ref, _, out_ref, sems, slots = refs[len(late) :]
    line = 2 * steps * (out_ref.shape[3] // HD)
    facts = -(-(line + 2) // TILE) * TILE
    me = lax.axis_index("inst")

    def store(piece):
        slot = jnp.maximum(slots[piece], 0)
        return pltpu.make_async_copy(blocks[piece], out_ref.at[slot], sems.at[piece])

    for piece, shift in enumerate(late):
        peer = peer_from(me, shift, count)
        slots[piece] = read_small(small_ref, peer, small_ref.shape[1] - facts, line)
    for piece in range(len(late)):
        pl.when(slots[piece] >= 0)(store(piece).start)
    for piece in range(len(late)):
        pl.when(slots[piece] >= 0)(store(piece).wait)


def finish(got, small, moved, steps, count, late):
    vmem = pl.BlockSpec(memory_space=pltpu.VMEM)
    hbm = pl.BlockSpec(memory_space=pl.ANY)
    return pl.pallas_call(
        functools.partial(finish_kernel, count, late, steps),
        out_shape=jax.ShapeDtypeStruct(moved.shape, moved.dtype),
        in_specs=[vmem] * len(got) + [vmem, hbm],
        out_specs=hbm,
        scratch_shapes=[
            pltpu.SemaphoreType.DMA((len(got),)),
            pltpu.SMEM((len(got),), jnp.int32),
        ],
        input_output_aliases={len(got) + 1: 0},
        compiler_params=pltpu.CompilerParams(vmem_limit_bytes=SMALL_LIMIT),
        cost_estimate=LIGHT,
        name="finish",
    )(*got, small, moved)


def local(hidden_new, queries, kv_cache, lengths, destination, key_weight, value_weight, key_gain):
    steps = queries.shape[0]
    group = queries.shape[2] // kv_cache.shape[3]
    count = lax.axis_size("inst")
    half = max(count // 2, 1)
    early = list(range(half, count - 1)) + [half - 1] * (half > 1)
    late = [count - 1] + list(range(half - 2, 0, -1))

    def send(block, shift):
        pairs = [(i, peer_to(i, shift, count)) for i in range(count)]
        return lax.ppermute(block, "inst", pairs)

    blocks, own, other = prepare(
        destination, lengths, hidden_new, kv_cache, key_weight, value_weight, count, early
    )
    early_got = [send(block, shift) for block, shift in zip(blocks, early)]
    got = lax.ppermute(other, "tp", [(0, 1), (1, 0)])
    moved, mixed, small, *late_blocks = attend(
        kv_cache,
        queries,
        own,
        got,
        key_gain[None, :],
        lengths,
        destination,
        count,
        late,
    )
    late_got = [send(block, shift) for block, shift in zip(late_blocks, late)]
    small_got = lax.all_to_all(small, "inst", 0, 0, tiled=True)
    moved, windows = land(early_got, moved)
    attended, moved = settle(mixed, small_got, windows, moved, queries.shape, group, count, early)
    return attended, finish(late_got, small_got, moved, steps, count, late)


def solution(mesh):
    return jax.shard_map(
        local,
        mesh=mesh,
        in_specs=(
            P(None, ("group", "inst"), "tp"),
            P(None, ("group", "inst"), "tp"),
            P(("group", "inst"), None, None, "tp"),
            P(("group", "inst")),
            P(("group", "inst")),
            P("tp", None),
            P("tp", None),
            P(),
        ),
        out_specs=(P(None, ("group", "inst"), "tp"), P(("group", "inst"), None, None, "tp")),
        check_vma=False,
    )
```
